32 devices in a mesh: dp: 8 (over z, y), mp: 4 (over x, core).
Axes of the slice: x: 2, y: 2, z: 4, core: 2. Of those that a mesh axis runs over, the one named last changes fastest.
Arguments:
- inputs: bfloat16 [16, 1024, 768], P('dp', 'mp'), may hold values from -6 to 6
- cotangent: bfloat16 [16, 1024, 768], P('dp', 'mp'), may hold values from -6 to 6
- lengths: int32 [16], P('dp'), may hold values from 64 to 1024, as said below
- attn_weights: float32 [4, 768, 768], P(None, 'dp', 'mp'), may hold values from -0.57735027 to 0.57735027
- attn_first: float32 [4, 768, 768], P(None, 'dp', 'mp'), may hold values from -0.00024414062 to 0.00024414062
- attn_second: float32 [4, 768, 768], P(None, 'dp', 'mp'), may hold values from 1.4124676e-10 to 5.6498706e-10
- ffn_weights: float32 [2, 768, 3072], P(None, 'dp', 'mp'), may hold values from -0.5412659 to 0.5412659
- ffn_first: float32 [2, 768, 3072], P(None, 'dp', 'mp'), may hold values from -0.00024414062 to 0.00024414062
- ffn_second: float32 [2, 768, 3072], P(None, 'dp', 'mp'), may hold values from 1.4124676e-10 to 5.6498706e-10
- norm_gains: float32 [2, 768], P(None, 'dp'), may hold values from 0.38 to 2.6
- gain_first: float32 [2, 768], P(None, 'dp'), may hold values from -0.0007324219 to 0.0007324219
- gain_second: float32 [2, 768], P(None, 'dp'), may hold values from 1.2712209e-09 to 5.0848836e-09
- bias_table: float32 [12, 32], replicated, may hold values from -4 to 4
- table_first: float32 [12, 32], replicated, may hold values from -0.0007324219 to 0.0007324219
- table_second: float32 [12, 32], replicated, may hold values from 1.2712209e-10 to 5.0848836e-10
Outputs:
- block_out: bfloat16 [16, 1024, 768], P('dp', 'mp')
- input_grad: bfloat16 [16, 1024, 768], P('dp', 'mp')
- attn_grads: float32 [4, 768, 768], P(None, 'dp', 'mp')
- ffn_grads: float32 [2, 768, 3072], P(None, 'dp', 'mp')
- gain_grads: float32 [2, 768], P(None, 'dp')
- table_grads: float32 [12, 32], replicated
- grad_norm: float32 [], replicated
- attn_new: float32 [4, 768, 768], P(None, 'dp', 'mp')
- attn_first_new: float32 [4, 768, 768], P(None, 'dp', 'mp')
- attn_second_new: float32 [4, 768, 768], P(None, 'dp', 'mp')
- ffn_new: float32 [2, 768, 3072], P(None, 'dp', 'mp')
- ffn_first_new: float32 [2, 768, 3072], P(None, 'dp', 'mp')
- ffn_second_new: float32 [2, 768, 3072], P(None, 'dp', 'mp')
- gain_new: float32 [2, 768], P(None, 'dp')
- gain_first_new: float32 [2, 768], P(None, 'dp')
- gain_second_new: float32 [2, 768], P(None, 'dp')
- table_new: float32 [12, 32], replicated
- table_first_new: float32 [12, 32], replicated
- table_second_new: float32 [12, 32], replicated
The draws below stay inside these ranges and needn't reach their ends.
Inputs may be any that keep to these rules, and one draw needn't show every extreme that they name: In each group of 2 sequences held by one index of dp, one has exactly 1024 real tokens; a sequence's first lengths positions are real and the rest is padding.
All inputs are finite; a program needn't handle non-finite values.
Results may differ from the reference program's by a relative error of at most 0.014.
The reference program's roundings to bfloat16 on the way count: a program that leaves them out, or rounds other values in their place, can miss the bound.
Values may be sent and summed in bfloat16 or wider, within the bound.
No kernel may reach another device: no remote copies, remote signals or barrier semaphores. Data moves between devices by JAX's collectives and lax.ppermute only.
A program may use at most 192 MiB of HBM per device.

```python
import math
import jax
import jax.numpy as jnp
from jax import lax

D = 768
H = 12
DH = 64
FF = 3072
NB = 32
SEQ = 1024
SEQS = 2
MIN_LEN = 64
STEP = 10
SEQUENCES = 16
PARAMS = 7079808


def draw_lengths(key, part):
    key = jax.random.fold_in(key, 1)
    first_key, second_key = jax.random.split(key)
    groups = SEQUENCES // SEQS
    drawn_len = jax.random.randint(first_key, (groups, SEQS), MIN_LEN, SEQ + 1)
    chosen = jax.random.randint(second_key, (groups, 1), 0, SEQS)
    slot_ids = jnp.arange(SEQS)[None, :]
    return jnp.where(slot_ids == chosen, SEQ, drawn_len).astype(jnp.int32).reshape(SEQUENCES)


def draw_attn_weights(key, part):
    key = jax.random.fold_in(key, 2)
    samples = jnp.clip(jax.random.normal(key, (4, D, H * DH), jnp.float32), -4.0, 4.0)
    fan_ins = jnp.array([4.0 * D, 4.0 * D, 1.0 * D, H * DH / 16.0], jnp.float32)
    return samples * (fan_ins ** (-0.5))[:, None, None]


def draw_ffn_weights(key, part):
    key = jax.random.fold_in(key, 3)
    sample_key, scale_key = jax.random.split(key)
    position = jnp.arange(FF, dtype=jnp.float32) / (FF - 1)
    rising = 0.6 * 3.0 ** position
    samples = jnp.clip(jax.random.normal(sample_key, (2, D, FF), jnp.float32), -4.0, 4.0)
    jitter = jax.random.uniform(scale_key, (FF,), jnp.float32, 0.8, 1.25)
    fan_ins = jnp.array([1.0 * D, 1.0 * FF], jnp.float32)
    return samples * (fan_ins ** (-0.5))[:, None, None] * (rising * jitter)[None, None, :]


def draw_norm_gains(key, part):
    key = jax.random.fold_in(key, 4)
    position = jnp.arange(D, dtype=jnp.float32) / (D - 1)
    rising = 0.6 * 3.0 ** position
    jitter = jax.random.uniform(key, (2, D), jnp.float32, 0.85, 1.15)
    return rising[None, :] * jitter


def level_of(key, shape, pieces, smallest, high):
    def one(dim, parts):
        heights = jax.random.uniform(jax.random.fold_in(jax.random.fold_in(key, 6), dim), (parts,), jnp.float32, smallest / len(pieces), high / len(pieces))
        return jnp.repeat(jnp.exp(heights), shape[dim] // parts).reshape((-1,) + (1,) * (len(shape) - dim - 1))

    loudness = one(*pieces[0])
    for cut in pieces[1:]:
        loudness = loudness * one(*cut)
    return loudness


def gaussian(stream_key, extent, scale, limit, shards=(), kind=jnp.bfloat16):
    values = jax.random.normal(stream_key, extent, jnp.float32) * scale
    if len(shards) > 0:
        values = level_of(stream_key, extent, shards, -0.22, 0.18) * values
    return jnp.clip(values, min=-limit, max=limit).astype(kind)


def setup_inputs(seed: int = 0) -> dict:
    arg_keys = jax.random.split(jax.random.key(seed), 16)
    return {
        "inputs": gaussian(arg_keys[0], (SEQUENCES, SEQ, D), 1.0, 6.0, ((0, 8), (1, 4))),
        "cotangent": gaussian(arg_keys[1], (SEQUENCES, SEQ, D), 1.0, 6.0, ((0, 8), (1, 4))),
        "lengths": draw_lengths(jax.random.fold_in(arg_keys[15], 71), 0),
        "attn_weights": draw_attn_weights(jax.random.fold_in(arg_keys[15], 71), 0),
        "attn_first": gaussian(arg_keys[4], (4, D, H * DH), (0.11 * PARAMS ** -0.5), 0.00024414062, ((1, 8), (2, 4)), jnp.float32),
        "attn_second": jnp.clip(jnp.exp(math.log(5.649870571389215e-10) - 1.3862944 * jax.random.uniform(arg_keys[5], (4, D, H * DH), jnp.float32) ** level_of(arg_keys[5], (4, D, H * DH), ((1, 8), (2, 4)), -0.2, 0.2)), 1.4124676428473038e-10, 5.649870571389215e-10),
        "ffn_weights": draw_ffn_weights(jax.random.fold_in(arg_keys[15], 71), 0),
        "ffn_first": gaussian(arg_keys[7], (2, D, FF), (0.11 * PARAMS ** -0.5), 0.00024414062, ((1, 8), (2, 4)), jnp.float32),
        "ffn_second": jnp.clip(jnp.exp(math.log(5.649870571389215e-10) - 1.3862944 * jax.random.uniform(arg_keys[8], (2, D, FF), jnp.float32) ** level_of(arg_keys[8], (2, D, FF), ((1, 8), (2, 4)), -0.2, 0.2)), 1.4124676428473038e-10, 5.649870571389215e-10),
        "norm_gains": draw_norm_gains(jax.random.fold_in(arg_keys[15], 71), 0),
        "gain_first": gaussian(arg_keys[10], (2, D), (0.33 * PARAMS ** -0.5), 0.0007324219, ((1, 8),), jnp.float32),
        "gain_second": jnp.clip(jnp.exp(math.log(5.084883625272596e-09) - 1.3862944 * jax.random.uniform(arg_keys[11], (2, D), jnp.float32) ** level_of(arg_keys[11], (2, D), ((1, 8),), -0.2, 0.2)), 1.271220906318149e-09, 5.084883625272596e-09),
        "bias_table": gaussian(arg_keys[12], (H, NB), 1.0, 4.0, (), jnp.float32),
        "table_first": gaussian(arg_keys[13], (H, NB), (0.33 * PARAMS ** -0.5), 0.0007324219, (), jnp.float32),
        "table_second": jnp.clip(jnp.exp(jax.random.uniform(arg_keys[14], (H, NB), jnp.float32, math.log(1.271220906318149e-10), math.log(5.084883625272596e-10))), 1.271220906318149e-10, 5.084883625272596e-10),
    }


@jax.custom_vjp
def low(v):
    return lax.optimization_barrier(v.astype(jnp.bfloat16)).astype(jnp.float32)

@jax.custom_vjp
def low_back(v):
    return v

def low_keep(v):
    return (low(v), None)

def low_pass(kept, grad):
    return (grad,)

def back_keep(v):
    return (v, None)

def back_low(kept, grad):
    return (low(grad),)
low.defvjp(low_keep, low_pass)
low_back.defvjp(back_keep, back_low)
norm_eps = 1e-06
beta_one = 0.9
beta_two = 0.999
adam_eps = 1e-08
matrix_decay = 0.01
rate_matrix = 0.05
rate_small = 0.4
clip_level = 1.0

def round_both(tensor):
    return low(low_back(tensor))

def bucket_of(offset):
    distance = jnp.abs(offset)
    coarse = jnp.full(offset.shape, 8, jnp.int32)
    for level_bit in range(1, 8):
        coarse = coarse + (distance * distance >= 64 * 2 ** level_bit).astype(jnp.int32)
    inside = jnp.where(distance < 8, distance, coarse)
    return inside + jnp.where(offset > 0, 16, 0).astype(jnp.int32)

def rms_scale(rows_in, gain_row):
    inverse = lax.rsqrt(lax.optimization_barrier(jnp.mean(rows_in * rows_in, axis=-1, keepdims=True)) + norm_eps)
    return rows_in * inverse * gain_row

def adam_step(weight, first_old, second_old, gradient, step_rate, weight_decay):
    first_new = beta_one * first_old + (1.0 - beta_one) * gradient
    second_new = beta_two * second_old + (1.0 - beta_two) * gradient * gradient
    first_hat = first_new / (1.0 - beta_one ** STEP)
    second_hat = second_new / (1.0 - beta_two ** STEP)
    weight_new = weight - step_rate * (first_hat / (jnp.sqrt(second_hat) + adam_eps) + weight_decay * weight)
    return (weight_new, first_new, second_new)

def attend_one(queries, key_rows, value_rows, length, bias_full):
    valid_keys = (jnp.arange(SEQ, dtype=jnp.int32) < length)[None, None, :]
    scores = low_back(jnp.einsum('qhd,khd->hqk', queries, key_rows, precision=lax.Precision.HIGHEST)) + bias_full
    scores = jnp.where(valid_keys, scores, -1e+30)
    row_max = lax.optimization_barrier(jnp.max(scores, axis=-1, keepdims=True))
    exp_terms = jnp.exp(scores - row_max)
    attn_prob = low(exp_terms / lax.optimization_barrier(jnp.sum(exp_terms, axis=-1, keepdims=True)))
    return round_both(jnp.einsum('hqk,khd->qhd', attn_prob, value_rows, precision=lax.Precision.HIGHEST))

def layer_forward(rows_in, attn_var, ffn_var, gain_var, table_var, seq_lengths, buckets):
    attn_low = low(attn_var)
    ffn_low = low(ffn_var)
    gain_low = low(gain_var)
    span_seqs = rows_in.shape[0]
    normed_one = low(rms_scale(rows_in, gain_low[0]))
    projected = round_both(jnp.einsum('srd,cde->csre', normed_one, attn_low[:3], precision=lax.Precision.HIGHEST))
    heads_view = projected.reshape(3, span_seqs, SEQ, H, DH)

    def per_sequence(packet):
        return attend_one(packet[0], packet[1], packet[2], packet[3], table_var[:, buckets])
    context = lax.map(jax.checkpoint(per_sequence), (heads_view[0], heads_view[1], heads_view[2], seq_lengths))
    context = context.reshape(span_seqs, SEQ, H * DH)
    resid_mid = rows_in + low_back(jnp.einsum('sre,de->srd', context, attn_low[3], precision=lax.Precision.HIGHEST))
    normed_two = low(rms_scale(resid_mid, gain_low[1]))
    pre_act = low_back(jnp.einsum('srd,df->srf', normed_two, ffn_low[0], precision=lax.Precision.HIGHEST))
    activated = low(jax.nn.gelu(pre_act, approximate=False))
    return resid_mid + low_back(jnp.einsum('srf,df->srd', activated, ffn_low[1], precision=lax.Precision.HIGHEST))

def reference(inputs, cotangent, lengths, attn_weights, attn_first, attn_second, ffn_weights, ffn_first, ffn_second, norm_gains, gain_first, gain_second, bias_table, table_first, table_second):
    positions = jnp.arange(SEQ, dtype=jnp.int32)
    buckets = bucket_of(positions[None, :] - positions[:, None])
    span_seqs = math.gcd(SEQUENCES, max(1, 4096 // SEQ))
    rounds_count = SEQUENCES // span_seqs
    rows_all = inputs.astype(jnp.float32).reshape(rounds_count, span_seqs, SEQ, D)
    back_all = cotangent.astype(jnp.float32).reshape(rounds_count, span_seqs, SEQ, D)
    length_all = lengths.reshape(rounds_count, span_seqs)
    params = (attn_weights, ffn_weights, norm_gains, bias_table)

    def one_round(totals, packet):
        rows_in, back_in, seq_lengths = packet

        def forward_part(rows_var, attn_var, ffn_var, gain_var, table_var):
            return layer_forward(rows_var, attn_var, ffn_var, gain_var, table_var, seq_lengths, buckets)
        outputs, pull_back = jax.vjp(forward_part, rows_in, *params)
        grads = pull_back(back_in)
        totals = jax.tree.map(jnp.add, totals, tuple(grads[1:]))
        return (totals, (outputs.astype(jnp.bfloat16), grads[0].astype(jnp.bfloat16)))
    start_totals = jax.tree.map(jnp.zeros_like, params)
    totals, (out_rows, grad_rows) = lax.scan(one_round, start_totals, (rows_all, back_all, length_all))
    attn_grads, ffn_grads, gain_grads, table_grads = totals
    grad_norm = jnp.sqrt(jnp.sum(attn_grads * attn_grads) + jnp.sum(ffn_grads * ffn_grads) + jnp.sum(gain_grads * gain_grads) + jnp.sum(table_grads * table_grads))
    clip_factor = jnp.minimum(1.0, clip_level / (grad_norm + 1e-06))
    attn_new, attn_first_new, attn_second_new = adam_step(attn_weights, attn_first, attn_second, attn_grads * clip_factor, rate_matrix, matrix_decay)
    ffn_new, ffn_first_new, ffn_second_new = adam_step(ffn_weights, ffn_first, ffn_second, ffn_grads * clip_factor, rate_matrix, matrix_decay)
    gain_new, gain_first_new, gain_second_new = adam_step(norm_gains, gain_first, gain_second, gain_grads * clip_factor, rate_small, 0.0)
    table_new, table_first_new, table_second_new = adam_step(bias_table, table_first, table_second, table_grads * clip_factor, rate_small, 0.0)
    block_out = out_rows.reshape(SEQUENCES, SEQ, D)
    input_grad = grad_rows.reshape(SEQUENCES, SEQ, D)
    return (block_out, input_grad, attn_grads, ffn_grads, gain_grads, table_grads, grad_norm, attn_new, attn_first_new, attn_second_new, ffn_new, ffn_first_new, ffn_second_new, gain_new, gain_first_new, gain_second_new, table_new, table_first_new, table_second_new)
```

```python
import functools

import jax
import jax.numpy as jnp
from jax import lax
from jax.experimental import pallas as pl
from jax.experimental.pallas import tpu as pltpu
from jax.sharding import PartitionSpec as P

H = 12
DH = 64
NB = 32
STEP = 10
D = 768

norm_eps = 1e-06
beta_one = 0.9
beta_two = 0.999
adam_eps = 1e-08
matrix_decay = 0.01
rate_matrix = 0.05
rate_small = 0.4
clip_level = 1.0

BF = jnp.bfloat16
F32 = jnp.float32
TILE = 128
GROUP = 3
WIDTH = GROUP * DH
NN = (((1,), (0,)), ((), ()))
NT = (((1,), (1,)), ((), ()))

shape_of = jax.ShapeDtypeStruct
in_smem = pl.BlockSpec(memory_space=pltpu.SMEM)
in_any = pl.BlockSpec(memory_space=pl.ANY)
in_vmem = pl.BlockSpec(memory_space=pltpu.VMEM)


def dot(left, right, dims):
    return lax.dot_general(left, right, dims, preferred_element_type=F32)


def params(mib):
    return pltpu.CompilerParams(vmem_limit_bytes=mib << 20)


def cost(flops, bytes_accessed, transcendentals=0):
    return pl.CostEstimate(
        flops=int(flops), bytes_accessed=int(bytes_accessed), transcendentals=int(transcendentals)
    )


def bucket_of(offset):
    distance = jnp.abs(offset)
    coarse = jnp.full(offset.shape, 8, jnp.int32)
    for level_bit in range(1, 8):
        coarse = coarse + (distance * distance >= 64 * 2**level_bit).astype(jnp.int32)
    inside = jnp.where(distance < 8, distance, coarse)
    return inside + jnp.where(offset > 0, 16, 0).astype(jnp.int32)


def adam_step(weight, first_old, second_old, gradient, step_rate, weight_decay):
    first_new = beta_one * first_old + (1.0 - beta_one) * gradient
    second_new = beta_two * second_old + (1.0 - beta_two) * gradient * gradient
    first_hat = first_new / (1.0 - beta_one**STEP)
    second_hat = second_new / (1.0 - beta_two**STEP)
    weight_new = weight - step_rate * (
        first_hat / (jnp.sqrt(second_hat) + adam_eps) + weight_decay * weight
    )
    return (weight_new, first_new, second_new)


def swap_core(v):
    return lax.ppermute(v, "mp", [(i, i ^ 1) for i in range(4)])


def swap_x(v):
    return lax.ppermute(v, "mp", [(i, i ^ 2) for i in range(4)])


def swap_y(v):
    n = lax.axis_size("dp")
    return lax.ppermute(v, "dp", [(i, i ^ 1) for i in range(n)])


def shift_z(v, step):
    n = lax.axis_size("dp")
    return lax.ppermute(v, "dp", [(i, (i + 2 * step) % n) for i in range(n)])


swap = {"x": swap_x, "y": swap_y}


def add_low(a, b):
    return (a.astype(F32) + b.astype(F32)).astype(BF)


def gather_weights(shard, order):
    depth = lax.axis_size("dp") // 2
    blocks = [shard]
    for _ in range(depth - 1):
        blocks.append(shift_z(blocks[-1], 1))
    ring = jnp.stack(blocks)
    second = swap[order[0]](ring)
    third, fourth = swap[order[1]](ring), swap[order[1]](second)
    if order == "xy":
        held = {(0, 0): ring, (1, 0): second, (0, 1): third, (1, 1): fourth}
    else:
        held = {(0, 0): ring, (0, 1): second, (1, 0): third, (1, 1): fourth}
    out = {}
    for (x, y), v in held.items():
        out[0, x, y] = v
        out[1, x, y] = swap_core(v)
    return out


def scatter_sums(held, order):
    depth = lax.axis_size("dp") // 2
    merged = {
        (x, y): add_low(held[0, x, y], swap_core(held[1, x, y])) for x in range(2) for y in range(2)
    }
    if order == "xy":
        half = [add_low(merged[x, 0], swap_y(merged[x, 1])) for x in range(2)]
        ring = add_low(half[0], swap_x(half[1]))
    else:
        half = [add_low(merged[0, y], swap_x(merged[1, y])) for y in range(2)]
        ring = add_low(half[0], swap_y(half[1]))
    total = ring[depth - 1]
    for s in range(depth - 2, 0, -1):
        total = add_low(ring[s], shift_z(total, -1))
    return ring[0].astype(F32) + shift_z(total, -1).astype(F32)


def sum_all(v):
    diagonal = lax.ppermute(v, "mp", [(i, i ^ 3) for i in range(4)])
    v = (v + swap_core(v)) + (swap_x(v) + diagonal)
    n = lax.axis_size("dp")
    if n != 8:
        return lax.psum(v, "dp")
    v = v + swap_y(v)
    far = [lax.ppermute(v, "dp", [(i, i ^ k) for i in range(n)]) for k in (2, 4, 6)]
    return (v + far[0]) + (far[1] + far[2])


def block_views(held, core, x):
    parts = [held[core, x, y] for y in range(2)]
    depth, rows, cols = parts[0].shape
    if rows % 16 == 0:
        return parts
    dp = lax.axis_index("dp")
    both = jnp.stack(parts)
    sides = jnp.take(both, jnp.arange(2) ^ (dp % 2), axis=0)
    lined = jnp.take(sides, (dp // 2 - jnp.arange(depth)) % depth, axis=1)
    return [jnp.transpose(lined, (1, 0, 2, 3)).reshape(1, D, cols)]


def block_shapes(depth, rows, cols):
    if rows % 16 == 0:
        return [shape_of((depth, rows, cols), BF)] * 2
    return [shape_of((1, D, cols), BF)]


def block_parts(outs, depth, rows):
    if rows % 16 == 0:
        return outs
    dp = lax.axis_index("dp")
    lined = jnp.transpose(outs[0].reshape(depth, 2, rows, -1), (1, 0, 2, 3))
    sides = jnp.take(lined, jnp.arange(2) ^ (dp % 2), axis=0)
    turned = jnp.take(sides, (dp // 2 - jnp.arange(depth)) % depth, axis=1)
    return [turned[0], turned[1]]


def piece_copies(refs, whole, place_ref, sems, first_sem, outward=False, cols=None):
    copies = []
    for i, ref in enumerate(refs):
        pieces, rows = ref.shape[0], ref.shape[1]
        for j in range(pieces):
            count = len(copies)
            start = pl.multiple_of(place_ref[4 + count], 16)
            there = whole.at[pl.ds(start, rows), :]
            here = ref.at[j] if cols is None else ref.at[j, :, pl.ds(cols[0], cols[1])]
            pair = (there, here) if outward else (here, there)
            copies.append(pltpu.make_async_copy(*pair, sems.at[first_sem + count]))
    return copies


def bias_kernel(place_ref, table_ref, out_ref):
    block = pl.program_id(0)
    head_base = (place_ref[3] ^ block) * GROUP
    row = lax.broadcasted_iota(jnp.int32, (TILE, TILE), 0)
    col = lax.broadcasted_iota(jnp.int32, (TILE, TILE), 1)
    for h in range(GROUP):
        out_ref[0, h, 0] = jnp.full((TILE, TILE), table_ref[head_base + h, 15], F32)
        out_ref[0, h, 4] = jnp.full((TILE, TILE), table_ref[head_base + h, 31], F32)
    for t in range(1, 4):
        bucket = bucket_of(col - row + (t - 2) * TILE)
        which = {1: range(16), 2: range(32), 3: range(16, 32)}[t]
        for h in range(GROUP):
            tile = jnp.zeros((TILE, TILE), F32)
            for b in which:
                tile = jnp.where(bucket == b, table_ref[head_base + h, b], tile)
            out_ref[0, h, t] = tile


def make_bias(place, table):
    return pl.pallas_call(
        bias_kernel,
        grid=(4,),
        in_specs=[in_smem, in_smem],
        out_specs=pl.BlockSpec((1, GROUP, 5, TILE, TILE), lambda i: (i, 0, 0, 0, 0)),
        out_shape=shape_of((4, GROUP, 5, TILE, TILE), F32),
        compiler_params=params(16),
        cost_estimate=cost(10e6, 4e6),
        name="bias_tiles",
    )(place, table)


def rms_of(v, gain):
    inverse = lax.rsqrt(jnp.mean(v * v, axis=-1, keepdims=True) + norm_eps)
    return v * inverse * gain


def rms_back(v, gain, t):
    inverse = lax.rsqrt(jnp.mean(v * v, axis=-1, keepdims=True) + norm_eps)
    along = jnp.mean(v * gain * t, axis=-1, keepdims=True)
    grad = inverse * gain * t - v * (inverse * inverse * inverse) * along
    return grad, jnp.sum(t * v * inverse, axis=0, keepdims=True)


def project_kernel(n_parts, place_ref, x_ref, gain_ref, *refs):
    w_refs, (q_ref, k_ref, v_ref, whole, sems) = refs[: 2 * n_parts], refs[2 * n_parts :]
    count = sems.shape[0] // 2
    copies = [
        piece_copies(w_refs[b * n_parts : (b + 1) * n_parts], whole.at[b], place_ref, sems, b * count)
        for b in range(2)
    ]
    for group in copies:
        for c in group:
            c.start()
    normed = rms_of(x_ref[...].astype(F32), gain_ref[0:1].astype(F32)).astype(BF)
    for b in range(2):
        for c in copies[b]:
            c.wait()
        out = dot(normed, whole[b, :, 0:640], NN).astype(BF)
        q_ref[b] = out[:, 0:WIDTH]
        k_ref[b] = out[:, WIDTH : 2 * WIDTH]
        v_ref[b] = out[:, 2 * WIDTH : 3 * WIDTH]


def project(place, rows_in, gain_low, blocks):
    rows = rows_in.shape[0]
    n_parts = len(blocks[0])
    pieces = sum(p.shape[0] for p in blocks[0])
    return pl.pallas_call(
        functools.partial(project_kernel, n_parts),
        in_specs=[in_smem, in_vmem, in_vmem] + [in_any] * (2 * n_parts),
        out_specs=[in_vmem] * 3,
        out_shape=[shape_of((2, rows, WIDTH), BF)] * 3,
        scratch_shapes=[pltpu.VMEM((2, D, D), BF), pltpu.SemaphoreType.DMA((2 * pieces,))],
        compiler_params=params(32),
        cost_estimate=cost(2 * 2 * rows * D * 576, 5e6),
        name="project",
    )(place, rows_in, gain_low, *blocks[0], *blocks[1])


def tile_places(place_ref):
    x, core = place_ref[0], place_ref[1]
    mine = [4 * (x if t < 2 else 1 - x) + 2 * core + t % 2 for t in range(4)]
    theirs = [4 * (x if t < 2 else 1 - x) + 2 * (1 - core) + t % 2 for t in range(4)]
    return mine, mine + theirs


def attend_kernel(place_ref, q_ref, ko_ref, vo_ref, kp_ref, vp_ref, bias_ref, ctx_ref, p_ref):
    rows = q_ref.shape[1]
    step = 256
    lane = lax.broadcasted_iota(jnp.int32, (1, 256), 1)
    key = lax.broadcasted_iota(jnp.int32, (1, TILE), 1)
    sub = lax.broadcasted_iota(jnp.int32, (64, 1), 0)
    row_tiles, key_tiles = tile_places(place_ref)
    length = place_ref[2]
    hide = jnp.concatenate([jnp.where(key + TILE * g < length, 0.0, -1e30) for g in key_tiles], 1)
    extra = jnp.where(sub == 0, hide, 0.0).astype(BF)
    keys_t = jnp.concatenate([jnp.concatenate([ko_ref[0].T, kp_ref[0].T], 1), extra], 0)
    values = jnp.concatenate([vo_ref[0], vp_ref[0]], 0)
    queries = jnp.concatenate([q_ref[0], jnp.ones((rows, 64), BF)], 1)
    total = [jnp.zeros((step, WIDTH), F32) for _ in range(rows // step)]
    for h in range(GROUP):
        inside = (lane >= h * DH) & (lane < (h + 1) * DH)
        used = inside | (lane == WIDTH)
        for r in range(rows // step):
            here = jnp.where(used, queries[r * step : (r + 1) * step], jnp.zeros((), BF))
            scores = dot(here, keys_t, NN)
            tiles = []
            for c in range(8):
                bias = []
                for u in range(step // TILE):
                    which = jnp.clip(key_tiles[c] - row_tiles[r * (step // TILE) + u] + 2, 0, 4)
                    bias.append(bias_ref[0, h, which])
                tiles.append(scores[:, c * TILE : (c + 1) * TILE] + jnp.concatenate(bias, 0))
            top = jnp.max(functools.reduce(jnp.maximum, tiles), axis=-1, keepdims=True)
            exps = [jnp.exp(t - top) for t in tiles]
            norm = jnp.sum(functools.reduce(jnp.add, exps), axis=-1, keepdims=True)
            scale = 1.0 / norm
            prob = jnp.concatenate([(e * scale).astype(BF) for e in exps], 1)
            p_ref[0, h, pl.ds(r * step, step), :] = prob
            total[r] = jnp.where(inside[:, :WIDTH], dot(prob, values, NN), total[r])
    for r in range(rows // step):
        ctx_ref[0, pl.ds(r * step, step), :] = total[r].astype(BF)


def attend(place, q, k_own, v_own, k_other, v_other, bias, blocks):
    n, rows = q.shape[0], q.shape[1]
    a, s = blocks
    spec = pl.BlockSpec((1, rows, WIDTH), lambda i: (i, 0, 0))
    return pl.pallas_call(
        attend_kernel,
        grid=(n,),
        in_specs=[in_smem]
        + [spec] * 5
        + [pl.BlockSpec((1, GROUP, 5, TILE, TILE), lambda i: (a + s * i, 0, 0, 0, 0))],
        out_specs=[spec, pl.BlockSpec((1, GROUP, rows, 2 * rows), lambda i: (i, 0, 0, 0))],
        out_shape=[
            shape_of((n, rows, WIDTH), BF),
            shape_of((n, GROUP, rows, 2 * rows), BF),
        ],
        compiler_params=params(40),
        cost_estimate=cost(n * GROUP * rows * 2 * rows * 256 * 4, 10e6, n * GROUP * rows * 2 * rows),
        name="attend",
    )(place, q, k_own, v_own, k_other, v_other, bias)


def middle_kernel(n_parts, place_ref, x_ref, gain_ref, back_ref, ctx_a_ref, ctx_b_ref, *refs):
    w_refs = refs[: 4 * n_parts]
    mid_ref, normed_ref, normed_t_ref, back_t_ref, whole, sems = refs[4 * n_parts :]
    count = sems.shape[0] // 4
    copies = [
        piece_copies(
            w_refs[b * n_parts : (b + 1) * n_parts],
            whole.at[b],
            place_ref,
            sems,
            b * count,
            cols=(512, 256),
        )
        for b in range(4)
    ]
    for group in copies:
        for c in group:
            c.start()
    rows = x_ref.shape[0]
    total = x_ref[...].astype(F32)
    back_t_ref[...] = back_ref[...].T
    blank = jnp.zeros((rows, 64), BF)
    for b in range(4):
        for c in copies[b]:
            c.wait()
        ctx = (ctx_a_ref if b % 2 == 0 else ctx_b_ref)[b // 2]
        total = total + dot(jnp.concatenate([blank, ctx], 1), whole[b], NT)
    mid_ref[...] = total
    normed = rms_of(total, gain_ref[1:2].astype(F32)).astype(BF)
    normed_ref[...] = normed
    normed_t_ref[...] = normed.T


def middle(place, rows_in, gain_low, back, ctx_a, ctx_b, blocks):
    rows = rows_in.shape[0]
    n_parts = len(blocks[0])
    pieces = sum(p.shape[0] for p in blocks[0])
    return pl.pallas_call(
        functools.partial(middle_kernel, n_parts),
        in_specs=[in_smem] + [in_vmem] * 5 + [in_any] * (4 * n_parts),
        out_specs=[in_vmem] * 4,
        out_shape=[
            shape_of((rows, D), F32),
            shape_of((rows, D), BF),
            shape_of((D, rows), BF),
            shape_of((D, rows), BF),
        ],
        scratch_shapes=[pltpu.VMEM((4, D, 256), BF), pltpu.SemaphoreType.DMA((4 * pieces,))],
        compiler_params=params(32),
        cost_estimate=cost(2 * rows * D * D, 8e6),
        name="middle",
    )(place, rows_in, gain_low, back, ctx_a, ctx_b, *[p for b in blocks for p in b])


def feed_kernel(n_parts, place_ref, n_ref, nt_ref, g_ref, gt_ref, acc_in, t_in, *refs):
    wi_refs, wf_refs = refs[: 2 * n_parts], refs[2 * n_parts : 4 * n_parts]
    rest = refs[4 * n_parts :]
    acc_ref, t_ref = rest[:2]
    gi_refs, gf_refs = rest[2 : 2 + 2 * n_parts], rest[2 + 2 * n_parts : 2 + 4 * n_parts]
    wi, wf, gi, gf, sems, out_sems = rest[2 + 4 * n_parts :]
    count = sems.shape[0] // 4
    loads = []
    for b in range(2):
        part = slice(b * n_parts, (b + 1) * n_parts)
        loads.append(
            piece_copies(wi_refs[part], wi.at[b], place_ref, sems, 2 * b * count)
            + piece_copies(wf_refs[part], wf.at[b], place_ref, sems, (2 * b + 1) * count)
        )
    for group in loads:
        for c in group:
            c.start()
    acc_ref[...] = acc_in[...]
    t_ref[...] = t_in[...]
    stores = []
    for b in range(2):
        for c in loads[b]:
            c.wait()

        def hidden(j, _):
            cols = pl.ds(pl.multiple_of(j * 256, 256), 256)
            wi_here, wf_here = wi[b, :, cols], wf[b, :, cols]
            pre = dot(n_ref[...], wi_here, NN)
            grad = dot(g_ref[...], wf_here, NN)
            cdf = 0.5 * (1.0 + lax.erf(pre * 0.7071067811865476))
            active = (pre * cdf).astype(BF)
            density = jnp.exp(pre * pre * -0.5) * 0.3989422804014327
            pre_grad = (grad * (cdf + pre * density)).astype(BF)
            acc_ref[...] += dot(active, wf_here, NT)
            t_ref[...] += dot(pre_grad, wi_here, NT)
            gi[b, :, cols] = dot(nt_ref[...], pre_grad, NN).astype(BF)
            gf[b, :, cols] = dot(gt_ref[...], active, NN).astype(BF)
            return 0

        lax.fori_loop(0, D // 256, hidden, 0)
        part = slice(b * n_parts, (b + 1) * n_parts)
        group = piece_copies(
            gi_refs[part], gi.at[b], place_ref, out_sems, 2 * b * count, outward=True
        ) + piece_copies(
            gf_refs[part], gf.at[b], place_ref, out_sems, (2 * b + 1) * count, outward=True
        )
        for c in group:
            c.start()
        stores.append(group)
    for group in stores:
        for c in group:
            c.wait()


def feed(place, normed, normed_t, back, back_t, acc, t_acc, wi_blocks, wf_blocks, out_shapes):
    rows = normed.shape[0]
    n_parts = len(wi_blocks[0])
    pieces = sum(p.shape[0] for p in wi_blocks[0])
    outs = pl.pallas_call(
        functools.partial(feed_kernel, n_parts),
        in_specs=[in_smem] + [in_vmem] * 6 + [in_any] * (4 * n_parts),
        out_specs=[in_vmem] * 2 + [in_any] * (4 * n_parts),
        out_shape=[shape_of((rows, D), F32)] * 2 + out_shapes * 4,
        scratch_shapes=[pltpu.VMEM((2, D, D), BF)] * 4
        + [pltpu.SemaphoreType.DMA((4 * pieces,))] * 2,
        compiler_params=params(48),
        cost_estimate=cost(2 * 6 * 2 * rows * D * D, 15e6, 4 * rows * D),
        name="feed",
    )(
        place,
        normed,
        normed_t,
        back,
        back_t,
        acc,
        t_acc,
        *[p for b in wi_blocks for p in b],
        *[p for b in wf_blocks for p in b],
    )
    n = n_parts
    groups = [outs[2 + i * n : 2 + (i + 1) * n] for i in range(4)]
    return outs[0], outs[1], groups[0:2], groups[2:4]


def turn_kernel(n_parts, place_ref, mid_ref, acc_ref, t_ref, back_ref, gain_ref, *refs):
    w_refs = refs[: 4 * n_parts]
    out_ref, grad_ref, low_ref, low_t_ref, gain_grad_ref, cg_a_ref, cg_b_ref, whole, sems = refs[
        4 * n_parts :
    ]
    count = sems.shape[0] // 4
    copies = [
        piece_copies(
            w_refs[b * n_parts : (b + 1) * n_parts],
            whole.at[b],
            place_ref,
            sems,
            b * count,
            cols=(512, 256),
        )
        for b in range(4)
    ]
    for group in copies:
        for c in group:
            c.start()
    mid = mid_ref[...]
    out_ref[...] = (mid + acc_ref[...]).astype(BF)
    grad, gain_grad = rms_back(mid, gain_ref[1:2].astype(F32), t_ref[...])
    gain_grad_ref[...] = gain_grad
    grad = back_ref[...].astype(F32) + grad
    grad_ref[...] = grad
    low = grad.astype(BF)
    low_ref[...] = low
    low_t_ref[...] = low.T
    for b in range(4):
        for c in copies[b]:
            c.wait()
        (cg_a_ref if b % 2 == 0 else cg_b_ref)[b // 2] = dot(low, whole[b], NN).astype(BF)[:, 64:]


def turn(place, mid, acc, t_acc, back, gain_low, blocks):
    rows = mid.shape[0]
    n_parts = len(blocks[0])
    pieces = sum(p.shape[0] for p in blocks[0])
    return pl.pallas_call(
        functools.partial(turn_kernel, n_parts),
        in_specs=[in_smem] + [in_vmem] * 5 + [in_any] * (4 * n_parts),
        out_specs=[in_vmem] * 7,
        out_shape=[
            shape_of((rows, D), BF),
            shape_of((rows, D), F32),
            shape_of((rows, D), BF),
            shape_of((D, rows), BF),
            shape_of((1, D), F32),
            shape_of((2, rows, WIDTH), BF),
            shape_of((2, rows, WIDTH), BF),
        ],
        scratch_shapes=[pltpu.VMEM((4, D, 256), BF), pltpu.SemaphoreType.DMA((4 * pieces,))],
        compiler_params=params(40),
        cost_estimate=cost(2 * rows * D * D, 10e6),
        name="turn",
    )(place, mid, acc, t_acc, back, gain_low, *[p for b in blocks for p in b])


def attend_back_kernel(
    place_ref,
    q_ref,
    ko_ref,
    vo_ref,
    kp_ref,
    vp_ref,
    g_ref,
    ctx_ref,
    p_ref,
    dq_ref,
    dko_ref,
    dvo_ref,
    dkp_ref,
    dvp_ref,
    sums_ref,
    ds_ref,
):
    rows = q_ref.shape[1]
    step = 128
    lane = lax.broadcasted_iota(jnp.int32, (1, WIDTH), 1)
    row_tiles, key_tiles = tile_places(place_ref)
    queries, grads = q_ref[0], g_ref[0]
    keys = jnp.concatenate([ko_ref[0], kp_ref[0]], 0)
    values_t = jnp.concatenate([vo_ref[0].T, vp_ref[0].T], 1)
    queries_t, grads_t = queries.T, grads.T
    product = grads.astype(F32) * ctx_ref[0].astype(F32)
    sums_ref[...] = jnp.zeros_like(sums_ref)
    total = [jnp.zeros((step, WIDTH), F32) for _ in range(rows // step)]
    key_grads, value_grads = [], []
    for h in range(GROUP):
        inside = (lane >= h * DH) & (lane < (h + 1) * DH)
        for r in range(rows // step):
            span = slice(r * step, (r + 1) * step)
            here = jnp.where(inside, grads[span], jnp.zeros((), BF))
            prob_grad = dot(here, values_t, NN)
            row_dot = jnp.sum(jnp.where(inside, product[span], 0.0), axis=-1, keepdims=True)
            lows = []
            for c in range(8):
                prob = p_ref[0, h, pl.ds(r * step, step), pl.ds(c * TILE, TILE)].astype(F32)
                dscore = prob * (prob_grad[:, c * TILE : (c + 1) * TILE] - row_dot)
                which = jnp.clip(key_tiles[c] - row_tiles[r] + 2, 0, 4)
                sums_ref[0, h, which] += dscore
                lows.append(dscore.astype(BF))
            low = jnp.concatenate(lows, 1)
            ds_ref[pl.ds(r * step, step), :] = low
            total[r] = jnp.where(inside, dot(low, keys, NN), total[r])
        key_grads.append(dot(queries_t[h * DH : (h + 1) * DH], ds_ref[...], NN))
        value_grads.append(dot(grads_t[h * DH : (h + 1) * DH], p_ref[0, h], NN))
    for r in range(rows // step):
        dq_ref[0, pl.ds(r * step, step), :] = total[r].astype(BF)
    key_grad = jnp.concatenate(key_grads, 0).T
    value_grad = jnp.concatenate(value_grads, 0).T
    dko_ref[0], dkp_ref[0] = key_grad[:rows], key_grad[rows:].astype(BF)
    dvo_ref[0], dvp_ref[0] = value_grad[:rows], value_grad[rows:].astype(BF)


def attend_back(place, q, k_own, v_own, k_other, v_other, grads, ctx, prob):
    n, rows = q.shape[0], q.shape[1]
    spec = pl.BlockSpec((1, rows, WIDTH), lambda i: (i, 0, 0))
    return pl.pallas_call(
        attend_back_kernel,
        grid=(n,),
        in_specs=[in_smem]
        + [spec] * 7
        + [pl.BlockSpec((1, GROUP, rows, 2 * rows), lambda i: (i, 0, 0, 0))],
        out_specs=[spec] * 5 + [pl.BlockSpec((1, GROUP, 5, TILE, TILE), lambda i: (i, 0, 0, 0, 0))],
        out_shape=[
            shape_of((n, rows, WIDTH), BF),
            shape_of((n, rows, WIDTH), F32),
            shape_of((n, rows, WIDTH), F32),
            shape_of((n, rows, WIDTH), BF),
            shape_of((n, rows, WIDTH), BF),
            shape_of((n, GROUP, 5, TILE, TILE), F32),
        ],
        scratch_shapes=[pltpu.VMEM((rows, 2 * rows), BF)],
        compiler_params=params(44),
        cost_estimate=cost(n * GROUP * rows * 2 * rows * 256 * 8, 12e6),
        name="attend_back",
    )(place, q, k_own, v_own, k_other, v_other, grads, ctx, prob)


def bucket_kernel(sums_ref, out_ref):
    row = lax.broadcasted_iota(jnp.int32, (TILE, TILE), 0)
    col = lax.broadcasted_iota(jnp.int32, (TILE, TILE), 1)
    buckets = {t: bucket_of(col - row + (t - 2) * TILE) for t in range(1, 4)}
    for h in range(GROUP):
        for b in range(NB):
            total = jnp.zeros((TILE, TILE), F32)
            if b == 15:
                total = sums_ref[0, h, 0]
            if b == 31:
                total = sums_ref[0, h, 4]
            for t in (1, 2) if b < 16 else (2, 3):
                total = total + jnp.where(buckets[t] == b, sums_ref[0, h, t], 0.0)
            out_ref[0, h, pl.ds(b, 1), :] = jnp.sum(total, axis=0, keepdims=True)


def bucket_sums(sums):
    n = sums.shape[0]
    return pl.pallas_call(
        bucket_kernel,
        grid=(n,),
        in_specs=[pl.BlockSpec((1, GROUP, 5, TILE, TILE), lambda i: (i, 0, 0, 0, 0))],
        out_specs=pl.BlockSpec((1, GROUP, NB, TILE), lambda i: (i, 0, 0, 0)),
        out_shape=shape_of((n, GROUP, NB, TILE), F32),
        compiler_params=params(16),
        cost_estimate=cost(n * 8e6, n * 1e6),
        name="bucket_sums",
    )(sums)


def project_back_kernel(n_parts, place_ref, x_ref, gain_ref, low_t_ref, acc_in, ctx_ref, dq_ref, *refs):
    dko_ref, dkp_ref, dvo_ref, dvp_ref = refs[:4]
    w_refs = refs[4 : 4 + 2 * n_parts]
    rest = refs[4 + 2 * n_parts :]
    acc_ref, g_refs = rest[0], rest[1 : 1 + 2 * n_parts]
    whole, grad, sems, out_sems = rest[1 + 2 * n_parts :]
    count = sems.shape[0] // 2
    copies = [
        piece_copies(w_refs[b * n_parts : (b + 1) * n_parts], whole.at[b], place_ref, sems, b * count)
        for b in range(2)
    ]
    for group in copies:
        for c in group:
            c.start()
    normed = rms_of(x_ref[...].astype(F32), gain_ref[0:1].astype(F32)).astype(BF)
    normed_t = normed.T
    low_t = low_t_ref[...]
    total = acc_in[...]
    stores = []
    for b in range(2):
        dk = (dko_ref[b] + dkp_ref[b].astype(F32)).astype(BF)
        dv = (dvo_ref[b] + dvp_ref[b].astype(F32)).astype(BF)
        heads = jnp.concatenate([dq_ref[b], dk, dv], 1)
        out = dot(normed_t, heads, NN).astype(BF)
        last = dot(low_t, ctx_ref[b], NN).astype(BF)
        grad[b] = jnp.concatenate([out, last], 1)
        group = piece_copies(
            g_refs[b * n_parts : (b + 1) * n_parts],
            grad.at[b],
            place_ref,
            out_sems,
            b * count,
            outward=True,
        )
        for c in group:
            c.start()
        stores.append(group)
        for c in copies[b]:
            c.wait()
        total = total + dot(heads, whole[b, :, 0:576], NT)
    acc_ref[...] = total
    for group in stores:
        for c in group:
            c.wait()


def project_back(place, rows_in, gain_low, low_t, acc, ctx, dq, dk, dv, blocks, out_shapes):
    rows = rows_in.shape[0]
    n_parts = len(blocks[0])
    pieces = sum(p.shape[0] for p in blocks[0])
    outs = pl.pallas_call(
        functools.partial(project_back_kernel, n_parts),
        in_specs=[in_smem] + [in_vmem] * 10 + [in_any] * (2 * n_parts),
        out_specs=[in_vmem] + [in_any] * (2 * n_parts),
        out_shape=[shape_of((rows, D), F32)] + out_shapes * 2,
        scratch_shapes=[pltpu.VMEM((2, D, D), BF)] * 2
        + [pltpu.SemaphoreType.DMA((2 * pieces,))] * 2,
        compiler_params=params(40),
        cost_estimate=cost(2 * 2 * 2 * rows * D * D, 10e6),
        name="project_back",
    )(place, rows_in, gain_low, low_t, acc, ctx, dq, *dk, *dv, *blocks[0], *blocks[1])
    return outs[0], [outs[1 : 1 + n_parts], outs[1 + n_parts :]]


def finish_kernel(x_ref, gain_ref, t_ref, mid_grad_ref, out_ref, gain_grad_ref):
    grad, gain_grad = rms_back(x_ref[...].astype(F32), gain_ref[0:1].astype(F32), t_ref[...])
    out_ref[...] = (mid_grad_ref[...] + grad).astype(BF)
    gain_grad_ref[...] = gain_grad


def finish(rows_in, gain_low, t_acc, mid_grad):
    rows = rows_in.shape[0]
    return pl.pallas_call(
        finish_kernel,
        in_specs=[in_vmem] * 4,
        out_specs=[in_vmem] * 2,
        out_shape=[shape_of((rows, D), BF), shape_of((1, D), F32)],
        compiler_params=params(24),
        cost_estimate=cost(rows * D * 12, 6e6),
        name="finish",
    )(rows_in, gain_low, t_acc, mid_grad)


def per_device(
    inputs,
    cotangent,
    lengths,
    attn_weights,
    attn_first,
    attn_second,
    ffn_weights,
    ffn_first,
    ffn_second,
    norm_gains,
    gain_first,
    gain_second,
    bias_table,
    table_first,
    table_second,
):
    assert lax.axis_size("mp") == 4 and inputs.shape[0] == 2
    depth = lax.axis_size("dp") // 2
    shard_rows = ffn_weights.shape[1]
    mp, dp = lax.axis_index("mp"), lax.axis_index("dp")
    x, core = mp // 2, mp % 2
    part = inputs.shape[1]

    def regroup(v):
        mine = lax.dynamic_index_in_dim(v, x, 0, keepdims=False)
        other = lax.dynamic_index_in_dim(v, 1 - x, 0, keepdims=False)
        return jnp.concatenate([mine, swap_x(other)], 0)

    def ungroup(v):
        mine, other = v[:part], swap_x(v[part:])
        low, high = jnp.where(x == 0, mine, other), jnp.where(x == 0, other, mine)
        return jnp.stack([low, high])

    length = lax.dynamic_index_in_dim(lengths, x, 0, keepdims=False)
    starts = [
        shard_rows * (((dp // 2 - s) % depth) * 2 + ((dp % 2) ^ y))
        for y in range(2)
        for s in range(depth)
    ]
    if shard_rows % 16:
        starts = [jnp.zeros((), jnp.int32)]
    place = jnp.stack([v.astype(jnp.int32) for v in [x, core, length, mp] + starts])

    gain_low = lax.all_gather(norm_gains.astype(BF), "dp", axis=1, tiled=True)
    rows_in = regroup(inputs)
    attn_low = jnp.transpose(attn_weights.astype(BF), (1, 0, 2)).reshape(shard_rows, D)
    ffn_low = ffn_weights.astype(BF)
    attn_held = gather_weights(attn_low, "xy")
    wi_held = gather_weights(ffn_low[0], "yx")
    wf_held = gather_weights(ffn_low[1], "xy")
    back = regroup(cotangent)
    bias = make_bias(place, bias_table)

    attn_blocks = {(c, xx): block_views(attn_held, c, xx) for c in range(2) for xx in range(2)}
    wi_blocks = {(c, xx): block_views(wi_held, c, xx) for c in range(2) for xx in range(2)}
    wf_blocks = {(c, xx): block_views(wf_held, c, xx) for c in range(2) for xx in range(2)}
    by_core = [[(c, 0), (c, 1)] for c in range(2)]
    every = [(0, 0), (1, 0), (0, 1), (1, 1)]
    out_shapes = block_shapes(depth, shard_rows, D)

    q, k, v = {}, {}, {}
    for c in range(2):
        q[c], k[c], v[c] = project(place, rows_in, gain_low, [attn_blocks[b] for b in by_core[c]])
    k_other = {1 - c: swap_core(k[c]) for c in range(2)}
    v_other = {1 - c: swap_core(v[c]) for c in range(2)}
    ctx, prob = {}, {}
    for c in (1, 0):
        ctx[c], prob[c] = attend(place, q[c], k[c], v[c], k_other[c], v_other[c], bias, (c, 2))
    mid, normed_two, normed_two_t, back_t = middle(
        place, rows_in, gain_low, back, ctx[0], ctx[1], [attn_blocks[b] for b in every]
    )
    acc = jnp.zeros(mid.shape, F32)
    t_acc = jnp.zeros(mid.shape, F32)
    wi_grads, wf_grads = {}, {}
    for c in range(2):
        acc, t_acc, gi, gf = feed(
            place,
            normed_two,
            normed_two_t,
            back,
            back_t,
            acc,
            t_acc,
            [wi_blocks[b] for b in by_core[c]],
            [wf_blocks[b] for b in by_core[c]],
            out_shapes,
        )
        for xx in range(2):
            for held, outs in ((wi_grads, gi), (wf_grads, gf)):
                held[c, xx, 0], held[c, xx, 1] = block_parts(outs[xx], depth, shard_rows)
    out_rows, mid_grad, mid_low, mid_low_t, gain_two_grad, cg_a, cg_b = turn(
        place, mid, acc, t_acc, back, gain_low, [attn_blocks[b] for b in every]
    )
    block_out = ungroup(out_rows)
    wi_total = scatter_sums(wi_grads, "yx")
    wf_total = scatter_sums(wf_grads, "xy")
    cg = {0: cg_a, 1: cg_b}
    dq, dko, dvo, dkp, dvp, sums = {}, {}, {}, {}, {}, {}
    for c in (1, 0):
        dq[c], dko[c], dvo[c], dkp[c], dvp[c], sums[c] = attend_back(
            place, q[c], k[c], v[c], k_other[c], v_other[c], cg[c], ctx[c], prob[c]
        )
    t_one = jnp.zeros(mid.shape, F32)
    attn_grads = {}
    for c in (1, 0):
        t_one, outs = project_back(
            place,
            rows_in,
            gain_low,
            mid_low_t,
            t_one,
            ctx[c],
            dq[c],
            (dko[c], swap_core(dkp[1 - c])),
            (dvo[c], swap_core(dvp[1 - c])),
            [attn_blocks[b] for b in by_core[c]],
            out_shapes,
        )
        for xx in range(2):
            attn_grads[c, xx, 0], attn_grads[c, xx, 1] = block_parts(outs[xx], depth, shard_rows)
    attn_total = scatter_sums(attn_grads, "xy")
    in_rows, gain_one_grad = finish(rows_in, gain_low, t_one, mid_grad)
    input_grad = ungroup(in_rows)

    lines = [bucket_sums(sums[c]) for c in range(2)]
    by_block = jnp.stack([lines[0][0], lines[1][0], lines[0][1], lines[1][1]])
    table_part = jnp.take(jnp.sum(by_block, -1), jnp.arange(4) ^ mp, axis=0).reshape(H * NB)
    small = jnp.concatenate([gain_one_grad[0], gain_two_grad[0], table_part])
    small = sum_all(small.reshape(-1, TILE)).reshape(-1)
    gain_total = small[: 2 * D].reshape(2, D)
    table_grads = small[2 * D :].reshape(H, NB)
    gain_cols = norm_gains.shape[1]
    gain_grads = lax.dynamic_slice_in_dim(gain_total, dp * gain_cols, gain_cols, 1)

    attn_reduced = jnp.transpose(attn_total.reshape(shard_rows, 4, WIDTH), (1, 0, 2))
    ffn_reduced = jnp.stack([wi_total, wf_total])
    squares = jnp.sum(attn_reduced * attn_reduced) + jnp.sum(ffn_reduced * ffn_reduced)
    squares = sum_all(jnp.full((8, TILE), squares))[0, 0]
    grad_norm = jnp.sqrt(squares + jnp.sum(small * small))
    clip_factor = jnp.minimum(1.0, clip_level / (grad_norm + 1e-06))
    attn_new, attn_first_new, attn_second_new = adam_step(
        attn_weights, attn_first, attn_second, attn_reduced * clip_factor, rate_matrix, matrix_decay
    )
    ffn_new, ffn_first_new, ffn_second_new = adam_step(
        ffn_weights, ffn_first, ffn_second, ffn_reduced * clip_factor, rate_matrix, matrix_decay
    )
    gain_new, gain_first_new, gain_second_new = adam_step(
        norm_gains, gain_first, gain_second, gain_grads * clip_factor, rate_small, 0.0
    )
    table_new, table_first_new, table_second_new = adam_step(
        bias_table, table_first, table_second, table_grads * clip_factor, rate_small, 0.0
    )
    return (
        block_out,
        input_grad,
        attn_reduced,
        ffn_reduced,
        gain_grads,
        table_grads,
        grad_norm,
        attn_new,
        attn_first_new,
        attn_second_new,
        ffn_new,
        ffn_first_new,
        ffn_second_new,
        gain_new,
        gain_first_new,
        gain_second_new,
        table_new,
        table_first_new,
        table_second_new,
    )


def solution(mesh):
    placed = (
        P("dp", "mp", None),
        P("dp", "mp", None),
        P("dp"),
        P(None, "dp", "mp"),
        P(None, "dp", "mp"),
        P(None, "dp", "mp"),
        P(None, "dp", "mp"),
        P(None, "dp", "mp"),
        P(None, "dp", "mp"),
        P(None, "dp"),
        P(None, "dp"),
        P(None, "dp"),
        P(),
        P(),
        P(),
    )
    return jax.shard_map(
        per_device,
        mesh=mesh,
        in_specs=placed,
        out_specs=(
            P("dp", "mp", None),
            P("dp", "mp", None),
            P(None, "dp", "mp"),
            P(None, "dp", "mp"),
            P(None, "dp"),
            P(),
            P(),
            P(None, "dp", "mp"),
            P(None, "dp", "mp"),
            P(None, "dp", "mp"),
            P(None, "dp", "mp"),
            P(None, "dp", "mp"),
            P(None, "dp", "mp"),
            P(None, "dp"),
            P(None, "dp"),
            P(None, "dp"),
            P(),
            P(),
            P(),
        ),
        check_vma=False,
    )
```

```python
import functools

import jax
import jax.numpy as jnp
from jax import lax
from jax.experimental import pallas as pl
from jax.experimental.pallas import tpu as pltpu
from jax.sharding import PartitionSpec as P

H = 12
DH = 64
NB = 32
STEP = 10
D = 768

norm_eps = 1e-06
beta_one = 0.9
beta_two = 0.999
adam_eps = 1e-08
matrix_decay = 0.01
rate_matrix = 0.05
rate_small = 0.4
clip_level = 1.0

BF = jnp.bfloat16
F32 = jnp.float32
TILE = 128
GROUP = 3
WIDTH = GROUP * DH
NN = (((1,), (0,)), ((), ()))
NT = (((1,), (1,)), ((), ()))

shape_of = jax.ShapeDtypeStruct
in_smem = pl.BlockSpec(memory_space=pltpu.SMEM)
in_hbm = pl.BlockSpec(memory_space=pltpu.HBM)
in_vmem = pl.BlockSpec(memory_space=pltpu.VMEM)


def dot(left, right, dims):
    return lax.dot_general(left, right, dims, preferred_element_type=F32)


def params(mib):
    return pltpu.CompilerParams(vmem_limit_bytes=mib << 20)


def cost(flops, bytes_accessed, transcendentals=0):
    return pl.CostEstimate(flops=1000, bytes_accessed=1000, transcendentals=0)


def bucket_of(offset):
    distance = jnp.abs(offset)
    coarse = jnp.full(offset.shape, 8, jnp.int32)
    for level_bit in range(1, 8):
        coarse = coarse + (distance * distance >= 64 * 2**level_bit).astype(jnp.int32)
    inside = jnp.where(distance < 8, distance, coarse)
    return inside + jnp.where(offset > 0, 16, 0).astype(jnp.int32)


def adam_step(weight, first_old, second_old, gradient, step_rate, weight_decay):
    first_new = beta_one * first_old + (1.0 - beta_one) * gradient
    second_new = beta_two * second_old + (1.0 - beta_two) * gradient * gradient
    first_hat = first_new / (1.0 - beta_one**STEP)
    second_hat = second_new / (1.0 - beta_two**STEP)
    weight_new = weight - step_rate * (
        first_hat / (jnp.sqrt(second_hat) + adam_eps) + weight_decay * weight
    )
    return (weight_new, first_new, second_new)


def swap_core(v):
    return lax.ppermute(v, "mp", [(i, i ^ 1) for i in range(4)])


def swap_x(v):
    return lax.ppermute(v, "mp", [(i, i ^ 2) for i in range(4)])


def swap_y(v):
    n = lax.axis_size("dp")
    return lax.ppermute(v, "dp", [(i, i ^ 1) for i in range(n)])


def swap_z(v, k):
    n = lax.axis_size("dp")
    return lax.ppermute(v, "dp", [(i, i ^ (2 * k)) for i in range(n)])


def add_low(a, b):
    return (a.astype(F32) + b.astype(F32)).astype(BF)


def fence(*values):
    return lax.optimization_barrier(values)


def sum_all(v):
    diagonal = lax.ppermute(v, "mp", [(i, i ^ 3) for i in range(4)])
    v = (v + swap_core(v)) + (swap_x(v) + diagonal)
    n = lax.axis_size("dp")
    if n != 8:
        return lax.psum(v, "dp")
    v = v + swap_y(v)
    far = [swap_z(v, k) for k in (1, 2, 3)]
    return (v + far[0]) + (far[1] + far[2])


def spread_gains(gains):
    count = gains.shape[1]
    start = lax.axis_index("dp") * count
    return lax.dynamic_update_slice(jnp.zeros((2, D), BF), gains.astype(BF), (0, start))


def join_gains(wide, step):
    n = lax.axis_size("dp")
    return wide + lax.ppermute(wide, "dp", [(i, i ^ step) for i in range(n)])


def block_views(by_y):
    rows, cols = by_y[0][0].shape[1:]
    if rows % 16 == 0:
        return [v for parts in by_y for v in parts]
    dp = lax.axis_index("dp")
    both = jnp.stack([jnp.concatenate(parts, 0) for parts in by_y])
    depth = both.shape[1]
    sides = jnp.take(both, jnp.arange(2) ^ (dp % 2), axis=0)
    lined = jnp.take(sides, jnp.arange(depth) ^ (dp // 2), axis=1)
    return [jnp.transpose(lined, (1, 0, 2, 3)).reshape(1, D, cols)]


def block_shapes(depth, rows, cols):
    if rows % 16 == 0:
        return [shape_of((depth, rows, cols), BF)] * 2
    return [shape_of((1, D, cols), BF)]


def block_parts(outs, depth, rows):
    if rows % 16 == 0:
        return outs
    dp = lax.axis_index("dp")
    lined = jnp.transpose(outs[0].reshape(depth, 2, rows, -1), (1, 0, 2, 3))
    sides = jnp.take(lined, jnp.arange(2) ^ (dp % 2), axis=0)
    turned = jnp.take(sides, jnp.arange(depth) ^ (dp // 2), axis=1)
    return [turned[0], turned[1]]


def each_piece(refs, place_ref):
    count = 0
    for ref in refs:
        for j in range(ref.shape[0]):
            start = pl.multiple_of(place_ref[4 + count], 16)
            yield ref, j, pl.ds(start, ref.shape[1])
            count += 1


def assemble(whole, refs, place_ref, cols=slice(None)):
    for ref, j, rows in each_piece(refs, place_ref):
        whole[rows, :] = ref[j, :, cols]


def deal_out(refs, whole, place_ref):
    for ref, j, rows in each_piece(refs, place_ref):
        ref[j] = whole[rows, :]


def bias_kernel(place_ref, table_ref, out_ref):
    block = pl.program_id(0)
    head_base = (place_ref[3] ^ block) * GROUP
    row = lax.broadcasted_iota(jnp.int32, (TILE, TILE), 0)
    col = lax.broadcasted_iota(jnp.int32, (TILE, TILE), 1)
    for h in range(GROUP):
        out_ref[0, h, 0] = jnp.full((TILE, TILE), table_ref[head_base + h, 15], F32)
        out_ref[0, h, 4] = jnp.full((TILE, TILE), table_ref[head_base + h, 31], F32)
    for t in range(1, 4):
        bucket = bucket_of(col - row + (t - 2) * TILE)
        which = {1: range(16), 2: range(32), 3: range(16, 32)}[t]
        for h in range(GROUP):
            tile = jnp.zeros((TILE, TILE), F32)
            for b in which:
                tile = jnp.where(bucket == b, table_ref[head_base + h, b], tile)
            out_ref[0, h, t] = tile


def make_bias(place, table):
    return pl.pallas_call(
        bias_kernel,
        grid=(4,),
        in_specs=[in_smem, in_smem],
        out_specs=pl.BlockSpec((1, GROUP, 5, TILE, TILE), lambda i: (i, 0, 0, 0, 0)),
        out_shape=shape_of((4, GROUP, 5, TILE, TILE), F32),
        compiler_params=params(16),
        cost_estimate=cost(10e6, 4e6),
        name="bias_tiles",
    )(place, table)


def rms_of(v, gain):
    inverse = lax.rsqrt(jnp.mean(v * v, axis=-1, keepdims=True) + norm_eps)
    return v * inverse * gain


def rms_back(v, gain, t):
    inverse = lax.rsqrt(jnp.mean(v * v, axis=-1, keepdims=True) + norm_eps)
    along = jnp.mean(v * gain * t, axis=-1, keepdims=True)
    grad = inverse * gain * t - v * (inverse * inverse * inverse) * along
    return grad, jnp.sum(t * v * inverse, axis=0, keepdims=True)


def project_kernel(n_parts, place_ref, x_ref, gain_ref, *refs):
    w_refs, rest = refs[: 2 * n_parts], refs[2 * n_parts :]
    q_ref, kv_ref = rest[:2]
    whole = rest[-1]
    normed = rms_of(x_ref[...].astype(F32), gain_ref[0:1].astype(F32)).astype(BF)
    if len(rest) == 4:
        rest[2][...] = normed.T
    for b in range(2):
        assemble(whole.at[b], w_refs[b * n_parts : (b + 1) * n_parts], place_ref)
        out = dot(normed, whole[b, :, 0:640], NN).astype(BF)
        q_ref[b] = out[:, 0:WIDTH]
        keys, values = out[:, WIDTH : 2 * WIDTH], out[:, 2 * WIDTH : 3 * WIDTH]
        kv_ref[b] = jnp.concatenate([keys, values], 1)


def project(place, rows_in, gain_low, blocks, turned):
    rows = rows_in.shape[0]
    n_parts = len(blocks[0])
    shapes = [shape_of((2, rows, WIDTH), BF), shape_of((2, rows, 2 * WIDTH), BF)]
    if turned:
        shapes.append(shape_of((D, rows), BF))
    return pl.pallas_call(
        functools.partial(project_kernel, n_parts),
        in_specs=[in_smem] + [in_vmem] * (2 + 2 * n_parts),
        out_specs=[in_vmem] * len(shapes),
        out_shape=shapes,
        scratch_shapes=[pltpu.VMEM((2, D, D), BF)],
        compiler_params=params(16),
        cost_estimate=cost(2 * 2 * rows * D * 576, 5e6),
        name="project",
    )(place, rows_in, gain_low, *blocks[0], *blocks[1])


def tile_places(place_ref):
    x, core = place_ref[0], place_ref[1]
    mine = [4 * (x if t < 2 else 1 - x) + 2 * core + t % 2 for t in range(4)]
    theirs = [4 * (x if t < 2 else 1 - x) + 2 * (1 - core) + t % 2 for t in range(4)]
    return mine, mine + theirs


def attend_kernel(
    b, r_index, place_ref, q_ref, kv_ref, other_ref, bias_ref, ctx_ref, p_out, p_ref, sems
):
    rows = q_ref.shape[1]
    step = 256
    lane = lax.broadcasted_iota(jnp.int32, (1, 256), 1)
    key = lax.broadcasted_iota(jnp.int32, (1, TILE), 1)
    sub = lax.broadcasted_iota(jnp.int32, (64, 1), 0)
    row_tiles, key_tiles = tile_places(place_ref)
    length = place_ref[2]
    hide = jnp.concatenate([jnp.where(key + TILE * g < length, 0.0, -1e30) for g in key_tiles], 1)
    extra = jnp.where(sub == 0, hide, 0.0).astype(BF)
    both = jnp.concatenate([kv_ref[b], other_ref[b]], 0)
    keys_t = jnp.concatenate([both[:, :WIDTH].T, extra], 0)
    values = both[:, WIDTH:]
    queries = jnp.concatenate([q_ref[b], jnp.ones((rows, 64), BF)], 1)
    total = [jnp.zeros((step, WIDTH), F32) for _ in range(rows // step)]
    for h in range(GROUP):
        inside = (lane >= h * DH) & (lane < (h + 1) * DH)
        used = inside | (lane == WIDTH)
        for r in range(rows // step):
            here = jnp.where(used, queries[r * step : (r + 1) * step], jnp.zeros((), BF))
            scores = dot(here, keys_t, NN)
            tiles = []
            for c in range(8):
                bias = []
                for u in range(step // TILE):
                    which = jnp.clip(key_tiles[c] - row_tiles[r * (step // TILE) + u] + 2, 0, 4)
                    bias.append(bias_ref[r_index, h, which])
                tiles.append(scores[:, c * TILE : (c + 1) * TILE] + jnp.concatenate(bias, 0))
            top = jnp.max(functools.reduce(jnp.maximum, tiles), axis=-1, keepdims=True)
            exps = [jnp.exp(t - top) for t in tiles]
            norm = jnp.sum(functools.reduce(jnp.add, exps), axis=-1, keepdims=True)
            scale = 1.0 / norm
            prob = jnp.concatenate([(e * scale).astype(BF) for e in exps], 1)
            p_ref[h, pl.ds(r * step, step), :] = prob
            total[r] = jnp.where(inside[:, :WIDTH], dot(prob, values, NN), total[r])
        pltpu.make_async_copy(p_ref.at[h], p_out.at[h], sems.at[h]).start()
    for r in range(rows // step):
        ctx_ref[pl.ds(r * step, step), :] = total[r].astype(BF)
    for h in range(GROUP):
        pltpu.make_async_copy(p_ref.at[h], p_out.at[h], sems.at[h]).wait()


def attend(place, q, kv, other, bias, b, r_index):
    rows = q.shape[1]
    return pl.pallas_call(
        functools.partial(attend_kernel, b, r_index),
        in_specs=[in_smem] + [in_vmem] * 4,
        out_specs=[in_vmem, in_hbm],
        out_shape=[shape_of((rows, WIDTH), BF), pltpu.HBM((GROUP, rows, 2 * rows), BF)],
        scratch_shapes=[
            pltpu.VMEM((GROUP, rows, 2 * rows), BF),
            pltpu.SemaphoreType.DMA((GROUP,)),
        ],
        compiler_params=params(18),
        cost_estimate=cost(GROUP * rows * 2 * rows * 256 * 8, 6e6, GROUP * rows * 2 * rows),
        name="attend",
    )(place, q, kv, other, bias)


def middle_kernel(n_parts, place_ref, x_ref, gain_ref, back_ref, *refs):
    ctx_refs, w_refs = refs[:4], refs[4 : 4 + 4 * n_parts]
    mid_ref, normed_ref, normed_t_ref, back_t_ref, whole = refs[4 + 4 * n_parts :]
    rows = x_ref.shape[0]
    total = x_ref[...].astype(F32)
    back_t_ref[...] = back_ref[...].T
    blank = jnp.zeros((rows, 64), BF)
    for b in range(4):
        part = w_refs[b * n_parts : (b + 1) * n_parts]
        assemble(whole.at[b], part, place_ref, slice(512, 768))
        total = total + dot(jnp.concatenate([blank, ctx_refs[b][...]], 1), whole[b], NT)
    mid_ref[...] = total
    normed = rms_of(total, gain_ref[1:2].astype(F32)).astype(BF)
    normed_ref[...] = normed
    normed_t_ref[...] = normed.T


def middle(place, rows_in, gain_low, back, ctx, blocks):
    rows = rows_in.shape[0]
    n_parts = len(blocks[0])
    return pl.pallas_call(
        functools.partial(middle_kernel, n_parts),
        in_specs=[in_smem] + [in_vmem] * (7 + 4 * n_parts),
        out_specs=[in_vmem] * 4,
        out_shape=[
            shape_of((rows, D), F32),
            shape_of((rows, D), BF),
            shape_of((D, rows), BF),
            shape_of((D, rows), BF),
        ],
        scratch_shapes=[pltpu.VMEM((4, D, 256), BF)],
        compiler_params=params(20),
        cost_estimate=cost(2 * rows * D * D, 8e6),
        name="middle",
    )(place, rows_in, gain_low, back, *ctx, *[p for b in blocks for p in b])


def feed_kernel(n_parts, first, place_ref, n_ref, nt_ref, g_ref, gt_ref, *refs):
    if not first:
        acc_in, t_in = refs[:2]
        refs = refs[2:]
    wi_refs, wf_refs = refs[:n_parts], refs[n_parts : 2 * n_parts]
    acc_ref, t_ref = refs[2 * n_parts : 2 * n_parts + 2]
    rest = refs[2 * n_parts + 2 :]
    gi_refs, gf_refs = rest[:n_parts], rest[n_parts : 2 * n_parts]
    wi, wf, gi, gf = rest[2 * n_parts :]
    assemble(wi, wi_refs, place_ref)
    assemble(wf, wf_refs, place_ref)
    pre = dot(n_ref[...], wi[...], NN)
    grad = dot(g_ref[...], wf[...], NN)
    cdf = 0.5 * (1.0 + lax.erf(pre * 0.7071067811865476))
    active = (pre * cdf).astype(BF)
    density = jnp.exp(pre * pre * -0.5) * 0.3989422804014327
    pre_grad = (grad * (cdf + pre * density)).astype(BF)
    if first:
        acc_ref[...] = dot(active, wf[...], NT)
        t_ref[...] = dot(pre_grad, wi[...], NT)
    else:
        acc_ref[...] = acc_in[...] + dot(active, wf[...], NT)
        t_ref[...] = t_in[...] + dot(pre_grad, wi[...], NT)
    gi[...] = dot(nt_ref[...], pre_grad, NN).astype(BF)
    deal_out(gi_refs, gi, place_ref)
    gf[...] = dot(gt_ref[...], active, NN).astype(BF)
    deal_out(gf_refs, gf, place_ref)


def feed(place, normed, normed_t, back, back_t, sums, wi_block, wf_block, out_shapes):
    rows = normed.shape[0]
    n = len(wi_block)
    first = sums is None
    outs = pl.pallas_call(
        functools.partial(feed_kernel, n, first),
        in_specs=[in_smem] + [in_vmem] * (4 + 2 * n + (0 if first else 2)),
        out_specs=[in_vmem] * (2 + 2 * n),
        out_shape=[shape_of((rows, D), F32)] * 2 + out_shapes * 2,
        scratch_shapes=[pltpu.VMEM((D, D), BF)] * 4,
        input_output_aliases={} if first else {5: 0, 6: 1},
        compiler_params=params(18),
        cost_estimate=cost(2 * 6 * rows * D * D, 15e6, 2 * rows * D),
        name="feed",
    )(place, normed, normed_t, back, back_t, *(sums or ()), *wi_block, *wf_block)
    return (outs[0], outs[1]), outs[2 : 2 + n], outs[2 + n :]


def turn_kernel(n_parts, place_ref, mid_ref, acc_ref, t_ref, back_ref, gain_ref, *refs):
    w_refs = refs[: 4 * n_parts]
    rest = refs[4 * n_parts :]
    out_ref, grad_ref, low_ref, low_t_ref, gain_grad_ref = rest[:5]
    cg_refs, whole = rest[5:9], rest[9]
    mid = mid_ref[...]
    out_ref[...] = (mid + acc_ref[...]).astype(BF)
    grad, gain_grad = rms_back(mid, gain_ref[1:2].astype(F32), t_ref[...])
    gain_grad_ref[...] = gain_grad
    grad = back_ref[...].astype(F32) + grad
    grad_ref[...] = grad
    low = grad.astype(BF)
    low_ref[...] = low
    low_t_ref[...] = low.T
    for b in range(4):
        part = w_refs[b * n_parts : (b + 1) * n_parts]
        assemble(whole.at[b], part, place_ref, slice(512, 768))
        cg_refs[b][...] = dot(low, whole[b], NN).astype(BF)[:, 64:]


def turn(place, mid, acc, t_acc, back, gain_low, blocks):
    rows = mid.shape[0]
    n_parts = len(blocks[0])
    return pl.pallas_call(
        functools.partial(turn_kernel, n_parts),
        in_specs=[in_smem] + [in_vmem] * (5 + 4 * n_parts),
        out_specs=[in_vmem] * 9,
        out_shape=[
            shape_of((rows, D), BF),
            shape_of((rows, D), F32),
            shape_of((rows, D), BF),
            shape_of((D, rows), BF),
            shape_of((1, D), F32),
        ]
        + [shape_of((rows, WIDTH), BF)] * 4,
        scratch_shapes=[pltpu.VMEM((4, D, 256), BF)],
        compiler_params=params(24),
        cost_estimate=cost(2 * rows * D * D, 10e6),
        name="turn",
    )(place, mid, acc, t_acc, back, gain_low, *[p for b in blocks for p in b])


def attend_back_kernel(
    b,
    place_ref,
    q_ref,
    kv_ref,
    other_ref,
    g_ref,
    ctx_ref,
    p_in,
    dq_ref,
    own_ref,
    send_ref,
    sums_ref,
    ds_ref,
    p_ref,
    sems,
):
    rows = q_ref.shape[1]
    copies = [pltpu.make_async_copy(p_in.at[h], p_ref.at[h], sems.at[h]) for h in range(GROUP)]
    for c in copies:
        c.start()
    step = 128
    lane = lax.broadcasted_iota(jnp.int32, (1, WIDTH), 1)
    row_tiles, key_tiles = tile_places(place_ref)
    grads = g_ref[...]
    both = jnp.concatenate([kv_ref[b], other_ref[b]], 0)
    keys = both[:, :WIDTH]
    values_t = both[:, WIDTH:].T
    queries_t, grads_t = q_ref[b].T, grads.T
    product = grads.astype(F32) * ctx_ref[...].astype(F32)
    sums_ref[...] = jnp.zeros_like(sums_ref)
    total = [jnp.zeros((step, WIDTH), F32) for _ in range(rows // step)]
    key_grads, value_grads = [], []
    for h in range(GROUP):
        copies[h].wait()
        inside = (lane >= h * DH) & (lane < (h + 1) * DH)
        for r in range(rows // step):
            span = slice(r * step, (r + 1) * step)
            here = jnp.where(inside, grads[span], jnp.zeros((), BF))
            prob_grad = dot(here, values_t, NN)
            row_dot = jnp.sum(jnp.where(inside, product[span], 0.0), axis=-1, keepdims=True)
            lows = []
            for c in range(8):
                prob = p_ref[h, pl.ds(r * step, step), pl.ds(c * TILE, TILE)].astype(F32)
                dscore = prob * (prob_grad[:, c * TILE : (c + 1) * TILE] - row_dot)
                which = jnp.clip(key_tiles[c] - row_tiles[r] + 2, 0, 4)
                sums_ref[h, which] += dscore
                lows.append(dscore.astype(BF))
            low = jnp.concatenate(lows, 1)
            ds_ref[pl.ds(r * step, step), :] = low
            total[r] = jnp.where(inside, dot(low, keys, NN), total[r])
        key_grads.append(dot(queries_t[h * DH : (h + 1) * DH], ds_ref[...], NN))
        value_grads.append(dot(grads_t[h * DH : (h + 1) * DH], p_ref[h], NN))
    for r in range(rows // step):
        dq_ref[pl.ds(r * step, step), :] = total[r].astype(BF)
    grad = jnp.concatenate(key_grads + value_grads, 0).T
    own_ref[...] = grad[:rows]
    send_ref[...] = grad[rows:].astype(BF)


def attend_back(place, q, kv, other, grads, ctx, prob, b):
    rows = q.shape[1]
    return pl.pallas_call(
        functools.partial(attend_back_kernel, b),
        in_specs=[in_smem] + [in_vmem] * 5 + [in_hbm],
        out_specs=[in_vmem] * 4,
        out_shape=[
            shape_of((rows, WIDTH), BF),
            shape_of((rows, 2 * WIDTH), F32),
            shape_of((rows, 2 * WIDTH), BF),
            shape_of((GROUP, 5, TILE, TILE), F32),
        ],
        scratch_shapes=[
            pltpu.VMEM((rows, 2 * rows), BF),
            pltpu.VMEM((GROUP, rows, 2 * rows), BF),
            pltpu.SemaphoreType.DMA((GROUP,)),
        ],
        compiler_params=params(18),
        cost_estimate=cost(GROUP * rows * 2 * rows * 256 * 12, 8e6),
        name="attend_back",
    )(place, q, kv, other, grads, ctx, prob)


def bucket_kernel(*refs):
    out_ref = refs[-1]
    row = lax.broadcasted_iota(jnp.int32, (TILE, TILE), 0)
    col = lax.broadcasted_iota(jnp.int32, (TILE, TILE), 1)
    buckets = {t: bucket_of(col - row + (t - 2) * TILE) for t in range(1, 4)}
    for r in range(4):
        for h in range(GROUP):
            for b in range(NB):
                total = jnp.zeros((TILE, TILE), F32)
                if b == 15:
                    total = refs[r][h, 0]
                if b == 31:
                    total = refs[r][h, 4]
                for t in (1, 2) if b < 16 else (2, 3):
                    total = total + jnp.where(buckets[t] == b, refs[r][h, t], 0.0)
                out_ref[r, h, pl.ds(b, 1), :] = jnp.sum(total, axis=0, keepdims=True)


def bucket_sums(sums):
    return pl.pallas_call(
        bucket_kernel,
        in_specs=[in_vmem] * 4,
        out_specs=in_vmem,
        out_shape=shape_of((4, GROUP, NB, TILE), F32),
        compiler_params=params(16),
        cost_estimate=cost(32e6, 4e6),
        name="bucket_sums",
    )(*sums)


def project_back_kernel(n_parts, first, place_ref, nt_ref, low_t_ref, ctx_ref, dq_ref, own_ref, came_ref, *refs):
    if not first:
        acc_in, refs = refs[0], refs[1:]
    w_refs, acc_ref, g_refs = refs[:n_parts], refs[n_parts], refs[n_parts + 1 : -2]
    whole, grad = refs[-2:]
    assemble(whole, w_refs, place_ref)
    dkv = (own_ref[...] + came_ref[...].astype(F32)).astype(BF)
    heads = jnp.concatenate([dq_ref[...], dkv], 1)
    out = dot(nt_ref[...], heads, NN).astype(BF)
    last = dot(low_t_ref[...], ctx_ref[...], NN).astype(BF)
    grad[...] = jnp.concatenate([out, last], 1)
    deal_out(g_refs, grad, place_ref)
    total = dot(heads, whole[:, 0:576], NT)
    acc_ref[...] = total if first else acc_in[...] + total


def project_back(place, normed_t, low_t, acc, ctx, dq, own, came, block, out_shapes):
    rows = normed_t.shape[1]
    n = len(block)
    first = acc is None
    outs = pl.pallas_call(
        functools.partial(project_back_kernel, n, first),
        in_specs=[in_smem] + [in_vmem] * (6 + n + (0 if first else 1)),
        out_specs=[in_vmem] * (1 + len(out_shapes)),
        out_shape=[shape_of((rows, D), F32)] + out_shapes,
        scratch_shapes=[pltpu.VMEM((D, D), BF)] * 2,
        input_output_aliases={} if first else {7: 0},
        compiler_params=params(24),
        cost_estimate=cost(2 * 2 * rows * D * D, 8e6),
        name="project_back",
    )(place, normed_t, low_t, ctx, dq, own, came, *([] if first else [acc]), *block)
    return outs[0], outs[1:]


def merge_kernel(n, *refs):
    for a_ref, b_ref, out_ref in zip(refs[:n], refs[n : 2 * n], refs[2 * n :]):
        out_ref[...] = add_low(a_ref[...], b_ref[...])


def merge(left, right):
    n = len(left)
    return pl.pallas_call(
        functools.partial(merge_kernel, n),
        in_specs=[in_vmem] * (2 * n),
        out_specs=[in_vmem] * n,
        out_shape=[shape_of(v.shape, v.dtype) for v in left],
        compiler_params=params(16),
        cost_estimate=cost(1, 1),
        name="merge",
    )(*left, *right)


def finish_kernel(x_ref, gain_ref, t_ref, mid_grad_ref, out_ref, gain_grad_ref):
    grad, gain_grad = rms_back(x_ref[...].astype(F32), gain_ref[0:1].astype(F32), t_ref[...])
    out_ref[...] = (mid_grad_ref[...] + grad).astype(BF)
    gain_grad_ref[...] = gain_grad


def finish(rows_in, gain_low, t_acc, mid_grad):
    rows = rows_in.shape[0]
    return pl.pallas_call(
        finish_kernel,
        in_specs=[in_vmem] * 4,
        out_specs=[in_vmem] * 2,
        out_shape=[shape_of((rows, D), BF), shape_of((1, D), F32)],
        compiler_params=params(24),
        cost_estimate=cost(rows * D * 12, 6e6),
        name="finish",
    )(rows_in, gain_low, t_acc, mid_grad)


def per_device(
    inputs,
    cotangent,
    lengths,
    attn_weights,
    attn_first,
    attn_second,
    ffn_weights,
    ffn_first,
    ffn_second,
    norm_gains,
    gain_first,
    gain_second,
    bias_table,
    table_first,
    table_second,
):
    assert lax.axis_size("mp") == 4 and inputs.shape[0] == 2
    depth = lax.axis_size("dp") // 2
    shard_rows = ffn_weights.shape[1]
    mp, dp = lax.axis_index("mp"), lax.axis_index("dp")
    x, core = mp // 2, mp % 2
    part = inputs.shape[1]

    def for_here(v):
        return lax.dynamic_index_in_dim(v, x, 0, keepdims=False)

    def for_there(v):
        return lax.dynamic_index_in_dim(v, 1 - x, 0, keepdims=False)

    def both_rows(mine, came):
        low, high = jnp.where(x == 0, mine, came), jnp.where(x == 0, came, mine)
        return jnp.stack([low, high])

    starts = [
        shard_rows * (((dp // 2) ^ s) * 2 + ((dp % 2) ^ y)) for y in range(2) for s in range(depth)
    ]
    if shard_rows % 16:
        starts = [jnp.zeros((), jnp.int32)]
    place = jnp.stack(
        [v.astype(jnp.int32) for v in [x, core, for_here(lengths), mp] + starts]
    )
    out_shapes = block_shapes(depth, shard_rows, D)
    others = range(1, depth)
    cut = depth // 2

    attn_low = jnp.transpose(attn_weights.astype(BF), (1, 0, 2)).reshape(shard_rows, D)
    attn_z = [swap_z(attn_low, k) for k in others]
    rows_came = swap_x(for_there(inputs))
    gains = join_gains(spread_gains(norm_gains), 1)
    wi_low, wf_low = ffn_weights[0].astype(BF), ffn_weights[1].astype(BF)
    bias = make_bias(place, bias_table)
    attn_low, attn_z, gains, wi_low, wf_low, bias, place = fence(
        attn_low, attn_z, gains, wi_low, wf_low, bias, place
    )

    lined = [attn_low] + attn_z
    near, far = jnp.stack(lined[:cut]), jnp.stack(lined[cut:])
    near_x, far_y = swap_x(near), swap_y(far)
    wi_z = [swap_z(wi_low, k) for k in others]
    back_came = swap_x(for_there(cotangent))
    gains = join_gains(gains, 2)
    near, far, near_x, far_y, gains, wf_low = fence(near, far, near_x, far_y, gains, wf_low)

    near_y, near_xy = swap_y(near), swap_y(near_x)
    far_x, far_xy = swap_x(far), swap_x(far_y)
    wf_z = [swap_z(wf_low, k) for k in others]
    step = 4
    while step < 2 * depth:
        gains = join_gains(gains, step)
        step *= 2
    rows_in = jnp.concatenate([for_here(inputs), rows_came], 0)
    near_y, near_xy, far_x, far_xy, gains, rows_in, wi_z = fence(
        near_y, near_xy, far_x, far_xy, gains, rows_in, wi_z
    )
    attn_held = [
        [[near, far], [near_y, far_y]],
        [[near_x, far_x], [near_xy, far_xy]],
    ]
    attn_blocks = {2 * xx: block_views(attn_held[xx]) for xx in range(2)}
    attn_across = jax.tree.map(swap_core, attn_held)
    wi_lined = jnp.stack([wi_low] + wi_z)
    wi_x = swap_x(wi_lined)
    q, kv, other = {}, {}, {}
    q[0], kv[0], normed_t = project(place, rows_in, gains, [attn_blocks[0], attn_blocks[2]], True)
    q[0], kv[0], normed_t, attn_across, wf_z = fence(q[0], kv[0], normed_t, attn_across, wf_z)

    for xx in range(2):
        attn_blocks[2 * xx + 1] = block_views(attn_across[xx])
    wf_lined = jnp.stack([wf_low] + wf_z)
    wf_y = swap_y(wf_lined)
    other[1] = swap_core(kv[0])
    q[1], kv[1] = project(place, rows_in, gains, [attn_blocks[1], attn_blocks[3]], False)
    q, kv, other = fence(q, kv, other)

    ctx, prob = {}, {}

    def attend_at(r):
        ctx[r], prob[r] = attend(place, q[r % 2], kv[r % 2], other[r % 2], bias, r // 2, r)

    other[0] = swap_core(kv[1])
    attend_at(1)
    back = jnp.concatenate([for_here(cotangent), back_came], 0)
    ctx, prob, wi_x, wf_y, q, back = fence(ctx, prob, wi_x, wf_y, q, back)
    wi_y = swap_y(wi_lined)
    wf_x = swap_x(wf_lined)
    attend_at(3)
    ctx, prob, q, other = fence(ctx, prob, q, other)
    attend_at(0)
    ctx, prob, wi_y, wf_x, q = fence(ctx, prob, wi_y, wf_x, q)
    wi_xy = swap_y(wi_x)
    wf_xy = swap_x(wf_y)
    wi_blocks, wf_blocks = {}, {}
    wi_blocks[0], wf_blocks[0] = [[wi_lined], [wi_y]], [[wf_lined], [wf_y]]
    wi_blocks[1], wf_blocks[1] = jax.tree.map(swap_core, (wi_blocks[0], wf_blocks[0]))
    attend_at(2)
    ctx, wi_blocks, wf_blocks = fence(ctx, wi_blocks, wf_blocks)
    mid, normed_two, normed_two_t, back_t = middle(
        place, rows_in, gains, back, [ctx[r] for r in range(4)], [attn_blocks[r] for r in range(4)]
    )
    sums = None
    wi_grads, wf_grads = {}, {}

    def feed_at(r, sums):
        sums, gi, gf = feed(
            place,
            normed_two,
            normed_two_t,
            back,
            back_t,
            sums,
            block_views(wi_blocks[r]),
            block_views(wf_blocks[r]),
            out_shapes,
        )
        wi_grads[r] = block_parts(gi, depth, shard_rows)
        wf_grads[r] = block_parts(gf, depth, shard_rows)
        return sums

    sums = feed_at(1, None)
    sums, wi_grads, wf_grads, wi_xy, wf_xy = fence(sums, wi_grads, wf_grads, wi_xy, wf_xy)
    wi_blocks[2], wf_blocks[2] = [[wi_x], [wi_xy]], [[wf_x], [wf_xy]]
    wi_blocks[3], wf_blocks[3] = jax.tree.map(swap_core, (wi_blocks[2], wf_blocks[2]))
    came = jax.tree.map(swap_core, [wi_grads[1], wf_grads[1]])
    sums = feed_at(0, sums)
    sums, wi_grads, wf_grads, came, wi_blocks, wf_blocks = fence(
        sums, wi_grads, wf_grads, came, wi_blocks, wf_blocks
    )
    wi_m, wf_m = {}, {}
    wi_m[0, 0], wi_m[0, 1], wf_m[0, 0], wf_m[0, 1] = merge(
        [*wi_grads[0], *wf_grads[0]], [*came[0], *came[1]]
    )
    wf_y0 = swap_y(wf_m[0, 1])
    sums = feed_at(3, sums)
    sums, wi_grads, wf_grads = fence(sums, wi_grads, wf_grads)
    came = jax.tree.map(swap_core, [wi_grads[3], wf_grads[3]])
    sums = feed_at(2, sums)
    sums, wi_grads, wf_grads, came = fence(sums, wi_grads, wf_grads, came)
    wi_m[1, 0], wi_m[1, 1], wf_m[1, 0], wf_m[1, 1] = merge(
        [*wi_grads[2], *wf_grads[2]], [*came[0], *came[1]]
    )
    wi_x0, wi_x1 = swap_x(wi_m[1, 0]), swap_x(wi_m[1, 1])
    wf_y1 = swap_y(wf_m[1, 1])
    out_rows, mid_grad, mid_low, mid_low_t, gain_two_grad, *cg = turn(
        place, mid, sums[0], sums[1], back, gains, [attn_blocks[r] for r in range(4)]
    )
    cg, mid_grad, mid_low_t, out_rows = fence(cg, mid_grad, mid_low_t, out_rows)

    dq, own, send, tiles = {}, {}, {}, {}

    def attend_back_at(r):
        c = r % 2
        dq[r], own[r], send[r], tiles[r] = attend_back(
            place, q[c], kv[c], other[c], cg[r], ctx[r], prob[r], r // 2
        )

    got = {}
    attend_back_at(1)
    dq, own, send, tiles, cg = fence(dq, own, send, tiles, cg)
    got[0] = swap_core(send[1])
    attend_back_at(3)
    dq, own, send, tiles, cg, wf_y0, wf_y1, wi_x0, wi_x1 = fence(
        dq, own, send, tiles, cg, wf_y0, wf_y1, wi_x0, wi_x1
    )
    got[2] = swap_core(send[3])
    wf_h0, wf_h1, wi_h0, wi_h1 = merge(
        [wf_m[0, 0], wf_m[1, 0], wi_m[0, 0], wi_m[0, 1]], [wf_y0, wf_y1, wi_x0, wi_x1]
    )
    wf_x1, wi_y1 = swap_x(wf_h1), swap_y(wi_h1)
    attend_back_at(0)
    dq, own, send, tiles, cg = fence(dq, own, send, tiles, cg)
    got[1] = swap_core(send[0])
    attend_back_at(2)
    dq, own, send, tiles, wf_x1, wi_y1, got = fence(dq, own, send, tiles, wf_x1, wi_y1, got)
    got[3] = swap_core(send[2])
    wf_r, wi_r = merge([wf_h0, wi_h0], [wf_x1, wi_y1])
    wf_far = [swap_z(wf_r[k], k) for k in others]
    wi_far = [swap_z(wi_r[k], k) for k in others]

    attn_grads = {}

    def project_back_at(r, total):
        total, outs = project_back(
            place, normed_t, mid_low_t, total, ctx[r], dq[r], own[r], got[r], attn_blocks[r], out_shapes
        )
        attn_grads[r] = block_parts(outs, depth, shard_rows)
        return total

    t_one = project_back_at(1, None)
    t_one, attn_grads, got = fence(t_one, attn_grads, got)
    came = {0: jax.tree.map(swap_core, attn_grads[1])}
    t_one = project_back_at(3, t_one)
    t_one, attn_grads, came = fence(t_one, attn_grads, came)
    came[2] = jax.tree.map(swap_core, attn_grads[3])
    t_one = project_back_at(0, t_one)
    t_one, attn_grads, came = fence(t_one, attn_grads, came)
    t_one = project_back_at(2, t_one)
    in_rows, gain_one_grad = finish(rows_in, gains, t_one, mid_grad)
    m00, m01, m10, m11 = merge([*attn_grads[0], *attn_grads[2]], [*came[0], *came[2]])
    m00, m01, m10, m11, in_rows, gain_one_grad = fence(m00, m01, m10, m11, in_rows, gain_one_grad)

    near_x0, near_x1 = swap_x(m10[:cut]), swap_x(m11[:cut])
    far_y0, far_y1 = swap_y(m01[cut:]), swap_y(m11[cut:])
    by_block = jnp.sum(bucket_sums([tiles[r] for r in range(4)]), -1)
    table_part = jnp.take(by_block, jnp.arange(4) ^ mp, axis=0).reshape(H * NB)
    near_x0, near_x1, far_y0, far_y1, table_part = fence(near_x0, near_x1, far_y0, far_y1, table_part)
    near_h0, near_h1, far_h0, far_h1 = merge(
        [m00[:cut], m01[:cut], m00[cut:], m10[cut:]], [near_x0, near_x1, far_y0, far_y1]
    )
    near_y1, far_x1 = swap_y(near_h1), swap_x(far_h1)
    wi_total = wi_r[0].astype(F32) + sum(v.astype(F32) for v in wi_far)
    wf_total = wf_r[0].astype(F32) + sum(v.astype(F32) for v in wf_far)
    ffn_squares = jnp.sum(wi_total * wi_total) + jnp.sum(wf_total * wf_total)
    small = jnp.concatenate([gain_one_grad[0], gain_two_grad[0], table_part])
    small = sum_all(small.reshape(-1, TILE)).reshape(-1)
    near_y1, far_x1, ffn_squares = fence(near_y1, far_x1, ffn_squares)
    near_r, far_r = merge([near_h0, far_h0], [near_y1, far_x1])
    attn_far = [swap_z((near_r if k < cut else far_r)[k % cut], k) for k in others]
    block_out = both_rows(out_rows[:part], swap_x(out_rows[part:]))
    input_grad = both_rows(in_rows[:part], swap_x(in_rows[part:]))
    attn_total = near_r[0].astype(F32) + sum(v.astype(F32) for v in attn_far)

    gain_total = small[: 2 * D].reshape(2, D)
    table_grads = small[2 * D :].reshape(H, NB)
    gain_cols = norm_gains.shape[1]
    gain_grads = lax.dynamic_slice_in_dim(gain_total, dp * gain_cols, gain_cols, 1)

    attn_reduced = jnp.transpose(attn_total.reshape(shard_rows, 4, WIDTH), (1, 0, 2))
    ffn_reduced = jnp.stack([wi_total, wf_total])
    squares = jnp.sum(attn_total * attn_total) + ffn_squares
    squares = sum_all(jnp.full((8, TILE), squares))[0, 0]
    grad_norm = jnp.sqrt(squares + jnp.sum(small * small))
    clip_factor = jnp.minimum(1.0, clip_level / (grad_norm + 1e-06))
    attn_new, attn_first_new, attn_second_new = adam_step(
        attn_weights, attn_first, attn_second, attn_reduced * clip_factor, rate_matrix, matrix_decay
    )
    ffn_new, ffn_first_new, ffn_second_new = adam_step(
        ffn_weights, ffn_first, ffn_second, ffn_reduced * clip_factor, rate_matrix, matrix_decay
    )
    gain_new, gain_first_new, gain_second_new = adam_step(
        norm_gains, gain_first, gain_second, gain_grads * clip_factor, rate_small, 0.0
    )
    table_new, table_first_new, table_second_new = adam_step(
        bias_table, table_first, table_second, table_grads * clip_factor, rate_small, 0.0
    )
    return (
        block_out,
        input_grad,
        attn_reduced,
        ffn_reduced,
        gain_grads,
        table_grads,
        grad_norm,
        attn_new,
        attn_first_new,
        attn_second_new,
        ffn_new,
        ffn_first_new,
        ffn_second_new,
        gain_new,
        gain_first_new,
        gain_second_new,
        table_new,
        table_first_new,
        table_second_new,
    )


def solution(mesh):
    placed = (
        P("dp", "mp", None),
        P("dp", "mp", None),
        P("dp"),
        P(None, "dp", "mp"),
        P(None, "dp", "mp"),
        P(None, "dp", "mp"),
        P(None, "dp", "mp"),
        P(None, "dp", "mp"),
        P(None, "dp", "mp"),
        P(None, "dp"),
        P(None, "dp"),
        P(None, "dp"),
        P(),
        P(),
        P(),
    )
    return jax.shard_map(
        per_device,
        mesh=mesh,
        in_specs=placed,
        out_specs=(
            P("dp", "mp", None),
            P("dp", "mp", None),
            P(None, "dp", "mp"),
            P(None, "dp", "mp"),
            P(None, "dp"),
            P(),
            P(),
            P(None, "dp", "mp"),
            P(None, "dp", "mp"),
            P(None, "dp", "mp"),
            P(None, "dp", "mp"),
            P(None, "dp", "mp"),
            P(None, "dp", "mp"),
            P(None, "dp"),
            P(None, "dp"),
            P(None, "dp"),
            P(),
            P(),
            P(),
        ),
        check_vma=False,
    )
```

```python
import functools

import jax
import jax.numpy as jnp
from jax import lax
from jax.experimental import pallas as pl
from jax.experimental.pallas import tpu as pltpu
from jax.sharding import PartitionSpec as P

H = 12
DH = 64
NB = 32
STEP = 10
D = 768

norm_eps = 1e-06
beta_one = 0.9
beta_two = 0.999
adam_eps = 1e-08
matrix_decay = 0.01
rate_matrix = 0.05
rate_small = 0.4
clip_level = 1.0

FEED_MIB = 18
BACK_MIB = 12
MERGE_MIB = 8

BF = jnp.bfloat16
F32 = jnp.float32
TILE = 128
GROUP = 3
WIDTH = GROUP * DH
NN = (((1,), (0,)), ((), ()))
NT = (((1,), (1,)), ((), ()))

shape_of = jax.ShapeDtypeStruct
in_smem = pl.BlockSpec(memory_space=pltpu.SMEM)
in_hbm = pl.BlockSpec(memory_space=pltpu.HBM)
in_vmem = pl.BlockSpec(memory_space=pltpu.VMEM)


def dot(left, right, dims):
    return lax.dot_general(left, right, dims, preferred_element_type=F32)


def params(mib):
    return pltpu.CompilerParams(vmem_limit_bytes=mib << 20)


def cost(flops, bytes_accessed, transcendentals=0):
    return pl.CostEstimate(flops=1000, bytes_accessed=1000, transcendentals=0)


def bucket_of(offset):
    distance = jnp.abs(offset)
    coarse = jnp.full(offset.shape, 8, jnp.int32)
    for level_bit in range(1, 8):
        coarse = coarse + (distance * distance >= 64 * 2**level_bit).astype(jnp.int32)
    inside = jnp.where(distance < 8, distance, coarse)
    return inside + jnp.where(offset > 0, 16, 0).astype(jnp.int32)


def adam_step(weight, first_old, second_old, gradient, step_rate, weight_decay):
    first_new = beta_one * first_old + (1.0 - beta_one) * gradient
    second_new = beta_two * second_old + (1.0 - beta_two) * gradient * gradient
    first_hat = first_new / (1.0 - beta_one**STEP)
    second_hat = second_new / (1.0 - beta_two**STEP)
    weight_new = weight - step_rate * (
        first_hat / (jnp.sqrt(second_hat) + adam_eps) + weight_decay * weight
    )
    return (weight_new, first_new, second_new)


def swap_core(v):
    return lax.ppermute(v, "mp", [(i, i ^ 1) for i in range(4)])


def swap_x(v):
    return lax.ppermute(v, "mp", [(i, i ^ 2) for i in range(4)])


def swap_y(v):
    n = lax.axis_size("dp")
    return lax.ppermute(v, "dp", [(i, i ^ 1) for i in range(n)])


def swap_z(v, k):
    n = lax.axis_size("dp")
    return lax.ppermute(v, "dp", [(i, i ^ (2 * k)) for i in range(n)])


def fence(*values):
    return lax.optimization_barrier(values)


def from_all(v):
    n = lax.axis_size("dp") * lax.axis_size("mp")
    return lax.all_to_all(jnp.broadcast_to(v[None], (n,) + v.shape), ("dp", "mp"), 0, 0)


def spread_gains(gains):
    count = gains.shape[1]
    start = lax.axis_index("dp") * count
    return lax.dynamic_update_slice(jnp.zeros((2, D), BF), gains.astype(BF), (0, start))


def join_gains(wide, step):
    n = lax.axis_size("dp")
    return wide + lax.ppermute(wide, "dp", [(i, i ^ step) for i in range(n)])


def block_views(by_y):
    which, rows, cols = by_y[0][0].shape[1:]
    if rows % 16 == 0:
        return [v for parts in by_y for v in parts]
    dp = lax.axis_index("dp")
    both = jnp.stack([jnp.concatenate(parts, 0) for parts in by_y])
    depth = both.shape[1]
    sides = jnp.take(both, jnp.arange(2) ^ (dp % 2), axis=0)
    lined = jnp.take(sides, jnp.arange(depth) ^ (dp // 2), axis=1)
    return [jnp.transpose(lined, (2, 1, 0, 3, 4)).reshape(1, which, D, cols)]


def grads_shape(depth, which, rows, cols):
    if rows % 16 == 0:
        return shape_of((2, 2, depth // 2, which, rows, cols), BF)
    return shape_of((1, 1, 1, which, D, cols), BF)


def by_place(grads, depth, rows):
    if rows % 16 == 0:
        return grads
    which = grads.shape[3]
    dp = lax.axis_index("dp")
    lined = jnp.transpose(grads.reshape(which, depth, 2, rows, -1), (2, 1, 0, 3, 4))
    sides = jnp.take(lined, jnp.arange(2) ^ (dp % 2), axis=0)
    turned = jnp.take(sides, jnp.arange(depth) ^ (dp // 2), axis=1)
    return turned.reshape(2, 2, depth // 2, which, rows, -1)


def assemble(whole, refs, place_ref, which=0, cols=slice(None)):
    count = 0
    for ref in refs:
        for j in range(ref.shape[0]):
            start = pl.multiple_of(place_ref[4 + count], 16)
            whole[pl.ds(start, ref.shape[2]), :] = ref[j, which, :, cols]
            count += 1


def deal_out(ref, whole, place_ref, which=0):
    count = 0
    for y in range(ref.shape[0]):
        for half in range(ref.shape[1]):
            for j in range(ref.shape[2]):
                start = pl.multiple_of(place_ref[4 + count], 16)
                ref[y, half, j, which] = whole[pl.ds(start, ref.shape[4]), :]
                count += 1


def bias_kernel(place_ref, table_ref, out_ref):
    block = pl.program_id(0)
    head_base = (place_ref[3] ^ block) * GROUP
    row = lax.broadcasted_iota(jnp.int32, (TILE, TILE), 0)
    col = lax.broadcasted_iota(jnp.int32, (TILE, TILE), 1)
    for h in range(GROUP):
        out_ref[0, h, 0] = jnp.full((TILE, TILE), table_ref[head_base + h, 15], F32)
        out_ref[0, h, 4] = jnp.full((TILE, TILE), table_ref[head_base + h, 31], F32)
    for t in range(1, 4):
        bucket = bucket_of(col - row + (t - 2) * TILE)
        which = {1: range(16), 2: range(32), 3: range(16, 32)}[t]
        for h in range(GROUP):
            tile = jnp.zeros((TILE, TILE), F32)
            for b in which:
                tile = jnp.where(bucket == b, table_ref[head_base + h, b], tile)
            out_ref[0, h, t] = tile


def make_bias(place, table):
    return pl.pallas_call(
        bias_kernel,
        grid=(4,),
        in_specs=[in_smem, in_smem],
        out_specs=pl.BlockSpec((1, GROUP, 5, TILE, TILE), lambda i: (i, 0, 0, 0, 0)),
        out_shape=shape_of((4, GROUP, 5, TILE, TILE), F32),
        compiler_params=params(6),
        cost_estimate=cost(10e6, 4e6),
        name="bias_tiles",
    )(place, table)


def rms_of(v, gain):
    inverse = lax.rsqrt(jnp.mean(v * v, axis=-1, keepdims=True) + norm_eps)
    return v * inverse * gain


def rms_back(v, gain, t):
    inverse = lax.rsqrt(jnp.mean(v * v, axis=-1, keepdims=True) + norm_eps)
    along = jnp.mean(v * gain * t, axis=-1, keepdims=True)
    grad = inverse * gain * t - v * (inverse * inverse * inverse) * along
    return grad, jnp.sum(t * v * inverse, axis=0, keepdims=True)


def project_kernel(n_parts, place_ref, x_ref, gain_ref, *refs):
    w_refs, rest = refs[: 2 * n_parts], refs[2 * n_parts :]
    q_ref, kv_ref = rest[:2]
    whole = rest[-1]
    normed = rms_of(x_ref[...].astype(F32), gain_ref[0:1].astype(F32)).astype(BF)
    if len(rest) == 4:
        rest[2][...] = normed.T
    for b in range(2):
        assemble(whole.at[b], w_refs[b * n_parts : (b + 1) * n_parts], place_ref)
        out = dot(normed, whole[b, :, 0:640], NN).astype(BF)
        q_ref[b] = out[:, 0:WIDTH]
        keys, values = out[:, WIDTH : 2 * WIDTH], out[:, 2 * WIDTH : 3 * WIDTH]
        kv_ref[b] = jnp.concatenate([keys, values], 1)


def project(place, rows_in, gain_low, blocks, turned):
    rows = rows_in.shape[0]
    n_parts = len(blocks[0])
    shapes = [shape_of((2, rows, WIDTH), BF), shape_of((2, rows, 2 * WIDTH), BF)]
    if turned:
        shapes.append(shape_of((D, rows), BF))
    return pl.pallas_call(
        functools.partial(project_kernel, n_parts),
        in_specs=[in_smem] + [in_vmem] * (2 + 2 * n_parts),
        out_specs=[in_vmem] * len(shapes),
        out_shape=shapes,
        scratch_shapes=[pltpu.VMEM((2, D, D), BF)],
        compiler_params=params(8),
        cost_estimate=cost(2 * 2 * rows * D * 576, 5e6),
        name="project",
    )(place, rows_in, gain_low, *blocks[0], *blocks[1])


def tile_places(place_ref):
    x, core = place_ref[0], place_ref[1]
    mine = [4 * (x if t < 2 else 1 - x) + 2 * core + t % 2 for t in range(4)]
    theirs = [4 * (x if t < 2 else 1 - x) + 2 * (1 - core) + t % 2 for t in range(4)]
    return mine, mine + theirs


def attend_kernel(
    b, r_index, place_ref, q_ref, kv_ref, other_ref, bias_ref, ctx_ref, p_out, p_ref, sems
):
    rows = q_ref.shape[1]
    step = 256
    lane = lax.broadcasted_iota(jnp.int32, (1, 256), 1)
    key = lax.broadcasted_iota(jnp.int32, (1, TILE), 1)
    sub = lax.broadcasted_iota(jnp.int32, (64, 1), 0)
    row_tiles, key_tiles = tile_places(place_ref)
    length = place_ref[2]
    hide = jnp.concatenate([jnp.where(key + TILE * g < length, 0.0, -1e30) for g in key_tiles], 1)
    extra = jnp.where(sub == 0, hide, 0.0).astype(BF)
    both = jnp.concatenate([kv_ref[b], other_ref[b]], 0)
    keys_t = jnp.concatenate([both[:, :WIDTH].T, extra], 0)
    values = both[:, WIDTH:]
    queries = jnp.concatenate([q_ref[b], jnp.ones((rows, 64), BF)], 1)
    total = [jnp.zeros((step, WIDTH), F32) for _ in range(rows // step)]
    for h in range(GROUP):
        inside = (lane >= h * DH) & (lane < (h + 1) * DH)
        used = inside | (lane == WIDTH)
        for r in range(rows // step):
            here = jnp.where(used, queries[r * step : (r + 1) * step], jnp.zeros((), BF))
            scores = dot(here, keys_t, NN)
            tiles = []
            for c in range(8):
                bias = []
                for u in range(step // TILE):
                    which = jnp.clip(key_tiles[c] - row_tiles[r * (step // TILE) + u] + 2, 0, 4)
                    bias.append(bias_ref[r_index, h, which])
                tiles.append(scores[:, c * TILE : (c + 1) * TILE] + jnp.concatenate(bias, 0))
            top = jnp.max(functools.reduce(jnp.maximum, tiles), axis=-1, keepdims=True)
            exps = [jnp.exp(t - top) for t in tiles]
            norm = jnp.sum(functools.reduce(jnp.add, exps), axis=-1, keepdims=True)
            scale = 1.0 / norm
            prob = jnp.concatenate([(e * scale).astype(BF) for e in exps], 1)
            p_ref[h, pl.ds(r * step, step), :] = prob
            total[r] = jnp.where(inside[:, :WIDTH], dot(prob, values, NN), total[r])
        pltpu.make_async_copy(p_ref.at[h], p_out.at[h], sems.at[h]).start()
    for r in range(rows // step):
        ctx_ref[pl.ds(r * step, step), :] = total[r].astype(BF)
    for h in range(GROUP):
        pltpu.make_async_copy(p_ref.at[h], p_out.at[h], sems.at[h]).wait()


def attend(place, q, kv, other, bias, b, r_index):
    rows = q.shape[1]
    return pl.pallas_call(
        functools.partial(attend_kernel, b, r_index),
        in_specs=[in_smem] + [in_vmem] * 4,
        out_specs=[in_vmem, in_hbm],
        out_shape=[shape_of((rows, WIDTH), BF), pltpu.HBM((GROUP, rows, 2 * rows), BF)],
        scratch_shapes=[
            pltpu.VMEM((GROUP, rows, 2 * rows), BF),
            pltpu.SemaphoreType.DMA((GROUP,)),
        ],
        compiler_params=params(12),
        cost_estimate=cost(GROUP * rows * 2 * rows * 256 * 8, 6e6, GROUP * rows * 2 * rows),
        name="attend",
    )(place, q, kv, other, bias)


def middle_kernel(n_parts, place_ref, x_ref, gain_ref, back_ref, *refs):
    ctx_refs, w_refs = refs[:4], refs[4 : 4 + 4 * n_parts]
    mid_ref, normed_ref, normed_t_ref, back_t_ref, whole = refs[4 + 4 * n_parts :]
    rows = x_ref.shape[0]
    total = x_ref[...].astype(F32)
    back_t_ref[...] = back_ref[...].T
    blank = jnp.zeros((rows, 64), BF)
    for b in range(4):
        part = w_refs[b * n_parts : (b + 1) * n_parts]
        assemble(whole.at[b], part, place_ref, 0, slice(512, 768))
        total = total + dot(jnp.concatenate([blank, ctx_refs[b][...]], 1), whole[b], NT)
    mid_ref[...] = total
    normed = rms_of(total, gain_ref[1:2].astype(F32)).astype(BF)
    normed_ref[...] = normed
    normed_t_ref[...] = normed.T


def middle(place, rows_in, gain_low, back, ctx, blocks):
    rows = rows_in.shape[0]
    n_parts = len(blocks[0])
    return pl.pallas_call(
        functools.partial(middle_kernel, n_parts),
        in_specs=[in_smem] + [in_vmem] * (7 + 4 * n_parts),
        out_specs=[in_vmem] * 4,
        out_shape=[
            shape_of((rows, D), F32),
            shape_of((rows, D), BF),
            shape_of((D, rows), BF),
            shape_of((D, rows), BF),
        ],
        scratch_shapes=[pltpu.VMEM((4, D, 256), BF)],
        compiler_params=params(10),
        cost_estimate=cost(2 * rows * D * D, 8e6),
        name="middle",
    )(place, rows_in, gain_low, back, *ctx, *[p for b in blocks for p in b])


def feed_kernel(n_parts, first, place_ref, n_ref, nt_ref, g_ref, gt_ref, *refs):
    if not first:
        acc_in, t_in = refs[:2]
        refs = refs[2:]
    w_refs, (acc_ref, t_ref, grads_ref, wi, wf, gi, gf) = refs[:n_parts], refs[n_parts:]
    assemble(wi, w_refs, place_ref, 0)
    assemble(wf, w_refs, place_ref, 1)
    pre = dot(n_ref[...], wi[...], NN)
    grad = dot(g_ref[...], wf[...], NN)
    cdf = 0.5 * (1.0 + lax.erf(pre * 0.7071067811865476))
    active = (pre * cdf).astype(BF)
    density = jnp.exp(pre * pre * -0.5) * 0.3989422804014327
    pre_grad = (grad * (cdf + pre * density)).astype(BF)
    if first:
        acc_ref[...] = dot(active, wf[...], NT)
        t_ref[...] = dot(pre_grad, wi[...], NT)
    else:
        acc_ref[...] = acc_in[...] + dot(active, wf[...], NT)
        t_ref[...] = t_in[...] + dot(pre_grad, wi[...], NT)
    gi[...] = dot(nt_ref[...], pre_grad, NN).astype(BF)
    deal_out(grads_ref, gi, place_ref, 0)
    gf[...] = dot(gt_ref[...], active, NN).astype(BF)
    deal_out(grads_ref, gf, place_ref, 1)


def feed(place, normed, normed_t, back, back_t, sums, block, grads):
    rows = normed.shape[0]
    n = len(block)
    first = sums is None
    outs = pl.pallas_call(
        functools.partial(feed_kernel, n, first),
        in_specs=[in_smem] + [in_vmem] * (4 + n + (0 if first else 2)),
        out_specs=[in_vmem] * 3,
        out_shape=[shape_of((rows, D), F32)] * 2 + [grads],
        scratch_shapes=[pltpu.VMEM((D, D), BF)] * 4,
        input_output_aliases={} if first else {5: 0, 6: 1},
        compiler_params=params(14),
        cost_estimate=cost(2 * 6 * rows * D * D, 15e6, 2 * rows * D),
        name="feed",
    )(place, normed, normed_t, back, back_t, *(sums or ()), *block)
    return (outs[0], outs[1]), outs[2]


def turn_kernel(n_parts, place_ref, mid_ref, acc_ref, t_ref, back_ref, gain_ref, *refs):
    w_refs = refs[: 4 * n_parts]
    rest = refs[4 * n_parts :]
    keep_ref, send_ref, grad_ref, low_t_ref, gain_grad_ref = rest[:5]
    cg_refs, whole = rest[5:9], rest[9]
    mid = mid_ref[...]
    out = (mid + acc_ref[...]).astype(BF)
    half = keep_ref.shape[0]
    keep_ref[...], send_ref[...] = out[:half], out[half:]
    grad, gain_grad = rms_back(mid, gain_ref[1:2].astype(F32), t_ref[...])
    gain_grad_ref[...] = gain_grad
    grad = back_ref[...].astype(F32) + grad
    grad_ref[...] = grad
    low = grad.astype(BF)
    low_t_ref[...] = low.T
    for b in range(4):
        part = w_refs[b * n_parts : (b + 1) * n_parts]
        assemble(whole.at[b], part, place_ref, 0, slice(512, 768))
        cg_refs[b][...] = dot(low, whole[b], NN).astype(BF)[:, 64:]


def turn(place, mid, acc, t_acc, back, gain_low, blocks):
    rows = mid.shape[0]
    n_parts = len(blocks[0])
    return pl.pallas_call(
        functools.partial(turn_kernel, n_parts),
        in_specs=[in_smem] + [in_vmem] * (5 + 4 * n_parts),
        out_specs=[in_vmem] * 9,
        out_shape=[
            shape_of((rows // 2, D), BF),
            shape_of((rows // 2, D), BF),
            shape_of((rows, D), F32),
            shape_of((D, rows), BF),
            shape_of((1, D), F32),
        ]
        + [shape_of((rows, WIDTH), BF)] * 4,
        scratch_shapes=[pltpu.VMEM((4, D, 256), BF)],
        compiler_params=params(12),
        cost_estimate=cost(2 * rows * D * D, 10e6),
        name="turn",
    )(place, mid, acc, t_acc, back, gain_low, *[p for b in blocks for p in b])


def attend_back_kernel(
    b,
    place_ref,
    q_ref,
    kv_ref,
    other_ref,
    g_ref,
    ctx_ref,
    p_ref,
    dq_ref,
    own_ref,
    send_ref,
    sums_ref,
    ds_ref,
):
    rows = q_ref.shape[1]
    step = 128
    lane = lax.broadcasted_iota(jnp.int32, (1, WIDTH), 1)
    row_tiles, key_tiles = tile_places(place_ref)
    grads = g_ref[...]
    both = jnp.concatenate([kv_ref[b], other_ref[b]], 0)
    keys = both[:, :WIDTH]
    values_t = both[:, WIDTH:].T
    queries_t, grads_t = q_ref[b].T, grads.T
    product = grads.astype(F32) * ctx_ref[...].astype(F32)
    sums_ref[...] = jnp.zeros_like(sums_ref)
    total = [jnp.zeros((step, WIDTH), F32) for _ in range(rows // step)]
    key_grads, value_grads = [], []
    for h in range(GROUP):
        inside = (lane >= h * DH) & (lane < (h + 1) * DH)
        for r in range(rows // step):
            span = slice(r * step, (r + 1) * step)
            here = jnp.where(inside, grads[span], jnp.zeros((), BF))
            prob_grad = dot(here, values_t, NN)
            row_dot = jnp.sum(jnp.where(inside, product[span], 0.0), axis=-1, keepdims=True)
            lows = []
            for c in range(8):
                prob = p_ref[h, pl.ds(r * step, step), pl.ds(c * TILE, TILE)].astype(F32)
                dscore = prob * (prob_grad[:, c * TILE : (c + 1) * TILE] - row_dot)
                which = jnp.clip(key_tiles[c] - row_tiles[r] + 2, 0, 4)
                sums_ref[h, which] += dscore
                lows.append(dscore.astype(BF))
            low = jnp.concatenate(lows, 1)
            ds_ref[pl.ds(r * step, step), :] = low
            total[r] = jnp.where(inside, dot(low, keys, NN), total[r])
        key_grads.append(dot(queries_t[h * DH : (h + 1) * DH], ds_ref[...], NN))
        value_grads.append(dot(grads_t[h * DH : (h + 1) * DH], p_ref[h], NN))
    for r in range(rows // step):
        dq_ref[pl.ds(r * step, step), :] = total[r].astype(BF)
    grad = jnp.concatenate(key_grads + value_grads, 0).T
    own_ref[...] = grad[:rows]
    send_ref[...] = grad[rows:].astype(BF)


def attend_back(place, q, kv, other, grads, ctx, prob, b):
    rows = q.shape[1]
    return pl.pallas_call(
        functools.partial(attend_back_kernel, b),
        in_specs=[in_smem] + [in_vmem] * 6,
        out_specs=[in_vmem] * 4,
        out_shape=[
            shape_of((rows, WIDTH), BF),
            shape_of((rows, 2 * WIDTH), F32),
            shape_of((rows, 2 * WIDTH), BF),
            shape_of((GROUP, 5, TILE, TILE), F32),
        ],
        scratch_shapes=[
            pltpu.VMEM((rows, 2 * rows), BF),
        ],
        compiler_params=params(8),
        cost_estimate=cost(GROUP * rows * 2 * rows * 256 * 12, 8e6),
        name="attend_back",
    )(place, q, kv, other, grads, ctx, prob)


def bucket_kernel(place_ref, *refs):
    out_ref = refs[-1]
    row = lax.broadcasted_iota(jnp.int32, (TILE, TILE), 0)
    col = lax.broadcasted_iota(jnp.int32, (TILE, TILE), 1)
    buckets = {t: bucket_of(col - row + (t - 2) * TILE) for t in range(1, 4)}
    for r in range(4):
        for h in range(GROUP):
            for b in range(NB):
                total = jnp.zeros((TILE, TILE), F32)
                if b == 15:
                    total = refs[r][h, 0]
                if b == 31:
                    total = refs[r][h, 4]
                for t in (1, 2) if b < 16 else (2, 3):
                    total = total + jnp.where(buckets[t] == b, refs[r][h, t], 0.0)
                total = jnp.sum(total, axis=0, keepdims=True)
                out_ref[place_ref[3] ^ r, h, pl.ds(b, 1), :] = total


def bucket_sums(place, sums):
    return pl.pallas_call(
        bucket_kernel,
        in_specs=[in_smem] + [in_vmem] * 4,
        out_specs=in_vmem,
        out_shape=shape_of((4, GROUP, NB, TILE), F32),
        compiler_params=params(4),
        cost_estimate=cost(32e6, 4e6),
        name="bucket_sums",
    )(place, *sums)


def project_back_kernel(n_parts, first, place_ref, nt_ref, low_t_ref, ctx_ref, dq_ref, own_ref, came_ref, *refs):
    if not first:
        acc_in, refs = refs[0], refs[1:]
    w_refs, (acc_ref, grads_ref, whole, grad) = refs[:n_parts], refs[n_parts:]
    assemble(whole, w_refs, place_ref)
    dkv = (own_ref[...] + came_ref[...].astype(F32)).astype(BF)
    heads = jnp.concatenate([dq_ref[...], dkv], 1)
    out = dot(nt_ref[...], heads, NN).astype(BF)
    last = dot(low_t_ref[...], ctx_ref[...], NN).astype(BF)
    grad[...] = jnp.concatenate([out, last], 1)
    deal_out(grads_ref, grad, place_ref)
    total = dot(heads, whole[:, 0:576], NT)
    acc_ref[...] = total if first else acc_in[...] + total


def project_back(place, normed_t, low_t, acc, ctx, dq, own, came, block, grads):
    rows = normed_t.shape[1]
    n = len(block)
    first = acc is None
    outs = pl.pallas_call(
        functools.partial(project_back_kernel, n, first),
        in_specs=[in_smem] + [in_vmem] * (6 + n + (0 if first else 1)),
        out_specs=[in_vmem] * 2,
        out_shape=[shape_of((rows, D), F32), grads],
        scratch_shapes=[pltpu.VMEM((D, D), BF)] * 2,
        input_output_aliases={} if first else {7: 0},
        compiler_params=params(8),
        cost_estimate=cost(2 * 2 * rows * D * D, 8e6),
        name="project_back",
    )(place, normed_t, low_t, ctx, dq, own, came, *([] if first else [acc]), *block)
    return outs


def add(a, b):
    return (a.astype(F32) + b.astype(F32)).astype(BF)


def merge_core_kernel(a_ref, b_ref, near_ref, far0_ref, far1_ref):
    for y, far_ref in enumerate((far0_ref, far1_ref)):
        near_ref[y] = add(a_ref[y, 0], b_ref[y, 0])
        far_ref[...] = add(a_ref[y, 1], b_ref[y, 1])


def merge_core(grads, came):
    part = shape_of(grads.shape[2:], BF)
    return pl.pallas_call(
        merge_core_kernel,
        in_specs=[in_vmem] * 2,
        out_specs=[in_vmem] * 3,
        out_shape=[shape_of(grads.shape[:1] + grads.shape[2:], BF), part, part],
        compiler_params=params(MERGE_MIB),
        cost_estimate=cost(1, 1),
        name="merge_core",
    )(grads, came)


def merge_half_kernel(near_ref, came_ref, a0_ref, b0_ref, a1_ref, b1_ref, y0_ref, y1_ref, x0_ref, x1_ref):
    y0_ref[...] = add(near_ref[0], came_ref[0])
    y1_ref[...] = add(near_ref[1], came_ref[1])
    x0_ref[...] = add(a0_ref[...], b0_ref[...])
    x1_ref[...] = add(a1_ref[...], b1_ref[...])


def merge_half(near, near_came, far, far_came):
    part = shape_of(near.shape[1:], BF)
    return pl.pallas_call(
        merge_half_kernel,
        in_specs=[in_vmem] * 6,
        out_specs=[in_vmem] * 4,
        out_shape=[part] * 4,
        compiler_params=params(MERGE_MIB),
        cost_estimate=cost(1, 1),
        name="merge_half",
    )(near, near_came, far[0], far_came[0], far[1], far_came[1])


def merge_last_kernel(near_ref, near_came_ref, far_ref, far_came_ref, own_ref, *outs):
    cut = near_ref.shape[0]
    own_ref[...] = near_ref[0].astype(F32) + near_came_ref[0].astype(F32)
    for k, out_ref in enumerate(outs, 1):
        a_ref, b_ref = (near_ref, near_came_ref) if k < cut else (far_ref, far_came_ref)
        out_ref[...] = add(a_ref[k % cut], b_ref[k % cut])


def merge_last(near, near_came, far, far_came):
    cut = near.shape[0]
    part = near.shape[1:]
    return pl.pallas_call(
        merge_last_kernel,
        in_specs=[in_vmem] * 4,
        out_specs=[in_vmem] * (2 * cut),
        out_shape=[shape_of(part, F32)] + [shape_of(part, BF)] * (2 * cut - 1),
        compiler_params=params(MERGE_MIB),
        cost_estimate=cost(1, 1),
        name="merge_last",
    )(near, near_came, far, far_came)


def total_kernel(own_ref, *refs):
    out_ref, squares_ref = refs[-2:]
    total = own_ref[...]
    for ref in refs[:-2]:
        total = total + ref[...].astype(F32)
    out_ref[...] = total
    squares_ref[...] = jnp.broadcast_to(jnp.sum(total * total), squares_ref.shape)


def total_of(own, came):
    return pl.pallas_call(
        total_kernel,
        in_specs=[in_vmem] * (1 + len(came)),
        out_specs=[in_vmem] * 2,
        out_shape=[shape_of(own.shape, F32), shape_of((1, TILE), F32)],
        compiler_params=params(MERGE_MIB),
        cost_estimate=cost(1, 1),
        name="total",
    )(own, *came)


def cast_attn_kernel(w_ref, out_ref):
    out_ref[0] = jnp.concatenate([w_ref[i].astype(BF) for i in range(4)], 1)


def cast_attn(weights):
    rows = weights.shape[1]
    return pl.pallas_call(
        cast_attn_kernel,
        in_specs=[in_vmem],
        out_specs=in_vmem,
        out_shape=shape_of((1, rows, D), BF),
        compiler_params=params(MERGE_MIB),
        cost_estimate=cost(1, 1),
        name="cast_attn",
    )(weights)


def sort_kernel(place_ref, in_ref, back_ref, in_keep, in_send, back_keep, back_send):
    here = place_ref[0]
    in_keep[...], in_send[...] = in_ref[here], in_ref[1 - here]
    back_keep[...], back_send[...] = back_ref[here], back_ref[1 - here]


def sort_rows(place, inputs, cotangent):
    part = shape_of(inputs.shape[1:], BF)
    return pl.pallas_call(
        sort_kernel,
        in_specs=[in_smem] + [in_vmem] * 2,
        out_specs=[in_vmem] * 4,
        out_shape=[part] * 4,
        compiler_params=params(MERGE_MIB),
        cost_estimate=cost(1, 1),
        name="sort_rows",
    )(place, inputs, cotangent)


def cast_ffn_kernel(w_ref, both_ref, wi_ref, wf_ref):
    low = w_ref[...].astype(BF)
    both_ref[...] = low
    wi_ref[...], wf_ref[...] = low[0:1], low[1:2]


def cast_ffn(weights):
    one = shape_of((1,) + weights.shape[1:], BF)
    return pl.pallas_call(
        cast_ffn_kernel,
        in_specs=[in_vmem],
        out_specs=[in_vmem] * 3,
        out_shape=[shape_of(weights.shape, BF), one, one],
        compiler_params=params(MERGE_MIB),
        cost_estimate=pl.CostEstimate(flops=10**12, bytes_accessed=10**9, transcendentals=0),
        name="cast_ffn",
    )(weights)


def line_up_kernel(n, *refs):
    out_ref = refs[n]
    cut, which = out_ref.shape[:2]
    per = n // cut
    for j in range(cut):
        for i in range(per):
            ref = refs[j * per + i]
            if per == 1:
                out_ref[j] = ref[...]
            else:
                out_ref[j, i] = ref[0]


def line_up(parts, cut):
    n = len(parts)
    which = parts[0].shape[0] * n // cut
    return pl.pallas_call(
        functools.partial(line_up_kernel, n),
        in_specs=[in_vmem] * n,
        out_specs=in_vmem,
        out_shape=shape_of((cut, which) + parts[0].shape[1:], BF),
        compiler_params=params(MERGE_MIB),
        cost_estimate=cost(1, 1),
        name="line_up",
    )(*parts)


def place_rows_kernel(place_ref, keep_ref, came_ref, out_ref):
    here = place_ref[0]
    out_ref[here] = keep_ref[...]
    out_ref[1 - here] = came_ref[...]


def place_rows(place, keep, came):
    return pl.pallas_call(
        place_rows_kernel,
        in_specs=[in_smem] + [in_vmem] * 2,
        out_specs=in_vmem,
        out_shape=shape_of((2,) + keep.shape, keep.dtype),
        compiler_params=params(MERGE_MIB),
        cost_estimate=cost(1, 1),
        name="place_rows",
    )(place, keep, came)


def finish_kernel(x_ref, gain_ref, t_ref, mid_grad_ref, keep_ref, send_ref, gain_grad_ref):
    grad, gain_grad = rms_back(x_ref[...].astype(F32), gain_ref[0:1].astype(F32), t_ref[...])
    out = (mid_grad_ref[...] + grad).astype(BF)
    half = keep_ref.shape[0]
    keep_ref[...], send_ref[...] = out[:half], out[half:]
    gain_grad_ref[...] = gain_grad


def finish(rows_in, gain_low, t_acc, mid_grad):
    rows = rows_in.shape[0]
    return pl.pallas_call(
        finish_kernel,
        in_specs=[in_vmem] * 4,
        out_specs=[in_vmem] * 3,
        out_shape=[shape_of((rows // 2, D), BF)] * 2 + [shape_of((1, D), F32)],
        compiler_params=params(8),
        cost_estimate=cost(rows * D * 12, 6e6),
        name="finish",
    )(rows_in, gain_low, t_acc, mid_grad)


def update_kernel(squares_ref, small_ref, *refs):
    grads, olds, outs = refs[:4], refs[4:16], refs[16:]
    squares = jnp.sum(squares_ref[...], axis=0, keepdims=True)[:, 0:1]
    small = small_ref[...]
    small = jnp.sum(jnp.sum(small * small, axis=0, keepdims=True), axis=1, keepdims=True)
    norm = jnp.sqrt(squares + small)
    outs[0][...] = norm
    clip = jnp.minimum(1.0, clip_level / (norm + 1e-06))
    settings = [(rate_matrix, matrix_decay)] * 2 + [(rate_small, 0.0)] * 2

    def step(kind, weight, first, second, gradient):
        return adam_step(weight, first, second, gradient * clip, *settings[kind])

    def spots(kind):
        return olds[3 * kind : 3 * kind + 3], outs[2 + 3 * kind : 5 + 3 * kind]

    old, new = spots(0)
    for i in range(4):
        gradient = grads[0][0, :, i * WIDTH : (i + 1) * WIDTH]
        outs[1][i] = gradient
        new[0][i], new[1][i], new[2][i] = step(0, old[0][i], old[1][i], old[2][i], gradient)
    for kind in range(1, 4):
        old, new = spots(kind)
        values = step(kind, old[0][...], old[1][...], old[2][...], grads[kind][...])
        new[0][...], new[1][...], new[2][...] = values


def update(squares, small, grads, olds):
    shapes = [shape_of((1, 1), F32), shape_of(olds[0].shape, F32)]
    shapes += [shape_of(v.shape, F32) for v in olds]
    return pl.pallas_call(
        update_kernel,
        in_specs=[in_vmem] * 18,
        out_specs=[in_vmem] * 14,
        out_shape=shapes,
        compiler_params=params(20),
        cost_estimate=cost(1, 1),
        name="update",
    )(squares, small, *grads, *olds)


def per_device(
    inputs,
    cotangent,
    lengths,
    attn_weights,
    attn_first,
    attn_second,
    ffn_weights,
    ffn_first,
    ffn_second,
    norm_gains,
    gain_first,
    gain_second,
    bias_table,
    table_first,
    table_second,
):
    assert lax.axis_size("mp") == 4 and inputs.shape[0] == 2
    depth = lax.axis_size("dp") // 2
    shard_rows = ffn_weights.shape[1]
    mp, dp = lax.axis_index("mp"), lax.axis_index("dp")
    x, core = mp // 2, mp % 2

    starts = [
        shard_rows * (((dp // 2) ^ s) * 2 + ((dp % 2) ^ y)) for y in range(2) for s in range(depth)
    ]
    if shard_rows % 16:
        starts = [jnp.zeros((), jnp.int32)]
    length = lax.dynamic_index_in_dim(lengths, x, 0, keepdims=False)
    place = jnp.stack([v.astype(jnp.int32) for v in [x, core, length, mp] + starts])
    cut = depth // 2
    feed_shape = grads_shape(depth, 2, shard_rows, D)
    attn_shape = grads_shape(depth, 1, shard_rows, D)

    attn_low = cast_attn(attn_weights)
    attn_z = [swap_z(attn_low, k) for k in range(1, depth)]
    rows_keep, rows_send, back_keep, back_send = sort_rows(place, inputs, cotangent)
    rows_came = swap_x(rows_send)
    gains = join_gains(spread_gains(norm_gains), 1)
    ffn_low, wi_low, wf_low = cast_ffn(ffn_weights)
    bias = make_bias(place, bias_table)
    attn_low, attn_z, gains, ffn_low, wi_low, wf_low, bias, place, back_send = fence(
        attn_low, attn_z, gains, ffn_low, wi_low, wf_low, bias, place, back_send
    )

    lined = [attn_low] + attn_z
    near, far = line_up(lined[:cut], cut), line_up(lined[cut:], cut)
    near_x, far_y = swap_x(near), swap_y(far)
    ffn_near_z = [swap_z(ffn_low, k) for k in range(1, cut)]
    gains = join_gains(gains, 2)
    near, far, near_x, far_y, gains, ffn_near_z, wi_low, rows_came = fence(
        near, far, near_x, far_y, gains, ffn_near_z, wi_low, rows_came
    )
    near_y, near_xy = swap_y(near), swap_y(near_x)
    far_x, far_xy = swap_x(far), swap_x(far_y)
    wi_far_z = [swap_z(wi_low, k) for k in range(cut, depth)]
    step = 4
    while step < 2 * depth:
        gains = join_gains(gains, step)
        step *= 2
    rows_in = jnp.concatenate([rows_keep, rows_came], 0)
    ffn_near = line_up([ffn_low] + ffn_near_z, cut)
    near_y, near_xy, far_x, far_xy, gains, rows_in, ffn_near, wi_far_z, wf_low, back_send = fence(
        near_y, near_xy, far_x, far_xy, gains, rows_in, ffn_near, wi_far_z, wf_low, back_send
    )

    attn_blocks = {
        0: block_views([[near, far], [near_y, far_y]]),
        2: block_views([[near_x, far_x], [near_xy, far_xy]]),
    }
    across = [swap_core(v) for v in (near, far, near_y, far_y, near_x, far_x, near_xy, far_xy)]
    wf_far_z = [swap_z(wf_low, k) for k in range(cut, depth)]
    ffn_near_x, ffn_near_y = swap_x(ffn_near), swap_y(ffn_near)
    q, kv, other = {}, {}, {}
    q[0], kv[0], normed_t = project(place, rows_in, gains, [attn_blocks[0], attn_blocks[2]], True)
    q, kv, normed_t = fence(q, kv, normed_t)
    other[1] = swap_core(kv[0])
    q, kv, across = fence(q, kv, across)
    attn_blocks[1] = block_views([across[0:2], across[2:4]])
    attn_blocks[3] = block_views([across[4:6], across[6:8]])
    q[1], kv[1] = project(place, rows_in, gains, [attn_blocks[1], attn_blocks[3]], False)
    q, kv = fence(q, kv)
    other[0] = swap_core(kv[1])
    q, kv, other[1] = fence(q, kv, other[1])

    ctx, prob = {}, {}

    def attend_at(r):
        ctx[r], prob[r] = attend(place, q[r % 2], kv[r % 2], other[r % 2], bias, r // 2, r)

    attend_at(1)
    ctx, prob, q = fence(ctx, prob, q)
    attend_at(3)
    ctx, prob, q = fence(ctx, prob, q)
    ctx, prob, q, other, wf_far_z, ffn_near_x, ffn_near_y, back_send = fence(
        ctx, prob, q, other, wf_far_z, ffn_near_x, ffn_near_y, back_send
    )
    ffn_far = line_up([v for pair in zip(wi_far_z, wf_far_z) for v in pair], cut)
    ffn_far_x, ffn_far_y = swap_x(ffn_far), swap_y(ffn_far)
    back_came = swap_x(back_send)
    attend_at(0)
    ctx, prob, q, ffn_far = fence(ctx, prob, q, ffn_far)
    attend_at(2)
    ctx, prob = fence(ctx, prob)
    ctx, back_came = fence(ctx, back_came)
    back = jnp.concatenate([back_keep, back_came], 0)
    mid, normed_two, normed_two_t, back_t = middle(
        place, rows_in, gains, back, [ctx[r] for r in range(4)], [attn_blocks[r] for r in range(4)]
    )
    mid, normed_two, normed_two_t, back_t = fence(mid, normed_two, normed_two_t, back_t)
    normed_two, ffn_far_x, ffn_far_y, ffn_near_x, ffn_near_y = fence(
        normed_two, ffn_far_x, ffn_far_y, ffn_near_x, ffn_near_y
    )
    ffn_near_xy, ffn_far_xy = swap_y(ffn_near_x), swap_x(ffn_far_y)
    feed_parts = {0: [[ffn_near, ffn_far], [ffn_near_y, ffn_far_y]]}
    feed_parts[1] = jax.tree.map(swap_core, feed_parts[0])
    grads = {}

    def feed_at(r, sums):
        sums, out = feed(
            place, normed_two, normed_two_t, back, back_t, sums, block_views(feed_parts[r]), feed_shape
        )
        grads[r] = by_place(out, depth, shard_rows)
        return sums

    sums = feed_at(0, None)
    sums, grads = fence(sums, grads)
    sums, grads, feed_parts[1] = fence(sums, grads, feed_parts[1])
    sums = feed_at(1, sums)
    sums, grads = fence(sums, grads)
    came = swap_core(grads[1])
    sums, ffn_near_xy, ffn_far_xy, ffn_far_x = fence(sums, ffn_near_xy, ffn_far_xy, ffn_far_x)
    feed_parts[2] = [[ffn_near_x, ffn_far_x], [ffn_near_xy, ffn_far_xy]]
    feed_parts[3] = jax.tree.map(swap_core, feed_parts[2])
    sums = feed_at(2, sums)
    sums, grads = fence(sums, grads)
    sums, grads, came, feed_parts[3] = fence(sums, grads, came, feed_parts[3])
    near0, far00, far01 = merge_core(grads[0], came)
    far01_y = swap_y(far01)
    sums = feed_at(3, sums)
    sums, grads, near0, far00 = fence(sums, grads, near0, far00)
    came = swap_core(grads[3])
    out_keep, out_send, mid_grad, mid_low_t, gain_two_grad, *cg = turn(
        place, mid, sums[0], sums[1], back, gains, [attn_blocks[r] for r in range(4)]
    )
    cg, mid_grad, mid_low_t, out_keep, out_send = fence(cg, mid_grad, mid_low_t, out_keep, out_send)
    cg, came, grads = fence(cg, came, grads)
    near1, far10, far11 = merge_core(grads[2], came)
    near1_x = swap_x(near1)
    far11_y = swap_y(far11)
    cg, far10 = fence(cg, far10)

    dq, own, send, tiles = {}, {}, {}, {}

    def attend_back_at(r):
        c = r % 2
        dq[r], own[r], send[r], tiles[r] = attend_back(
            place, q[c], kv[c], other[c], cg[r], ctx[r], prob[r], r // 2
        )

    got = {}
    attend_back_at(1)
    dq, own, send, tiles, cg = fence(dq, own, send, tiles, cg)
    got[0] = swap_core(send[1])
    attend_back_at(3)
    dq, own, send, tiles, cg = fence(dq, own, send, tiles, cg)
    got[2] = swap_core(send[3])
    attend_back_at(0)
    dq, own, send, tiles, cg = fence(dq, own, send, tiles, cg)
    got[1] = swap_core(send[0])
    attend_back_at(2)
    dq, own, send, tiles = fence(dq, own, send, tiles)
    got[3] = swap_core(send[2])
    send, far01_y, far11_y, near1_x, out_send = fence(send, far01_y, far11_y, near1_x, out_send)
    ffn_y0, ffn_y1, ffn_x0, ffn_x1 = merge_half(near0, near1_x, (far00, far10), (far01_y, far11_y))
    ffn_y1, ffn_x1 = swap_y(ffn_y1), swap_x(ffn_x1)
    got, ffn_y0, ffn_x0 = fence(got, ffn_y0, ffn_x0)
    attn_grads = {}

    def project_back_at(r, total):
        total, outs = project_back(
            place, normed_t, mid_low_t, total, ctx[r], dq[r], own[r], got[r], attn_blocks[r], attn_shape
        )
        attn_grads[r] = by_place(outs, depth, shard_rows)
        return total

    t_one = project_back_at(1, None)
    t_one, attn_grads = fence(t_one, attn_grads)
    came = {0: swap_core(attn_grads[1])}
    t_one = project_back_at(3, t_one)
    t_one, attn_grads = fence(t_one, attn_grads)
    came[2] = swap_core(attn_grads[3])
    t_one = project_back_at(0, t_one)
    t_one, attn_grads = fence(t_one, attn_grads)
    t_one = project_back_at(2, t_one)
    t_one, attn_grads, came = fence(t_one, attn_grads, came)
    near0, far00, far01 = merge_core(attn_grads[0], came[0])
    near1, far10, far11 = merge_core(attn_grads[2], came[2])
    near1_x = swap_x(near1)
    far01_y, far11_y = swap_y(far01), swap_y(far11)
    near0, far00, far10, ffn_y1, ffn_x1 = fence(near0, far00, far10, ffn_y1, ffn_x1)
    ffn_own, *ffn_far_own = merge_last(ffn_y0, ffn_y1, ffn_x0, ffn_x1)
    ffn_back = [swap_z(v, k) for k, v in enumerate(ffn_far_own, 1)]
    in_keep, in_send, gain_one_grad = finish(rows_in, gains, t_one, mid_grad)
    buckets = bucket_sums(place, [tiles[r] for r in range(4)])
    in_keep, in_send, gain_one_grad, buckets, ffn_own, out_send = fence(
        in_keep, in_send, gain_one_grad, buckets, ffn_own, out_send
    )
    table_part = jnp.sum(buckets, -1).reshape(H * NB)
    small = jnp.concatenate([gain_one_grad[0], gain_two_grad[0], table_part])
    small, near1_x, far01_y, far11_y = fence(small, near1_x, far01_y, far11_y)
    attn_y0, attn_y1, attn_x0, attn_x1 = merge_half(near0, near1_x, (far00, far10), (far01_y, far11_y))
    attn_y1, attn_x1 = swap_y(attn_y1), swap_x(attn_x1)
    small = jnp.sum(from_all(small.reshape(-1, TILE)), 0)
    small, attn_y1, attn_x1, attn_y0, attn_x0, out_send, in_send = fence(
        small, attn_y1, attn_x1, attn_y0, attn_x0, out_send, in_send
    )
    attn_own, *attn_far_own = merge_last(attn_y0, attn_y1, attn_x0, attn_x1)
    attn_back = [swap_z(v, k) for k, v in enumerate(attn_far_own, 1)]
    out_came, in_came = swap_x(out_send), swap_x(in_send)
    attn_own, small, ffn_back = fence(attn_own, small, ffn_back)
    ffn_total, ffn_squares = total_of(ffn_own, ffn_back)
    gain_total = small.reshape(-1)[: 2 * D].reshape(2, D)
    table_grads = small.reshape(-1)[2 * D :].reshape(H, NB)
    gain_cols = norm_gains.shape[1]
    gain_grads = lax.dynamic_slice_in_dim(gain_total, dp * gain_cols, gain_cols, 1)
    ffn_total, ffn_squares, gain_grads, table_grads, attn_back = fence(
        ffn_total, ffn_squares, gain_grads, table_grads, attn_back
    )
    attn_total, attn_squares = total_of(attn_own, attn_back)
    squares = from_all(attn_squares + ffn_squares)
    out_keep, in_keep, out_came, in_came = fence(out_keep, in_keep, out_came, in_came)
    block_out = place_rows(place, out_keep, out_came)
    input_grad = place_rows(place, in_keep, in_came)
    grad_norm, attn_reduced, *news = update(
        squares.reshape(-1, TILE),
        small,
        (attn_total, ffn_total, gain_grads, table_grads),
        (
            attn_weights,
            attn_first,
            attn_second,
            ffn_weights,
            ffn_first,
            ffn_second,
            norm_gains,
            gain_first,
            gain_second,
            bias_table,
            table_first,
            table_second,
        ),
    )
    return (
        block_out,
        input_grad,
        attn_reduced,
        ffn_total,
        gain_grads,
        table_grads,
        grad_norm.reshape(()),
        *news,
    )


def solution(mesh):
    placed = (
        P("dp", "mp", None),
        P("dp", "mp", None),
        P("dp"),
        P(None, "dp", "mp"),
        P(None, "dp", "mp"),
        P(None, "dp", "mp"),
        P(None, "dp", "mp"),
        P(None, "dp", "mp"),
        P(None, "dp", "mp"),
        P(None, "dp"),
        P(None, "dp"),
        P(None, "dp"),
        P(),
        P(),
        P(),
    )
    return jax.shard_map(
        per_device,
        mesh=mesh,
        in_specs=placed,
        out_specs=(
            P("dp", "mp", None),
            P("dp", "mp", None),
            P(None, "dp", "mp"),
            P(None, "dp", "mp"),
            P(None, "dp"),
            P(),
            P(),
            P(None, "dp", "mp"),
            P(None, "dp", "mp"),
            P(None, "dp", "mp"),
            P(None, "dp", "mp"),
            P(None, "dp", "mp"),
            P(None, "dp", "mp"),
            P(None, "dp"),
            P(None, "dp"),
            P(None, "dp"),
            P(),
            P(),
            P(),
        ),
        check_vma=False,
    )
```

```python
import functools

import jax
import jax.numpy as jnp
from jax import lax
from jax.experimental import pallas as pl
from jax.experimental.pallas import tpu as pltpu
from jax.sharding import PartitionSpec as P

H = 12
DH = 64
NB = 32
STEP = 10
D = 768

norm_eps = 1e-06
beta_one = 0.9
beta_two = 0.999
adam_eps = 1e-08
matrix_decay = 0.01
rate_matrix = 0.05
rate_small = 0.4
clip_level = 1.0

FEED_MIB = 18
BACK_MIB = 12
MERGE_MIB = 8

BF = jnp.bfloat16
F32 = jnp.float32
TILE = 128
GROUP = 3
WIDTH = GROUP * DH
NN = (((1,), (0,)), ((), ()))
NT = (((1,), (1,)), ((), ()))

shape_of = jax.ShapeDtypeStruct
in_smem = pl.BlockSpec(memory_space=pltpu.SMEM)
in_hbm = pl.BlockSpec(memory_space=pltpu.HBM)
in_vmem = pl.BlockSpec(memory_space=pltpu.VMEM)


def keep_hbm(v):
    return pltpu.with_memory_space_constraint(v, pltpu.HBM)


def dot(left, right, dims):
    return lax.dot_general(left, right, dims, preferred_element_type=F32)


def params(mib):
    return pltpu.CompilerParams(vmem_limit_bytes=mib << 20)


def cost(flops, bytes_accessed, transcendentals=0):
    return pl.CostEstimate(flops=1000, bytes_accessed=1000, transcendentals=0)


def bucket_of(offset):
    distance = jnp.abs(offset)
    coarse = jnp.full(offset.shape, 8, jnp.int32)
    for level_bit in range(1, 8):
        coarse = coarse + (distance * distance >= 64 * 2**level_bit).astype(jnp.int32)
    inside = jnp.where(distance < 8, distance, coarse)
    return inside + jnp.where(offset > 0, 16, 0).astype(jnp.int32)


def adam_step(weight, first_old, second_old, gradient, step_rate, weight_decay):
    first_new = beta_one * first_old + (1.0 - beta_one) * gradient
    second_new = beta_two * second_old + (1.0 - beta_two) * gradient * gradient
    first_hat = first_new / (1.0 - beta_one**STEP)
    second_hat = second_new / (1.0 - beta_two**STEP)
    weight_new = weight - step_rate * (
        first_hat / (jnp.sqrt(second_hat) + adam_eps) + weight_decay * weight
    )
    return (weight_new, first_new, second_new)


def swap_core(v):
    return lax.ppermute(v, "mp", [(i, i ^ 1) for i in range(4)])


def swap_x(v):
    return lax.ppermute(v, "mp", [(i, i ^ 2) for i in range(4)])


def swap_y(v):
    n = lax.axis_size("dp")
    return lax.ppermute(v, "dp", [(i, i ^ 1) for i in range(n)])


def swap_z(v, k):
    n = lax.axis_size("dp")
    return lax.ppermute(v, "dp", [(i, i ^ (2 * k)) for i in range(n)])


def fence(*values):
    return lax.optimization_barrier(values)


def from_all(v):
    n = lax.axis_size("dp") * lax.axis_size("mp")
    return lax.all_to_all(jnp.broadcast_to(v[None], (n,) + v.shape), ("dp", "mp"), 0, 0)


def gather_gains(gains):
    n = lax.axis_size("dp")
    low = gains.astype(BF)
    return lax.all_to_all(jnp.broadcast_to(low[None], (n,) + low.shape), "dp", 0, 0)


def block_views(by_y):
    entries = [e if isinstance(e, tuple) else (e, None) for parts in by_y for e in parts]
    rows = entries[0][0].shape[-2]
    if rows % 16 == 0:
        return [v for v, _ in entries], tuple(i for _, i in entries)
    plain = [v if i is None else v[i] for v, i in entries]
    which, cols = plain[0].shape[1], plain[0].shape[3]
    dp = lax.axis_index("dp")
    both = jnp.stack([jnp.concatenate(plain[2 * y : 2 * y + 2], 0) for y in range(2)])
    depth = both.shape[1]
    sides = jnp.take(both, jnp.arange(2) ^ (dp % 2), axis=0)
    lined = jnp.take(sides, jnp.arange(depth) ^ (dp // 2), axis=1)
    return [jnp.transpose(lined, (2, 1, 0, 3, 4)).reshape(1, which, D, cols)], (None,)


def pick(refs, indices):
    return [ref if i is None else ref.at[i] for ref, i in zip(refs, indices)]


def grads_shape(depth, which, rows, cols):
    if rows % 16 == 0:
        return shape_of((2, 2, depth // 2, which, rows, cols), BF)
    return shape_of((1, 1, 1, which, D, cols), BF)


def by_place(grads, depth, rows):
    if rows % 16 == 0:
        return grads
    which = grads.shape[3]
    dp = lax.axis_index("dp")
    lined = jnp.transpose(grads.reshape(which, depth, 2, rows, -1), (2, 1, 0, 3, 4))
    sides = jnp.take(lined, jnp.arange(2) ^ (dp % 2), axis=0)
    turned = jnp.take(sides, jnp.arange(depth) ^ (dp // 2), axis=1)
    return turned.reshape(2, 2, depth // 2, which, rows, -1)


def assemble(whole, refs, place_ref, which=0, cols=slice(None)):
    count = 0
    for ref in refs:
        for j in range(ref.shape[0]):
            start = pl.multiple_of(place_ref[5 + count], 16)
            whole[pl.ds(start, ref.shape[2]), :] = ref[j, which, :, cols]
            count += 1


def deal_out(ref, whole, place_ref, which=0):
    count = 0
    for y in range(ref.shape[0]):
        for half in range(ref.shape[1]):
            for j in range(ref.shape[2]):
                start = pl.multiple_of(place_ref[5 + count], 16)
                ref[y, half, j, which] = whole[pl.ds(start, ref.shape[4]), :]
                count += 1


def bias_kernel(place_ref, table_ref, out_ref):
    block = pl.program_id(0)
    head_base = (place_ref[2] ^ block) * GROUP
    row = lax.broadcasted_iota(jnp.int32, (TILE, TILE), 0)
    col = lax.broadcasted_iota(jnp.int32, (TILE, TILE), 1)
    for h in range(GROUP):
        out_ref[0, h, 0] = jnp.full((TILE, TILE), table_ref[head_base + h, 15], F32)
        out_ref[0, h, 4] = jnp.full((TILE, TILE), table_ref[head_base + h, 31], F32)
    for t in range(1, 4):
        bucket = bucket_of(col - row + (t - 2) * TILE)
        which = {1: range(16), 2: range(32), 3: range(16, 32)}[t]
        for h in range(GROUP):
            tile = jnp.zeros((TILE, TILE), F32)
            for b in which:
                tile = jnp.where(bucket == b, table_ref[head_base + h, b], tile)
            out_ref[0, h, t] = tile


def make_bias(place, table):
    return pl.pallas_call(
        bias_kernel,
        grid=(4,),
        in_specs=[in_smem, in_smem],
        out_specs=pl.BlockSpec((1, GROUP, 5, TILE, TILE), lambda i: (i, 0, 0, 0, 0)),
        out_shape=shape_of((4, GROUP, 5, TILE, TILE), F32),
        compiler_params=params(6),
        cost_estimate=cost(10e6, 4e6),
        name="bias_tiles",
    )(place, table)


def rms_of(v, gain):
    inverse = lax.rsqrt(jnp.mean(v * v, axis=-1, keepdims=True) + norm_eps)
    return v * inverse * gain


def rms_back(v, gain, t):
    inverse = lax.rsqrt(jnp.mean(v * v, axis=-1, keepdims=True) + norm_eps)
    along = jnp.mean(v * gain * t, axis=-1, keepdims=True)
    grad = inverse * gain * t - v * (inverse * inverse * inverse) * along
    return grad, jnp.sum(t * v * inverse, axis=0, keepdims=True)


def project_kernel(indices, place_ref, x_ref, gain_ref, *refs):
    n_parts = len(indices[0])
    w_refs, rest = refs[: 2 * n_parts], refs[2 * n_parts :]
    q_ref, kv_ref = rest[:2]
    whole = rest[-1]
    normed = rms_of(x_ref[...].astype(F32), gain_ref[0:1].astype(F32)).astype(BF)
    if len(rest) == 4:
        rest[2][...] = normed.T
    for b in range(2):
        part = pick(w_refs[b * n_parts : (b + 1) * n_parts], indices[b])
        assemble(whole.at[b], part, place_ref)
        out = dot(normed, whole[b, :, 0:640], NN).astype(BF)
        q_ref[b] = out[:, 0:WIDTH]
        keys, values = out[:, WIDTH : 2 * WIDTH], out[:, 2 * WIDTH : 3 * WIDTH]
        kv_ref[b] = jnp.concatenate([keys, values], 1)


def project(place, rows_in, gain_low, blocks, turned):
    rows = rows_in.shape[0]
    n_parts = len(blocks[0][0])
    shapes = [shape_of((2, rows, WIDTH), BF), shape_of((2, rows, 2 * WIDTH), BF)]
    if turned:
        shapes.append(shape_of((D, rows), BF))
    return pl.pallas_call(
        functools.partial(project_kernel, [i for _, i in blocks]),
        in_specs=[in_smem] + [in_vmem] * (2 + 2 * n_parts),
        out_specs=[in_vmem] * len(shapes),
        out_shape=shapes,
        scratch_shapes=[pltpu.VMEM((2, D, D), BF)],
        compiler_params=params(8),
        cost_estimate=cost(2 * 2 * rows * D * 576, 5e6),
        name="project",
    )(place, rows_in, gain_low, *blocks[0][0], *blocks[1][0])


def tile_places(place_ref):
    x, core = place_ref[0], place_ref[1]
    mine = [4 * (x if t < 2 else 1 - x) + 2 * core + t % 2 for t in range(4)]
    theirs = [4 * (x if t < 2 else 1 - x) + 2 * (1 - core) + t % 2 for t in range(4)]
    return mine, mine + theirs


def attend_kernel(
    b, r_index, place_ref, q_ref, kv_ref, other_ref, bias_ref, ctx_ref, p_out, p_ref, sems
):
    rows = q_ref.shape[1]
    step = 256
    lane = lax.broadcasted_iota(jnp.int32, (1, 256), 1)
    key = lax.broadcasted_iota(jnp.int32, (1, TILE), 1)
    sub = lax.broadcasted_iota(jnp.int32, (64, 1), 0)
    row_tiles, key_tiles = tile_places(place_ref)
    length = place_ref[3 + place_ref[0]]
    hide = jnp.concatenate([jnp.where(key + TILE * g < length, 0.0, -1e30) for g in key_tiles], 1)
    extra = jnp.where(sub == 0, hide, 0.0).astype(BF)
    both = jnp.concatenate([kv_ref[b], other_ref[b]], 0)
    keys_t = jnp.concatenate([both[:, :WIDTH].T, extra], 0)
    values = both[:, WIDTH:]
    queries = jnp.concatenate([q_ref[b], jnp.ones((rows, 64), BF)], 1)
    total = [jnp.zeros((step, WIDTH), F32) for _ in range(rows // step)]
    for h in range(GROUP):
        inside = (lane >= h * DH) & (lane < (h + 1) * DH)
        used = inside | (lane == WIDTH)
        for r in range(rows // step):
            here = jnp.where(used, queries[r * step : (r + 1) * step], jnp.zeros((), BF))
            scores = dot(here, keys_t, NN)
            tiles = []
            for c in range(8):
                bias = []
                for u in range(step // TILE):
                    which = jnp.clip(key_tiles[c] - row_tiles[r * (step // TILE) + u] + 2, 0, 4)
                    bias.append(bias_ref[r_index, h, which])
                tiles.append(scores[:, c * TILE : (c + 1) * TILE] + jnp.concatenate(bias, 0))
            top = jnp.max(functools.reduce(jnp.maximum, tiles), axis=-1, keepdims=True)
            exps = [jnp.exp(t - top) for t in tiles]
            norm = jnp.sum(functools.reduce(jnp.add, exps), axis=-1, keepdims=True)
            scale = 1.0 / norm
            prob = jnp.concatenate([(e * scale).astype(BF) for e in exps], 1)
            p_ref[h, pl.ds(r * step, step), :] = prob
            total[r] = jnp.where(inside[:, :WIDTH], dot(prob, values, NN), total[r])
        pltpu.make_async_copy(p_ref.at[h], p_out.at[h], sems.at[h]).start()
    for r in range(rows // step):
        ctx_ref[pl.ds(r * step, step), :] = total[r].astype(BF)
    for h in range(GROUP):
        pltpu.make_async_copy(p_ref.at[h], p_out.at[h], sems.at[h]).wait()


def attend(place, q, kv, other, bias, b, r_index):
    rows = q.shape[1]
    return pl.pallas_call(
        functools.partial(attend_kernel, b, r_index),
        in_specs=[in_smem] + [in_vmem] * 4,
        out_specs=[in_vmem, in_hbm],
        out_shape=[shape_of((rows, WIDTH), BF), pltpu.HBM((GROUP, rows, 2 * rows), BF)],
        scratch_shapes=[
            pltpu.VMEM((GROUP, rows, 2 * rows), BF),
            pltpu.SemaphoreType.DMA((GROUP,)),
        ],
        compiler_params=params(12),
        cost_estimate=cost(GROUP * rows * 2 * rows * 256 * 8, 6e6, GROUP * rows * 2 * rows),
        name="attend",
    )(place, q, kv, other, bias)


def middle_kernel(indices, place_ref, x_ref, gain_ref, back_ref, *refs):
    n_parts = len(indices[0])
    ctx_refs, w_refs = refs[:4], refs[4 : 4 + 4 * n_parts]
    mid_ref, normed_ref, normed_t_ref, back_t_ref, whole = refs[4 + 4 * n_parts :]
    rows = x_ref.shape[0]
    total = x_ref[...].astype(F32)
    back_t_ref[...] = back_ref[...].T
    blank = jnp.zeros((rows, 64), BF)
    for b in range(4):
        part = pick(w_refs[b * n_parts : (b + 1) * n_parts], indices[b])
        assemble(whole.at[b], part, place_ref, 0, slice(512, 768))
        total = total + dot(jnp.concatenate([blank, ctx_refs[b][...]], 1), whole[b], NT)
    mid_ref[...] = total
    normed = rms_of(total, gain_ref[1:2].astype(F32)).astype(BF)
    normed_ref[...] = normed
    normed_t_ref[...] = normed.T


def middle(place, rows_in, gain_low, back, ctx, blocks):
    rows = rows_in.shape[0]
    n_parts = len(blocks[0][0])
    return pl.pallas_call(
        functools.partial(middle_kernel, [i for _, i in blocks]),
        in_specs=[in_smem] + [in_vmem] * (7 + 4 * n_parts),
        out_specs=[in_vmem] * 4,
        out_shape=[
            shape_of((rows, D), F32),
            shape_of((rows, D), BF),
            shape_of((D, rows), BF),
            shape_of((D, rows), BF),
        ],
        scratch_shapes=[pltpu.VMEM((4, D, 256), BF)],
        compiler_params=params(10),
        cost_estimate=cost(2 * rows * D * D, 8e6),
        name="middle",
    )(place, rows_in, gain_low, back, *ctx, *[p for b, _ in blocks for p in b])


def feed_kernel(indices, first, place_ref, n_ref, nt_ref, g_ref, gt_ref, *refs):
    if not first:
        acc_in, t_in = refs[:2]
        refs = refs[2:]
    n_parts = len(indices)
    w_refs, (acc_ref, t_ref, grads_ref, wi, wf, gi, gf) = refs[:n_parts], refs[n_parts:]
    w_refs = pick(w_refs, indices)
    assemble(wi, w_refs, place_ref, 0)
    assemble(wf, w_refs, place_ref, 1)
    pre = dot(n_ref[...], wi[...], NN)
    grad = dot(g_ref[...], wf[...], NN)
    cdf = 0.5 * (1.0 + lax.erf(pre * 0.7071067811865476))
    active = (pre * cdf).astype(BF)
    density = jnp.exp(pre * pre * -0.5) * 0.3989422804014327
    pre_grad = (grad * (cdf + pre * density)).astype(BF)
    if first:
        acc_ref[...] = dot(active, wf[...], NT)
        t_ref[...] = dot(pre_grad, wi[...], NT)
    else:
        acc_ref[...] = acc_in[...] + dot(active, wf[...], NT)
        t_ref[...] = t_in[...] + dot(pre_grad, wi[...], NT)
    gi[...] = dot(nt_ref[...], pre_grad, NN).astype(BF)
    deal_out(grads_ref, gi, place_ref, 0)
    gf[...] = dot(gt_ref[...], active, NN).astype(BF)
    deal_out(grads_ref, gf, place_ref, 1)


def feed(place, normed, normed_t, back, back_t, sums, block, grads):
    rows = normed.shape[0]
    block, indices = block
    n = len(block)
    first = sums is None
    outs = pl.pallas_call(
        functools.partial(feed_kernel, indices, first),
        in_specs=[in_smem] + [in_vmem] * (4 + n + (0 if first else 2)),
        out_specs=[in_vmem] * 3,
        out_shape=[shape_of((rows, D), F32)] * 2 + [grads],
        scratch_shapes=[pltpu.VMEM((D, D), BF)] * 4,
        input_output_aliases={} if first else {5: 0, 6: 1},
        compiler_params=params(14),
        cost_estimate=cost(2 * 6 * rows * D * D, 15e6, 2 * rows * D),
        name="feed",
    )(place, normed, normed_t, back, back_t, *(sums or ()), *block)
    return (outs[0], outs[1]), outs[2]


def turn_kernel(indices, place_ref, mid_ref, acc_ref, t_ref, back_ref, gain_ref, *refs):
    n_parts = len(indices[0])
    w_refs = refs[: 4 * n_parts]
    rest = refs[4 * n_parts :]
    keep_ref, send_ref, grad_ref, low_t_ref, gain_grad_ref = rest[:5]
    cg_refs, whole = rest[5:9], rest[9]
    mid = mid_ref[...]
    out = (mid + acc_ref[...]).astype(BF)
    half = keep_ref.shape[0]
    keep_ref[...], send_ref[...] = out[:half], out[half:]
    grad, gain_grad = rms_back(mid, gain_ref[1:2].astype(F32), t_ref[...])
    gain_grad_ref[...] = gain_grad
    grad = back_ref[...].astype(F32) + grad
    grad_ref[...] = grad
    low = grad.astype(BF)
    low_t_ref[...] = low.T
    for b in range(4):
        part = pick(w_refs[b * n_parts : (b + 1) * n_parts], indices[b])
        assemble(whole.at[b], part, place_ref, 0, slice(512, 768))
        cg_refs[b][...] = dot(low, whole[b], NN).astype(BF)[:, 64:]


def turn(place, mid, acc, t_acc, back, gain_low, blocks):
    rows = mid.shape[0]
    n_parts = len(blocks[0][0])
    return pl.pallas_call(
        functools.partial(turn_kernel, [i for _, i in blocks]),
        in_specs=[in_smem] + [in_vmem] * (5 + 4 * n_parts),
        out_specs=[in_vmem] * 9,
        out_shape=[
            shape_of((rows // 2, D), BF),
            shape_of((rows // 2, D), BF),
            shape_of((rows, D), F32),
            shape_of((D, rows), BF),
            shape_of((1, D), F32),
        ]
        + [shape_of((rows, WIDTH), BF)] * 4,
        scratch_shapes=[pltpu.VMEM((4, D, 256), BF)],
        compiler_params=params(12),
        cost_estimate=cost(2 * rows * D * D, 10e6),
        name="turn",
    )(place, mid, acc, t_acc, back, gain_low, *[p for b, _ in blocks for p in b])


def attend_back_kernel(
    b,
    place_ref,
    q_ref,
    kv_ref,
    other_ref,
    g_ref,
    ctx_ref,
    p_ref,
    dq_ref,
    own_ref,
    send_ref,
    bucket_ref,
    ds_ref,
    sums_ref,
):
    rows = q_ref.shape[1]
    step = 128
    lane = lax.broadcasted_iota(jnp.int32, (1, WIDTH), 1)
    row_tiles, key_tiles = tile_places(place_ref)
    grads = g_ref[...]
    both = jnp.concatenate([kv_ref[b], other_ref[b]], 0)
    keys = both[:, :WIDTH]
    values_t = both[:, WIDTH:].T
    queries_t, grads_t = q_ref[b].T, grads.T
    product = grads.astype(F32) * ctx_ref[...].astype(F32)
    sums_ref[...] = jnp.zeros_like(sums_ref)
    total = [jnp.zeros((step, WIDTH), F32) for _ in range(rows // step)]
    key_grads, value_grads = [], []
    for h in range(GROUP):
        inside = (lane >= h * DH) & (lane < (h + 1) * DH)
        for r in range(rows // step):
            span = slice(r * step, (r + 1) * step)
            here = jnp.where(inside, grads[span], jnp.zeros((), BF))
            prob_grad = dot(here, values_t, NN)
            row_dot = jnp.sum(jnp.where(inside, product[span], 0.0), axis=-1, keepdims=True)
            lows = []
            for c in range(8):
                prob = p_ref[h, pl.ds(r * step, step), pl.ds(c * TILE, TILE)].astype(F32)
                dscore = prob * (prob_grad[:, c * TILE : (c + 1) * TILE] - row_dot)
                which = jnp.clip(key_tiles[c] - row_tiles[r] + 2, 0, 4)
                sums_ref[h, which] += dscore
                lows.append(dscore.astype(BF))
            low = jnp.concatenate(lows, 1)
            ds_ref[pl.ds(r * step, step), :] = low
            total[r] = jnp.where(inside, dot(low, keys, NN), total[r])
        key_grads.append(dot(queries_t[h * DH : (h + 1) * DH], ds_ref[...], NN))
        value_grads.append(dot(grads_t[h * DH : (h + 1) * DH], p_ref[h], NN))
    for r in range(rows // step):
        dq_ref[pl.ds(r * step, step), :] = total[r].astype(BF)
    grad = jnp.concatenate(key_grads + value_grads, 0).T
    own_ref[...] = grad[:rows]
    send_ref[...] = grad[rows:].astype(BF)
    row = lax.broadcasted_iota(jnp.int32, (TILE, TILE), 0)
    col = lax.broadcasted_iota(jnp.int32, (TILE, TILE), 1)
    buckets = {t: bucket_of(col - row + (t - 2) * TILE) for t in range(1, 4)}
    for b in range(NB):
        masks = {t: buckets[t] == b for t in ((1, 2) if b < 16 else (2, 3))}
        for h in range(GROUP):
            total = jnp.zeros((TILE, TILE), F32)
            if b % 16 == 15:
                total = sums_ref[h, 0 if b == 15 else 4]
            for t, mask in masks.items():
                total = total + jnp.where(mask, sums_ref[h, t], 0.0)
            bucket_ref[h, pl.ds(b, 1), :] = jnp.sum(total, axis=0, keepdims=True)


def attend_back(place, q, kv, other, grads, ctx, prob, b):
    rows = q.shape[1]
    return pl.pallas_call(
        functools.partial(attend_back_kernel, b),
        in_specs=[in_smem] + [in_vmem] * 6,
        out_specs=[in_vmem] * 4,
        out_shape=[
            shape_of((rows, WIDTH), BF),
            shape_of((rows, 2 * WIDTH), F32),
            shape_of((rows, 2 * WIDTH), BF),
            shape_of((GROUP, NB, TILE), F32),
        ],
        scratch_shapes=[
            pltpu.VMEM((rows, 2 * rows), BF),
            pltpu.VMEM((GROUP, 5, TILE, TILE), F32),
        ],
        compiler_params=params(8),
        cost_estimate=cost(GROUP * rows * 2 * rows * 256 * 12, 8e6),
        name="attend_back",
    )(place, q, kv, other, grads, ctx, prob)


def project_back_kernel(indices, first, place_ref, nt_ref, low_t_ref, ctx_ref, dq_ref, own_ref, came_ref, *refs):
    if not first:
        acc_in, refs = refs[0], refs[1:]
    n_parts = len(indices)
    w_refs, (acc_ref, grads_ref, whole, grad) = refs[:n_parts], refs[n_parts:]
    w_refs = pick(w_refs, indices)
    assemble(whole, w_refs, place_ref)
    dkv = (own_ref[...] + came_ref[...].astype(F32)).astype(BF)
    heads = jnp.concatenate([dq_ref[...], dkv], 1)
    out = dot(nt_ref[...], heads, NN).astype(BF)
    last = dot(low_t_ref[...], ctx_ref[...], NN).astype(BF)
    grad[...] = jnp.concatenate([out, last], 1)
    deal_out(grads_ref, grad, place_ref)
    total = dot(heads, whole[:, 0:576], NT)
    acc_ref[...] = total if first else acc_in[...] + total


def project_back(place, normed_t, low_t, acc, ctx, dq, own, came, block, grads):
    rows = normed_t.shape[1]
    block, indices = block
    n = len(block)
    first = acc is None
    outs = pl.pallas_call(
        functools.partial(project_back_kernel, indices, first),
        in_specs=[in_smem] + [in_vmem] * (6 + n + (0 if first else 1)),
        out_specs=[in_vmem] * 2,
        out_shape=[shape_of((rows, D), F32), grads],
        scratch_shapes=[pltpu.VMEM((D, D), BF)] * 2,
        input_output_aliases={} if first else {7: 0},
        compiler_params=params(8),
        cost_estimate=cost(2 * 2 * rows * D * D, 8e6),
        name="project_back",
    )(place, normed_t, low_t, ctx, dq, own, came, *([] if first else [acc]), *block)
    return outs


def add(a, b):
    return (a.astype(F32) + b.astype(F32)).astype(BF)


def merge_core_kernel(*refs):
    near0_ref, near1_ref, far0_ref, far1_ref = refs[4:]
    for i, near_ref in enumerate((near0_ref, near1_ref)):
        a_ref, b_ref = refs[2 * i : 2 * i + 2]
        for y, far_ref in enumerate((far0_ref, far1_ref)):
            near_ref[y] = add(a_ref[y, 0], b_ref[y, 0])
            far_ref[i] = add(a_ref[y, 1], b_ref[y, 1])


def merge_core(grads0, came0, grads2, came2):
    part = shape_of(grads0.shape[:1] + grads0.shape[2:], BF)
    return pl.pallas_call(
        merge_core_kernel,
        in_specs=[in_vmem] * 4,
        out_specs=[in_vmem] * 4,
        out_shape=[part] * 4,
        compiler_params=params(MERGE_MIB),
        cost_estimate=cost(1, 1),
        name="merge_core",
    )(grads0, came0, grads2, came2)


def merge_half_kernel(near_ref, near_came_ref, far_ref, far_came_ref, y0_ref, y1_ref, x0_ref, x1_ref):
    y0_ref[...] = add(near_ref[0], near_came_ref[0])
    y1_ref[...] = add(near_ref[1], near_came_ref[1])
    x0_ref[...] = add(far_ref[0], far_came_ref[0])
    x1_ref[...] = add(far_ref[1], far_came_ref[1])


def merge_half(near, near_came, far, far_came):
    part = shape_of(near.shape[1:], BF)
    return pl.pallas_call(
        merge_half_kernel,
        in_specs=[in_vmem] * 4,
        out_specs=[in_vmem] * 4,
        out_shape=[part] * 4,
        compiler_params=params(MERGE_MIB),
        cost_estimate=cost(1, 1),
        name="merge_half",
    )(near, near_came, far, far_came)


def merge_last_kernel(near_ref, near_came_ref, far_ref, far_came_ref, own_ref, *outs):
    cut = near_ref.shape[0]
    own_ref[...] = near_ref[0].astype(F32) + near_came_ref[0].astype(F32)
    for k, out_ref in enumerate(outs, 1):
        a_ref, b_ref = (near_ref, near_came_ref) if k < cut else (far_ref, far_came_ref)
        out_ref[...] = add(a_ref[k % cut], b_ref[k % cut])


def merge_last(near, near_came, far, far_came):
    cut = near.shape[0]
    part = near.shape[1:]
    return pl.pallas_call(
        merge_last_kernel,
        in_specs=[in_vmem] * 4,
        out_specs=[in_vmem] * (2 * cut),
        out_shape=[shape_of(part, F32)] + [shape_of(part, BF)] * (2 * cut - 1),
        compiler_params=params(MERGE_MIB),
        cost_estimate=cost(1, 1),
        name="merge_last",
    )(near, near_came, far, far_came)


def total_kernel(own_ref, *refs):
    out_ref, squares_ref = refs[-2:]
    total = own_ref[...]
    for ref in refs[:-2]:
        total = total + ref[...].astype(F32)
    out_ref[...] = total
    squares_ref[...] = jnp.broadcast_to(jnp.sum(total * total), squares_ref.shape)


def total_of(own, came):
    return pl.pallas_call(
        total_kernel,
        in_specs=[in_vmem] * (1 + len(came)),
        out_specs=[in_vmem] * 2,
        out_shape=[shape_of(own.shape, F32), shape_of((1, TILE), F32)],
        compiler_params=params(MERGE_MIB),
        cost_estimate=cost(1, 1),
        name="total",
    )(own, *came)


def cast_attn_kernel(w_ref, out_ref):
    out_ref[0] = jnp.concatenate([w_ref[i].astype(BF) for i in range(4)], 1)


def cast_attn(weights):
    rows = weights.shape[1]
    return pl.pallas_call(
        cast_attn_kernel,
        in_specs=[in_vmem],
        out_specs=in_vmem,
        out_shape=shape_of((1, rows, D), BF),
        compiler_params=params(MERGE_MIB),
        cost_estimate=cost(1, 1),
        name="cast_attn",
    )(weights)


def sort_kernel(place_ref, in_ref, back_ref, in_keep, in_send, back_keep, back_send, sems):
    here = place_ref[0]
    pairs = [
        (in_ref.at[1 - here], in_send),
        (back_ref.at[1 - here], back_send),
        (in_ref.at[here], in_keep),
        (back_ref.at[here], back_keep),
    ]
    copies = [pltpu.make_async_copy(a, b, sems.at[i]) for i, (a, b) in enumerate(pairs)]
    for c in copies:
        c.start()
    for c in copies:
        c.wait()


def sort_rows(place, inputs, cotangent):
    part = shape_of(inputs.shape[1:], BF)
    return pl.pallas_call(
        sort_kernel,
        in_specs=[in_smem] + [in_hbm] * 2,
        out_specs=[in_vmem] * 4,
        out_shape=[part] * 4,
        scratch_shapes=[pltpu.SemaphoreType.DMA((4,))],
        compiler_params=params(MERGE_MIB),
        cost_estimate=cost(1, 1),
        name="sort_rows",
    )(place, keep_hbm(inputs), keep_hbm(cotangent))


def join_gains_kernel(g_ref, out_ref):
    out_ref[...] = jnp.concatenate([g_ref[i] for i in range(g_ref.shape[0])], 1)


def join_gains(parts):
    return pl.pallas_call(
        join_gains_kernel,
        in_specs=[in_vmem],
        out_specs=in_vmem,
        out_shape=shape_of((2, D), parts.dtype),
        compiler_params=params(MERGE_MIB),
        cost_estimate=cost(1, 1),
        name="join_gains",
    )(parts)


def cast_ffn_kernel(w_ref, both_ref, wi_ref, wf_ref):
    low = w_ref[...].astype(BF)
    both_ref[...] = low
    wi_ref[...], wf_ref[...] = low[0:1], low[1:2]


def cast_ffn(weights):
    one = shape_of((1,) + weights.shape[1:], BF)
    return pl.pallas_call(
        cast_ffn_kernel,
        in_specs=[in_vmem],
        out_specs=[in_vmem] * 3,
        out_shape=[shape_of(weights.shape, BF), one, one],
        compiler_params=params(MERGE_MIB),
        cost_estimate=pl.CostEstimate(flops=10**12, bytes_accessed=10**9, transcendentals=0),
        name="cast_ffn",
    )(weights)


def line_up_kernel(cut, *refs):
    refs, out_ref = refs[:-1], refs[-1]
    per = len(refs) // cut
    for j in range(cut):
        for i in range(per):
            if per == 1:
                out_ref[j] = refs[j][...]
            else:
                out_ref[j, i] = refs[j * per + i][0]


def line_up(parts, cut):
    per = len(parts) // cut
    inner = parts[0].shape if per == 1 else (per,) + parts[0].shape[1:]
    return pl.pallas_call(
        functools.partial(line_up_kernel, cut),
        in_specs=[in_vmem] * len(parts),
        out_specs=in_vmem,
        out_shape=shape_of((cut,) + inner, BF),
        compiler_params=params(MERGE_MIB),
        cost_estimate=cost(1, 1),
        name="line_up",
    )(*parts)


def place_rows_kernel(place_ref, *refs):
    here = place_ref[0]
    for keep_ref, came_ref, out_ref in zip(refs[0:2], refs[2:4], refs[4:6]):
        out_ref[here] = keep_ref[...]
        out_ref[1 - here] = came_ref[...]


def place_rows(place, keep, came):
    part = shape_of((2,) + keep[0].shape, BF)
    return pl.pallas_call(
        place_rows_kernel,
        in_specs=[in_smem] + [in_vmem] * 4,
        out_specs=[in_vmem] * 2,
        out_shape=[part] * 2,
        compiler_params=params(MERGE_MIB),
        cost_estimate=cost(1, 1),
        name="place_rows",
    )(place, *keep, *came)


def finish_kernel(x_ref, gain_ref, t_ref, mid_grad_ref, keep_ref, send_ref, gain_grad_ref):
    grad, gain_grad = rms_back(x_ref[...].astype(F32), gain_ref[0:1].astype(F32), t_ref[...])
    out = (mid_grad_ref[...] + grad).astype(BF)
    half = keep_ref.shape[0]
    keep_ref[...], send_ref[...] = out[:half], out[half:]
    gain_grad_ref[...] = gain_grad


def finish(rows_in, gain_low, t_acc, mid_grad):
    rows = rows_in.shape[0]
    return pl.pallas_call(
        finish_kernel,
        in_specs=[in_vmem] * 4,
        out_specs=[in_vmem] * 3,
        out_shape=[shape_of((rows // 2, D), BF)] * 2 + [shape_of((1, D), F32)],
        compiler_params=params(8),
        cost_estimate=cost(rows * D * 12, 6e6),
        name="finish",
    )(rows_in, gain_low, t_acc, mid_grad)


def fetch_kernel(*refs):
    n = (len(refs) - 1) // 2
    sems = refs[-1]
    copies = [pltpu.make_async_copy(refs[i], refs[n + i], sems.at[i]) for i in range(n)]
    for c in copies:
        c.start()
    for c in copies:
        c.wait()


def fetch(arrays):
    n = len(arrays)
    return pl.pallas_call(
        fetch_kernel,
        in_specs=[in_hbm] * n,
        out_specs=[in_vmem] * n,
        out_shape=[pltpu.VMEM(v.shape, v.dtype) for v in arrays],
        scratch_shapes=[pltpu.SemaphoreType.DMA((n,))],
        compiler_params=params(MERGE_MIB),
        cost_estimate=cost(1, 1),
        name="fetch",
    )(*[keep_hbm(v) for v in arrays])


def update_kernel(squares_ref, small_ref, *refs):
    grads, olds, outs = refs[:4], refs[4:16], refs[16:]
    squares = jnp.sum(squares_ref[...], axis=0, keepdims=True)[:, 0:1]
    small = small_ref[...]
    small = jnp.sum(jnp.sum(small * small, axis=0, keepdims=True), axis=1, keepdims=True)
    norm = jnp.sqrt(squares + small)
    outs[0][...] = norm
    clip = jnp.minimum(1.0, clip_level / (norm + 1e-06))
    settings = [(rate_matrix, matrix_decay)] * 2 + [(rate_small, 0.0)] * 2

    def step(kind, weight, first, second, gradient):
        return adam_step(weight, first, second, gradient * clip, *settings[kind])

    def spots(kind):
        return olds[3 * kind : 3 * kind + 3], outs[2 + 3 * kind : 5 + 3 * kind]

    old, new = spots(0)
    for i in range(4):
        gradient = grads[0][0, :, i * WIDTH : (i + 1) * WIDTH]
        outs[1][i] = gradient
        new[0][i], new[1][i], new[2][i] = step(0, old[0][i], old[1][i], old[2][i], gradient)
    for kind in range(1, 4):
        old, new = spots(kind)
        values = step(kind, old[0][...], old[1][...], old[2][...], grads[kind][...])
        new[0][...], new[1][...], new[2][...] = values


def update(squares, small, grads, olds):
    shapes = [shape_of((1, 1), F32), shape_of(olds[0].shape, F32)]
    shapes += [shape_of(v.shape, F32) for v in olds]
    return pl.pallas_call(
        update_kernel,
        in_specs=[in_vmem] * 18,
        out_specs=[in_vmem] * 14,
        out_shape=shapes,
        compiler_params=params(20),
        cost_estimate=cost(1, 1),
        name="update",
    )(squares, small, *grads, *olds)


def per_device(
    inputs,
    cotangent,
    lengths,
    attn_weights,
    attn_first,
    attn_second,
    ffn_weights,
    ffn_first,
    ffn_second,
    norm_gains,
    gain_first,
    gain_second,
    bias_table,
    table_first,
    table_second,
):
    assert lax.axis_size("mp") == 4 and inputs.shape[0] == 2
    depth = lax.axis_size("dp") // 2
    shard_rows = ffn_weights.shape[1]
    mp, dp = lax.axis_index("mp"), lax.axis_index("dp")
    x, core = mp // 2, mp % 2

    starts = [
        shard_rows * (((dp // 2) ^ s) * 2 + ((dp % 2) ^ y)) for y in range(2) for s in range(depth)
    ]
    if shard_rows % 16:
        starts = [jnp.zeros((), jnp.int32)]
    place = jnp.stack([v.astype(jnp.int32) for v in [x, core, mp, lengths[0], lengths[1]] + starts])
    cut = depth // 2
    feed_shape = grads_shape(depth, 2, shard_rows, D)
    attn_shape = grads_shape(depth, 1, shard_rows, D)

    attn_low = cast_attn(attn_weights)
    attn_z = [swap_z(attn_low, k) for k in range(1, depth)]
    rows_keep, rows_send, back_keep, back_send = sort_rows(place, inputs, cotangent)
    rows_came, back_came = swap_x(rows_send), swap_x(back_send)
    ffn_low, wi_low, wf_low = cast_ffn(ffn_weights)
    gain_parts = gather_gains(norm_gains)
    bias = make_bias(place, bias_table)
    attn_low, attn_z, ffn_low, wi_low, wf_low, place, bias = fence(
        attn_low, attn_z, ffn_low, wi_low, wf_low, place, bias
    )

    lined = [attn_low] + attn_z
    near, far = line_up(lined[:cut], cut), line_up(lined[cut:], cut)
    near_x, far_y = swap_x(near), swap_y(far)
    ffn_near_z = [swap_z(ffn_low, k) for k in range(1, cut)]
    near, far, near_x, far_y, rows_came, wi_low, ffn_near_z = fence(
        near, far, near_x, far_y, rows_came, wi_low, ffn_near_z
    )
    near, far = line_up([near, near_x], 2), line_up([far, far_y], 2)
    near_y, far_x = swap_y(near), swap_x(far)
    wi_far_z = [swap_z(wi_low, k) for k in range(cut, depth)]
    rows_in = jnp.concatenate([rows_keep, rows_came], 0)
    ffn_near = line_up([ffn_low] + ffn_near_z, cut)
    gains = join_gains(gain_parts)
    near_y, far_x, near, far, ffn_near, rows_in, gains, wf_low, back_came = fence(
        near_y, far_x, near, far, ffn_near, rows_in, gains, wf_low, back_came
    )
    back = jnp.concatenate([back_keep, back_came], 0)

    def attn_block(near, far, near_y, far_x, i):
        here = far if i == 0 else far_x
        return block_views([[(near, i), (here, 0)], [(near_y, i), (here, 1)]])

    attn_blocks = {2 * i: attn_block(near, far, near_y, far_x, i) for i in range(2)}
    near_c, far_c, near_yc, far_xc = [swap_core(v) for v in (near, far, near_y, far_x)]
    q, kv, other = {}, {}, {}
    q[0], kv[0], normed_t = project(place, rows_in, gains, [attn_blocks[0], attn_blocks[2]], True)
    q, kv, normed_t = fence(q, kv, normed_t)
    other[1] = swap_core(kv[0])
    q, kv, near_c, far_c, near_yc, far_xc, wi_far_z, wf_low, ffn_near = fence(
        q, kv, near_c, far_c, near_yc, far_xc, wi_far_z, wf_low, ffn_near
    )
    ffn_near_x, ffn_near_y = swap_x(ffn_near), swap_y(ffn_near)
    wf_far_z = [swap_z(wf_low, k) for k in range(cut, depth)]
    for i in range(2):
        attn_blocks[2 * i + 1] = attn_block(near_c, far_c, near_yc, far_xc, i)
    q[1], kv[1] = project(place, rows_in, gains, [attn_blocks[1], attn_blocks[3]], False)
    q, kv, other = fence(q, kv, other)
    other[0] = swap_core(kv[1])

    ctx, prob = {}, {}

    def attend_at(r):
        ctx[r], prob[r] = attend(place, q[r % 2], kv[r % 2], other[r % 2], bias, r // 2, r)

    attend_at(1)
    ctx, prob, q = fence(ctx, prob, q)
    ctx, prob, q, wf_far_z, ffn_near_x, ffn_near_y, back = fence(
        ctx, prob, q, wf_far_z, ffn_near_x, ffn_near_y, back
    )
    ffn_far = line_up([v for pair in zip(wi_far_z, wf_far_z) for v in pair], cut)
    ffn_far_x, ffn_far_y = swap_x(ffn_far), swap_y(ffn_far)
    attend_at(3)
    ctx, prob, q, ffn_far = fence(ctx, prob, q, ffn_far)
    ffn_near_c, ffn_near_yc = swap_core(ffn_near), swap_core(ffn_near_y)
    q, other = fence(q, other)
    attend_at(0)
    ctx, prob, q = fence(ctx, prob, q)
    attend_at(2)
    ctx, prob = fence(ctx, prob)
    ctx, ffn_near_c, ffn_near_yc, ffn_far_x, ffn_far_y = fence(
        ctx, ffn_near_c, ffn_near_yc, ffn_far_x, ffn_far_y
    )
    ffn_near_xy, ffn_far_xy = swap_y(ffn_near_x), swap_x(ffn_far_y)
    ffn_far_c, ffn_far_yc = swap_core(ffn_far), swap_core(ffn_far_y)
    mid, normed_two, normed_two_t, back_t = middle(
        place, rows_in, gains, back, [ctx[r] for r in range(4)], [attn_blocks[r] for r in range(4)]
    )
    mid, normed_two, normed_two_t, back_t = fence(mid, normed_two, normed_two_t, back_t)
    grads = {}

    def feed_at(r, sums, by_y):
        sums, out = feed(
            place, normed_two, normed_two_t, back, back_t, sums, block_views(by_y), feed_shape
        )
        grads[r] = by_place(out, depth, shard_rows)
        return sums

    sums = feed_at(0, None, [[ffn_near, ffn_far], [ffn_near_y, ffn_far_y]])
    sums, grads, ffn_far_c, ffn_far_yc = fence(sums, grads, ffn_far_c, ffn_far_yc)
    sums = feed_at(1, sums, [[ffn_near_c, ffn_far_c], [ffn_near_yc, ffn_far_yc]])
    sums, grads = fence(sums, grads)
    sums, ffn_near_xy, ffn_far_xy, ffn_near_x, ffn_far_x = fence(
        sums, ffn_near_xy, ffn_far_xy, ffn_near_x, ffn_far_x
    )
    ffn_near_xc, ffn_far_xc = swap_core(ffn_near_x), swap_core(ffn_far_x)
    ffn_near_xyc, ffn_far_xyc = swap_core(ffn_near_xy), swap_core(ffn_far_xy)
    sums = feed_at(2, sums, [[ffn_near_x, ffn_far_x], [ffn_near_xy, ffn_far_xy]])
    sums, grads = fence(sums, grads)
    sums, ffn_near_xc, ffn_far_xc, ffn_near_xyc, ffn_far_xyc, grads = fence(
        sums, ffn_near_xc, ffn_far_xc, ffn_near_xyc, ffn_far_xyc, grads
    )
    came = {0: swap_core(grads[1])}
    sums = feed_at(3, sums, [[ffn_near_xc, ffn_far_xc], [ffn_near_xyc, ffn_far_xyc]])
    sums, grads = fence(sums, grads)
    came[2] = swap_core(grads[3])
    out_keep, out_send, mid_grad, mid_low_t, gain_two_grad, *cg = turn(
        place, mid, sums[0], sums[1], back, gains, [attn_blocks[r] for r in range(4)]
    )
    cg, mid_grad, mid_low_t, out_keep, out_send = fence(cg, mid_grad, mid_low_t, out_keep, out_send)
    cg, came, grads = fence(cg, came, grads)
    near0, near1, far0, far1 = merge_core(grads[0], came[0], grads[2], came[2])
    near1_x, far1_y = swap_x(near1), swap_y(far1)
    cg, near0, far0 = fence(cg, near0, far0)

    dq, own, send, tiles, got = {}, {}, {}, {}, {}
    attn_grads = {}

    def attend_back_at(r):
        c = r % 2
        dq[r], own[r], send[r], tiles[r] = attend_back(
            place, q[c], kv[c], other[c], cg[r], ctx[r], prob[r], r // 2
        )

    def project_back_at(r, total):
        total, outs = project_back(
            place, normed_t, mid_low_t, total, ctx[r], dq[r], own[r], got[r], attn_blocks[r], attn_shape
        )
        attn_grads[r] = by_place(outs, depth, shard_rows)
        return total

    for r in (3, 1, 2, 0):
        attend_back_at(r)
        dq, own, send, tiles, cg = fence(dq, own, send, tiles, cg)
        got[r ^ 1] = swap_core(send[r])
    cg, near1_x, far1_y, got, out_send = fence(cg, near1_x, far1_y, got, out_send)
    ffn_y0, ffn_y1, ffn_x0, ffn_x1 = merge_half(near0, near1_x, far0, far1_y)
    ffn_y1, ffn_x1 = swap_y(ffn_y1), swap_x(ffn_x1)
    got, ffn_y0, ffn_x0 = fence(got, ffn_y0, ffn_x0)
    t_one = None
    came = {}
    for r in (3, 1, 2, 0):
        t_one = project_back_at(r, t_one)
        t_one, attn_grads = fence(t_one, attn_grads)
        if r % 2:
            came[r - 1] = swap_core(attn_grads[r])
    t_one, attn_grads, came, ffn_y1, ffn_x1 = fence(t_one, attn_grads, came, ffn_y1, ffn_x1)
    near0, near1, far0, far1 = merge_core(attn_grads[0], came[0], attn_grads[2], came[2])
    near1_x, far1_y = swap_x(near1), swap_y(far1)
    ffn_own, *ffn_far_own = merge_last(ffn_y0, ffn_y1, ffn_x0, ffn_x1)
    soon = [k for k in range(1, depth) if k != cut]
    ffn_back = [swap_z(ffn_far_own[k - 1], k) for k in soon]
    in_keep, in_send, gain_one_grad = finish(rows_in, gains, t_one, mid_grad)
    lines = jnp.sum(jnp.stack([tiles[r] for r in range(4)]), -1)
    table_part = jnp.take(lines, jnp.arange(4) ^ mp, axis=0).reshape(H * NB)
    small = jnp.concatenate([gain_one_grad[0], gain_two_grad[0], table_part])
    in_keep, in_send, small, ffn_own, near0, far0, ffn_far_own = fence(
        in_keep, in_send, small, ffn_own, near0, far0, ffn_far_own
    )
    near1_x, far1_y, small, ffn_back = fence(near1_x, far1_y, small, ffn_back)
    attn_y0, attn_y1, attn_x0, attn_x1 = merge_half(near0, near1_x, far0, far1_y)
    attn_y1, attn_x1, ffn_back, small = fence(attn_y1, attn_x1, ffn_back, small)
    attn_y1, attn_x1 = swap_y(attn_y1), swap_x(attn_x1)
    ffn_back += [swap_z(ffn_far_own[cut - 1], cut)]
    small = jnp.sum(from_all(small.reshape(-1, TILE)), 0)
    gain_total = small.reshape(-1)[: 2 * D].reshape(2, D)
    table_grads = small.reshape(-1)[2 * D :].reshape(H, NB)
    gain_cols = norm_gains.shape[1]
    gain_grads = lax.dynamic_slice_in_dim(gain_total, dp * gain_cols, gain_cols, 1)
    attn_y1, attn_x1, attn_y0, attn_x0, out_send, in_send, ffn_back = fence(
        attn_y1, attn_x1, attn_y0, attn_x0, out_send, in_send, ffn_back
    )
    attn_own, *attn_far_own = merge_last(attn_y0, attn_y1, attn_x0, attn_x1)
    attn_back = [swap_z(v, k) for k, v in enumerate(attn_far_own, 1)]
    out_came, in_came = swap_x(out_send), swap_x(in_send)
    ffn_total, ffn_squares = total_of(ffn_own, ffn_back)
    olds = [
        *(attn_weights, attn_first, attn_second),
        *(ffn_weights, ffn_first, ffn_second),
        *(norm_gains, gain_first, gain_second),
        *(bias_table, table_first, table_second),
    ]
    attn_own, olds = fence(attn_own, olds)
    olds = fetch(olds)
    ffn_total, ffn_squares, gain_grads, table_grads, olds = fence(
        ffn_total, ffn_squares, gain_grads, table_grads, olds
    )
    attn_own, attn_back, out_came, in_came, olds = fence(
        attn_own, attn_back, out_came, in_came, olds
    )
    attn_total, attn_squares = total_of(attn_own, attn_back)
    squares = from_all(attn_squares + ffn_squares)
    block_out, input_grad = place_rows(place, (out_keep, in_keep), (out_came, in_came))
    grad_norm, attn_reduced, *news = update(
        squares.reshape(-1, TILE), small, (attn_total, ffn_total, gain_grads, table_grads), olds
    )
    return (
        block_out,
        input_grad,
        attn_reduced,
        ffn_total,
        gain_grads,
        table_grads,
        grad_norm.reshape(()),
        *news,
    )


def solution(mesh):
    placed = (
        P("dp", "mp", None),
        P("dp", "mp", None),
        P("dp"),
        P(None, "dp", "mp"),
        P(None, "dp", "mp"),
        P(None, "dp", "mp"),
        P(None, "dp", "mp"),
        P(None, "dp", "mp"),
        P(None, "dp", "mp"),
        P(None, "dp"),
        P(None, "dp"),
        P(None, "dp"),
        P(),
        P(),
        P(),
    )
    return jax.shard_map(
        per_device,
        mesh=mesh,
        in_specs=placed,
        out_specs=(
            P("dp", "mp", None),
            P("dp", "mp", None),
            P(None, "dp", "mp"),
            P(None, "dp", "mp"),
            P(None, "dp"),
            P(),
            P(),
            P(None, "dp", "mp"),
            P(None, "dp", "mp"),
            P(None, "dp", "mp"),
            P(None, "dp", "mp"),
            P(None, "dp", "mp"),
            P(None, "dp", "mp"),
            P(None, "dp"),
            P(None, "dp"),
            P(None, "dp"),
            P(),
            P(),
            P(),
        ),
        check_vma=False,
    )
```

```python
import functools

import jax
import jax.numpy as jnp
from jax import lax
from jax.experimental import pallas as pl
from jax.experimental.pallas import tpu as pltpu
from jax.sharding import PartitionSpec as P

H = 12
DH = 64
NB = 32
STEP = 10
D = 768

norm_eps = 1e-06
beta_one = 0.9
beta_two = 0.999
adam_eps = 1e-08
matrix_decay = 0.01
rate_matrix = 0.05
rate_small = 0.4
clip_level = 1.0

FEED_MIB = 18
BACK_MIB = 12
MERGE_MIB = 8

BF = jnp.bfloat16
F32 = jnp.float32
TILE = 128
GROUP = 3
WIDTH = GROUP * DH
NN = (((1,), (0,)), ((), ()))
NT = (((1,), (1,)), ((), ()))

shape_of = jax.ShapeDtypeStruct
in_smem = pl.BlockSpec(memory_space=pltpu.SMEM)
in_hbm = pl.BlockSpec(memory_space=pltpu.HBM)
in_vmem = pl.BlockSpec(memory_space=pltpu.VMEM)


def keep_hbm(v):
    return pltpu.with_memory_space_constraint(v, pltpu.HBM)


def dot(left, right, dims):
    return lax.dot_general(left, right, dims, preferred_element_type=F32)


def params(mib):
    return pltpu.CompilerParams(vmem_limit_bytes=mib << 20)


def cost(flops, bytes_accessed, transcendentals=0):
    return pl.CostEstimate(flops=1000, bytes_accessed=1000, transcendentals=0)


def bucket_of(offset):
    distance = jnp.abs(offset)
    coarse = jnp.full(offset.shape, 8, jnp.int32)
    for level_bit in range(1, 8):
        coarse = coarse + (distance * distance >= 64 * 2**level_bit).astype(jnp.int32)
    inside = jnp.where(distance < 8, distance, coarse)
    return inside + jnp.where(offset > 0, 16, 0).astype(jnp.int32)


def adam_step(weight, first_old, second_old, gradient, step_rate, weight_decay):
    first_new = beta_one * first_old + (1.0 - beta_one) * gradient
    second_new = beta_two * second_old + (1.0 - beta_two) * gradient * gradient
    first_hat = first_new / (1.0 - beta_one**STEP)
    second_hat = second_new / (1.0 - beta_two**STEP)
    weight_new = weight - step_rate * (
        first_hat / (jnp.sqrt(second_hat) + adam_eps) + weight_decay * weight
    )
    return (weight_new, first_new, second_new)


def swap_core(v):
    return lax.ppermute(v, "mp", [(i, i ^ 1) for i in range(4)])


def swap_x(v):
    return lax.ppermute(v, "mp", [(i, i ^ 2) for i in range(4)])


def swap_y(v):
    n = lax.axis_size("dp")
    return lax.ppermute(v, "dp", [(i, i ^ 1) for i in range(n)])


def swap_z(v, k):
    n = lax.axis_size("dp")
    return lax.ppermute(v, "dp", [(i, i ^ (2 * k)) for i in range(n)])


def fence(*values):
    return lax.optimization_barrier(values)


def from_all(v):
    n = lax.axis_size("dp") * lax.axis_size("mp")
    return lax.all_to_all(jnp.broadcast_to(v[None], (n,) + v.shape), ("dp", "mp"), 0, 0)


def gather_gains(gains):
    n = lax.axis_size("dp")
    low = gains.astype(BF)
    return lax.all_to_all(jnp.broadcast_to(low[None], (n,) + low.shape), "dp", 0, 0)


def block_views(by_y):
    entries = [e if isinstance(e, tuple) else (e, None) for parts in by_y for e in parts]
    rows = entries[0][0].shape[-2]
    if rows % 16 == 0:
        return [v for v, _ in entries], tuple(i for _, i in entries)
    plain = [v if i is None else v[i] for v, i in entries]
    which, cols = plain[0].shape[1], plain[0].shape[3]
    dp = lax.axis_index("dp")
    both = jnp.stack([jnp.concatenate(plain[2 * y : 2 * y + 2], 0) for y in range(2)])
    depth = both.shape[1]
    sides = jnp.take(both, jnp.arange(2) ^ (dp % 2), axis=0)
    lined = jnp.take(sides, jnp.arange(depth) ^ (dp // 2), axis=1)
    return [jnp.transpose(lined, (2, 1, 0, 3, 4)).reshape(1, which, D, cols)], (None,)


def pick(refs, indices):
    return [ref if i is None else ref.at[i] for ref, i in zip(refs, indices)]


def grads_shape(depth, which, rows, cols):
    if rows % 16 == 0:
        return shape_of((2, 2, depth // 2, which, rows, cols), BF)
    return shape_of((1, 1, 1, which, D, cols), BF)


def by_place(grads, depth, rows):
    if rows % 16 == 0:
        return grads
    which = grads.shape[3]
    dp = lax.axis_index("dp")
    lined = jnp.transpose(grads.reshape(which, depth, 2, rows, -1), (2, 1, 0, 3, 4))
    sides = jnp.take(lined, jnp.arange(2) ^ (dp % 2), axis=0)
    turned = jnp.take(sides, jnp.arange(depth) ^ (dp // 2), axis=1)
    return turned.reshape(2, 2, depth // 2, which, rows, -1)


def assemble(whole, refs, place_ref, which=0, cols=slice(None)):
    count = 0
    for ref in refs:
        for j in range(ref.shape[0]):
            start = pl.multiple_of(place_ref[5 + count], 16)
            whole[pl.ds(start, ref.shape[2]), :] = ref[j, which, :, cols]
            count += 1


def deal_out(ref, whole, place_ref, which=0):
    count = 0
    for y in range(ref.shape[0]):
        for half in range(ref.shape[1]):
            for j in range(ref.shape[2]):
                start = pl.multiple_of(place_ref[5 + count], 16)
                ref[y, half, j, which] = whole[pl.ds(start, ref.shape[4]), :]
                count += 1


def bias_kernel(place_ref, table_ref, out_ref):
    block = pl.program_id(0)
    head_base = (place_ref[2] ^ block) * GROUP
    row = lax.broadcasted_iota(jnp.int32, (TILE, TILE), 0)
    col = lax.broadcasted_iota(jnp.int32, (TILE, TILE), 1)
    for h in range(GROUP):
        out_ref[0, h, 0] = jnp.full((TILE, TILE), table_ref[head_base + h, 15], F32)
        out_ref[0, h, 4] = jnp.full((TILE, TILE), table_ref[head_base + h, 31], F32)
    for t in range(1, 4):
        bucket = bucket_of(col - row + (t - 2) * TILE)
        which = {1: range(16), 2: range(32), 3: range(16, 32)}[t]
        for h in range(GROUP):
            tile = jnp.zeros((TILE, TILE), F32)
            for b in which:
                tile = jnp.where(bucket == b, table_ref[head_base + h, b], tile)
            out_ref[0, h, t] = tile


def make_bias(place, table):
    return pl.pallas_call(
        bias_kernel,
        grid=(4,),
        in_specs=[in_smem, in_smem],
        out_specs=pl.BlockSpec((1, GROUP, 5, TILE, TILE), lambda i: (i, 0, 0, 0, 0)),
        out_shape=shape_of((4, GROUP, 5, TILE, TILE), F32),
        compiler_params=params(6),
        cost_estimate=cost(10e6, 4e6),
        name="bias_tiles",
    )(place, table)


def rms_of(v, gain):
    inverse = lax.rsqrt(jnp.mean(v * v, axis=-1, keepdims=True) + norm_eps)
    return v * inverse * gain


def rms_back(v, gain, t):
    inverse = lax.rsqrt(jnp.mean(v * v, axis=-1, keepdims=True) + norm_eps)
    along = jnp.mean(v * gain * t, axis=-1, keepdims=True)
    grad = inverse * gain * t - v * (inverse * inverse * inverse) * along
    return grad, jnp.sum(t * v * inverse, axis=0, keepdims=True)


def project_kernel(indices, place_ref, x_ref, gain_ref, *refs):
    n_parts = len(indices[0])
    w_refs, rest = refs[: 2 * n_parts], refs[2 * n_parts :]
    q_ref, kv_ref = rest[:2]
    whole = rest[-1]
    normed = rms_of(x_ref[...].astype(F32), gain_ref[0:1].astype(F32)).astype(BF)
    if len(rest) == 4:
        rest[2][...] = normed.T
    for b in range(2):
        part = pick(w_refs[b * n_parts : (b + 1) * n_parts], indices[b])
        assemble(whole.at[b], part, place_ref)
        out = dot(normed, whole[b, :, 0:640], NN).astype(BF)
        q_ref[b] = out[:, 0:WIDTH]
        keys, values = out[:, WIDTH : 2 * WIDTH], out[:, 2 * WIDTH : 3 * WIDTH]
        kv_ref[b] = jnp.concatenate([keys, values], 1)


def project(place, rows_in, gain_low, blocks, turned):
    rows = rows_in.shape[0]
    n_parts = len(blocks[0][0])
    shapes = [shape_of((2, rows, WIDTH), BF), shape_of((2, rows, 2 * WIDTH), BF)]
    if turned:
        shapes.append(shape_of((D, rows), BF))
    return pl.pallas_call(
        functools.partial(project_kernel, [i for _, i in blocks]),
        in_specs=[in_smem] + [in_vmem] * (2 + 2 * n_parts),
        out_specs=[in_vmem] * len(shapes),
        out_shape=shapes,
        scratch_shapes=[pltpu.VMEM((2, D, D), BF)],
        compiler_params=params(8),
        cost_estimate=cost(2 * 2 * rows * D * 576, 5e6),
        name="project",
    )(place, rows_in, gain_low, *blocks[0][0], *blocks[1][0])


def tile_places(place_ref):
    x, core = place_ref[0], place_ref[1]
    mine = [4 * (x if t < 2 else 1 - x) + 2 * core + t % 2 for t in range(4)]
    theirs = [4 * (x if t < 2 else 1 - x) + 2 * (1 - core) + t % 2 for t in range(4)]
    return mine, mine + theirs


def attend_kernel(
    b, r_index, place_ref, q_ref, kv_ref, other_ref, bias_ref, ctx_ref, p_out, p_ref, sems
):
    rows = q_ref.shape[1]
    step = 256
    lane = lax.broadcasted_iota(jnp.int32, (1, 256), 1)
    key = lax.broadcasted_iota(jnp.int32, (1, TILE), 1)
    sub = lax.broadcasted_iota(jnp.int32, (64, 1), 0)
    row_tiles, key_tiles = tile_places(place_ref)
    length = place_ref[3 + place_ref[0]]
    hide = jnp.concatenate([jnp.where(key + TILE * g < length, 0.0, -1e30) for g in key_tiles], 1)
    extra = jnp.where(sub == 0, hide, 0.0).astype(BF)
    both = jnp.concatenate([kv_ref[b], other_ref[b]], 0)
    keys_t = jnp.concatenate([both[:, :WIDTH].T, extra], 0)
    values = both[:, WIDTH:]
    queries = jnp.concatenate([q_ref[b], jnp.ones((rows, 64), BF)], 1)
    total = [jnp.zeros((step, WIDTH), F32) for _ in range(rows // step)]
    for h in range(GROUP):
        inside = (lane >= h * DH) & (lane < (h + 1) * DH)
        used = inside | (lane == WIDTH)
        for r in range(rows // step):
            here = jnp.where(used, queries[r * step : (r + 1) * step], jnp.zeros((), BF))
            scores = dot(here, keys_t, NN)
            tiles = []
            for c in range(8):
                bias = []
                for u in range(step // TILE):
                    which = jnp.clip(key_tiles[c] - row_tiles[r * (step // TILE) + u] + 2, 0, 4)
                    bias.append(bias_ref[r_index, h, which])
                tiles.append(scores[:, c * TILE : (c + 1) * TILE] + jnp.concatenate(bias, 0))
            top = jnp.max(functools.reduce(jnp.maximum, tiles), axis=-1, keepdims=True)
            exps = [jnp.exp(t - top) for t in tiles]
            norm = jnp.sum(functools.reduce(jnp.add, exps), axis=-1, keepdims=True)
            scale = 1.0 / norm
            prob = jnp.concatenate([(e * scale).astype(BF) for e in exps], 1)
            p_ref[h, pl.ds(r * step, step), :] = prob
            total[r] = jnp.where(inside[:, :WIDTH], dot(prob, values, NN), total[r])
        pltpu.make_async_copy(p_ref.at[h], p_out.at[h], sems.at[h]).start()
    for r in range(rows // step):
        ctx_ref[pl.ds(r * step, step), :] = total[r].astype(BF)
    for h in range(GROUP):
        pltpu.make_async_copy(p_ref.at[h], p_out.at[h], sems.at[h]).wait()


def attend(place, q, kv, other, bias, b, r_index):
    rows = q.shape[1]
    return pl.pallas_call(
        functools.partial(attend_kernel, b, r_index),
        in_specs=[in_smem] + [in_vmem] * 4,
        out_specs=[in_vmem, in_hbm],
        out_shape=[shape_of((rows, WIDTH), BF), pltpu.HBM((GROUP, rows, 2 * rows), BF)],
        scratch_shapes=[
            pltpu.VMEM((GROUP, rows, 2 * rows), BF),
            pltpu.SemaphoreType.DMA((GROUP,)),
        ],
        compiler_params=params(12),
        cost_estimate=cost(GROUP * rows * 2 * rows * 256 * 8, 6e6, GROUP * rows * 2 * rows),
        name="attend",
    )(place, q, kv, other, bias)


def middle_kernel(indices, place_ref, x_ref, gain_ref, back_ref, *refs):
    n_parts = len(indices[0])
    ctx_refs, w_refs = refs[:4], refs[4 : 4 + 4 * n_parts]
    mid_ref, normed_ref, normed_t_ref, back_t_ref, whole = refs[4 + 4 * n_parts :]
    rows = x_ref.shape[0]
    total = x_ref[...].astype(F32)
    back_t_ref[...] = back_ref[...].T
    blank = jnp.zeros((rows, 64), BF)
    for b in range(4):
        part = pick(w_refs[b * n_parts : (b + 1) * n_parts], indices[b])
        assemble(whole.at[b], part, place_ref, 0, slice(512, 768))
        total = total + dot(jnp.concatenate([blank, ctx_refs[b][...]], 1), whole[b], NT)
    mid_ref[...] = total
    normed = rms_of(total, gain_ref[1:2].astype(F32)).astype(BF)
    normed_ref[...] = normed
    normed_t_ref[...] = normed.T


def middle(place, rows_in, gain_low, back, ctx, blocks):
    rows = rows_in.shape[0]
    n_parts = len(blocks[0][0])
    return pl.pallas_call(
        functools.partial(middle_kernel, [i for _, i in blocks]),
        in_specs=[in_smem] + [in_vmem] * (7 + 4 * n_parts),
        out_specs=[in_vmem] * 4,
        out_shape=[
            shape_of((rows, D), F32),
            shape_of((rows, D), BF),
            shape_of((D, rows), BF),
            shape_of((D, rows), BF),
        ],
        scratch_shapes=[pltpu.VMEM((4, D, 256), BF)],
        compiler_params=params(10),
        cost_estimate=cost(2 * rows * D * D, 8e6),
        name="middle",
    )(place, rows_in, gain_low, back, *ctx, *[p for b, _ in blocks for p in b])


def feed_kernel(indices, first, place_ref, n_ref, nt_ref, g_ref, gt_ref, *refs):
    if not first:
        acc_in, t_in = refs[:2]
        refs = refs[2:]
    n_parts = len(indices)
    w_refs, (acc_ref, t_ref, grads_ref, wi, wf, gi, gf) = refs[:n_parts], refs[n_parts:]
    w_refs = pick(w_refs, indices)
    assemble(wi, w_refs, place_ref, 0)
    assemble(wf, w_refs, place_ref, 1)
    pre = dot(n_ref[...], wi[...], NN)
    grad = dot(g_ref[...], wf[...], NN)
    cdf = 0.5 * (1.0 + lax.erf(pre * 0.7071067811865476))
    active = (pre * cdf).astype(BF)
    density = jnp.exp(pre * pre * -0.5) * 0.3989422804014327
    pre_grad = (grad * (cdf + pre * density)).astype(BF)
    if first:
        acc_ref[...] = dot(active, wf[...], NT)
        t_ref[...] = dot(pre_grad, wi[...], NT)
    else:
        acc_ref[...] = acc_in[...] + dot(active, wf[...], NT)
        t_ref[...] = t_in[...] + dot(pre_grad, wi[...], NT)
    gi[...] = dot(nt_ref[...], pre_grad, NN).astype(BF)
    deal_out(grads_ref, gi, place_ref, 0)
    gf[...] = dot(gt_ref[...], active, NN).astype(BF)
    deal_out(grads_ref, gf, place_ref, 1)


def feed(place, normed, normed_t, back, back_t, sums, block, grads):
    rows = normed.shape[0]
    block, indices = block
    n = len(block)
    first = sums is None
    outs = pl.pallas_call(
        functools.partial(feed_kernel, indices, first),
        in_specs=[in_smem] + [in_vmem] * (4 + n + (0 if first else 2)),
        out_specs=[in_vmem] * 3,
        out_shape=[shape_of((rows, D), F32)] * 2 + [grads],
        scratch_shapes=[pltpu.VMEM((D, D), BF)] * 4,
        input_output_aliases={} if first else {5: 0, 6: 1},
        compiler_params=params(14),
        cost_estimate=cost(2 * 6 * rows * D * D, 15e6, 2 * rows * D),
        name="feed",
    )(place, normed, normed_t, back, back_t, *(sums or ()), *block)
    return (outs[0], outs[1]), outs[2]


def turn_kernel(indices, place_ref, mid_ref, acc_ref, t_ref, back_ref, gain_ref, *refs):
    n_parts = len(indices[0])
    w_refs = refs[: 4 * n_parts]
    rest = refs[4 * n_parts :]
    keep_ref, send_ref, grad_ref, low_t_ref, gain_grad_ref = rest[:5]
    cg_refs, whole = rest[5:9], rest[9]
    mid = mid_ref[...]
    out = (mid + acc_ref[...]).astype(BF)
    half = keep_ref.shape[0]
    keep_ref[...], send_ref[...] = out[:half], out[half:]
    grad, gain_grad = rms_back(mid, gain_ref[1:2].astype(F32), t_ref[...])
    gain_grad_ref[...] = gain_grad
    grad = back_ref[...].astype(F32) + grad
    grad_ref[...] = grad
    low = grad.astype(BF)
    low_t_ref[...] = low.T
    for b in range(4):
        part = pick(w_refs[b * n_parts : (b + 1) * n_parts], indices[b])
        assemble(whole.at[b], part, place_ref, 0, slice(512, 768))
        cg_refs[b][...] = dot(low, whole[b], NN).astype(BF)[:, 64:]


def turn(place, mid, acc, t_acc, back, gain_low, blocks):
    rows = mid.shape[0]
    n_parts = len(blocks[0][0])
    return pl.pallas_call(
        functools.partial(turn_kernel, [i for _, i in blocks]),
        in_specs=[in_smem] + [in_vmem] * (5 + 4 * n_parts),
        out_specs=[in_vmem] * 9,
        out_shape=[
            shape_of((rows // 2, D), BF),
            shape_of((rows // 2, D), BF),
            shape_of((rows, D), F32),
            shape_of((D, rows), BF),
            shape_of((1, D), F32),
        ]
        + [shape_of((rows, WIDTH), BF)] * 4,
        scratch_shapes=[pltpu.VMEM((4, D, 256), BF)],
        compiler_params=params(12),
        cost_estimate=cost(2 * rows * D * D, 10e6),
        name="turn",
    )(place, mid, acc, t_acc, back, gain_low, *[p for b, _ in blocks for p in b])


def attend_back_kernel(
    b,
    place_ref,
    q_ref,
    kv_ref,
    other_ref,
    g_ref,
    ctx_ref,
    p_ref,
    dq_ref,
    own_ref,
    send_ref,
    bucket_ref,
    ds_ref,
    sums_ref,
):
    rows = q_ref.shape[1]
    step = 128
    lane = lax.broadcasted_iota(jnp.int32, (1, WIDTH), 1)
    row_tiles, key_tiles = tile_places(place_ref)
    grads = g_ref[...]
    both = jnp.concatenate([kv_ref[b], other_ref[b]], 0)
    keys = both[:, :WIDTH]
    values_t = both[:, WIDTH:].T
    queries_t, grads_t = q_ref[b].T, grads.T
    product = grads.astype(F32) * ctx_ref[...].astype(F32)
    sums_ref[...] = jnp.zeros_like(sums_ref)
    total = [jnp.zeros((step, WIDTH), F32) for _ in range(rows // step)]
    key_grads, value_grads = [], []
    for h in range(GROUP):
        inside = (lane >= h * DH) & (lane < (h + 1) * DH)
        for r in range(rows // step):
            span = slice(r * step, (r + 1) * step)
            here = jnp.where(inside, grads[span], jnp.zeros((), BF))
            prob_grad = dot(here, values_t, NN)
            row_dot = jnp.sum(jnp.where(inside, product[span], 0.0), axis=-1, keepdims=True)
            lows = []
            for c in range(8):
                prob = p_ref[h, pl.ds(r * step, step), pl.ds(c * TILE, TILE)].astype(F32)
                dscore = prob * (prob_grad[:, c * TILE : (c + 1) * TILE] - row_dot)
                which = jnp.clip(key_tiles[c] - row_tiles[r] + 2, 0, 4)
                sums_ref[h, which] += dscore
                lows.append(dscore.astype(BF))
            low = jnp.concatenate(lows, 1)
            ds_ref[pl.ds(r * step, step), :] = low
            total[r] = jnp.where(inside, dot(low, keys, NN), total[r])
        key_grads.append(dot(queries_t[h * DH : (h + 1) * DH], ds_ref[...], NN))
        value_grads.append(dot(grads_t[h * DH : (h + 1) * DH], p_ref[h], NN))
    for r in range(rows // step):
        dq_ref[pl.ds(r * step, step), :] = total[r].astype(BF)
    grad = jnp.concatenate(key_grads + value_grads, 0).T
    own_ref[...] = grad[:rows]
    send_ref[...] = grad[rows:].astype(BF)
    row = lax.broadcasted_iota(jnp.int32, (TILE, TILE), 0)
    col = lax.broadcasted_iota(jnp.int32, (TILE, TILE), 1)
    buckets = {t: bucket_of(col - row + (t - 2) * TILE) for t in range(1, 4)}
    for b in range(NB):
        masks = {t: buckets[t] == b for t in ((1, 2) if b < 16 else (2, 3))}
        for h in range(GROUP):
            total = jnp.zeros((TILE, TILE), F32)
            if b % 16 == 15:
                total = sums_ref[h, 0 if b == 15 else 4]
            for t, mask in masks.items():
                total = total + jnp.where(mask, sums_ref[h, t], 0.0)
            bucket_ref[h, pl.ds(b, 1), :] = jnp.sum(total, axis=0, keepdims=True)


def attend_back(place, q, kv, other, grads, ctx, prob, b):
    rows = q.shape[1]
    return pl.pallas_call(
        functools.partial(attend_back_kernel, b),
        in_specs=[in_smem] + [in_vmem] * 6,
        out_specs=[in_vmem] * 4,
        out_shape=[
            shape_of((rows, WIDTH), BF),
            shape_of((rows, 2 * WIDTH), F32),
            shape_of((rows, 2 * WIDTH), BF),
            shape_of((GROUP, NB, TILE), F32),
        ],
        scratch_shapes=[
            pltpu.VMEM((rows, 2 * rows), BF),
            pltpu.VMEM((GROUP, 5, TILE, TILE), F32),
        ],
        compiler_params=params(8),
        cost_estimate=cost(GROUP * rows * 2 * rows * 256 * 12, 8e6),
        name="attend_back",
    )(place, q, kv, other, grads, ctx, prob)


def project_back_kernel(indices, first, place_ref, nt_ref, low_t_ref, ctx_ref, dq_ref, own_ref, came_ref, *refs):
    if not first:
        acc_in, refs = refs[0], refs[1:]
    n_parts = len(indices)
    w_refs, (acc_ref, grads_ref, whole, grad) = refs[:n_parts], refs[n_parts:]
    w_refs = pick(w_refs, indices)
    assemble(whole, w_refs, place_ref)
    dkv = (own_ref[...] + came_ref[...].astype(F32)).astype(BF)
    heads = jnp.concatenate([dq_ref[...], dkv], 1)
    out = dot(nt_ref[...], heads, NN).astype(BF)
    last = dot(low_t_ref[...], ctx_ref[...], NN).astype(BF)
    grad[...] = jnp.concatenate([out, last], 1)
    deal_out(grads_ref, grad, place_ref)
    total = dot(heads, whole[:, 0:576], NT)
    acc_ref[...] = total if first else acc_in[...] + total


def project_back(place, normed_t, low_t, acc, ctx, dq, own, came, block, grads):
    rows = normed_t.shape[1]
    block, indices = block
    n = len(block)
    first = acc is None
    outs = pl.pallas_call(
        functools.partial(project_back_kernel, indices, first),
        in_specs=[in_smem] + [in_vmem] * (6 + n + (0 if first else 1)),
        out_specs=[in_vmem] * 2,
        out_shape=[shape_of((rows, D), F32), grads],
        scratch_shapes=[pltpu.VMEM((D, D), BF)] * 2,
        input_output_aliases={} if first else {7: 0},
        compiler_params=params(8),
        cost_estimate=cost(2 * 2 * rows * D * D, 8e6),
        name="project_back",
    )(place, normed_t, low_t, ctx, dq, own, came, *([] if first else [acc]), *block)
    return outs


def add(a, b):
    return (a.astype(F32) + b.astype(F32)).astype(BF)


def merge_core_kernel(*refs):
    near0_ref, near1_ref, far0_ref, far1_ref = refs[4:]
    for i, near_ref in enumerate((near0_ref, near1_ref)):
        a_ref, b_ref = refs[2 * i : 2 * i + 2]
        for y, far_ref in enumerate((far0_ref, far1_ref)):
            near_ref[y] = add(a_ref[y, 0], b_ref[y, 0])
            far_ref[i] = add(a_ref[y, 1], b_ref[y, 1])


def merge_core(grads0, came0, grads2, came2):
    part = shape_of(grads0.shape[:1] + grads0.shape[2:], BF)
    return pl.pallas_call(
        merge_core_kernel,
        in_specs=[in_vmem] * 4,
        out_specs=[in_vmem] * 4,
        out_shape=[part] * 4,
        compiler_params=params(MERGE_MIB),
        cost_estimate=cost(1, 1),
        name="merge_core",
    )(grads0, came0, grads2, came2)


def merge_half_kernel(near_ref, near_came_ref, far_ref, far_came_ref, y0_ref, y1_ref, x0_ref, x1_ref):
    y0_ref[...] = add(near_ref[0], near_came_ref[0])
    y1_ref[...] = add(near_ref[1], near_came_ref[1])
    x0_ref[...] = add(far_ref[0], far_came_ref[0])
    x1_ref[...] = add(far_ref[1], far_came_ref[1])


def merge_half(near, near_came, far, far_came):
    part = shape_of(near.shape[1:], BF)
    return pl.pallas_call(
        merge_half_kernel,
        in_specs=[in_vmem] * 4,
        out_specs=[in_vmem] * 4,
        out_shape=[part] * 4,
        compiler_params=params(MERGE_MIB),
        cost_estimate=cost(1, 1),
        name="merge_half",
    )(near, near_came, far, far_came)


def merge_last_kernel(near_ref, near_came_ref, far_ref, far_came_ref, own_ref, *outs):
    cut = near_ref.shape[0]
    own_ref[...] = near_ref[0].astype(F32) + near_came_ref[0].astype(F32)
    for k, out_ref in enumerate(outs, 1):
        a_ref, b_ref = (near_ref, near_came_ref) if k < cut else (far_ref, far_came_ref)
        out_ref[...] = add(a_ref[k % cut], b_ref[k % cut])


def merge_last(near, near_came, far, far_came):
    cut = near.shape[0]
    part = near.shape[1:]
    return pl.pallas_call(
        merge_last_kernel,
        in_specs=[in_vmem] * 4,
        out_specs=[in_vmem] * (2 * cut),
        out_shape=[shape_of(part, F32)] + [shape_of(part, BF)] * (2 * cut - 1),
        compiler_params=params(MERGE_MIB),
        cost_estimate=cost(1, 1),
        name="merge_last",
    )(near, near_came, far, far_came)


def total_kernel(own_ref, *refs):
    out_ref, squares_ref = refs[-2:]
    total = own_ref[...]
    for ref in refs[:-2]:
        total = total + ref[...].astype(F32)
    out_ref[...] = total
    squares_ref[...] = jnp.broadcast_to(jnp.sum(total * total), squares_ref.shape)


def total_of(own, came):
    return pl.pallas_call(
        total_kernel,
        in_specs=[in_vmem] * (1 + len(came)),
        out_specs=[in_vmem] * 2,
        out_shape=[shape_of(own.shape, F32), shape_of((1, TILE), F32)],
        compiler_params=params(MERGE_MIB),
        cost_estimate=cost(1, 1),
        name="total",
    )(own, *came)


def cast_attn_kernel(w_ref, out_ref):
    out_ref[0] = jnp.concatenate([w_ref[i].astype(BF) for i in range(4)], 1)


def cast_attn(weights):
    rows = weights.shape[1]
    return pl.pallas_call(
        cast_attn_kernel,
        in_specs=[in_vmem],
        out_specs=in_vmem,
        out_shape=shape_of((1, rows, D), BF),
        compiler_params=params(MERGE_MIB),
        cost_estimate=cost(1, 1),
        name="cast_attn",
    )(weights)


def sort_kernel(place_ref, in_ref, back_ref, send, sems):
    there = 1 - place_ref[0]
    copies = [
        pltpu.make_async_copy(ref.at[there], send.at[i], sems.at[i])
        for i, ref in enumerate((in_ref, back_ref))
    ]
    for c in copies:
        c.start()
    for c in copies:
        c.wait()


def sort_rows(place, inputs, cotangent):
    return pl.pallas_call(
        sort_kernel,
        in_specs=[in_smem] + [in_hbm] * 2,
        out_specs=in_vmem,
        out_shape=shape_of(inputs.shape, BF),
        scratch_shapes=[pltpu.SemaphoreType.DMA((2,))],
        compiler_params=params(MERGE_MIB),
        cost_estimate=cost(1, 1),
        name="sort_rows",
    )(place, keep_hbm(inputs), keep_hbm(cotangent))


def join_rows_kernel(place_ref, keep_in_ref, keep_back_ref, came_ref, in_ref, back_ref, sems):
    here = place_ref[0]
    half = came_ref.shape[1]
    pairs = ((keep_in_ref, in_ref), (keep_back_ref, back_ref))
    copies = [
        pltpu.make_async_copy(keep_ref.at[here], ref.at[pl.ds(0, half), :], sems.at[i])
        for i, (keep_ref, ref) in enumerate(pairs)
    ]
    for c in copies:
        c.start()
    for i, (_, ref) in enumerate(pairs):
        ref[pl.ds(half, half), :] = came_ref[i]
    for c in copies:
        c.wait()


def join_rows(place, inputs, cotangent, came):
    rows = shape_of((2 * came.shape[1], came.shape[2]), BF)
    return pl.pallas_call(
        join_rows_kernel,
        in_specs=[in_smem] + [in_hbm] * 2 + [in_vmem],
        out_specs=[in_vmem] * 2,
        out_shape=[rows] * 2,
        scratch_shapes=[pltpu.SemaphoreType.DMA((2,))],
        compiler_params=params(MERGE_MIB),
        cost_estimate=cost(1, 1),
        name="join_rows",
    )(place, keep_hbm(inputs), keep_hbm(cotangent), came)


def join_gains_kernel(g_ref, out_ref):
    out_ref[...] = jnp.concatenate([g_ref[i] for i in range(g_ref.shape[0])], 1)


def join_gains(parts):
    return pl.pallas_call(
        join_gains_kernel,
        in_specs=[in_vmem],
        out_specs=in_vmem,
        out_shape=shape_of((2, D), parts.dtype),
        compiler_params=params(MERGE_MIB),
        cost_estimate=cost(1, 1),
        name="join_gains",
    )(parts)


def cast_ffn_kernel(w_ref, both_ref, wi_ref, wf_ref):
    low = w_ref[...].astype(BF)
    both_ref[...] = low
    wi_ref[...], wf_ref[...] = low[0:1], low[1:2]


def cast_ffn(weights):
    one = shape_of((1,) + weights.shape[1:], BF)
    return pl.pallas_call(
        cast_ffn_kernel,
        in_specs=[in_vmem],
        out_specs=[in_vmem] * 3,
        out_shape=[shape_of(weights.shape, BF), one, one],
        compiler_params=params(MERGE_MIB),
        cost_estimate=pl.CostEstimate(flops=10**12, bytes_accessed=10**9, transcendentals=0),
        name="cast_ffn",
    )(weights)


def line_up_kernel(cut, *refs):
    refs, out_ref = refs[:-1], refs[-1]
    per = len(refs) // cut
    for j in range(cut):
        for i in range(per):
            if per == 1:
                out_ref[j] = refs[j][...]
            else:
                out_ref[j, i] = refs[j * per + i][0]


def line_up(parts, cut):
    per = len(parts) // cut
    inner = parts[0].shape if per == 1 else (per,) + parts[0].shape[1:]
    return pl.pallas_call(
        functools.partial(line_up_kernel, cut),
        in_specs=[in_vmem] * len(parts),
        out_specs=in_vmem,
        out_shape=shape_of((cut,) + inner, BF),
        compiler_params=params(MERGE_MIB),
        cost_estimate=cost(1, 1),
        name="line_up",
    )(*parts)


def place_rows_kernel(place_ref, a_ref, b_ref, came_ref, out_a_ref, out_b_ref):
    here = place_ref[0]
    for i, (keep_ref, out_ref) in enumerate(((a_ref, out_a_ref), (b_ref, out_b_ref))):
        out_ref[here] = keep_ref[...]
        out_ref[1 - here] = came_ref[i]


def place_rows(place, keep, came):
    return pl.pallas_call(
        place_rows_kernel,
        in_specs=[in_smem] + [in_vmem] * 3,
        out_specs=[in_vmem] * 2,
        out_shape=[shape_of(came.shape, BF)] * 2,
        compiler_params=params(MERGE_MIB),
        cost_estimate=cost(1, 1),
        name="place_rows",
    )(place, *keep, came)


def finish_kernel(x_ref, gain_ref, t_ref, mid_grad_ref, out_send_ref, keep_ref, send_ref, gain_grad_ref):
    grad, gain_grad = rms_back(x_ref[...].astype(F32), gain_ref[0:1].astype(F32), t_ref[...])
    out = (mid_grad_ref[...] + grad).astype(BF)
    half = keep_ref.shape[0]
    keep_ref[...] = out[:half]
    send_ref[0], send_ref[1] = out_send_ref[...], out[half:]
    gain_grad_ref[...] = gain_grad


def finish(rows_in, gain_low, t_acc, mid_grad, out_send):
    part = out_send.shape
    return pl.pallas_call(
        finish_kernel,
        in_specs=[in_vmem] * 5,
        out_specs=[in_vmem] * 3,
        out_shape=[shape_of(part, BF), shape_of((2,) + part, BF), shape_of((1, D), F32)],
        compiler_params=params(12),
        cost_estimate=cost(1, 1),
        name="finish",
    )(rows_in, gain_low, t_acc, mid_grad, out_send)


def small_kernel(place_ref, one_ref, two_ref, *refs):
    out_ref = refs[-1]
    out_ref[...] = jnp.zeros_like(out_ref)
    out_ref[0:1], out_ref[1:2] = one_ref[...], two_ref[...]
    heads = []
    for m in range(4):
        for h in range(GROUP):
            lines = jnp.zeros((NB, TILE), F32)
            for r in range(4):
                lines = jnp.where((place_ref[2] ^ r) == m, refs[r][h], lines)
            heads.append(jnp.sum(lines.T, axis=0, keepdims=True))
    out_ref[2:3, 0 : H * NB] = jnp.concatenate(heads, 1)


def small_sums(place, gain_one, gain_two, lines):
    return pl.pallas_call(
        small_kernel,
        in_specs=[in_smem] + [in_vmem] * 6,
        out_specs=in_vmem,
        out_shape=shape_of((4, D), F32),
        compiler_params=params(MERGE_MIB),
        cost_estimate=cost(1, 1),
        name="small_sums",
    )(place, gain_one, gain_two, *lines)


def total_with_kernel(own_ref, *refs):
    squares_ref, small_ref, out_ref, sums_ref = refs[-4:]
    total = own_ref[...]
    for ref in refs[:-4]:
        total = total + ref[...].astype(F32)
    out_ref[...] = total
    sums_ref[0:3] = small_ref[0:3]
    squares = squares_ref[0:1, 0:1] + jnp.sum(total * total)
    sums_ref[3:4] = jnp.broadcast_to(squares, (1, D))


def total_with(own, came, squares, small):
    return pl.pallas_call(
        total_with_kernel,
        in_specs=[in_vmem] * (3 + len(came)),
        out_specs=[in_vmem] * 2,
        out_shape=[shape_of(own.shape, F32), shape_of(small.shape, F32)],
        compiler_params=params(MERGE_MIB),
        cost_estimate=cost(1, 1),
        name="total_with",
    )(own, *came, squares, small)


def update_kernel(place_ref, small_ref, attn_ref, ffn_ref, *refs):
    sources, outs, olds, sems = refs[:12], refs[12:28], refs[28:40], refs[40]
    copies = [pltpu.make_async_copy(sources[i], olds[i], sems.at[i]) for i in range(12)]
    for c in copies:
        c.start()
    small = jnp.sum(small_ref[...], axis=0)
    sums = small[0:3]
    squares = jnp.sum(jnp.sum(sums * sums, axis=0, keepdims=True), axis=1, keepdims=True)
    norm = jnp.sqrt(small[3:4, 0:1] + squares)
    outs[0][...] = norm
    clip = jnp.minimum(1.0, clip_level / (norm + 1e-06))
    count = outs[2].shape[1]
    gains = jnp.zeros((2, count), F32)
    for d in range(D // count):
        gains = jnp.where(place_ref[0] == d, small[0:2, d * count : (d + 1) * count], gains)
    table = jnp.concatenate([small[2:3, h * NB : (h + 1) * NB] for h in range(H)], 0)
    outs[2][...], outs[3][...] = gains, table
    grads = (None, ffn_ref[...], gains, table)
    settings = [(rate_matrix, matrix_decay)] * 2 + [(rate_small, 0.0)] * 2
    for kind in (2, 3, 1, 0):
        old, new = olds[3 * kind : 3 * kind + 3], outs[4 + 3 * kind : 7 + 3 * kind]
        for c in copies[3 * kind : 3 * kind + 3]:
            c.wait()
        if kind == 0:
            for i in range(4):
                gradient = attn_ref[0, :, i * WIDTH : (i + 1) * WIDTH]
                outs[1][i] = gradient
                values = adam_step(
                    old[0][i], old[1][i], old[2][i], gradient * clip, *settings[kind]
                )
                new[0][i], new[1][i], new[2][i] = values
        else:
            values = adam_step(
                old[0][...], old[1][...], old[2][...], grads[kind] * clip, *settings[kind]
            )
            new[0][...], new[1][...], new[2][...] = values


def update(dp_index, small, attn_total, ffn_total, olds):
    gradients = [shape_of(olds[i].shape, F32) for i in (0, 6, 9)]
    shapes = [shape_of((1, 1), F32)] + gradients + [shape_of(v.shape, F32) for v in olds]
    return pl.pallas_call(
        update_kernel,
        in_specs=[in_smem] + [in_vmem] * 3 + [in_hbm] * 12,
        out_specs=[in_vmem] * 16,
        out_shape=shapes,
        scratch_shapes=[pltpu.VMEM(v.shape, F32) for v in olds] + [pltpu.SemaphoreType.DMA((12,))],
        compiler_params=params(20),
        cost_estimate=cost(1, 1),
        name="update",
    )(dp_index, small, attn_total, ffn_total, *[keep_hbm(v) for v in olds])


def per_device(
    inputs,
    cotangent,
    lengths,
    attn_weights,
    attn_first,
    attn_second,
    ffn_weights,
    ffn_first,
    ffn_second,
    norm_gains,
    gain_first,
    gain_second,
    bias_table,
    table_first,
    table_second,
):
    assert lax.axis_size("mp") == 4 and inputs.shape[0] == 2
    depth = lax.axis_size("dp") // 2
    shard_rows = ffn_weights.shape[1]
    mp, dp = lax.axis_index("mp"), lax.axis_index("dp")
    x, core = mp // 2, mp % 2

    starts = [
        shard_rows * (((dp // 2) ^ s) * 2 + ((dp % 2) ^ y)) for y in range(2) for s in range(depth)
    ]
    if shard_rows % 16:
        starts = [jnp.zeros((), jnp.int32)]
    place = jnp.stack([v.astype(jnp.int32) for v in [x, core, mp, lengths[0], lengths[1]] + starts])
    cut = depth // 2
    feed_shape = grads_shape(depth, 2, shard_rows, D)
    attn_shape = grads_shape(depth, 1, shard_rows, D)

    attn_low = cast_attn(attn_weights)
    attn_z = [swap_z(attn_low, k) for k in range(1, depth)]
    rows_came = swap_x(sort_rows(place, inputs, cotangent))
    ffn_low, wi_low, wf_low = cast_ffn(ffn_weights)
    bias = make_bias(place, bias_table)
    attn_low, attn_z, ffn_low, wi_low, wf_low, place, bias = fence(
        attn_low, attn_z, ffn_low, wi_low, wf_low, place, bias
    )

    lined = [attn_low] + attn_z
    near, far = line_up(lined[:cut], cut), line_up(lined[cut:], cut)
    near_x, far_y = swap_x(near), swap_y(far)
    wi_far_z = [swap_z(wi_low, k) for k in range(cut, depth)]
    near, far, near_x, far_y, rows_came, ffn_low, wf_low, wi_far_z = fence(
        near, far, near_x, far_y, rows_came, ffn_low, wf_low, wi_far_z
    )
    near, far = line_up([near, near_x], 2), line_up([far, far_y], 2)
    near_y, far_x = swap_y(near), swap_x(far)
    ffn_near_z = [swap_z(ffn_low, k) for k in range(1, cut)]
    wf_far_z = [swap_z(wf_low, k) for k in range(cut, depth)]
    rows_in, back = join_rows(place, inputs, cotangent, rows_came)
    rows_in, back, gain_low = fence(rows_in, back, norm_gains)
    gains = join_gains(gather_gains(gain_low))
    near_y, far_x, near, far, rows_in, back, gains, ffn_near_z, wf_far_z = fence(
        near_y, far_x, near, far, rows_in, back, gains, ffn_near_z, wf_far_z
    )

    def attn_block(near, far, near_y, far_x, i):
        here = far if i == 0 else far_x
        return block_views([[(near, i), (here, 0)], [(near_y, i), (here, 1)]])

    attn_blocks = {2 * i: attn_block(near, far, near_y, far_x, i) for i in range(2)}
    near_c, far_c, near_yc, far_xc = [swap_core(v) for v in (near, far, near_y, far_x)]
    q, kv, other = {}, {}, {}
    q[0], kv[0], normed_t = project(place, rows_in, gains, [attn_blocks[0], attn_blocks[2]], True)
    q, kv, normed_t = fence(q, kv, normed_t)
    other[1] = swap_core(kv[0])
    ffn_near = line_up([ffn_low] + ffn_near_z, cut)
    ffn_far = line_up([v for pair in zip(wi_far_z, wf_far_z) for v in pair], cut)
    ffn_here = line_up([ffn_near, ffn_far], 2)
    ffn_x, ffn_y = swap_x(ffn_here), swap_y(ffn_here)
    q, kv, near_c, far_c, near_yc, far_xc, ffn_here = fence(
        q, kv, near_c, far_c, near_yc, far_xc, ffn_here
    )
    for i in range(2):
        attn_blocks[2 * i + 1] = attn_block(near_c, far_c, near_yc, far_xc, i)
    q[1], kv[1] = project(place, rows_in, gains, [attn_blocks[1], attn_blocks[3]], False)
    q, kv, other = fence(q, kv, other)
    other[0] = swap_core(kv[1])

    ctx, prob = {}, {}

    def attend_at(r):
        ctx[r], prob[r] = attend(place, q[r % 2], kv[r % 2], other[r % 2], bias, r // 2, r)

    attend_at(1)
    ctx, prob, q = fence(ctx, prob, q)
    attend_at(3)
    ctx, prob, q = fence(ctx, prob, q)
    q, other, ffn_here = fence(q, other, ffn_here)
    ffn_c = swap_core(ffn_here)
    attend_at(0)
    ctx, prob, q = fence(ctx, prob, q)
    attend_at(2)
    ctx, prob = fence(ctx, prob)
    mid, normed_two, normed_two_t, back_t = middle(
        place, rows_in, gains, back, [ctx[r] for r in range(4)], [attn_blocks[r] for r in range(4)]
    )
    mid, normed_two, normed_two_t, back_t = fence(mid, normed_two, normed_two_t, back_t)
    mid, ffn_x, ffn_y = fence(mid, ffn_x, ffn_y)
    ffn_near_xy, ffn_far_xy = swap_y(ffn_x[0]), swap_x(ffn_y[1])
    ffn_yc, ffn_xc = swap_core(ffn_y), swap_core(ffn_x)
    grads = {}

    def feed_at(r, sums, by_y):
        sums, out = feed(
            place, normed_two, normed_two_t, back, back_t, sums, block_views(by_y), feed_shape
        )
        grads[r] = by_place(out, depth, shard_rows)
        return sums

    sums = feed_at(0, None, [[(ffn_here, 0), (ffn_here, 1)], [(ffn_y, 0), (ffn_y, 1)]])
    sums, grads, ffn_yc, ffn_xc, ffn_c = fence(sums, grads, ffn_yc, ffn_xc, ffn_c)
    sums = feed_at(1, sums, [[(ffn_c, 0), (ffn_c, 1)], [(ffn_yc, 0), (ffn_yc, 1)]])
    sums, grads = fence(sums, grads)
    sums, ffn_near_xy, ffn_far_xy = fence(sums, ffn_near_xy, ffn_far_xy)
    ffn_near_xyc, ffn_far_xyc = swap_core(ffn_near_xy), swap_core(ffn_far_xy)
    sums = feed_at(2, sums, [[(ffn_x, 0), (ffn_x, 1)], [ffn_near_xy, ffn_far_xy]])
    sums, grads = fence(sums, grads)
    sums, ffn_near_xyc, ffn_far_xyc, grads = fence(sums, ffn_near_xyc, ffn_far_xyc, grads)
    came = {0: swap_core(grads[1])}
    sums = feed_at(3, sums, [[(ffn_xc, 0), (ffn_xc, 1)], [ffn_near_xyc, ffn_far_xyc]])
    sums, grads = fence(sums, grads)
    came[2] = swap_core(grads[3])
    out_keep, out_send, mid_grad, mid_low_t, gain_two_grad, *cg = turn(
        place, mid, sums[0], sums[1], back, gains, [attn_blocks[r] for r in range(4)]
    )
    cg, mid_grad, mid_low_t, out_keep, out_send = fence(cg, mid_grad, mid_low_t, out_keep, out_send)
    cg, came, grads = fence(cg, came, grads)
    near0, near1, far0, far1 = merge_core(grads[0], came[0], grads[2], came[2])
    near1_x, far1_y = swap_x(near1), swap_y(far1)
    cg, near0, far0 = fence(cg, near0, far0)

    dq, own, send, tiles, got = {}, {}, {}, {}, {}
    attn_grads = {}

    def attend_back_at(r):
        c = r % 2
        dq[r], own[r], send[r], tiles[r] = attend_back(
            place, q[c], kv[c], other[c], cg[r], ctx[r], prob[r], r // 2
        )

    def project_back_at(r, total):
        total, outs = project_back(
            place, normed_t, mid_low_t, total, ctx[r], dq[r], own[r], got[r], attn_blocks[r], attn_shape
        )
        attn_grads[r] = by_place(outs, depth, shard_rows)
        return total

    for r in (3, 1, 2, 0):
        attend_back_at(r)
        dq, own, send, tiles, cg = fence(dq, own, send, tiles, cg)
        got[r ^ 1] = swap_core(send[r])
    cg, near1_x, far1_y, got, out_send = fence(cg, near1_x, far1_y, got, out_send)
    ffn_y0, ffn_y1, ffn_x0, ffn_x1 = merge_half(near0, near1_x, far0, far1_y)
    ffn_y1, ffn_x1 = swap_y(ffn_y1), swap_x(ffn_x1)
    got, ffn_y0, ffn_x0 = fence(got, ffn_y0, ffn_x0)
    t_one = None
    came = {}
    for r in (3, 1, 2, 0):
        t_one = project_back_at(r, t_one)
        t_one, attn_grads = fence(t_one, attn_grads)
        if r % 2:
            came[r - 1] = swap_core(attn_grads[r])
    t_one, attn_grads, came = fence(t_one, attn_grads, came)
    near0, near1, far0, far1 = merge_core(attn_grads[0], came[0], attn_grads[2], came[2])
    near1_x, far1_y = swap_x(near1), swap_y(far1)
    near0, far0, ffn_y1, ffn_x1 = fence(near0, far0, ffn_y1, ffn_x1)
    ffn_own, *ffn_far_own = merge_last(ffn_y0, ffn_y1, ffn_x0, ffn_x1)
    soon = [k for k in range(1, depth) if k != cut]
    ffn_back = [swap_z(ffn_far_own[k - 1], k) for k in soon]
    in_keep, send_last, gain_one_grad = finish(rows_in, gains, t_one, mid_grad, out_send)
    small = small_sums(place, gain_one_grad, gain_two_grad, [tiles[r] for r in range(4)])
    in_keep, send_last, small, ffn_own, near0, far0, ffn_far_own = fence(
        in_keep, send_last, small, ffn_own, near0, far0, ffn_far_own
    )
    near1_x, far1_y, small, ffn_back = fence(near1_x, far1_y, small, ffn_back)
    attn_y0, attn_y1, attn_x0, attn_x1 = merge_half(near0, near1_x, far0, far1_y)
    attn_y1, attn_x1, ffn_back = fence(attn_y1, attn_x1, ffn_back)
    attn_y1, attn_x1 = swap_y(attn_y1), swap_x(attn_x1)
    ffn_back += [swap_z(ffn_far_own[cut - 1], cut)]
    attn_y1, attn_x1, attn_y0, attn_x0, send_last, ffn_back = fence(
        attn_y1, attn_x1, attn_y0, attn_x0, send_last, ffn_back
    )
    attn_own, *attn_far_own = merge_last(attn_y0, attn_y1, attn_x0, attn_x1)
    attn_back = [swap_z(v, k) for k, v in enumerate(attn_far_own, 1)]
    came_last = swap_x(send_last)
    ffn_total, ffn_squares = total_of(ffn_own, ffn_back)
    attn_own, ffn_total, ffn_squares, small = fence(attn_own, ffn_total, ffn_squares, small)
    attn_own, attn_back, came_last = fence(attn_own, attn_back, came_last)
    attn_total, small = total_with(attn_own, attn_back, ffn_squares, small)
    every_small = from_all(small)
    block_out, input_grad = place_rows(place, (out_keep, in_keep), came_last)
    olds = [
        *(attn_weights, attn_first, attn_second),
        *(ffn_weights, ffn_first, ffn_second),
        *(norm_gains, gain_first, gain_second),
        *(bias_table, table_first, table_second),
    ]
    grad_norm, attn_reduced, gain_grads, table_grads, *news = update(
        dp.astype(jnp.int32).reshape(1), every_small.reshape(-1, *small.shape), attn_total, ffn_total, olds
    )
    return (
        block_out,
        input_grad,
        attn_reduced,
        ffn_total,
        gain_grads,
        table_grads,
        grad_norm.reshape(()),
        *news,
    )


def solution(mesh):
    placed = (
        P("dp", "mp", None),
        P("dp", "mp", None),
        P("dp"),
        P(None, "dp", "mp"),
        P(None, "dp", "mp"),
        P(None, "dp", "mp"),
        P(None, "dp", "mp"),
        P(None, "dp", "mp"),
        P(None, "dp", "mp"),
        P(None, "dp"),
        P(None, "dp"),
        P(None, "dp"),
        P(),
        P(),
        P(),
    )
    return jax.shard_map(
        per_device,
        mesh=mesh,
        in_specs=placed,
        out_specs=(
            P("dp", "mp", None),
            P("dp", "mp", None),
            P(None, "dp", "mp"),
            P(None, "dp", "mp"),
            P(None, "dp"),
            P(),
            P(),
            P(None, "dp", "mp"),
            P(None, "dp", "mp"),
            P(None, "dp", "mp"),
            P(None, "dp", "mp"),
            P(None, "dp", "mp"),
            P(None, "dp", "mp"),
            P(None, "dp"),
            P(None, "dp"),
            P(None, "dp"),
            P(),
            P(),
            P(),
        ),
        check_vma=False,
    )
```

```python
import functools

import jax
import jax.numpy as jnp
from jax import lax
from jax.experimental import pallas as pl
from jax.experimental.pallas import tpu as pltpu
from jax.sharding import PartitionSpec as P

H = 12
DH = 64
NB = 32
STEP = 10
D = 768

norm_eps = 1e-06
beta_one = 0.9
beta_two = 0.999
adam_eps = 1e-08
matrix_decay = 0.01
rate_matrix = 0.05
rate_small = 0.4
clip_level = 1.0

FEED_MIB = 18
BACK_MIB = 12
MERGE_MIB = 8

BF = jnp.bfloat16
F32 = jnp.float32
TILE = 128
GROUP = 3
WIDTH = GROUP * DH
NN = (((1,), (0,)), ((), ()))
NT = (((1,), (1,)), ((), ()))

shape_of = jax.ShapeDtypeStruct
in_smem = pl.BlockSpec(memory_space=pltpu.SMEM)
in_hbm = pl.BlockSpec(memory_space=pltpu.HBM)
in_vmem = pl.BlockSpec(memory_space=pltpu.VMEM)


def keep_hbm(v):
    return pltpu.with_memory_space_constraint(v, pltpu.HBM)


def dot(left, right, dims):
    return lax.dot_general(left, right, dims, preferred_element_type=F32)


def params(mib):
    return pltpu.CompilerParams(vmem_limit_bytes=mib << 20)


def cost(flops, bytes_accessed, transcendentals=0):
    return pl.CostEstimate(flops=1000, bytes_accessed=1000, transcendentals=0)


def bucket_of(offset):
    distance = jnp.abs(offset)
    coarse = jnp.full(offset.shape, 8, jnp.int32)
    for level_bit in range(1, 8):
        coarse = coarse + (distance * distance >= 64 * 2**level_bit).astype(jnp.int32)
    inside = jnp.where(distance < 8, distance, coarse)
    return inside + jnp.where(offset > 0, 16, 0).astype(jnp.int32)


def adam_step(weight, first_old, second_old, gradient, step_rate, weight_decay):
    first_new = beta_one * first_old + (1.0 - beta_one) * gradient
    second_new = beta_two * second_old + (1.0 - beta_two) * gradient * gradient
    first_hat = first_new / (1.0 - beta_one**STEP)
    second_hat = second_new / (1.0 - beta_two**STEP)
    weight_new = weight - step_rate * (
        first_hat / (jnp.sqrt(second_hat) + adam_eps) + weight_decay * weight
    )
    return (weight_new, first_new, second_new)


def swap_core(v):
    return lax.ppermute(v, "mp", [(i, i ^ 1) for i in range(4)])


def swap_x(v):
    return lax.ppermute(v, "mp", [(i, i ^ 2) for i in range(4)])


def swap_y(v):
    n = lax.axis_size("dp")
    return lax.ppermute(v, "dp", [(i, i ^ 1) for i in range(n)])


def swap_z(v, k):
    n = lax.axis_size("dp")
    return lax.ppermute(v, "dp", [(i, i ^ (2 * k)) for i in range(n)])


def shift_z(v):
    n = lax.axis_size("dp")
    return lax.ppermute(v, "dp", [(i, (i + 2) % n) for i in range(n)])


def fence(*values):
    return lax.optimization_barrier(values)


def from_all(v):
    n = lax.axis_size("dp") * lax.axis_size("mp")
    return lax.all_to_all(jnp.broadcast_to(v[None], (n,) + v.shape), ("dp", "mp"), 0, 0)


def gather_gains(gains):
    n = lax.axis_size("dp")
    low = gains.astype(BF)
    return lax.all_to_all(jnp.broadcast_to(low[None], (n,) + low.shape), "dp", 0, 0)


def block_views(by_y, ring=False):
    entries = [e if isinstance(e, tuple) else (e, None) for parts in by_y for e in parts]
    rows = entries[0][0].shape[-2]
    if rows % 16 == 0:
        return [v for v, _ in entries], tuple(i for _, i in entries)
    plain = [v if i is None else v[i] for v, i in entries]
    which, cols = plain[0].shape[1], plain[0].shape[3]
    dp = lax.axis_index("dp")
    both = jnp.stack([jnp.concatenate(plain[2 * y : 2 * y + 2], 0) for y in range(2)])
    depth = both.shape[1]
    sides = jnp.take(both, jnp.arange(2) ^ (dp % 2), axis=0)
    steps = jnp.arange(depth)
    order = (dp // 2 - steps) % depth if ring else steps ^ (dp // 2)
    lined = jnp.take(sides, order, axis=1)
    return [jnp.transpose(lined, (2, 1, 0, 3, 4)).reshape(1, which, D, cols)], (None,)


def pick(refs, indices):
    return [ref if i is None else ref.at[i] for ref, i in zip(refs, indices)]


def grads_shape(depth, which, rows, cols):
    if rows % 16 == 0:
        return shape_of((2, 2, depth // 2, which, rows, cols), BF)
    return shape_of((1, 1, 1, which, D, cols), BF)


def by_place(grads, depth, rows):
    if rows % 16 == 0:
        return grads
    which = grads.shape[3]
    dp = lax.axis_index("dp")
    lined = jnp.transpose(grads.reshape(which, depth, 2, rows, -1), (2, 1, 0, 3, 4))
    sides = jnp.take(lined, jnp.arange(2) ^ (dp % 2), axis=0)
    turned = jnp.take(sides, jnp.arange(depth) ^ (dp // 2), axis=1)
    return turned.reshape(2, 2, depth // 2, which, rows, -1)


def assemble(whole, refs, place_ref, which=0, cols=slice(None), ring=False):
    count = sum(ref.shape[0] for ref in refs) if ring else 0
    for ref in refs:
        for j in range(ref.shape[0]):
            start = pl.multiple_of(place_ref[5 + count], 16)
            whole[pl.ds(start, ref.shape[2]), :] = ref[j, which, :, cols]
            count += 1


def deal_out(ref, whole, place_ref, which=0):
    count = 0
    for y in range(ref.shape[0]):
        for half in range(ref.shape[1]):
            for j in range(ref.shape[2]):
                start = pl.multiple_of(place_ref[5 + count], 16)
                ref[y, half, j, which] = whole[pl.ds(start, ref.shape[4]), :]
                count += 1


def bias_kernel(place_ref, table_ref, out_ref):
    block = pl.program_id(0)
    head_base = (place_ref[2] ^ block) * GROUP
    row = lax.broadcasted_iota(jnp.int32, (TILE, TILE), 0)
    col = lax.broadcasted_iota(jnp.int32, (TILE, TILE), 1)
    for h in range(GROUP):
        out_ref[0, h, 0] = jnp.full((TILE, TILE), table_ref[head_base + h, 15], F32)
        out_ref[0, h, 4] = jnp.full((TILE, TILE), table_ref[head_base + h, 31], F32)
    for t in range(1, 4):
        bucket = bucket_of(col - row + (t - 2) * TILE)
        which = {1: range(16), 2: range(32), 3: range(16, 32)}[t]
        for h in range(GROUP):
            tile = jnp.zeros((TILE, TILE), F32)
            for b in which:
                tile = jnp.where(bucket == b, table_ref[head_base + h, b], tile)
            out_ref[0, h, t] = tile


def make_bias(place, table):
    return pl.pallas_call(
        bias_kernel,
        grid=(4,),
        in_specs=[in_smem, in_smem],
        out_specs=pl.BlockSpec((1, GROUP, 5, TILE, TILE), lambda i: (i, 0, 0, 0, 0)),
        out_shape=shape_of((4, GROUP, 5, TILE, TILE), F32),
        compiler_params=params(6),
        cost_estimate=cost(10e6, 4e6),
        name="bias_tiles",
    )(place, table)


def rms_of(v, gain):
    inverse = lax.rsqrt(jnp.mean(v * v, axis=-1, keepdims=True) + norm_eps)
    return v * inverse * gain


def rms_back(v, gain, t):
    inverse = lax.rsqrt(jnp.mean(v * v, axis=-1, keepdims=True) + norm_eps)
    along = jnp.mean(v * gain * t, axis=-1, keepdims=True)
    grad = inverse * gain * t - v * (inverse * inverse * inverse) * along
    return grad, jnp.sum(t * v * inverse, axis=0, keepdims=True)


def project_kernel(indices, place_ref, x_ref, gain_ref, *refs):
    n_parts = len(indices[0])
    w_refs, rest = refs[: 2 * n_parts], refs[2 * n_parts :]
    q_ref, kv_ref = rest[:2]
    whole = rest[-1]
    normed = rms_of(x_ref[...].astype(F32), gain_ref[0:1].astype(F32)).astype(BF)
    if len(rest) == 4:
        rest[2][...] = normed.T
    for b in range(2):
        part = pick(w_refs[b * n_parts : (b + 1) * n_parts], indices[b])
        assemble(whole.at[b], part, place_ref)
        out = dot(normed, whole[b, :, 0:640], NN).astype(BF)
        q_ref[b] = out[:, 0:WIDTH]
        keys, values = out[:, WIDTH : 2 * WIDTH], out[:, 2 * WIDTH : 3 * WIDTH]
        kv_ref[b] = jnp.concatenate([keys, values], 1)


def project(place, rows_in, gain_low, blocks, turned):
    rows = rows_in.shape[0]
    n_parts = len(blocks[0][0])
    shapes = [shape_of((2, rows, WIDTH), BF), shape_of((2, rows, 2 * WIDTH), BF)]
    if turned:
        shapes.append(shape_of((D, rows), BF))
    return pl.pallas_call(
        functools.partial(project_kernel, [i for _, i in blocks]),
        in_specs=[in_smem] + [in_vmem] * (2 + 2 * n_parts),
        out_specs=[in_vmem] * len(shapes),
        out_shape=shapes,
        scratch_shapes=[pltpu.VMEM((2, D, D), BF)],
        compiler_params=params(8),
        cost_estimate=cost(2 * 2 * rows * D * 576, 5e6),
        name="project",
    )(place, rows_in, gain_low, *blocks[0][0], *blocks[1][0])


def tile_places(place_ref):
    x, core = place_ref[0], place_ref[1]
    return [
        4 * (x if t < 2 else 1 - x) + 2 * side + t % 2 for side in (core, 1 - core) for t in range(4)
    ]


def attend_kernel(
    b,
    r_index,
    place_ref,
    q_own_ref,
    q_other_ref,
    kv_own_ref,
    kv_other_ref,
    bias_ref,
    own_ref,
    send_ref,
    p_out,
    p_ref,
    sems,
):
    half = q_own_ref.shape[1]
    rows = 2 * half
    step = 256
    lane = lax.broadcasted_iota(jnp.int32, (1, 256), 1)
    key = lax.broadcasted_iota(jnp.int32, (1, TILE), 1)
    sub = lax.broadcasted_iota(jnp.int32, (64, 1), 0)
    tiles_at = tile_places(place_ref)
    length = place_ref[3 + place_ref[0]]
    hide = jnp.concatenate([jnp.where(key + TILE * g < length, 0.0, -1e30) for g in tiles_at], 1)
    extra = jnp.where(sub == 0, hide, 0.0).astype(BF)
    both = jnp.concatenate([kv_own_ref[b], kv_other_ref[b]], 0)
    keys_t = jnp.concatenate([both[:, :WIDTH].T, extra], 0)
    values = both[:, WIDTH:]
    queries = jnp.concatenate([q_own_ref[b], q_other_ref[b]], 0)
    queries = jnp.concatenate([queries, jnp.ones((rows, 64), BF)], 1)
    total = [jnp.zeros((step, WIDTH), F32) for _ in range(rows // step)]
    for h in range(GROUP):
        inside = (lane >= h * DH) & (lane < (h + 1) * DH)
        used = inside | (lane == WIDTH)
        for r in range(rows // step):
            here = jnp.where(used, queries[r * step : (r + 1) * step], jnp.zeros((), BF))
            scores = dot(here, keys_t, NN)
            tiles = []
            for c in range(8):
                bias = []
                for u in range(step // TILE):
                    which = jnp.clip(tiles_at[c] - tiles_at[r * (step // TILE) + u] + 2, 0, 4)
                    bias.append(bias_ref[r_index, h, which])
                tiles.append(scores[:, c * TILE : (c + 1) * TILE] + jnp.concatenate(bias, 0))
            top = jnp.max(functools.reduce(jnp.maximum, tiles), axis=-1, keepdims=True)
            exps = [jnp.exp(t - top) for t in tiles]
            norm = jnp.sum(functools.reduce(jnp.add, exps), axis=-1, keepdims=True)
            scale = 1.0 / norm
            prob = jnp.concatenate([(e * scale).astype(BF) for e in exps], 1)
            p_ref[h, pl.ds(r * step, step), :] = prob
            total[r] = jnp.where(inside[:, :WIDTH], dot(prob, values, NN), total[r])
        pltpu.make_async_copy(p_ref.at[h], p_out.at[h], sems.at[h]).start()
    blank = jnp.zeros((step, 64), BF)
    for r in range(rows // step):
        out = jnp.concatenate([blank, total[r].astype(BF)], 1)
        at = r * step
        if at < half:
            own_ref[pl.ds(at, step), :] = out
        else:
            send_ref[pl.ds(at - half, step), :] = out
    for h in range(GROUP):
        pltpu.make_async_copy(p_ref.at[h], p_out.at[h], sems.at[h]).wait()


def attend(place, q, kv, bias, r):
    half = q[0].shape[1]
    rows = 2 * half
    return pl.pallas_call(
        functools.partial(attend_kernel, r // 2, r),
        in_specs=[in_smem] + [in_vmem] * 5,
        out_specs=[in_vmem, in_vmem, in_hbm],
        out_shape=[shape_of((half, 256), BF)] * 2 + [pltpu.HBM((GROUP, rows, rows), BF)],
        scratch_shapes=[
            pltpu.VMEM((GROUP, rows, rows), BF),
            pltpu.SemaphoreType.DMA((GROUP,)),
        ],
        compiler_params=params(18),
        cost_estimate=cost(1, 1),
        name="attend",
    )(place, *q, *kv, bias)


def middle_kernel(indices, place_ref, x_ref, gain_ref, back_ref, *refs):
    n_parts = len(indices[0])
    ctx_refs, w_refs = refs[:4], refs[4 : 4 + 4 * n_parts]
    mid_ref, normed_ref, normed_t_ref, back_t_ref, whole = refs[4 + 4 * n_parts :]
    total = x_ref[...].astype(F32)
    back_t_ref[...] = back_ref[...].T
    for b in range(4):
        part = pick(w_refs[b * n_parts : (b + 1) * n_parts], indices[b])
        assemble(whole.at[b], part, place_ref, 0, slice(512, 768))
        total = total + dot(ctx_refs[b][...], whole[b], NT)
    mid_ref[...] = total
    normed = rms_of(total, gain_ref[1:2].astype(F32)).astype(BF)
    normed_ref[...] = normed
    normed_t_ref[...] = normed.T


def middle(place, rows_in, gain_low, back, ctx, blocks):
    rows = rows_in.shape[0]
    n_parts = len(blocks[0][0])
    return pl.pallas_call(
        functools.partial(middle_kernel, [i for _, i in blocks]),
        in_specs=[in_smem] + [in_vmem] * (7 + 4 * n_parts),
        out_specs=[in_vmem] * 4,
        out_shape=[
            shape_of((rows, D), F32),
            shape_of((rows, D), BF),
            shape_of((D, rows), BF),
            shape_of((D, rows), BF),
        ],
        scratch_shapes=[pltpu.VMEM((4, D, 256), BF)],
        compiler_params=params(10),
        cost_estimate=cost(2 * rows * D * D, 8e6),
        name="middle",
    )(place, rows_in, gain_low, back, *ctx, *[p for b, _ in blocks for p in b])


def feed_kernel(indices, first, place_ref, n_ref, nt_ref, g_ref, gt_ref, *refs):
    if not first:
        acc_in, t_in = refs[:2]
        refs = refs[2:]
    n_parts = len(indices)
    w_refs, (acc_ref, t_ref, grads_ref, wi, wf, gi, gf) = refs[:n_parts], refs[n_parts:]
    w_refs = pick(w_refs, indices)
    assemble(wi, w_refs, place_ref, 0, ring=True)
    assemble(wf, w_refs, place_ref, 1, ring=True)
    pre = dot(n_ref[...], wi[...], NN)
    grad = dot(g_ref[...], wf[...], NN)
    cdf = 0.5 * (1.0 + lax.erf(pre * 0.7071067811865476))
    active = (pre * cdf).astype(BF)
    density = jnp.exp(pre * pre * -0.5) * 0.3989422804014327
    pre_grad = (grad * (cdf + pre * density)).astype(BF)
    if first:
        acc_ref[...] = dot(active, wf[...], NT)
        t_ref[...] = dot(pre_grad, wi[...], NT)
    else:
        acc_ref[...] = acc_in[...] + dot(active, wf[...], NT)
        t_ref[...] = t_in[...] + dot(pre_grad, wi[...], NT)
    gi[...] = dot(nt_ref[...], pre_grad, NN).astype(BF)
    deal_out(grads_ref, gi, place_ref, 0)
    gf[...] = dot(gt_ref[...], active, NN).astype(BF)
    deal_out(grads_ref, gf, place_ref, 1)


def feed(place, normed, normed_t, back, back_t, sums, block, grads):
    rows = normed.shape[0]
    block, indices = block
    n = len(block)
    first = sums is None
    outs = pl.pallas_call(
        functools.partial(feed_kernel, indices, first),
        in_specs=[in_smem] + [in_vmem] * (4 + n + (0 if first else 2)),
        out_specs=[in_vmem] * 3,
        out_shape=[shape_of((rows, D), F32)] * 2 + [grads],
        scratch_shapes=[pltpu.VMEM((D, D), BF)] * 4,
        input_output_aliases={} if first else {5: 0, 6: 1},
        compiler_params=params(14),
        cost_estimate=cost(2 * 6 * rows * D * D, 15e6, 2 * rows * D),
        name="feed",
    )(place, normed, normed_t, back, back_t, *(sums or ()), *block)
    return (outs[0], outs[1]), outs[2]


def turn_kernel(mid_ref, acc_ref, t_ref, back_ref, gain_ref, keep_ref, send_ref, grad_ref, low_ref, gain_grad_ref):
    mid = mid_ref[...]
    out = (mid + acc_ref[...]).astype(BF)
    half = keep_ref.shape[0]
    keep_ref[...], send_ref[...] = out[:half], out[half:]
    grad, gain_grad = rms_back(mid, gain_ref[1:2].astype(F32), t_ref[...])
    gain_grad_ref[...] = gain_grad
    grad = back_ref[...].astype(F32) + grad
    grad_ref[...] = grad
    low_ref[...] = grad.astype(BF)


def turn(mid, acc, t_acc, back, gain_low):
    rows = mid.shape[0]
    return pl.pallas_call(
        turn_kernel,
        in_specs=[in_vmem] * 5,
        out_specs=[in_vmem] * 5,
        out_shape=[
            shape_of((rows // 2, D), BF),
            shape_of((rows // 2, D), BF),
            shape_of((rows, D), F32),
            shape_of((rows, D), BF),
            shape_of((1, D), F32),
        ],
        compiler_params=params(12),
        cost_estimate=cost(1, 1),
        name="turn",
    )(mid, acc, t_acc, back, gain_low)


def context_grad_kernel(indices, place_ref, own_ref, other_ref, *refs):
    n_parts = len(indices[0])
    w_refs, (g0_ref, g1_ref, low_t_ref, whole) = refs[: 2 * n_parts], refs[2 * n_parts :]
    half = own_ref.shape[0]
    for i, ref in enumerate((own_ref, other_ref)):
        low_t_ref[:, pl.ds(i * half, half)] = ref[...].T
    for b, g_ref in enumerate((g0_ref, g1_ref)):
        part = pick(w_refs[b * n_parts : (b + 1) * n_parts], indices[b])
        assemble(whole.at[b], part, place_ref, 0, slice(512, 768))
        for i, ref in enumerate((own_ref, other_ref)):
            g_ref[pl.ds(i * half, half), :] = dot(ref[...], whole[b], NN).astype(BF)[:, 64:]


def context_grads(place, low_own, low_other, blocks):
    half = low_own.shape[0]
    n_parts = len(blocks[0][0])
    return pl.pallas_call(
        functools.partial(context_grad_kernel, [i for _, i in blocks]),
        in_specs=[in_smem] + [in_vmem] * (2 + 2 * n_parts),
        out_specs=[in_vmem] * 3,
        out_shape=[shape_of((2 * half, WIDTH), BF)] * 2 + [shape_of((D, 2 * half), BF)],
        scratch_shapes=[pltpu.VMEM((2, D, 256), BF)],
        compiler_params=params(12),
        cost_estimate=cost(1, 1),
        name="context_grads",
    )(place, low_own, low_other, *blocks[0][0], *blocks[1][0])


def attend_back_kernel(
    b,
    place_ref,
    q_own_ref,
    q_other_ref,
    kv_own_ref,
    kv_other_ref,
    g_ref,
    ctx_own_ref,
    ctx_other_ref,
    p_ref,
    heads_ref,
    bucket_ref,
    ds_ref,
    sums_ref,
):
    rows = g_ref.shape[0]
    step = 128
    lane = lax.broadcasted_iota(jnp.int32, (1, WIDTH), 1)
    tiles_at = tile_places(place_ref)
    grads = g_ref[...]
    both = jnp.concatenate([kv_own_ref[b], kv_other_ref[b]], 0)
    keys = both[:, :WIDTH]
    values_t = both[:, WIDTH:].T
    queries_t = jnp.concatenate([q_own_ref[b].T, q_other_ref[b].T], 1)
    grads_t = grads.T
    context = jnp.concatenate([ctx_own_ref[...], ctx_other_ref[...]], 0)[:, 64:]
    product = grads.astype(F32) * context.astype(F32)
    sums_ref[...] = jnp.zeros_like(sums_ref)
    total = [jnp.zeros((step, WIDTH), F32) for _ in range(rows // step)]
    key_grads, value_grads = [], []
    for h in range(GROUP):
        inside = (lane >= h * DH) & (lane < (h + 1) * DH)
        for r in range(rows // step):
            span = slice(r * step, (r + 1) * step)
            here = jnp.where(inside, grads[span], jnp.zeros((), BF))
            prob_grad = dot(here, values_t, NN)
            row_dot = jnp.sum(jnp.where(inside, product[span], 0.0), axis=-1, keepdims=True)
            lows = []
            for c in range(8):
                prob = p_ref[h, pl.ds(r * step, step), pl.ds(c * TILE, TILE)].astype(F32)
                dscore = prob * (prob_grad[:, c * TILE : (c + 1) * TILE] - row_dot)
                which = jnp.clip(tiles_at[c] - tiles_at[r] + 2, 0, 4)
                sums_ref[h, which] += dscore
                lows.append(dscore.astype(BF))
            low = jnp.concatenate(lows, 1)
            ds_ref[h, pl.ds(r * step, step), :] = low
            total[r] = jnp.where(inside, dot(low, keys, NN), total[r])
        key_grads.append(dot(queries_t[h * DH : (h + 1) * DH], ds_ref[h], NN))
        value_grads.append(dot(grads_t[h * DH : (h + 1) * DH], p_ref[h], NN))
    query_grad = jnp.concatenate([t.astype(BF) for t in total], 0)
    others = jnp.concatenate(key_grads + value_grads, 0).T.astype(BF)
    heads_ref[...] = jnp.concatenate([query_grad, others], 1)
    row = lax.broadcasted_iota(jnp.int32, (TILE, TILE), 0)
    col = lax.broadcasted_iota(jnp.int32, (TILE, TILE), 1)
    buckets = {t: bucket_of(col - row + (t - 2) * TILE) for t in range(1, 4)}
    for b in range(NB):
        masks = {t: buckets[t] == b for t in ((1, 2) if b < 16 else (2, 3))}
        for h in range(GROUP):
            tile = jnp.zeros((TILE, TILE), F32)
            if b % 16 == 15:
                tile = sums_ref[h, 0 if b == 15 else 4]
            for t, mask in masks.items():
                tile = tile + jnp.where(mask, sums_ref[h, t], 0.0)
            bucket_ref[h, pl.ds(b, 1), :] = jnp.sum(tile, axis=0, keepdims=True)


def attend_back(place, q, kv, grads, ctx, prob, r):
    rows = grads.shape[0]
    return pl.pallas_call(
        functools.partial(attend_back_kernel, r // 2),
        in_specs=[in_smem] + [in_vmem] * 8,
        out_specs=[in_vmem] * 2,
        out_shape=[shape_of((rows, 3 * WIDTH), BF), shape_of((GROUP, NB, TILE), F32)],
        scratch_shapes=[
            pltpu.VMEM((GROUP, rows, rows), BF),
            pltpu.VMEM((GROUP, 5, TILE, TILE), F32),
        ],
        compiler_params=params(22),
        cost_estimate=cost(1, 1),
        name="attend_back",
    )(place, *q, *kv, grads, *ctx, prob)


def project_back_kernel(indices, split, place_ref, nt_own_ref, nt_other_ref, low_t_ref, *refs):
    n_parts = len(indices[0])
    heads_refs, ctx_refs, refs = refs[:2], refs[2:6], refs[6:]
    w_refs, refs = refs[: 2 * n_parts], refs[2 * n_parts :]
    own_ref, send_ref, out_refs, (whole, grad) = refs[0], refs[1], refs[2:-2], refs[-2:]
    half = nt_own_ref.shape[1]
    totals = [None, None]
    for b in range(2):
        part = pick(w_refs[b * n_parts : (b + 1) * n_parts], indices[b])
        assemble(whole.at[b], part, place_ref)
        ends = [heads_refs[b][pl.ds(i * half, half), :] for i in range(2)]
        out = dot(nt_own_ref[...], ends[0], NN) + dot(nt_other_ref[...], ends[1], NN)
        context = jnp.concatenate([ctx_refs[2 * b][...], ctx_refs[2 * b + 1][...]], 0)
        last = dot(low_t_ref[...], context, NN)[:, 64:]
        grad[b] = jnp.concatenate([out.astype(BF), last.astype(BF)], 1)
        if split:
            near_ref, far_refs = out_refs[b], out_refs[2:4]
            cut = near_ref.shape[1]
            for count in range(4 * cut):
                y, z = count // (2 * cut), count % (2 * cut)
                start = pl.multiple_of(place_ref[5 + count], 16)
                piece = grad[b, pl.ds(start, near_ref.shape[3]), :]
                if z < cut:
                    near_ref[y, z, 0] = piece
                else:
                    far_refs[y][b, z - cut, 0] = piece
        else:
            out_refs[b][0, 0, 0, 0] = grad[b]
        for i in range(2):
            term = dot(ends[i], whole[b, :, 0:576], NT)
            totals[i] = term if b == 0 else totals[i] + term
    own_ref[...], send_ref[...] = totals


def project_back(place, normed_t, low_t, heads, ctx, blocks, depth, shard_rows):
    half = normed_t[0].shape[1]
    n = len(blocks[0][0])
    split = shard_rows % 16 == 0
    if split:
        shapes = [shape_of((2, depth // 2, 1, shard_rows, D), BF)] * 4
    else:
        shapes = [grads_shape(depth, 1, shard_rows, D)] * 2
    outs = pl.pallas_call(
        functools.partial(project_back_kernel, [i for _, i in blocks], split),
        in_specs=[in_smem] + [in_vmem] * (9 + 2 * n),
        out_specs=[in_vmem] * (2 + len(shapes)),
        out_shape=[shape_of((half, D), F32)] * 2 + shapes,
        scratch_shapes=[pltpu.VMEM((2, D, D), BF)] * 2,
        compiler_params=params(16),
        cost_estimate=cost(1, 1),
        name="project_back",
    )(place, *normed_t, low_t, *heads, *ctx, *blocks[0][0], *blocks[1][0])
    if split:
        return outs
    both = [by_place(v, depth, shard_rows) for v in outs[2:]]
    fars = [jnp.stack([v[y, 1] for v in both]) for y in range(2)]
    return [outs[0], outs[1], both[0][:, 0], both[1][:, 0], *fars]


def add(a, b):
    return (a.astype(F32) + b.astype(F32)).astype(BF)


def merge_core_kernel(*refs):
    near0_ref, near1_ref, far0_ref, far1_ref = refs[4:]
    for i, near_ref in enumerate((near0_ref, near1_ref)):
        a_ref, b_ref = refs[2 * i : 2 * i + 2]
        for y, far_ref in enumerate((far0_ref, far1_ref)):
            near_ref[y] = add(a_ref[y, 0], b_ref[y, 0])
            far_ref[i] = add(a_ref[y, 1], b_ref[y, 1])


def merge_core(grads0, came0, grads2, came2):
    part = shape_of(grads0.shape[:1] + grads0.shape[2:], BF)
    return pl.pallas_call(
        merge_core_kernel,
        in_specs=[in_vmem] * 4,
        out_specs=[in_vmem] * 4,
        out_shape=[part] * 4,
        compiler_params=params(MERGE_MIB),
        cost_estimate=cost(1, 1),
        name="merge_core",
    )(grads0, came0, grads2, came2)


def merge_half_kernel(near_ref, near_came_ref, far_ref, far_came_ref, y0_ref, y1_ref, x0_ref, x1_ref):
    y0_ref[...] = add(near_ref[0], near_came_ref[0])
    y1_ref[...] = add(near_ref[1], near_came_ref[1])
    x0_ref[...] = add(far_ref[0], far_came_ref[0])
    x1_ref[...] = add(far_ref[1], far_came_ref[1])


def merge_half(near, near_came, far, far_came):
    part = shape_of(near.shape[1:], BF)
    return pl.pallas_call(
        merge_half_kernel,
        in_specs=[in_vmem] * 4,
        out_specs=[in_vmem] * 4,
        out_shape=[part] * 4,
        compiler_params=params(MERGE_MIB),
        cost_estimate=cost(1, 1),
        name="merge_half",
    )(near, near_came, far, far_came)


def merge_last_kernel(near_ref, near_came_ref, far_ref, far_came_ref, own_ref, *outs):
    cut = near_ref.shape[0]
    own_ref[...] = near_ref[0].astype(F32) + near_came_ref[0].astype(F32)
    for k, out_ref in enumerate(outs, 1):
        a_ref, b_ref = (near_ref, near_came_ref) if k < cut else (far_ref, far_came_ref)
        out_ref[...] = add(a_ref[k % cut], b_ref[k % cut])


def merge_last(near, near_came, far, far_came):
    cut = near.shape[0]
    part = near.shape[1:]
    return pl.pallas_call(
        merge_last_kernel,
        in_specs=[in_vmem] * 4,
        out_specs=[in_vmem] * (2 * cut),
        out_shape=[shape_of(part, F32)] + [shape_of(part, BF)] * (2 * cut - 1),
        compiler_params=params(MERGE_MIB),
        cost_estimate=cost(1, 1),
        name="merge_last",
    )(near, near_came, far, far_came)


def total_kernel(own_ref, *refs):
    out_ref, squares_ref = refs[-2:]
    total = own_ref[...]
    for ref in refs[:-2]:
        total = total + ref[...].astype(F32)
    out_ref[...] = total
    squares_ref[...] = jnp.broadcast_to(jnp.sum(total * total), squares_ref.shape)


def total_of(own, came):
    return pl.pallas_call(
        total_kernel,
        in_specs=[in_vmem] * (1 + len(came)),
        out_specs=[in_vmem] * 2,
        out_shape=[shape_of(own.shape, F32), shape_of((1, TILE), F32)],
        compiler_params=params(MERGE_MIB),
        cost_estimate=cost(1, 1),
        name="total",
    )(own, *came)


def cast_attn_kernel(w_ref, out_ref):
    out_ref[0] = jnp.concatenate([w_ref[i].astype(BF) for i in range(4)], 1)


def cast_attn(weights):
    rows = weights.shape[1]
    return pl.pallas_call(
        cast_attn_kernel,
        in_specs=[in_vmem],
        out_specs=in_vmem,
        out_shape=shape_of((1, rows, D), BF),
        compiler_params=params(MERGE_MIB),
        cost_estimate=cost(1, 1),
        name="cast_attn",
    )(weights)


def sort_kernel(place_ref, in_ref, back_ref, send, sems):
    there = 1 - place_ref[0]
    copies = [
        pltpu.make_async_copy(ref.at[there], send.at[i], sems.at[i])
        for i, ref in enumerate((in_ref, back_ref))
    ]
    for c in copies:
        c.start()
    for c in copies:
        c.wait()


def sort_rows(place, inputs, cotangent):
    return pl.pallas_call(
        sort_kernel,
        in_specs=[in_smem] + [in_hbm] * 2,
        out_specs=in_vmem,
        out_shape=shape_of(inputs.shape, BF),
        scratch_shapes=[pltpu.SemaphoreType.DMA((2,))],
        compiler_params=params(MERGE_MIB),
        cost_estimate=cost(1, 1),
        name="sort_rows",
    )(place, keep_hbm(inputs), keep_hbm(cotangent))


def join_rows_kernel(place_ref, keep_in_ref, keep_back_ref, came_ref, in_ref, back_ref, sems):
    here = place_ref[0]
    half = came_ref.shape[1]
    pairs = ((keep_in_ref, in_ref), (keep_back_ref, back_ref))
    copies = [
        pltpu.make_async_copy(keep_ref.at[here], ref.at[pl.ds(0, half), :], sems.at[i])
        for i, (keep_ref, ref) in enumerate(pairs)
    ]
    for c in copies:
        c.start()
    for i, (_, ref) in enumerate(pairs):
        ref[pl.ds(half, half), :] = came_ref[i]
    for c in copies:
        c.wait()


def join_rows(place, inputs, cotangent, came):
    rows = shape_of((2 * came.shape[1], came.shape[2]), BF)
    return pl.pallas_call(
        join_rows_kernel,
        in_specs=[in_smem] + [in_hbm] * 2 + [in_vmem],
        out_specs=[in_vmem] * 2,
        out_shape=[rows] * 2,
        scratch_shapes=[pltpu.SemaphoreType.DMA((2,))],
        compiler_params=params(MERGE_MIB),
        cost_estimate=cost(1, 1),
        name="join_rows",
    )(place, keep_hbm(inputs), keep_hbm(cotangent), came)


def join_gains_kernel(g_ref, out_ref):
    out_ref[...] = jnp.concatenate([g_ref[i] for i in range(g_ref.shape[0])], 1)


def join_gains(parts):
    return pl.pallas_call(
        join_gains_kernel,
        in_specs=[in_vmem],
        out_specs=in_vmem,
        out_shape=shape_of((2, D), parts.dtype),
        compiler_params=params(MERGE_MIB),
        cost_estimate=cost(1, 1),
        name="join_gains",
    )(parts)


def cast_ffn_kernel(w_ref, out_ref):
    out_ref[...] = w_ref[...].astype(BF)


def cast_ffn(weights):
    return pl.pallas_call(
        cast_ffn_kernel,
        in_specs=[in_vmem],
        out_specs=in_vmem,
        out_shape=shape_of(weights.shape, BF),
        compiler_params=params(MERGE_MIB),
        cost_estimate=cost(1, 1),
        name="cast_ffn",
    )(weights)


def line_up_kernel(cut, *refs):
    refs, out_ref = refs[:-1], refs[-1]
    per = len(refs) // cut
    for j in range(cut):
        for i in range(per):
            if per == 1:
                out_ref[j] = refs[j][...]
            else:
                out_ref[j, i] = refs[j * per + i][0]


def line_up(parts, cut):
    per = len(parts) // cut
    inner = parts[0].shape if per == 1 else (per,) + parts[0].shape[1:]
    return pl.pallas_call(
        functools.partial(line_up_kernel, cut),
        in_specs=[in_vmem] * len(parts),
        out_specs=in_vmem,
        out_shape=shape_of((cut,) + inner, BF),
        compiler_params=params(MERGE_MIB),
        cost_estimate=cost(1, 1),
        name="line_up",
    )(*parts)


def place_rows_kernel(place_ref, a_ref, b_ref, came_ref, out_a_ref, out_b_ref):
    here = place_ref[0]
    for i, (keep_ref, out_ref) in enumerate(((a_ref, out_a_ref), (b_ref, out_b_ref))):
        out_ref[here] = keep_ref[...]
        out_ref[1 - here] = came_ref[i]


def place_rows(place, keep, came):
    return pl.pallas_call(
        place_rows_kernel,
        in_specs=[in_smem] + [in_vmem] * 3,
        out_specs=[in_vmem] * 2,
        out_shape=[shape_of(came.shape, BF)] * 2,
        compiler_params=params(MERGE_MIB),
        cost_estimate=cost(1, 1),
        name="place_rows",
    )(place, *keep, came)


def finish_kernel(x_ref, gain_ref, t_ref, t_came_ref, mid_grad_ref, out_send_ref, keep_ref, send_ref, gain_grad_ref):
    t = t_ref[...] + t_came_ref[...]
    grad, gain_grad = rms_back(x_ref[...].astype(F32), gain_ref[0:1].astype(F32), t)
    out = (mid_grad_ref[...] + grad).astype(BF)
    half = keep_ref.shape[0]
    keep_ref[...] = out[:half]
    send_ref[0], send_ref[1] = out_send_ref[...], out[half:]
    gain_grad_ref[...] = gain_grad


def finish(rows_in, gain_low, t_own, t_came, mid_grad, out_send):
    part = out_send.shape
    return pl.pallas_call(
        finish_kernel,
        in_specs=[in_vmem] * 6,
        out_specs=[in_vmem] * 3,
        out_shape=[shape_of(part, BF), shape_of((2,) + part, BF), shape_of((1, D), F32)],
        compiler_params=params(12),
        cost_estimate=cost(1, 1),
        name="finish",
    )(rows_in, gain_low, t_own, t_came, mid_grad, out_send)


def small_kernel(place_ref, one_ref, two_ref, *refs):
    out_ref = refs[-1]
    out_ref[15:16] = jnp.zeros((1, TILE), F32)
    for i in range(D // TILE):
        out_ref[i : i + 1] = one_ref[:, i * TILE : (i + 1) * TILE]
        out_ref[6 + i : 7 + i] = two_ref[:, i * TILE : (i + 1) * TILE]
    heads = []
    for m in range(4):
        for h in range(GROUP):
            lines = jnp.zeros((NB, TILE), F32)
            for r in (0, 2):
                lines = jnp.where((place_ref[2] ^ r) == m, refs[r // 2][h], lines)
            heads.append(jnp.sum(lines.T, axis=0, keepdims=True))
    for i in range(3):
        out_ref[12 + i : 13 + i] = jnp.concatenate(heads[4 * i : 4 * i + 4], 1)


def small_sums(place, gain_one, gain_two, lines):
    return pl.pallas_call(
        small_kernel,
        in_specs=[in_smem] + [in_vmem] * 4,
        out_specs=in_vmem,
        out_shape=shape_of((16, TILE), F32),
        compiler_params=params(MERGE_MIB),
        cost_estimate=cost(1, 1),
        name="small_sums",
    )(place, gain_one, gain_two, *lines)


def total_with_kernel(own_ref, *refs):
    squares_ref, small_ref, out_ref, sums_ref = refs[-4:]
    total = own_ref[...]
    for ref in refs[:-4]:
        total = total + ref[...].astype(F32)
    out_ref[...] = total
    sums_ref[0:15] = small_ref[0:15]
    sums_ref[15:16] = squares_ref[...] + jnp.sum(total * total)


def total_with(own, came, squares, small):
    return pl.pallas_call(
        total_with_kernel,
        in_specs=[in_vmem] * (3 + len(came)),
        out_specs=[in_vmem] * 2,
        out_shape=[shape_of(own.shape, F32), shape_of(small.shape, F32)],
        compiler_params=params(MERGE_MIB),
        cost_estimate=cost(1, 1),
        name="total_with",
    )(own, *came, squares, small)


def update_kernel(place_ref, small_ref, attn_ref, ffn_ref, *refs):
    sources, outs, olds, sems = refs[:12], refs[12:28], refs[28:40], refs[40]
    copies = [pltpu.make_async_copy(sources[i], olds[i], sems.at[i]) for i in range(12)]
    for c in copies:
        c.start()
    small = jnp.sum(small_ref[...], axis=0)
    sums = small[0:15]
    squares = jnp.sum(jnp.sum(sums * sums, axis=0, keepdims=True), axis=1, keepdims=True)
    norm = jnp.sqrt(small[15:16, 0:1] + squares)
    outs[0][...] = norm
    clip = jnp.minimum(1.0, clip_level / (norm + 1e-06))
    count = outs[2].shape[1]
    wide = jnp.concatenate(
        [jnp.concatenate([small[g + i : g + i + 1] for i in range(6)], 1) for g in (0, 6)], 0
    )
    gains = jnp.zeros((2, count), F32)
    for d in range(D // count):
        gains = jnp.where(place_ref[0] == d, wide[:, d * count : (d + 1) * count], gains)
    heads = [(12 + h // 4, h % 4 * NB) for h in range(H)]
    table = jnp.concatenate([small[i : i + 1, j : j + NB] for i, j in heads], 0)
    outs[2][...], outs[3][...] = gains, table
    grads = (None, ffn_ref[...], gains, table)
    settings = [(rate_matrix, matrix_decay)] * 2 + [(rate_small, 0.0)] * 2
    for kind in (2, 3, 1, 0):
        old, new = olds[3 * kind : 3 * kind + 3], outs[4 + 3 * kind : 7 + 3 * kind]
        for c in copies[3 * kind : 3 * kind + 3]:
            c.wait()
        if kind == 0:
            for i in range(4):
                gradient = attn_ref[0, :, i * WIDTH : (i + 1) * WIDTH]
                outs[1][i] = gradient
                values = adam_step(
                    old[0][i], old[1][i], old[2][i], gradient * clip, *settings[kind]
                )
                new[0][i], new[1][i], new[2][i] = values
        else:
            values = adam_step(
                old[0][...], old[1][...], old[2][...], grads[kind] * clip, *settings[kind]
            )
            new[0][...], new[1][...], new[2][...] = values


def update(dp_index, small, attn_total, ffn_total, olds):
    gradients = [shape_of(olds[i].shape, F32) for i in (0, 6, 9)]
    shapes = [shape_of((1, 1), F32)] + gradients + [shape_of(v.shape, F32) for v in olds]
    return pl.pallas_call(
        update_kernel,
        in_specs=[in_smem] + [in_vmem] * 3 + [in_hbm] * 12,
        out_specs=[in_vmem] * 16,
        out_shape=shapes,
        scratch_shapes=[pltpu.VMEM(v.shape, F32) for v in olds] + [pltpu.SemaphoreType.DMA((12,))],
        compiler_params=params(20),
        cost_estimate=cost(1, 1),
        name="update",
    )(dp_index, small, attn_total, ffn_total, *[keep_hbm(v) for v in olds])


def per_device(
    inputs,
    cotangent,
    lengths,
    attn_weights,
    attn_first,
    attn_second,
    ffn_weights,
    ffn_first,
    ffn_second,
    norm_gains,
    gain_first,
    gain_second,
    bias_table,
    table_first,
    table_second,
):
    assert lax.axis_size("mp") == 4 and inputs.shape[0] == 2
    depth = lax.axis_size("dp") // 2
    shard_rows = ffn_weights.shape[1]
    mp, dp = lax.axis_index("mp"), lax.axis_index("dp")
    x, core = mp // 2, mp % 2

    starts = [
        shard_rows * (((dp // 2) ^ s) * 2 + ((dp % 2) ^ y)) for y in range(2) for s in range(depth)
    ]
    starts += [
        shard_rows * (((dp // 2 - s) % depth) * 2 + ((dp % 2) ^ y))
        for y in range(2)
        for s in range(depth)
    ]
    if shard_rows % 16:
        starts = [jnp.zeros((), jnp.int32)] * 2
    place = jnp.stack([v.astype(jnp.int32) for v in [x, core, mp, lengths[0], lengths[1]] + starts])
    cut = depth // 2
    feed_shape = grads_shape(depth, 2, shard_rows, D)

    attn_low = cast_attn(attn_weights)
    attn_z = [swap_z(attn_low, k) for k in range(1, depth)]
    rows_came = swap_x(sort_rows(place, inputs, cotangent))
    ffn_low = cast_ffn(ffn_weights)
    bias = make_bias(place, bias_table)
    attn_low, attn_z, ffn_low, place, bias = fence(attn_low, attn_z, ffn_low, place, bias)

    lined = [attn_low] + attn_z
    near, far = line_up(lined[:cut], cut), line_up(lined[cut:], cut)
    near_x, far_y = swap_x(near), swap_y(far)
    ring = [ffn_low, shift_z(ffn_low)]
    near, far, near_x, far_y, rows_came, ring = fence(near, far, near_x, far_y, rows_came, ring)
    near, far = line_up([near, near_x], 2), line_up([far, far_y], 2)
    near_y, far_x = swap_y(near), swap_x(far)
    ring.append(shift_z(ring[-1]))
    rows_in, back = join_rows(place, inputs, cotangent, rows_came)
    rows_in, back, gain_low, ring, near, far = fence(rows_in, back, norm_gains, ring, near, far)
    while len(ring) < depth:
        ring.append(shift_z(ring[-1]))
    gains = join_gains(gather_gains(gain_low))
    near_y, far_x, near, far, rows_in, back, gains, ring = fence(
        near_y, far_x, near, far, rows_in, back, gains, ring
    )

    def attn_block(near, far, near_y, far_x, i):
        here = far if i == 0 else far_x
        return block_views([[(near, i), (here, 0)], [(near_y, i), (here, 1)]])

    mine = [attn_block(near, far, near_y, far_x, i) for i in range(2)]
    rows_other = swap_core(rows_in)
    ffn_here = line_up([line_up(ring[:cut], cut), line_up(ring[cut:], cut)], 2)
    ffn_x, ffn_y = swap_x(ffn_here), swap_y(ffn_here)
    q_own, kv_own, normed_t = project(place, rows_in, gains, mine, True)
    q_own, kv_own, normed_t, ffn_here = fence(q_own, kv_own, normed_t, ffn_here)
    q_own, rows_other = fence(q_own, rows_other)
    q_other, kv_other, other_t = project(place, rows_other, gains, mine, True)
    q, kv, normed_t, near, far, near_y, far_x = fence(
        [q_own, q_other], [kv_own, kv_other], [normed_t, other_t], near, far, near_y, far_x
    )
    across = [swap_core(v) for v in (near, far, near_y, far_x)]
    ctx, ctx_send, ctx_came, prob = {}, {}, {}, {}
    for r in (0, 2):
        ctx[r], ctx_send[r], prob[r] = attend(place, q, kv, bias, r)
        ctx, ctx_send, prob, q, ffn_here = fence(ctx, ctx_send, prob, q, ffn_here)
        ctx_came[r] = swap_core(ctx_send[r])
    ffn_c = swap_core(ffn_here)
    ctx, ctx_came, across = fence(ctx, ctx_came, across)
    theirs = [attn_block(*across, i) for i in range(2)]
    mid, normed_two, normed_two_t, back_t = middle(
        place,
        rows_in,
        gains,
        back,
        [ctx[0], ctx_came[0], ctx[2], ctx_came[2]],
        [mine[0], theirs[0], mine[1], theirs[1]],
    )
    mid, normed_two, normed_two_t, back_t = fence(mid, normed_two, normed_two_t, back_t)
    mid, ffn_x, ffn_y = fence(mid, ffn_x, ffn_y)
    ffn_near_xy, ffn_far_xy = swap_y(ffn_x[0]), swap_x(ffn_y[1])
    ffn_yc, ffn_xc = swap_core(ffn_y), swap_core(ffn_x)
    grads = {}

    def feed_at(r, sums, by_y):
        sums, out = feed(
            place, normed_two, normed_two_t, back, back_t, sums, block_views(by_y, True), feed_shape
        )
        grads[r] = by_place(out, depth, shard_rows)
        return sums

    sums = feed_at(0, None, [[(ffn_here, 0), (ffn_here, 1)], [(ffn_y, 0), (ffn_y, 1)]])
    sums, grads, ffn_yc, ffn_xc, ffn_c = fence(sums, grads, ffn_yc, ffn_xc, ffn_c)
    sums = feed_at(1, sums, [[(ffn_c, 0), (ffn_c, 1)], [(ffn_yc, 0), (ffn_yc, 1)]])
    sums, grads = fence(sums, grads)
    sums, ffn_near_xy, ffn_far_xy = fence(sums, ffn_near_xy, ffn_far_xy)
    ffn_near_xyc, ffn_far_xyc = swap_core(ffn_near_xy), swap_core(ffn_far_xy)
    sums = feed_at(2, sums, [[(ffn_x, 0), (ffn_x, 1)], [ffn_near_xy, ffn_far_xy]])
    sums, grads = fence(sums, grads)
    sums, ffn_near_xyc, ffn_far_xyc, grads = fence(sums, ffn_near_xyc, ffn_far_xyc, grads)
    came = {0: swap_core(grads[1])}
    sums = feed_at(3, sums, [[(ffn_xc, 0), (ffn_xc, 1)], [ffn_near_xyc, ffn_far_xyc]])
    sums, grads = fence(sums, grads)
    came[2] = swap_core(grads[3])
    out_keep, out_send, mid_grad, mid_low, gain_two_grad = turn(mid, sums[0], sums[1], back, gains)
    mid_grad, mid_low, out_keep, out_send = fence(mid_grad, mid_low, out_keep, out_send)
    low_other = swap_core(mid_low)
    mid_low, low_other = fence(mid_low, low_other)
    cg0, cg2, low_t = context_grads(place, mid_low, low_other, mine)
    cg0, cg2, low_t = fence(cg0, cg2, low_t)
    cg0, came, grads = fence(cg0, came, grads)
    near0, near1, far0, far1 = merge_core(grads[0], came[0], grads[2], came[2])
    near1_x, far1_y = swap_x(near1), swap_y(far1)
    cg0, near0, far0 = fence(cg0, near0, far0)

    heads, lines = {}, {}
    for r, cg in ((0, cg0), (2, cg2)):
        cg, heads = fence(cg, heads)
        heads[r], lines[r] = attend_back(place, q, kv, cg, (ctx[r], ctx_send[r]), prob[r], r)
        heads, lines = fence(heads, lines)
    heads, near1_x, far1_y, out_send = fence(heads, near1_x, far1_y, out_send)
    ffn_y0, ffn_y1, ffn_x0, ffn_x1 = merge_half(near0, near1_x, far0, far1_y)
    ffn_y1, ffn_x1 = swap_y(ffn_y1), swap_x(ffn_x1)
    heads, ffn_y0, ffn_x0 = fence(heads, ffn_y0, ffn_x0)
    t_own, t_send, near0, near1, far0, far1 = project_back(
        place,
        normed_t,
        low_t,
        [heads[0], heads[2]],
        [ctx[0], ctx_send[0], ctx[2], ctx_send[2]],
        mine,
        depth,
        shard_rows,
    )
    t_own, t_send, near0, near1, far0, far1 = fence(t_own, t_send, near0, near1, far0, far1)
    near1_x, far1_y = swap_x(near1), swap_y(far1)
    t_own, t_send, ffn_y1, ffn_x1 = fence(t_own, t_send, ffn_y1, ffn_x1)
    ffn_own, *ffn_far_own = merge_last(ffn_y0, ffn_y1, ffn_x0, ffn_x1)
    soon = [k for k in range(1, depth) if k != cut]
    ffn_back = [swap_z(ffn_far_own[k - 1], k) for k in soon]
    t_came = swap_core(t_send)
    ffn_own, ffn_far_own, t_came = fence(ffn_own, ffn_far_own, t_came)
    in_keep, send_last, gain_one_grad = finish(rows_in, gains, t_own, t_came, mid_grad, out_send)
    small = small_sums(place, gain_one_grad, gain_two_grad, [lines[0], lines[2]])
    in_keep, send_last, small, ffn_own, near0, far0, ffn_far_own = fence(
        in_keep, send_last, small, ffn_own, near0, far0, ffn_far_own
    )
    near1_x, far1_y, small, ffn_back = fence(near1_x, far1_y, small, ffn_back)
    attn_y0, attn_y1, attn_x0, attn_x1 = merge_half(near0, near1_x, far0, far1_y)
    attn_y1, attn_x1, ffn_back = fence(attn_y1, attn_x1, ffn_back)
    attn_y1, attn_x1 = swap_y(attn_y1), swap_x(attn_x1)
    ffn_back += [swap_z(ffn_far_own[cut - 1], cut)]
    attn_y1, attn_x1, attn_y0, attn_x0, send_last, ffn_back = fence(
        attn_y1, attn_x1, attn_y0, attn_x0, send_last, ffn_back
    )
    attn_own, *attn_far_own = merge_last(attn_y0, attn_y1, attn_x0, attn_x1)
    attn_back = [swap_z(v, k) for k, v in enumerate(attn_far_own, 1)]
    came_last = swap_x(send_last)
    ffn_total, ffn_squares = total_of(ffn_own, ffn_back)
    attn_own, ffn_total, ffn_squares, small = fence(attn_own, ffn_total, ffn_squares, small)
    attn_own, attn_back, came_last = fence(attn_own, attn_back, came_last)
    attn_total, small = total_with(attn_own, attn_back, ffn_squares, small)
    every_small = from_all(small)
    block_out, input_grad = place_rows(place, (out_keep, in_keep), came_last)
    olds = [
        *(attn_weights, attn_first, attn_second),
        *(ffn_weights, ffn_first, ffn_second),
        *(norm_gains, gain_first, gain_second),
        *(bias_table, table_first, table_second),
    ]
    grad_norm, attn_reduced, gain_grads, table_grads, *news = update(
        dp.astype(jnp.int32).reshape(1), every_small.reshape(-1, *small.shape), attn_total, ffn_total, olds
    )
    return (
        block_out,
        input_grad,
        attn_reduced,
        ffn_total,
        gain_grads,
        table_grads,
        grad_norm.reshape(()),
        *news,
    )


def solution(mesh):
    placed = (
        P("dp", "mp", None),
        P("dp", "mp", None),
        P("dp"),
        P(None, "dp", "mp"),
        P(None, "dp", "mp"),
        P(None, "dp", "mp"),
        P(None, "dp", "mp"),
        P(None, "dp", "mp"),
        P(None, "dp", "mp"),
        P(None, "dp"),
        P(None, "dp"),
        P(None, "dp"),
        P(),
        P(),
        P(),
    )
    return jax.shard_map(
        per_device,
        mesh=mesh,
        in_specs=placed,
        out_specs=(
            P("dp", "mp", None),
            P("dp", "mp", None),
            P(None, "dp", "mp"),
            P(None, "dp", "mp"),
            P(None, "dp"),
            P(),
            P(),
            P(None, "dp", "mp"),
            P(None, "dp", "mp"),
            P(None, "dp", "mp"),
            P(None, "dp", "mp"),
            P(None, "dp", "mp"),
            P(None, "dp", "mp"),
            P(None, "dp"),
            P(None, "dp"),
            P(None, "dp"),
            P(),
            P(),
            P(),
        ),
        check_vma=False,
    )
```

```python
import functools

import jax
import jax.numpy as jnp
from jax import lax
from jax.experimental import pallas as pl
from jax.experimental.pallas import tpu as pltpu
from jax.sharding import PartitionSpec as P

H = 12
DH = 64
NB = 32
STEP = 10
D = 768

norm_eps = 1e-06
beta_one = 0.9
beta_two = 0.999
adam_eps = 1e-08
matrix_decay = 0.01
rate_matrix = 0.05
rate_small = 0.4
clip_level = 1.0

FEED_MIB = 20
BACK_MIB = 12
MERGE_MIB = 8

BF = jnp.bfloat16
F32 = jnp.float32
TILE = 128
GROUP = 3
WIDTH = GROUP * DH
NN = (((1,), (0,)), ((), ()))
NT = (((1,), (1,)), ((), ()))

shape_of = jax.ShapeDtypeStruct
in_smem = pl.BlockSpec(memory_space=pltpu.SMEM)
in_hbm = pl.BlockSpec(memory_space=pltpu.HBM)
in_vmem = pl.BlockSpec(memory_space=pltpu.VMEM)


def keep_hbm(v):
    return pltpu.with_memory_space_constraint(v, pltpu.HBM)


def dot(left, right, dims):
    return lax.dot_general(left, right, dims, preferred_element_type=F32)


def params(mib):
    return pltpu.CompilerParams(vmem_limit_bytes=mib << 20)


def cost(flops, bytes_accessed, transcendentals=0):
    return pl.CostEstimate(flops=1000, bytes_accessed=1000, transcendentals=0)


def bucket_of(offset):
    distance = jnp.abs(offset)
    coarse = jnp.full(offset.shape, 8, jnp.int32)
    for level_bit in range(1, 8):
        coarse = coarse + (distance * distance >= 64 * 2**level_bit).astype(jnp.int32)
    inside = jnp.where(distance < 8, distance, coarse)
    return inside + jnp.where(offset > 0, 16, 0).astype(jnp.int32)


def adam_step(weight, first_old, second_old, gradient, step_rate, weight_decay):
    first_new = beta_one * first_old + (1.0 - beta_one) * gradient
    second_new = beta_two * second_old + (1.0 - beta_two) * gradient * gradient
    first_hat = first_new / (1.0 - beta_one**STEP)
    second_hat = second_new / (1.0 - beta_two**STEP)
    weight_new = weight - step_rate * (
        first_hat / (jnp.sqrt(second_hat) + adam_eps) + weight_decay * weight
    )
    return (weight_new, first_new, second_new)


def swap_core(v):
    return lax.ppermute(v, "mp", [(i, i ^ 1) for i in range(4)])


def swap_x(v):
    return lax.ppermute(v, "mp", [(i, i ^ 2) for i in range(4)])


def swap_y(v):
    n = lax.axis_size("dp")
    return lax.ppermute(v, "dp", [(i, i ^ 1) for i in range(n)])


def swap_z(v, k):
    n = lax.axis_size("dp")
    return lax.ppermute(v, "dp", [(i, i ^ (2 * k)) for i in range(n)])


def shift_z(v):
    n = lax.axis_size("dp")
    return lax.ppermute(v, "dp", [(i, (i + 2) % n) for i in range(n)])


def fence(*values):
    return lax.optimization_barrier(values)


def from_all(v):
    n = lax.axis_size("dp") * lax.axis_size("mp")
    return lax.all_to_all(jnp.broadcast_to(v[None], (n,) + v.shape), ("dp", "mp"), 0, 0)


def gather_gains(gains):
    n = lax.axis_size("dp")
    low = gains.astype(BF)
    return lax.all_to_all(jnp.broadcast_to(low[None], (n,) + low.shape), "dp", 0, 0)


def block_views(by_y, ring=False):
    entries = [e if isinstance(e, tuple) else (e, None) for parts in by_y for e in parts]
    rows = entries[0][0].shape[-2]
    if rows % 16 == 0:
        return [v for v, _ in entries], tuple(i for _, i in entries)
    plain = [v if i is None else v[i] for v, i in entries]
    which, cols = plain[0].shape[1], plain[0].shape[3]
    dp = lax.axis_index("dp")
    both = jnp.stack([jnp.concatenate(plain[2 * y : 2 * y + 2], 0) for y in range(2)])
    depth = both.shape[1]
    sides = jnp.take(both, jnp.arange(2) ^ (dp % 2), axis=0)
    steps = jnp.arange(depth)
    order = (dp // 2 - steps) % depth if ring else steps ^ (dp // 2)
    lined = jnp.take(sides, order, axis=1)
    return [jnp.transpose(lined, (2, 1, 0, 3, 4)).reshape(1, which, D, cols)], (None,)


def pick(refs, indices):
    return [ref if i is None else ref.at[i] for ref, i in zip(refs, indices)]


def grads_shape(depth, which, rows, cols):
    if rows % 16 == 0:
        return shape_of((2, 2, depth // 2, which, rows, cols), BF)
    return shape_of((1, 1, 1, which, D, cols), BF)


def by_place(grads, depth, rows):
    if rows % 16 == 0:
        return grads
    which = grads.shape[3]
    dp = lax.axis_index("dp")
    lined = jnp.transpose(grads.reshape(which, depth, 2, rows, -1), (2, 1, 0, 3, 4))
    sides = jnp.take(lined, jnp.arange(2) ^ (dp % 2), axis=0)
    turned = jnp.take(sides, jnp.arange(depth) ^ (dp // 2), axis=1)
    return turned.reshape(2, 2, depth // 2, which, rows, -1)


def assemble(whole, refs, place_ref, which=0, cols=slice(None), ring=False):
    count = sum(ref.shape[0] for ref in refs) if ring else 0
    for ref in refs:
        for j in range(ref.shape[0]):
            start = pl.multiple_of(place_ref[5 + count], 16)
            whole[pl.ds(start, ref.shape[2]), :] = ref[j, which, :, cols]
            count += 1


def deal_out(ref, whole, place_ref, which=0):
    count = 0
    for y in range(ref.shape[0]):
        for half in range(ref.shape[1]):
            for j in range(ref.shape[2]):
                start = pl.multiple_of(place_ref[5 + count], 16)
                ref[y, half, j, which] = whole[pl.ds(start, ref.shape[4]), :]
                count += 1


def bias_kernel(place_ref, table_ref, out_ref):
    block = pl.program_id(0)
    head_base = (place_ref[2] ^ block) * GROUP
    row = lax.broadcasted_iota(jnp.int32, (TILE, TILE), 0)
    col = lax.broadcasted_iota(jnp.int32, (TILE, TILE), 1)
    for h in range(GROUP):
        out_ref[0, h, 0] = jnp.full((TILE, TILE), table_ref[head_base + h, 15], F32)
        out_ref[0, h, 4] = jnp.full((TILE, TILE), table_ref[head_base + h, 31], F32)
    for t in range(1, 4):
        bucket = bucket_of(col - row + (t - 2) * TILE)
        which = {1: range(16), 2: range(32), 3: range(16, 32)}[t]
        for h in range(GROUP):
            tile = jnp.zeros((TILE, TILE), F32)
            for b in which:
                tile = jnp.where(bucket == b, table_ref[head_base + h, b], tile)
            out_ref[0, h, t] = tile


def make_bias(place, table):
    return pl.pallas_call(
        bias_kernel,
        grid=(4,),
        in_specs=[in_smem, in_smem],
        out_specs=pl.BlockSpec((1, GROUP, 5, TILE, TILE), lambda i: (i, 0, 0, 0, 0)),
        out_shape=shape_of((4, GROUP, 5, TILE, TILE), F32),
        compiler_params=params(6),
        cost_estimate=cost(10e6, 4e6),
        name="bias_tiles",
    )(place, table)


def rms_of(v, gain):
    inverse = lax.rsqrt(jnp.mean(v * v, axis=-1, keepdims=True) + norm_eps)
    return v * inverse * gain


def rms_back(v, gain, t):
    inverse = lax.rsqrt(jnp.mean(v * v, axis=-1, keepdims=True) + norm_eps)
    along = jnp.mean(v * gain * t, axis=-1, keepdims=True)
    grad = inverse * gain * t - v * (inverse * inverse * inverse) * along
    return grad, jnp.sum(t * v * inverse, axis=0, keepdims=True)


def project_kernel(indices, place_ref, x_ref, gain_ref, *refs):
    n_parts = len(indices[0])
    w_refs, rest = refs[: 2 * n_parts], refs[2 * n_parts :]
    q_ref, kv_ref = rest[:2]
    whole = rest[-1]
    normed = rms_of(x_ref[...].astype(F32), gain_ref[0:1].astype(F32)).astype(BF)
    if len(rest) == 4:
        rest[2][...] = normed.T
    for b in range(2):
        part = pick(w_refs[b * n_parts : (b + 1) * n_parts], indices[b])
        assemble(whole.at[b], part, place_ref)
        out = dot(normed, whole[b, :, 0:640], NN).astype(BF)
        q_ref[b] = out[:, 0:WIDTH]
        keys, values = out[:, WIDTH : 2 * WIDTH], out[:, 2 * WIDTH : 3 * WIDTH]
        kv_ref[b] = jnp.concatenate([keys, values], 1)


def project(place, rows_in, gain_low, blocks, turned):
    rows = rows_in.shape[0]
    n_parts = len(blocks[0][0])
    shapes = [shape_of((2, rows, WIDTH), BF), shape_of((2, rows, 2 * WIDTH), BF)]
    if turned:
        shapes.append(shape_of((D, rows), BF))
    return pl.pallas_call(
        functools.partial(project_kernel, [i for _, i in blocks]),
        in_specs=[in_smem] + [in_vmem] * (2 + 2 * n_parts),
        out_specs=[in_vmem] * len(shapes),
        out_shape=shapes,
        scratch_shapes=[pltpu.VMEM((2, D, D), BF)],
        compiler_params=params(8),
        cost_estimate=cost(2 * 2 * rows * D * 576, 5e6),
        name="project",
    )(place, rows_in, gain_low, *blocks[0][0], *blocks[1][0])


def tile_places(place_ref):
    x, core = place_ref[0], place_ref[1]
    return [
        4 * (x if t < 2 else 1 - x) + 2 * side + t % 2 for side in (core, 1 - core) for t in range(4)
    ]


def attend_kernel(
    b,
    r_index,
    place_ref,
    q_own_ref,
    q_other_ref,
    kv_own_ref,
    kv_other_ref,
    bias_ref,
    own_ref,
    send_ref,
    p_out,
    p_ref,
    sems,
):
    half = q_own_ref.shape[1]
    rows = 2 * half
    step = 256
    lane = lax.broadcasted_iota(jnp.int32, (1, 256), 1)
    key = lax.broadcasted_iota(jnp.int32, (1, TILE), 1)
    sub = lax.broadcasted_iota(jnp.int32, (64, 1), 0)
    tiles_at = tile_places(place_ref)
    length = place_ref[3 + place_ref[0]]
    hide = jnp.concatenate([jnp.where(key + TILE * g < length, 0.0, -1e30) for g in tiles_at], 1)
    extra = jnp.where(sub == 0, hide, 0.0).astype(BF)
    both = jnp.concatenate([kv_own_ref[b], kv_other_ref[b]], 0)
    keys_t = jnp.concatenate([both[:, :WIDTH].T, extra], 0)
    values = both[:, WIDTH:]
    queries = jnp.concatenate([q_own_ref[b], q_other_ref[b]], 0)
    queries = jnp.concatenate([queries, jnp.ones((rows, 64), BF)], 1)
    total = [jnp.zeros((step, WIDTH), F32) for _ in range(rows // step)]
    for h in range(GROUP):
        inside = (lane >= h * DH) & (lane < (h + 1) * DH)
        used = inside | (lane == WIDTH)
        for r in range(rows // step):
            here = jnp.where(used, queries[r * step : (r + 1) * step], jnp.zeros((), BF))
            scores = dot(here, keys_t, NN)
            tiles = []
            for c in range(8):
                bias = []
                for u in range(step // TILE):
                    which = jnp.clip(tiles_at[c] - tiles_at[r * (step // TILE) + u] + 2, 0, 4)
                    bias.append(bias_ref[r_index, h, which])
                tiles.append(scores[:, c * TILE : (c + 1) * TILE] + jnp.concatenate(bias, 0))
            top = jnp.max(functools.reduce(jnp.maximum, tiles), axis=-1, keepdims=True)
            exps = [jnp.exp(t - top) for t in tiles]
            norm = jnp.sum(functools.reduce(jnp.add, exps), axis=-1, keepdims=True)
            scale = 1.0 / norm
            prob = jnp.concatenate([(e * scale).astype(BF) for e in exps], 1)
            p_ref[h, pl.ds(r * step, step), :] = prob
            total[r] = jnp.where(inside[:, :WIDTH], dot(prob, values, NN), total[r])
        pltpu.make_async_copy(p_ref.at[h], p_out.at[h], sems.at[h]).start()
    blank = jnp.zeros((step, 64), BF)
    for r in range(rows // step):
        out = jnp.concatenate([blank, total[r].astype(BF)], 1)
        at = r * step
        if at < half:
            own_ref[pl.ds(at, step), :] = out
        else:
            send_ref[pl.ds(at - half, step), :] = out
    for h in range(GROUP):
        pltpu.make_async_copy(p_ref.at[h], p_out.at[h], sems.at[h]).wait()


def attend(place, q, kv, bias, r):
    half = q[0].shape[1]
    rows = 2 * half
    return pl.pallas_call(
        functools.partial(attend_kernel, r // 2, r),
        in_specs=[in_smem] + [in_vmem] * 5,
        out_specs=[in_vmem, in_vmem, in_hbm],
        out_shape=[shape_of((half, 256), BF)] * 2 + [pltpu.HBM((GROUP, rows, rows), BF)],
        scratch_shapes=[
            pltpu.VMEM((GROUP, rows, rows), BF),
            pltpu.SemaphoreType.DMA((GROUP,)),
        ],
        compiler_params=params(18),
        cost_estimate=cost(1, 1),
        name="attend",
    )(place, *q, *kv, bias)


def middle_kernel(indices, place_ref, x_ref, gain_ref, *refs):
    n_parts = len(indices[0])
    ctx_refs, w_refs = refs[:4], refs[4 : 4 + 4 * n_parts]
    mid_ref, normed_ref, normed_t_ref, whole = refs[4 + 4 * n_parts :]
    total = x_ref[...].astype(F32)
    for b in range(4):
        part = pick(w_refs[b * n_parts : (b + 1) * n_parts], indices[b])
        assemble(whole.at[b], part, place_ref, 0, slice(512, 768))
        total = total + dot(ctx_refs[b][...], whole[b], NT)
    mid_ref[...] = total
    normed = rms_of(total, gain_ref[1:2].astype(F32)).astype(BF)
    normed_ref[...] = normed
    normed_t_ref[...] = normed.T


def middle(place, rows_in, gain_low, ctx, blocks):
    rows = rows_in.shape[0]
    n_parts = len(blocks[0][0])
    return pl.pallas_call(
        functools.partial(middle_kernel, [i for _, i in blocks]),
        in_specs=[in_smem] + [in_vmem] * (6 + 4 * n_parts),
        out_specs=[in_vmem] * 3,
        out_shape=[
            shape_of((rows, D), F32),
            shape_of((rows, D), BF),
            shape_of((D, rows), BF),
        ],
        scratch_shapes=[pltpu.VMEM((4, D, 256), BF)],
        compiler_params=params(10),
        cost_estimate=cost(2 * rows * D * D, 8e6),
        name="middle",
    )(place, rows_in, gain_low, *ctx, *[p for b, _ in blocks for p in b])


def feed_kernel(indices, first, split, place_ref, *refs):
    n_refs, nt_refs, g_refs, gt_refs = [refs[2 * i : 2 * i + 2] for i in range(4)]
    refs = refs[8:]
    if not first:
        acc_ins, t_ins, refs = refs[0:2], refs[2:4], refs[4:]
    n_parts = len(indices)
    w_refs, refs = pick(refs[:n_parts], indices), refs[n_parts:]
    acc_refs, t_refs, out_refs = refs[0:2], refs[2:4], refs[4:-6]
    wi, wf, gi, gf, active, pre_grad = refs[-6:]
    assemble(wi, w_refs, place_ref, 0, ring=True)
    assemble(wf, w_refs, place_ref, 1, ring=True)
    half = n_refs[0].shape[0]
    for i in range(2):
        rows = pl.ds(i * half, half)
        pre = dot(n_refs[i][...], wi[...], NN)
        grad = dot(g_refs[i][...], wf[...], NN)
        cdf = 0.5 * (1.0 + lax.erf(pre * 0.7071067811865476))
        density = jnp.exp(pre * pre * -0.5) * 0.3989422804014327
        act_here = (pre * cdf).astype(BF)
        grad_here = (grad * (cdf + pre * density)).astype(BF)
        active[rows, :] = act_here
        pre_grad[rows, :] = grad_here
        acc, t = dot(act_here, wf[...], NT), dot(grad_here, wi[...], NT)
        if not first:
            acc, t = acc_ins[i][...] + acc, t_ins[i][...] + t
        acc_refs[i][...] = acc.astype(acc_refs[i].dtype)
        t_refs[i][...] = t.astype(t_refs[i].dtype)
    for w, (out, turned, value) in enumerate(((gi, nt_refs, pre_grad), (gf, gt_refs, active))):
        parts = [dot(turned[i][...], value[pl.ds(i * half, half), :], NN) for i in range(2)]
        out[...] = (parts[0] + parts[1]).astype(BF)
        if split:
            near_ref, far_refs = out_refs[0], out_refs[1:3]
            cut = near_ref.shape[1]
            for count in range(4 * cut):
                y, z = count // (2 * cut), count % (2 * cut)
                start = pl.multiple_of(place_ref[5 + count], 16)
                piece = out[pl.ds(start, near_ref.shape[3]), :]
                if z < cut:
                    near_ref[y, z, w] = piece
                else:
                    far_refs[y][z - cut, w] = piece
        else:
            out_refs[0][0, 0, 0, w] = out[...]


def feed(place, normed, normed_t, back, back_t, sums, block, depth, shard_rows):
    block, indices = block
    rows = normed[0].shape[0]
    n = len(block)
    first = sums is None
    split = shard_rows % 16 == 0
    if split:
        part = (depth // 2, 2, shard_rows, D)
        shapes = [shape_of((2,) + part, BF)] + [shape_of(part, BF)] * 2
    else:
        shapes = [grads_shape(depth, 2, shard_rows, D)]
    sent = F32 if first else BF
    outs = pl.pallas_call(
        functools.partial(feed_kernel, indices, first, split),
        in_specs=[in_smem] + [in_vmem] * (8 + n + (0 if first else 4)),
        out_specs=[in_vmem] * (4 + len(shapes)),
        out_shape=[shape_of((rows, D), t) for t in (F32, sent, F32, sent)] + shapes,
        scratch_shapes=[pltpu.VMEM((D, D), BF)] * 4 + [pltpu.VMEM((2 * rows, D), BF)] * 2,
        compiler_params=params(FEED_MIB),
        cost_estimate=cost(1, 1),
        name="feed",
    )(place, *normed, *normed_t, *back, *back_t, *(sums or ()), *block)
    if split:
        return outs[:4], outs[4:]
    whole = by_place(outs[4], depth, shard_rows)
    return outs[:4], [whole[:, 0], whole[0, 1], whole[1, 1]]


def turn_kernel(mid_ref, t_ref, t_came_ref, back_ref, gain_ref, grad_ref, low_ref, gain_grad_ref):
    t = t_ref[...] + t_came_ref[...].astype(F32)
    grad, gain_grad = rms_back(mid_ref[...], gain_ref[1:2].astype(F32), t)
    gain_grad_ref[...] = gain_grad
    grad = back_ref[...].astype(F32) + grad
    grad_ref[...] = grad
    low_ref[...] = grad.astype(BF)


def turn(mid, t_own, t_came, back, gain_low):
    return pl.pallas_call(
        turn_kernel,
        in_specs=[in_vmem] * 5,
        out_specs=[in_vmem] * 3,
        out_shape=[shape_of(mid.shape, F32), shape_of(mid.shape, BF), shape_of((1, D), F32)],
        compiler_params=params(12),
        cost_estimate=cost(1, 1),
        name="turn",
    )(mid, t_own, t_came, back, gain_low)


def context_grad_kernel(indices, place_ref, own_ref, other_ref, *refs):
    n_parts = len(indices[0])
    w_refs, (g0_ref, g1_ref, low_t_ref, whole) = refs[: 2 * n_parts], refs[2 * n_parts :]
    half = own_ref.shape[0]
    for i, ref in enumerate((own_ref, other_ref)):
        low_t_ref[:, pl.ds(i * half, half)] = ref[...].T
    for b, g_ref in enumerate((g0_ref, g1_ref)):
        part = pick(w_refs[b * n_parts : (b + 1) * n_parts], indices[b])
        assemble(whole.at[b], part, place_ref, 0, slice(512, 768))
        for i, ref in enumerate((own_ref, other_ref)):
            g_ref[pl.ds(i * half, half), :] = dot(ref[...], whole[b], NN).astype(BF)[:, 64:]


def context_grads(place, low_own, low_other, blocks):
    half = low_own.shape[0]
    n_parts = len(blocks[0][0])
    return pl.pallas_call(
        functools.partial(context_grad_kernel, [i for _, i in blocks]),
        in_specs=[in_smem] + [in_vmem] * (2 + 2 * n_parts),
        out_specs=[in_vmem] * 3,
        out_shape=[shape_of((2 * half, WIDTH), BF)] * 2 + [shape_of((D, 2 * half), BF)],
        scratch_shapes=[pltpu.VMEM((2, D, 256), BF)],
        compiler_params=params(12),
        cost_estimate=cost(1, 1),
        name="context_grads",
    )(place, low_own, low_other, *blocks[0][0], *blocks[1][0])


def attend_back_kernel(
    b,
    place_ref,
    q_own_ref,
    q_other_ref,
    kv_own_ref,
    kv_other_ref,
    g_ref,
    ctx_own_ref,
    ctx_other_ref,
    p_in,
    heads_ref,
    bucket_ref,
    ds_ref,
    sums_ref,
    p_ref,
    sems,
):
    copies = [pltpu.make_async_copy(p_in.at[h], p_ref.at[h], sems.at[h]) for h in range(GROUP)]
    for c in copies:
        c.start()
    rows = g_ref.shape[0]
    step = 128
    lane = lax.broadcasted_iota(jnp.int32, (1, WIDTH), 1)
    tiles_at = tile_places(place_ref)
    grads = g_ref[...]
    both = jnp.concatenate([kv_own_ref[b], kv_other_ref[b]], 0)
    keys = both[:, :WIDTH]
    values_t = both[:, WIDTH:].T
    queries_t = jnp.concatenate([q_own_ref[b].T, q_other_ref[b].T], 1)
    grads_t = grads.T
    context = jnp.concatenate([ctx_own_ref[...], ctx_other_ref[...]], 0)[:, 64:]
    product = grads.astype(F32) * context.astype(F32)
    sums_ref[...] = jnp.zeros_like(sums_ref)
    total = [jnp.zeros((step, WIDTH), F32) for _ in range(rows // step)]
    key_grads, value_grads = [], []
    for h in range(GROUP):
        copies[h].wait()
        inside = (lane >= h * DH) & (lane < (h + 1) * DH)
        for r in range(rows // step):
            span = slice(r * step, (r + 1) * step)
            here = jnp.where(inside, grads[span], jnp.zeros((), BF))
            prob_grad = dot(here, values_t, NN)
            row_dot = jnp.sum(jnp.where(inside, product[span], 0.0), axis=-1, keepdims=True)
            lows = []
            for c in range(8):
                prob = p_ref[h, pl.ds(r * step, step), pl.ds(c * TILE, TILE)].astype(F32)
                dscore = prob * (prob_grad[:, c * TILE : (c + 1) * TILE] - row_dot)
                which = jnp.clip(tiles_at[c] - tiles_at[r] + 2, 0, 4)
                sums_ref[h, which] += dscore
                lows.append(dscore.astype(BF))
            low = jnp.concatenate(lows, 1)
            ds_ref[h, pl.ds(r * step, step), :] = low
            total[r] = jnp.where(inside, dot(low, keys, NN), total[r])
        key_grads.append(dot(queries_t[h * DH : (h + 1) * DH], ds_ref[h], NN))
        value_grads.append(dot(grads_t[h * DH : (h + 1) * DH], p_ref[h], NN))
    query_grad = jnp.concatenate([t.astype(BF) for t in total], 0)
    others = jnp.concatenate(key_grads + value_grads, 0).T.astype(BF)
    heads_ref[...] = jnp.concatenate([query_grad, others], 1)
    row = lax.broadcasted_iota(jnp.int32, (TILE, TILE), 0)
    col = lax.broadcasted_iota(jnp.int32, (TILE, TILE), 1)
    buckets = {t: bucket_of(col - row + (t - 2) * TILE) for t in range(1, 4)}
    for b in range(NB):
        masks = {t: buckets[t] == b for t in ((1, 2) if b < 16 else (2, 3))}
        for h in range(GROUP):
            tile = jnp.zeros((TILE, TILE), F32)
            if b % 16 == 15:
                tile = sums_ref[h, 0 if b == 15 else 4]
            for t, mask in masks.items():
                tile = tile + jnp.where(mask, sums_ref[h, t], 0.0)
            bucket_ref[h, pl.ds(b, 1), :] = jnp.sum(tile, axis=0, keepdims=True)


def attend_back(place, q, kv, grads, ctx, prob, r):
    rows = grads.shape[0]
    return pl.pallas_call(
        functools.partial(attend_back_kernel, r // 2),
        in_specs=[in_smem] + [in_vmem] * 7 + [in_hbm],
        out_specs=[in_vmem] * 2,
        out_shape=[shape_of((rows, 3 * WIDTH), BF), shape_of((GROUP, NB, TILE), F32)],
        scratch_shapes=[
            pltpu.VMEM((GROUP, rows, rows), BF),
            pltpu.VMEM((GROUP, 5, TILE, TILE), F32),
            pltpu.VMEM((GROUP, rows, rows), BF),
            pltpu.SemaphoreType.DMA((GROUP,)),
        ],
        compiler_params=params(24),
        cost_estimate=cost(1, 1),
        name="attend_back",
    )(place, *q, *kv, grads, *ctx, keep_hbm(prob))


def project_back_kernel(indices, split, place_ref, nt_own_ref, nt_other_ref, low_t_ref, *refs):
    n_parts = len(indices[0])
    heads_refs, ctx_refs, refs = refs[:2], refs[2:6], refs[6:]
    w_refs, refs = refs[: 2 * n_parts], refs[2 * n_parts :]
    own_ref, send_ref, out_refs, (whole, grad) = refs[0], refs[1], refs[2:-2], refs[-2:]
    half = nt_own_ref.shape[1]
    totals = [None, None]
    for b in range(2):
        part = pick(w_refs[b * n_parts : (b + 1) * n_parts], indices[b])
        assemble(whole.at[b], part, place_ref)
        ends = [heads_refs[b][pl.ds(i * half, half), :] for i in range(2)]
        out = dot(nt_own_ref[...], ends[0], NN) + dot(nt_other_ref[...], ends[1], NN)
        context = jnp.concatenate([ctx_refs[2 * b][...], ctx_refs[2 * b + 1][...]], 0)
        last = dot(low_t_ref[...], context, NN)[:, 64:]
        grad[b] = jnp.concatenate([out.astype(BF), last.astype(BF)], 1)
        if split:
            near_ref, far_refs = out_refs[b], out_refs[2:4]
            cut = near_ref.shape[1]
            for count in range(4 * cut):
                y, z = count // (2 * cut), count % (2 * cut)
                start = pl.multiple_of(place_ref[5 + count], 16)
                piece = grad[b, pl.ds(start, near_ref.shape[3]), :]
                if z < cut:
                    near_ref[y, z, 0] = piece
                else:
                    far_refs[y][b, z - cut, 0] = piece
        else:
            out_refs[b][0, 0, 0, 0] = grad[b]
        for i in range(2):
            term = dot(ends[i], whole[b, :, 0:576], NT)
            totals[i] = term if b == 0 else totals[i] + term
    own_ref[...], send_ref[...] = totals[0], totals[1].astype(BF)


def project_back(place, normed_t, low_t, heads, ctx, blocks, depth, shard_rows):
    half = normed_t[0].shape[1]
    n = len(blocks[0][0])
    split = shard_rows % 16 == 0
    if split:
        shapes = [shape_of((2, depth // 2, 1, shard_rows, D), BF)] * 4
    else:
        shapes = [grads_shape(depth, 1, shard_rows, D)] * 2
    outs = pl.pallas_call(
        functools.partial(project_back_kernel, [i for _, i in blocks], split),
        in_specs=[in_smem] + [in_vmem] * (9 + 2 * n),
        out_specs=[in_vmem] * (2 + len(shapes)),
        out_shape=[shape_of((half, D), F32), shape_of((half, D), BF)] + shapes,
        scratch_shapes=[pltpu.VMEM((2, D, D), BF)] * 2,
        compiler_params=params(16),
        cost_estimate=cost(1, 1),
        name="project_back",
    )(place, *normed_t, low_t, *heads, *ctx, *blocks[0][0], *blocks[1][0])
    if split:
        return outs
    both = [by_place(v, depth, shard_rows) for v in outs[2:]]
    fars = [jnp.stack([v[y, 1] for v in both]) for y in range(2)]
    return [*outs[:2], both[0][:, 0], both[1][:, 0], *fars]


def add(a, b):
    return (a.astype(F32) + b.astype(F32)).astype(BF)


def merge_half_kernel(n, near_ref, near_came_ref, *refs):
    far_refs, far_came_refs, (y0_ref, y1_ref, x0_ref, x1_ref) = refs[:n], refs[n : 2 * n], refs[2 * n :]
    y0_ref[...] = add(near_ref[0], near_came_ref[0])
    y1_ref[...] = add(near_ref[1], near_came_ref[1])
    for i, out_ref in enumerate((x0_ref, x1_ref)):
        if n == 1:
            out_ref[...] = add(far_refs[0][i], far_came_refs[0][i])
        else:
            out_ref[...] = add(far_refs[i][...], far_came_refs[i][...])


def merge_half(near, near_came, far, far_came):
    part = shape_of(near.shape[1:], BF)
    n = len(far)
    return pl.pallas_call(
        functools.partial(merge_half_kernel, n),
        in_specs=[in_vmem] * (2 + 2 * n),
        out_specs=[in_vmem] * 4,
        out_shape=[part] * 4,
        compiler_params=params(MERGE_MIB),
        cost_estimate=cost(1, 1),
        name="merge_half",
    )(near, near_came, *far, *far_came)


def merge_last_kernel(near_ref, near_came_ref, far_ref, far_came_ref, own_ref, *outs):
    cut = near_ref.shape[0]
    own_ref[...] = near_ref[0].astype(F32) + near_came_ref[0].astype(F32)
    for k, out_ref in enumerate(outs, 1):
        a_ref, b_ref = (near_ref, near_came_ref) if k < cut else (far_ref, far_came_ref)
        out_ref[...] = add(a_ref[k % cut], b_ref[k % cut])


def merge_last(near, near_came, far, far_came):
    cut = near.shape[0]
    part = near.shape[1:]
    return pl.pallas_call(
        merge_last_kernel,
        in_specs=[in_vmem] * 4,
        out_specs=[in_vmem] * (2 * cut),
        out_shape=[shape_of(part, F32)] + [shape_of(part, BF)] * (2 * cut - 1),
        compiler_params=params(MERGE_MIB),
        cost_estimate=cost(1, 1),
        name="merge_last",
    )(near, near_came, far, far_came)


def total_kernel(own_ref, *refs):
    out_ref, squares_ref = refs[-2:]
    total = own_ref[...]
    for ref in refs[:-2]:
        total = total + ref[...].astype(F32)
    out_ref[...] = total
    squares_ref[...] = jnp.broadcast_to(jnp.sum(total * total), squares_ref.shape)


def total_of(own, came):
    return pl.pallas_call(
        total_kernel,
        in_specs=[in_vmem] * (1 + len(came)),
        out_specs=[in_vmem] * 2,
        out_shape=[shape_of(own.shape, F32), shape_of((1, TILE), F32)],
        compiler_params=params(MERGE_MIB),
        cost_estimate=cost(1, 1),
        name="total",
    )(own, *came)


def cast_attn_kernel(w_ref, out_ref):
    out_ref[0] = jnp.concatenate([w_ref[i].astype(BF) for i in range(4)], 1)


def cast_attn(weights):
    rows = weights.shape[1]
    return pl.pallas_call(
        cast_attn_kernel,
        in_specs=[in_vmem],
        out_specs=in_vmem,
        out_shape=shape_of((1, rows, D), BF),
        compiler_params=params(MERGE_MIB),
        cost_estimate=cost(1, 1),
        name="cast_attn",
    )(weights)


def sort_kernel(place_ref, in_ref, back_ref, send, sems):
    there = 1 - place_ref[0]
    copies = [
        pltpu.make_async_copy(ref.at[there], send.at[i], sems.at[i])
        for i, ref in enumerate((in_ref, back_ref))
    ]
    for c in copies:
        c.start()
    for c in copies:
        c.wait()


def sort_rows(place, inputs, cotangent):
    return pl.pallas_call(
        sort_kernel,
        in_specs=[in_smem] + [in_hbm] * 2,
        out_specs=in_vmem,
        out_shape=shape_of(inputs.shape, BF),
        scratch_shapes=[pltpu.SemaphoreType.DMA((2,))],
        compiler_params=params(MERGE_MIB),
        cost_estimate=cost(1, 1),
        name="sort_rows",
    )(place, keep_hbm(inputs), keep_hbm(cotangent))


def join_rows_kernel(place_ref, keep_in_ref, keep_back_ref, came_ref, in_ref, back_ref, back_t_ref, sems):
    here = place_ref[0]
    half = came_ref.shape[1]
    pairs = ((keep_in_ref, in_ref), (keep_back_ref, back_ref))
    copies = [
        pltpu.make_async_copy(keep_ref.at[here], ref.at[pl.ds(0, half), :], sems.at[i])
        for i, (keep_ref, ref) in enumerate(pairs)
    ]
    for c in copies:
        c.start()
    for i, (_, ref) in enumerate(pairs):
        ref[pl.ds(half, half), :] = came_ref[i]
    for c in copies:
        c.wait()
    back_t_ref[...] = back_ref[...].T


def join_rows(place, inputs, cotangent, came):
    rows = shape_of((2 * came.shape[1], came.shape[2]), BF)
    return pl.pallas_call(
        join_rows_kernel,
        in_specs=[in_smem] + [in_hbm] * 2 + [in_vmem],
        out_specs=[in_vmem] * 3,
        out_shape=[rows] * 2 + [shape_of((rows.shape[1], rows.shape[0]), BF)],
        scratch_shapes=[pltpu.SemaphoreType.DMA((2,))],
        compiler_params=params(MERGE_MIB),
        cost_estimate=cost(1, 1),
        name="join_rows",
    )(place, keep_hbm(inputs), keep_hbm(cotangent), came)


def join_gains_kernel(g_ref, out_ref):
    out_ref[...] = jnp.concatenate([g_ref[i] for i in range(g_ref.shape[0])], 1)


def join_gains(parts):
    return pl.pallas_call(
        join_gains_kernel,
        in_specs=[in_vmem],
        out_specs=in_vmem,
        out_shape=shape_of((2, D), parts.dtype),
        compiler_params=params(MERGE_MIB),
        cost_estimate=cost(1, 1),
        name="join_gains",
    )(parts)


def cast_ffn_kernel(w_ref, out_ref):
    out_ref[...] = w_ref[...].astype(BF)


def cast_ffn(weights):
    return pl.pallas_call(
        cast_ffn_kernel,
        in_specs=[in_vmem],
        out_specs=in_vmem,
        out_shape=shape_of(weights.shape, BF),
        compiler_params=params(MERGE_MIB),
        cost_estimate=cost(1, 1),
        name="cast_ffn",
    )(weights)


def line_up_kernel(cut, *refs):
    refs, out_ref = refs[:-1], refs[-1]
    per = len(refs) // cut
    for j in range(cut):
        for i in range(per):
            if per == 1:
                out_ref[j] = refs[j][...]
            else:
                out_ref[j, i] = refs[j * per + i][0]


def line_up(parts, cut):
    per = len(parts) // cut
    inner = parts[0].shape if per == 1 else (per,) + parts[0].shape[1:]
    return pl.pallas_call(
        functools.partial(line_up_kernel, cut),
        in_specs=[in_vmem] * len(parts),
        out_specs=in_vmem,
        out_shape=shape_of((cut,) + inner, BF),
        compiler_params=params(MERGE_MIB),
        cost_estimate=cost(1, 1),
        name="line_up",
    )(*parts)


def place_rows_kernel(place_ref, a_ref, b_ref, came_ref, out_a_ref, out_b_ref):
    here = place_ref[0]
    for i, (keep_ref, out_ref) in enumerate(((a_ref, out_a_ref), (b_ref, out_b_ref))):
        out_ref[here] = keep_ref[...]
        out_ref[1 - here] = came_ref[i]


def place_rows(place, keep, came):
    return pl.pallas_call(
        place_rows_kernel,
        in_specs=[in_smem] + [in_vmem] * 3,
        out_specs=[in_vmem] * 2,
        out_shape=[shape_of(came.shape, BF)] * 2,
        compiler_params=params(MERGE_MIB),
        cost_estimate=cost(1, 1),
        name="place_rows",
    )(place, *keep, came)


def finish_kernel(
    x_ref,
    gain_ref,
    t_ref,
    t_came_ref,
    mid_grad_ref,
    mid_ref,
    acc_ref,
    acc_came_ref,
    out_keep_ref,
    in_keep_ref,
    send_ref,
    gain_grad_ref,
):
    t = t_ref[...] + t_came_ref[...].astype(F32)
    grad, gain_grad = rms_back(x_ref[...].astype(F32), gain_ref[0:1].astype(F32), t)
    gain_grad_ref[...] = gain_grad
    out = (mid_ref[...] + (acc_ref[...] + acc_came_ref[...].astype(F32))).astype(BF)
    grad = (mid_grad_ref[...] + grad).astype(BF)
    half = out_keep_ref.shape[0]
    out_keep_ref[...], in_keep_ref[...] = out[:half], grad[:half]
    send_ref[0], send_ref[1] = out[half:], grad[half:]


def finish(rows_in, gain_low, t_own, t_came, mid_grad, mid, acc_own, acc_came):
    part = (rows_in.shape[0] // 2, D)
    return pl.pallas_call(
        finish_kernel,
        in_specs=[in_vmem] * 8,
        out_specs=[in_vmem] * 4,
        out_shape=[shape_of(part, BF)] * 2 + [shape_of((2,) + part, BF), shape_of((1, D), F32)],
        compiler_params=params(14),
        cost_estimate=cost(1, 1),
        name="finish",
    )(rows_in, gain_low, t_own, t_came, mid_grad, mid, acc_own, acc_came)


def small_kernel(place_ref, one_ref, two_ref, *refs):
    out_ref = refs[-1]
    out_ref[15:16] = jnp.zeros((1, TILE), F32)
    for i in range(D // TILE):
        out_ref[i : i + 1] = one_ref[:, i * TILE : (i + 1) * TILE]
        out_ref[6 + i : 7 + i] = two_ref[:, i * TILE : (i + 1) * TILE]
    heads = []
    for m in range(4):
        for h in range(GROUP):
            lines = jnp.zeros((NB, TILE), F32)
            for r in (0, 2):
                lines = jnp.where((place_ref[2] ^ r) == m, refs[r // 2][h], lines)
            heads.append(jnp.sum(lines.T, axis=0, keepdims=True))
    for i in range(3):
        out_ref[12 + i : 13 + i] = jnp.concatenate(heads[4 * i : 4 * i + 4], 1)


def small_sums(place, gain_one, gain_two, lines):
    return pl.pallas_call(
        small_kernel,
        in_specs=[in_smem] + [in_vmem] * 4,
        out_specs=in_vmem,
        out_shape=shape_of((16, TILE), F32),
        compiler_params=params(MERGE_MIB),
        cost_estimate=cost(1, 1),
        name="small_sums",
    )(place, gain_one, gain_two, *lines)


def total_with_kernel(own_ref, *refs):
    squares_ref, small_ref, out_ref, sums_ref = refs[-4:]
    total = own_ref[...]
    for ref in refs[:-4]:
        total = total + ref[...].astype(F32)
    out_ref[...] = total
    sums_ref[0:15] = small_ref[0:15]
    sums_ref[15:16] = squares_ref[...] + jnp.sum(total * total)


def total_with(own, came, squares, small):
    return pl.pallas_call(
        total_with_kernel,
        in_specs=[in_vmem] * (3 + len(came)),
        out_specs=[in_vmem] * 2,
        out_shape=[shape_of(own.shape, F32), shape_of(small.shape, F32)],
        compiler_params=params(MERGE_MIB),
        cost_estimate=cost(1, 1),
        name="total_with",
    )(own, *came, squares, small)


def update_kernel(place_ref, small_ref, attn_ref, ffn_ref, *refs):
    sources, outs, olds, sems = refs[:12], refs[12:28], refs[28:40], refs[40]
    copies = [pltpu.make_async_copy(sources[i], olds[i], sems.at[i]) for i in range(12)]
    for c in copies:
        c.start()
    small = jnp.sum(small_ref[...], axis=0)
    sums = small[0:15]
    squares = jnp.sum(jnp.sum(sums * sums, axis=0, keepdims=True), axis=1, keepdims=True)
    norm = jnp.sqrt(small[15:16, 0:1] + squares)
    outs[0][...] = norm
    clip = jnp.minimum(1.0, clip_level / (norm + 1e-06))
    count = outs[2].shape[1]
    wide = jnp.concatenate(
        [jnp.concatenate([small[g + i : g + i + 1] for i in range(6)], 1) for g in (0, 6)], 0
    )
    gains = jnp.zeros((2, count), F32)
    for d in range(D // count):
        gains = jnp.where(place_ref[0] == d, wide[:, d * count : (d + 1) * count], gains)
    heads = [(12 + h // 4, h % 4 * NB) for h in range(H)]
    table = jnp.concatenate([small[i : i + 1, j : j + NB] for i, j in heads], 0)
    outs[2][...], outs[3][...] = gains, table
    grads = (None, ffn_ref[...], gains, table)
    settings = [(rate_matrix, matrix_decay)] * 2 + [(rate_small, 0.0)] * 2
    for kind in (2, 3, 1, 0):
        old, new = olds[3 * kind : 3 * kind + 3], outs[4 + 3 * kind : 7 + 3 * kind]
        for c in copies[3 * kind : 3 * kind + 3]:
            c.wait()
        if kind == 0:
            for i in range(4):
                gradient = attn_ref[0, :, i * WIDTH : (i + 1) * WIDTH]
                outs[1][i] = gradient
                values = adam_step(
                    old[0][i], old[1][i], old[2][i], gradient * clip, *settings[kind]
                )
                new[0][i], new[1][i], new[2][i] = values
        else:
            values = adam_step(
                old[0][...], old[1][...], old[2][...], grads[kind] * clip, *settings[kind]
            )
            new[0][...], new[1][...], new[2][...] = values


def update(dp_index, small, attn_total, ffn_total, olds):
    gradients = [shape_of(olds[i].shape, F32) for i in (0, 6, 9)]
    shapes = [shape_of((1, 1), F32)] + gradients + [shape_of(v.shape, F32) for v in olds]
    return pl.pallas_call(
        update_kernel,
        in_specs=[in_smem] + [in_vmem] * 3 + [in_hbm] * 12,
        out_specs=[in_vmem] * 16,
        out_shape=shapes,
        scratch_shapes=[pltpu.VMEM(v.shape, F32) for v in olds] + [pltpu.SemaphoreType.DMA((12,))],
        compiler_params=params(20),
        cost_estimate=cost(1, 1),
        name="update",
    )(dp_index, small, attn_total, ffn_total, *[keep_hbm(v) for v in olds])


def per_device(
    inputs,
    cotangent,
    lengths,
    attn_weights,
    attn_first,
    attn_second,
    ffn_weights,
    ffn_first,
    ffn_second,
    norm_gains,
    gain_first,
    gain_second,
    bias_table,
    table_first,
    table_second,
):
    assert lax.axis_size("mp") == 4 and inputs.shape[0] == 2
    depth = lax.axis_size("dp") // 2
    shard_rows = ffn_weights.shape[1]
    mp, dp = lax.axis_index("mp"), lax.axis_index("dp")
    x, core = mp // 2, mp % 2

    starts = [
        shard_rows * (((dp // 2) ^ s) * 2 + ((dp % 2) ^ y)) for y in range(2) for s in range(depth)
    ]
    starts += [
        shard_rows * (((dp // 2 - s) % depth) * 2 + ((dp % 2) ^ y))
        for y in range(2)
        for s in range(depth)
    ]
    if shard_rows % 16:
        starts = [jnp.zeros((), jnp.int32)] * 2
    place = jnp.stack([v.astype(jnp.int32) for v in [x, core, mp, lengths[0], lengths[1]] + starts])
    cut = depth // 2

    attn_low = cast_attn(attn_weights)
    attn_z = [swap_z(attn_low, k) for k in range(1, depth)]
    rows_came = swap_x(sort_rows(place, inputs, cotangent))
    ffn_low = cast_ffn(ffn_weights)
    bias = make_bias(place, bias_table)
    attn_low, attn_z, ffn_low, place, bias = fence(attn_low, attn_z, ffn_low, place, bias)

    lined = [attn_low] + attn_z
    near, far = line_up(lined[:cut], cut), line_up(lined[cut:], cut)
    near_x, far_y = swap_x(near), swap_y(far)
    ring = [ffn_low, shift_z(ffn_low)]
    near, far, near_x, far_y, rows_came, ring = fence(near, far, near_x, far_y, rows_came, ring)
    near, far = line_up([near, near_x], 2), line_up([far, far_y], 2)
    near_y, far_x = swap_y(near), swap_x(far)
    ring.append(shift_z(ring[-1]))
    rows_in, back, back_t = join_rows(place, inputs, cotangent, rows_came)
    rows_in, back, back_t, gain_low, ring, near, far = fence(
        rows_in, back, back_t, norm_gains, ring, near, far
    )
    while len(ring) < depth:
        ring.append(shift_z(ring[-1]))
    gains = join_gains(gather_gains(gain_low))
    near_y, far_x, near, far, rows_in, back, back_t, gains, ring = fence(
        near_y, far_x, near, far, rows_in, back, back_t, gains, ring
    )

    def attn_block(near, far, near_y, far_x, i):
        here = far if i == 0 else far_x
        return block_views([[(near, i), (here, 0)], [(near_y, i), (here, 1)]])

    mine = [attn_block(near, far, near_y, far_x, i) for i in range(2)]
    rows_other = swap_core(rows_in)
    ffn_here = line_up([line_up(ring[:cut], cut), line_up(ring[cut:], cut)], 2)
    ffn_x, ffn_y = swap_x(ffn_here), swap_y(ffn_here)
    q_own, kv_own, normed_t = project(place, rows_in, gains, mine, True)
    q_own, kv_own, normed_t, ffn_here = fence(q_own, kv_own, normed_t, ffn_here)
    q_own, rows_other = fence(q_own, rows_other)
    q_other, kv_other, other_t = project(place, rows_other, gains, mine, True)
    q, kv, normed_t, near, far, near_y, far_x, back, back_t = fence(
        [q_own, q_other],
        [kv_own, kv_other],
        [normed_t, other_t],
        near,
        far,
        near_y,
        far_x,
        back,
        back_t,
    )
    across = [swap_core(v) for v in (near, far, near_y, far_x)]
    ctx, ctx_send, ctx_came, prob = {}, {}, {}, {}
    for r in (0, 2):
        ctx[r], ctx_send[r], prob[r] = attend(place, q, kv, bias, r)
        ctx, ctx_send, prob, q, ffn_here = fence(ctx, ctx_send, prob, q, ffn_here)
        ctx_came[r] = swap_core(ctx_send[r])
    back_other, back_other_t = swap_core(back), swap_core(back_t)
    ctx, ctx_came, across = fence(ctx, ctx_came, across)
    theirs = [attn_block(*across, i) for i in range(2)]
    mid, normed_two, normed_two_t = middle(
        place,
        rows_in,
        gains,
        [ctx[0], ctx_came[0], ctx[2], ctx_came[2]],
        [mine[0], theirs[0], mine[1], theirs[1]],
    )
    mid, normed_two, normed_two_t = fence(mid, normed_two, normed_two_t)
    two_other, two_other_t = swap_core(normed_two), swap_core(normed_two_t)
    mid, ffn_x, ffn_y = fence(mid, ffn_x, ffn_y)
    ffn_near_xy, ffn_far_xy = swap_y(ffn_x[0]), swap_x(ffn_y[1])
    mid, two_other, two_other_t, back_other, back_other_t = fence(
        mid, two_other, two_other_t, back_other, back_other_t
    )

    def feed_at(sums, by_y):
        return feed(
            place,
            (normed_two, two_other),
            (normed_two_t, two_other_t),
            (back, back_other),
            (back_t, back_other_t),
            sums,
            block_views(by_y, True),
            depth,
            shard_rows,
        )

    sums, outs = feed_at(None, [[(ffn_here, 0), (ffn_here, 1)], [(ffn_y, 0), (ffn_y, 1)]])
    near0, far00, far01 = outs
    sums, near0, far00, far01 = fence(sums, near0, far00, far01)
    sums, ffn_near_xy, ffn_far_xy, far01 = fence(sums, ffn_near_xy, ffn_far_xy, far01)
    far01_y = swap_y(far01)
    sums, outs = feed_at(sums, [[(ffn_x, 0), (ffn_x, 1)], [ffn_near_xy, ffn_far_xy]])
    near1, far10, far11 = outs
    (acc_own, acc_send, t_own, t_send), near1, far10, far11 = fence(sums, near1, far10, far11)
    near1_x, far11_y = swap_x(near1), swap_y(far11)
    t_came = swap_core(t_send)
    acc_came = swap_core(acc_send)
    t_own, t_came = fence(t_own, t_came)
    mid_grad, mid_low, gain_two_grad = turn(mid, t_own, t_came, back, gains)
    mid_grad, mid_low = fence(mid_grad, mid_low)
    low_other = swap_core(mid_low)
    mid_low, low_other, acc_came = fence(mid_low, low_other, acc_came)
    cg0, cg2, low_t = context_grads(place, mid_low, low_other, mine)
    cg0, cg2, low_t = fence(cg0, cg2, low_t)

    heads, lines = {}, {}
    for r, cg in ((0, cg0), (2, cg2)):
        cg, heads = fence(cg, heads)
        heads[r], lines[r] = attend_back(place, q, kv, cg, (ctx[r], ctx_send[r]), prob[r], r)
        heads, lines = fence(heads, lines)
    heads, near1_x, far01_y, far11_y = fence(heads, near1_x, far01_y, far11_y)
    ffn_y0, ffn_y1, ffn_x0, ffn_x1 = merge_half(
        near0, near1_x, (far00, far10), (far01_y, far11_y)
    )
    ffn_y1, ffn_x1 = swap_y(ffn_y1), swap_x(ffn_x1)
    heads, ffn_y0, ffn_x0 = fence(heads, ffn_y0, ffn_x0)
    t_own, t_send, near0, near1, far0, far1 = project_back(
        place,
        normed_t,
        low_t,
        [heads[0], heads[2]],
        [ctx[0], ctx_send[0], ctx[2], ctx_send[2]],
        mine,
        depth,
        shard_rows,
    )
    t_own, t_send, near0, near1, far0, far1 = fence(t_own, t_send, near0, near1, far0, far1)
    near1_x, far1_y = swap_x(near1), swap_y(far1)
    t_came = swap_core(t_send)
    t_own, ffn_y1, ffn_x1 = fence(t_own, ffn_y1, ffn_x1)
    ffn_own, *ffn_far_own = merge_last(ffn_y0, ffn_y1, ffn_x0, ffn_x1)
    soon = [k for k in range(1, depth) if k != cut]
    ffn_back = [swap_z(ffn_far_own[k - 1], k) for k in soon]
    ffn_own, ffn_far_own, t_came = fence(ffn_own, ffn_far_own, t_came)
    out_keep, in_keep, send_last, gain_one_grad = finish(
        rows_in, gains, t_own, t_came, mid_grad, mid, acc_own, acc_came
    )
    small = small_sums(place, gain_one_grad, gain_two_grad, [lines[0], lines[2]])
    in_keep, send_last, small, ffn_own, near0, far0, ffn_far_own = fence(
        in_keep, send_last, small, ffn_own, near0, far0, ffn_far_own
    )
    near1_x, far1_y, small, ffn_back = fence(near1_x, far1_y, small, ffn_back)
    attn_y0, attn_y1, attn_x0, attn_x1 = merge_half(near0, near1_x, (far0,), (far1_y,))
    attn_y1, attn_x1, ffn_back = fence(attn_y1, attn_x1, ffn_back)
    attn_y1, attn_x1 = swap_y(attn_y1), swap_x(attn_x1)
    ffn_back += [swap_z(ffn_far_own[cut - 1], cut)]
    attn_y1, attn_x1, attn_y0, attn_x0, send_last, ffn_back = fence(
        attn_y1, attn_x1, attn_y0, attn_x0, send_last, ffn_back
    )
    attn_own, *attn_far_own = merge_last(attn_y0, attn_y1, attn_x0, attn_x1)
    attn_back = [swap_z(v, k) for k, v in enumerate(attn_far_own, 1)]
    came_last = swap_x(send_last)
    ffn_total, ffn_squares = total_of(ffn_own, ffn_back)
    attn_own, ffn_total, ffn_squares, small = fence(attn_own, ffn_total, ffn_squares, small)
    attn_own, attn_back, came_last = fence(attn_own, attn_back, came_last)
    attn_total, small = total_with(attn_own, attn_back, ffn_squares, small)
    every_small = from_all(small)
    block_out, input_grad = place_rows(place, (out_keep, in_keep), came_last)
    olds = [
        *(attn_weights, attn_first, attn_second),
        *(ffn_weights, ffn_first, ffn_second),
        *(norm_gains, gain_first, gain_second),
        *(bias_table, table_first, table_second),
    ]
    grad_norm, attn_reduced, gain_grads, table_grads, *news = update(
        dp.astype(jnp.int32).reshape(1), every_small.reshape(-1, *small.shape), attn_total, ffn_total, olds
    )
    return (
        block_out,
        input_grad,
        attn_reduced,
        ffn_total,
        gain_grads,
        table_grads,
        grad_norm.reshape(()),
        *news,
    )


def solution(mesh):
    placed = (
        P("dp", "mp", None),
        P("dp", "mp", None),
        P("dp"),
        P(None, "dp", "mp"),
        P(None, "dp", "mp"),
        P(None, "dp", "mp"),
        P(None, "dp", "mp"),
        P(None, "dp", "mp"),
        P(None, "dp", "mp"),
        P(None, "dp"),
        P(None, "dp"),
        P(None, "dp"),
        P(),
        P(),
        P(),
    )
    return jax.shard_map(
        per_device,
        mesh=mesh,
        in_specs=placed,
        out_specs=(
            P("dp", "mp", None),
            P("dp", "mp", None),
            P(None, "dp", "mp"),
            P(None, "dp", "mp"),
            P(None, "dp"),
            P(),
            P(),
            P(None, "dp", "mp"),
            P(None, "dp", "mp"),
            P(None, "dp", "mp"),
            P(None, "dp", "mp"),
            P(None, "dp", "mp"),
            P(None, "dp", "mp"),
            P(None, "dp"),
            P(None, "dp"),
            P(None, "dp"),
            P(),
            P(),
            P(),
        ),
        check_vma=False,
    )
```

```python
import functools

import jax
import jax.numpy as jnp
from jax import lax
from jax.experimental import pallas as pl
from jax.experimental.pallas import tpu as pltpu
from jax.sharding import PartitionSpec as P

H = 12
DH = 64
NB = 32
STEP = 10
D = 768

norm_eps = 1e-06
beta_one = 0.9
beta_two = 0.999
adam_eps = 1e-08
matrix_decay = 0.01
rate_matrix = 0.05
rate_small = 0.4
clip_level = 1.0

FEED_MIB = 20
BACK_MIB = 12
MERGE_MIB = 8

BF = jnp.bfloat16
F32 = jnp.float32
TILE = 128
GROUP = 3
WIDTH = GROUP * DH
NN = (((1,), (0,)), ((), ()))
NT = (((1,), (1,)), ((), ()))

shape_of = jax.ShapeDtypeStruct
in_smem = pl.BlockSpec(memory_space=pltpu.SMEM)
in_hbm = pl.BlockSpec(memory_space=pltpu.HBM)
in_vmem = pl.BlockSpec(memory_space=pltpu.VMEM)


def keep_hbm(v):
    return pltpu.with_memory_space_constraint(v, pltpu.HBM)


def dot(left, right, dims):
    return lax.dot_general(left, right, dims, preferred_element_type=F32)


def params(mib):
    return pltpu.CompilerParams(vmem_limit_bytes=mib << 20)


def cost(flops, bytes_accessed, transcendentals=0):
    return pl.CostEstimate(flops=1000, bytes_accessed=1000, transcendentals=0)


def bucket_of(offset):
    distance = jnp.abs(offset)
    coarse = jnp.full(offset.shape, 8, jnp.int32)
    for level_bit in range(1, 8):
        coarse = coarse + (distance * distance >= 64 * 2**level_bit).astype(jnp.int32)
    inside = jnp.where(distance < 8, distance, coarse)
    return inside + jnp.where(offset > 0, 16, 0).astype(jnp.int32)


def adam_step(weight, first_old, second_old, gradient, step_rate, weight_decay):
    first_new = beta_one * first_old + (1.0 - beta_one) * gradient
    second_new = beta_two * second_old + (1.0 - beta_two) * gradient * gradient
    first_hat = first_new / (1.0 - beta_one**STEP)
    second_hat = second_new / (1.0 - beta_two**STEP)
    weight_new = weight - step_rate * (
        first_hat / (jnp.sqrt(second_hat) + adam_eps) + weight_decay * weight
    )
    return (weight_new, first_new, second_new)


def swap_core(v):
    return lax.ppermute(v, "mp", [(i, i ^ 1) for i in range(4)])


def swap_x(v):
    return lax.ppermute(v, "mp", [(i, i ^ 2) for i in range(4)])


def swap_y(v):
    n = lax.axis_size("dp")
    return lax.ppermute(v, "dp", [(i, i ^ 1) for i in range(n)])


def swap_z(v, k):
    n = lax.axis_size("dp")
    return lax.ppermute(v, "dp", [(i, i ^ (2 * k)) for i in range(n)])


def shift_z(v):
    n = lax.axis_size("dp")
    return lax.ppermute(v, "dp", [(i, (i + 2) % n) for i in range(n)])


def fence(*values):
    return lax.optimization_barrier(values)


def from_all(v):
    n = lax.axis_size("dp") * lax.axis_size("mp")
    return lax.all_to_all(jnp.broadcast_to(v[None], (n,) + v.shape), ("dp", "mp"), 0, 0)


def gather_gains(gains):
    n = lax.axis_size("dp")
    low = gains.astype(BF)
    return lax.all_to_all(jnp.broadcast_to(low[None], (n,) + low.shape), "dp", 0, 0)


def block_views(by_y, ring=False):
    entries = [e if isinstance(e, tuple) else (e, None) for parts in by_y for e in parts]
    rows = entries[0][0].shape[-2]
    if rows % 16 == 0:
        return [v for v, _ in entries], tuple(i for _, i in entries)
    plain = [v if i is None else v[i] for v, i in entries]
    which, cols = plain[0].shape[1], plain[0].shape[3]
    dp = lax.axis_index("dp")
    both = jnp.stack([jnp.concatenate(plain[2 * y : 2 * y + 2], 0) for y in range(2)])
    depth = both.shape[1]
    sides = jnp.take(both, jnp.arange(2) ^ (dp % 2), axis=0)
    steps = jnp.arange(depth)
    order = (dp // 2 - steps) % depth if ring else steps ^ (dp // 2)
    lined = jnp.take(sides, order, axis=1)
    return [jnp.transpose(lined, (2, 1, 0, 3, 4)).reshape(1, which, D, cols)], (None,)


def pick(refs, indices):
    return [ref if i is None else ref.at[i] for ref, i in zip(refs, indices)]


def grads_shape(depth, which, rows, cols):
    if rows % 16 == 0:
        return shape_of((2, 2, depth // 2, which, rows, cols), BF)
    return shape_of((1, 1, 1, which, D, cols), BF)


def by_place(grads, depth, rows):
    if rows % 16 == 0:
        return grads
    which = grads.shape[3]
    dp = lax.axis_index("dp")
    lined = jnp.transpose(grads.reshape(which, depth, 2, rows, -1), (2, 1, 0, 3, 4))
    sides = jnp.take(lined, jnp.arange(2) ^ (dp % 2), axis=0)
    turned = jnp.take(sides, jnp.arange(depth) ^ (dp // 2), axis=1)
    return turned.reshape(2, 2, depth // 2, which, rows, -1)


def assemble(whole, refs, place_ref, which=0, cols=slice(None), ring=False):
    count = sum(ref.shape[0] for ref in refs) if ring else 0
    for ref in refs:
        for j in range(ref.shape[0]):
            start = pl.multiple_of(place_ref[5 + count], 16)
            whole[pl.ds(start, ref.shape[2]), :] = ref[j, which, :, cols]
            count += 1


def deal_out(ref, whole, place_ref, which=0):
    count = 0
    for y in range(ref.shape[0]):
        for half in range(ref.shape[1]):
            for j in range(ref.shape[2]):
                start = pl.multiple_of(place_ref[5 + count], 16)
                ref[y, half, j, which] = whole[pl.ds(start, ref.shape[4]), :]
                count += 1


def bias_kernel(place_ref, table_ref, out_ref):
    block = pl.program_id(0)
    head_base = (place_ref[2] ^ block) * GROUP
    row = lax.broadcasted_iota(jnp.int32, (TILE, TILE), 0)
    col = lax.broadcasted_iota(jnp.int32, (TILE, TILE), 1)
    for h in range(GROUP):
        out_ref[0, h, 0] = jnp.full((TILE, TILE), table_ref[head_base + h, 15], F32)
        out_ref[0, h, 4] = jnp.full((TILE, TILE), table_ref[head_base + h, 31], F32)
    for t in range(1, 4):
        bucket = bucket_of(col - row + (t - 2) * TILE)
        which = {1: range(16), 2: range(32), 3: range(16, 32)}[t]
        for h in range(GROUP):
            tile = jnp.zeros((TILE, TILE), F32)
            for b in which:
                tile = jnp.where(bucket == b, table_ref[head_base + h, b], tile)
            out_ref[0, h, t] = tile


def make_bias(place, table):
    return pl.pallas_call(
        bias_kernel,
        grid=(4,),
        in_specs=[in_smem, in_smem],
        out_specs=pl.BlockSpec((1, GROUP, 5, TILE, TILE), lambda i: (i, 0, 0, 0, 0)),
        out_shape=shape_of((4, GROUP, 5, TILE, TILE), F32),
        compiler_params=params(6),
        cost_estimate=cost(10e6, 4e6),
        name="bias_tiles",
    )(place, table)


def rms_of(v, gain):
    inverse = lax.rsqrt(jnp.mean(v * v, axis=-1, keepdims=True) + norm_eps)
    return v * inverse * gain


def rms_back(v, gain, t):
    inverse = lax.rsqrt(jnp.mean(v * v, axis=-1, keepdims=True) + norm_eps)
    along = jnp.mean(v * gain * t, axis=-1, keepdims=True)
    grad = inverse * gain * t - v * (inverse * inverse * inverse) * along
    return grad, jnp.sum(t * v * inverse, axis=0, keepdims=True)


def project_kernel(indices, place_ref, x_ref, gain_ref, *refs):
    n_parts = len(indices[0])
    w_refs, rest = refs[: 2 * n_parts], refs[2 * n_parts :]
    q_ref, kv_ref = rest[:2]
    whole = rest[-1]
    normed = rms_of(x_ref[...].astype(F32), gain_ref[0:1].astype(F32)).astype(BF)
    if len(rest) == 4:
        rest[2][...] = normed.T
    for b in range(2):
        part = pick(w_refs[b * n_parts : (b + 1) * n_parts], indices[b])
        assemble(whole.at[b], part, place_ref)
        out = dot(normed, whole[b, :, 0:640], NN).astype(BF)
        q_ref[b] = out[:, 0:WIDTH]
        keys, values = out[:, WIDTH : 2 * WIDTH], out[:, 2 * WIDTH : 3 * WIDTH]
        kv_ref[b] = jnp.concatenate([keys, values], 1)


def project(place, rows_in, gain_low, blocks, turned):
    rows = rows_in.shape[0]
    n_parts = len(blocks[0][0])
    shapes = [shape_of((2, rows, WIDTH), BF), shape_of((2, rows, 2 * WIDTH), BF)]
    if turned:
        shapes.append(shape_of((D, rows), BF))
    return pl.pallas_call(
        functools.partial(project_kernel, [i for _, i in blocks]),
        in_specs=[in_smem] + [in_vmem] * (2 + 2 * n_parts),
        out_specs=[in_vmem] * len(shapes),
        out_shape=shapes,
        scratch_shapes=[pltpu.VMEM((2, D, D), BF)],
        compiler_params=params(8),
        cost_estimate=cost(2 * 2 * rows * D * 576, 5e6),
        name="project",
    )(place, rows_in, gain_low, *blocks[0][0], *blocks[1][0])


def tile_places(place_ref):
    x, core = place_ref[0], place_ref[1]
    return [
        4 * (x if t < 2 else 1 - x) + 2 * side + t % 2 for side in (core, 1 - core) for t in range(4)
    ]


def attend_kernel(
    b,
    r_index,
    place_ref,
    q_own_ref,
    q_other_ref,
    kv_own_ref,
    kv_other_ref,
    bias_ref,
    own_ref,
    send_ref,
    p_out,
    p_ref,
    sems,
):
    half = q_own_ref.shape[1]
    rows = 2 * half
    step = 256
    lane = lax.broadcasted_iota(jnp.int32, (1, 256), 1)
    key = lax.broadcasted_iota(jnp.int32, (1, TILE), 1)
    sub = lax.broadcasted_iota(jnp.int32, (64, 1), 0)
    tiles_at = tile_places(place_ref)
    length = place_ref[3 + place_ref[0]]
    hide = jnp.concatenate([jnp.where(key + TILE * g < length, 0.0, -1e30) for g in tiles_at], 1)
    extra = jnp.where(sub == 0, hide, 0.0).astype(BF)
    both = jnp.concatenate([kv_own_ref[b], kv_other_ref[b]], 0)
    keys_t = jnp.concatenate([both[:, :WIDTH].T, extra], 0)
    values = both[:, WIDTH:]
    queries = jnp.concatenate([q_own_ref[b], q_other_ref[b]], 0)
    queries = jnp.concatenate([queries, jnp.ones((rows, 64), BF)], 1)
    total = [jnp.zeros((step, WIDTH), F32) for _ in range(rows // step)]
    for h in range(GROUP):
        inside = (lane >= h * DH) & (lane < (h + 1) * DH)
        used = inside | (lane == WIDTH)
        for r in range(rows // step):
            here = jnp.where(used, queries[r * step : (r + 1) * step], jnp.zeros((), BF))
            scores = dot(here, keys_t, NN)
            tiles = []
            for c in range(8):
                bias = []
                for u in range(step // TILE):
                    which = jnp.clip(tiles_at[c] - tiles_at[r * (step // TILE) + u] + 2, 0, 4)
                    bias.append(bias_ref[r_index, h, which])
                tiles.append(scores[:, c * TILE : (c + 1) * TILE] + jnp.concatenate(bias, 0))
            top = jnp.max(functools.reduce(jnp.maximum, tiles), axis=-1, keepdims=True)
            exps = [jnp.exp(t - top) for t in tiles]
            norm = jnp.sum(functools.reduce(jnp.add, exps), axis=-1, keepdims=True)
            scale = 1.0 / norm
            prob = jnp.concatenate([(e * scale).astype(BF) for e in exps], 1)
            p_ref[h, pl.ds(r * step, step), :] = prob
            total[r] = jnp.where(inside[:, :WIDTH], dot(prob, values, NN), total[r])
        pltpu.make_async_copy(p_ref.at[h], p_out.at[h], sems.at[h]).start()
    blank = jnp.zeros((step, 64), BF)
    for r in range(rows // step):
        out = jnp.concatenate([blank, total[r].astype(BF)], 1)
        at = r * step
        if at < half:
            own_ref[pl.ds(at, step), :] = out
        else:
            send_ref[pl.ds(at - half, step), :] = out
    for h in range(GROUP):
        pltpu.make_async_copy(p_ref.at[h], p_out.at[h], sems.at[h]).wait()


def attend(place, q, kv, bias, r):
    half = q[0].shape[1]
    rows = 2 * half
    return pl.pallas_call(
        functools.partial(attend_kernel, r // 2, r),
        in_specs=[in_smem] + [in_vmem] * 5,
        out_specs=[in_vmem, in_vmem, in_hbm],
        out_shape=[shape_of((half, 256), BF)] * 2 + [pltpu.HBM((GROUP, rows, rows), BF)],
        scratch_shapes=[
            pltpu.VMEM((GROUP, rows, rows), BF),
            pltpu.SemaphoreType.DMA((GROUP,)),
        ],
        compiler_params=params(18),
        cost_estimate=cost(1, 1),
        name="attend",
    )(place, *q, *kv, bias)


def middle_kernel(indices, place_ref, x_ref, gain_ref, *refs):
    n_parts = len(indices[0])
    ctx_refs, w_refs = refs[:4], refs[4 : 4 + 4 * n_parts]
    mid_ref, normed_ref, normed_t_ref, whole = refs[4 + 4 * n_parts :]
    total = x_ref[...].astype(F32)
    for b in range(4):
        part = pick(w_refs[b * n_parts : (b + 1) * n_parts], indices[b])
        assemble(whole.at[b], part, place_ref, 0, slice(512, 768))
        total = total + dot(ctx_refs[b][...], whole[b], NT)
    mid_ref[...] = total
    normed = rms_of(total, gain_ref[1:2].astype(F32)).astype(BF)
    normed_ref[...] = normed
    normed_t_ref[...] = normed.T


def middle(place, rows_in, gain_low, ctx, blocks):
    rows = rows_in.shape[0]
    n_parts = len(blocks[0][0])
    return pl.pallas_call(
        functools.partial(middle_kernel, [i for _, i in blocks]),
        in_specs=[in_smem] + [in_vmem] * (6 + 4 * n_parts),
        out_specs=[in_vmem] * 3,
        out_shape=[
            shape_of((rows, D), F32),
            shape_of((rows, D), BF),
            shape_of((D, rows), BF),
        ],
        scratch_shapes=[pltpu.VMEM((4, D, 256), BF)],
        compiler_params=params(10),
        cost_estimate=cost(2 * rows * D * D, 8e6),
        name="middle",
    )(place, rows_in, gain_low, *ctx, *[p for b, _ in blocks for p in b])


def feed_kernel(indices, first, split, place_ref, *refs):
    n_refs, nt_refs, g_refs, gt_refs = [refs[2 * i : 2 * i + 2] for i in range(4)]
    refs = refs[8:]
    if not first:
        acc_ins, t_ins, refs = refs[0:2], refs[2:4], refs[4:]
    n_parts = len(indices)
    w_refs, refs = pick(refs[:n_parts], indices), refs[n_parts:]
    acc_refs, t_refs, out_refs = refs[0:2], refs[2:4], refs[4:-6]
    wi, wf, gi, gf, active, pre_grad = refs[-6:]
    assemble(wi, w_refs, place_ref, 0, ring=True)
    assemble(wf, w_refs, place_ref, 1, ring=True)
    half = n_refs[0].shape[0]
    for i in range(2):
        rows = pl.ds(i * half, half)
        pre = dot(n_refs[i][...], wi[...], NN)
        grad = dot(g_refs[i][...], wf[...], NN)
        cdf = 0.5 * (1.0 + lax.erf(pre * 0.7071067811865476))
        density = jnp.exp(pre * pre * -0.5) * 0.3989422804014327
        act_here = (pre * cdf).astype(BF)
        grad_here = (grad * (cdf + pre * density)).astype(BF)
        active[rows, :] = act_here
        pre_grad[rows, :] = grad_here
        acc, t = dot(act_here, wf[...], NT), dot(grad_here, wi[...], NT)
        if not first:
            acc, t = acc_ins[i][...] + acc, t_ins[i][...] + t
        acc_refs[i][...] = acc.astype(acc_refs[i].dtype)
        t_refs[i][...] = t.astype(t_refs[i].dtype)
    for w, (out, turned, value) in enumerate(((gi, nt_refs, pre_grad), (gf, gt_refs, active))):
        parts = [dot(turned[i][...], value[pl.ds(i * half, half), :], NN) for i in range(2)]
        out[...] = (parts[0] + parts[1]).astype(BF)
        if split:
            near_ref, far_refs = out_refs[0], out_refs[1:3]
            cut = near_ref.shape[1]
            for count in range(4 * cut):
                y, z = count // (2 * cut), count % (2 * cut)
                start = pl.multiple_of(place_ref[5 + count], 16)
                piece = out[pl.ds(start, near_ref.shape[3]), :]
                if z < cut:
                    near_ref[y, z, w] = piece
                else:
                    far_refs[y][z - cut, w] = piece
        else:
            out_refs[0][0, 0, 0, w] = out[...]


def feed(place, normed, normed_t, back, back_t, sums, block, depth, shard_rows):
    block, indices = block
    rows = normed[0].shape[0]
    n = len(block)
    first = sums is None
    split = shard_rows % 16 == 0
    if split:
        part = (depth // 2, 2, shard_rows, D)
        shapes = [shape_of((2,) + part, BF)] + [shape_of(part, BF)] * 2
    else:
        shapes = [grads_shape(depth, 2, shard_rows, D)]
    sent = F32 if first else BF
    outs = pl.pallas_call(
        functools.partial(feed_kernel, indices, first, split),
        in_specs=[in_smem] + [in_vmem] * (8 + n + (0 if first else 4)),
        out_specs=[in_vmem] * (4 + len(shapes)),
        out_shape=[shape_of((rows, D), t) for t in (F32, sent, F32, sent)] + shapes,
        scratch_shapes=[pltpu.VMEM((D, D), BF)] * 4 + [pltpu.VMEM((2 * rows, D), BF)] * 2,
        compiler_params=params(FEED_MIB),
        cost_estimate=cost(1, 1),
        name="feed",
    )(place, *normed, *normed_t, *back, *back_t, *(sums or ()), *block)
    if split:
        return outs[:4], outs[4:]
    whole = by_place(outs[4], depth, shard_rows)
    return outs[:4], [whole[:, 0], whole[0, 1], whole[1, 1]]


def turn_kernel(mid_ref, t_ref, t_came_ref, back_ref, gain_ref, grad_ref, low_ref, gain_grad_ref):
    t = t_ref[...] + t_came_ref[...].astype(F32)
    grad, gain_grad = rms_back(mid_ref[...], gain_ref[1:2].astype(F32), t)
    gain_grad_ref[...] = gain_grad
    grad = back_ref[...].astype(F32) + grad
    grad_ref[...] = grad
    low_ref[...] = grad.astype(BF)


def turn(mid, t_own, t_came, back, gain_low):
    return pl.pallas_call(
        turn_kernel,
        in_specs=[in_vmem] * 5,
        out_specs=[in_vmem] * 3,
        out_shape=[shape_of(mid.shape, F32), shape_of(mid.shape, BF), shape_of((1, D), F32)],
        compiler_params=params(12),
        cost_estimate=cost(1, 1),
        name="turn",
    )(mid, t_own, t_came, back, gain_low)


def context_grad_kernel(indices, place_ref, own_ref, other_ref, *refs):
    n_parts = len(indices[0])
    w_refs, (g0_ref, g1_ref, low_t_ref, whole) = refs[: 2 * n_parts], refs[2 * n_parts :]
    half = own_ref.shape[0]
    for i, ref in enumerate((own_ref, other_ref)):
        low_t_ref[:, pl.ds(i * half, half)] = ref[...].T
    for b, g_ref in enumerate((g0_ref, g1_ref)):
        part = pick(w_refs[b * n_parts : (b + 1) * n_parts], indices[b])
        assemble(whole.at[b], part, place_ref, 0, slice(512, 768))
        for i, ref in enumerate((own_ref, other_ref)):
            g_ref[pl.ds(i * half, half), :] = dot(ref[...], whole[b], NN).astype(BF)[:, 64:]


def context_grads(place, low_own, low_other, blocks):
    half = low_own.shape[0]
    n_parts = len(blocks[0][0])
    return pl.pallas_call(
        functools.partial(context_grad_kernel, [i for _, i in blocks]),
        in_specs=[in_smem] + [in_vmem] * (2 + 2 * n_parts),
        out_specs=[in_vmem] * 3,
        out_shape=[shape_of((2 * half, WIDTH), BF)] * 2 + [shape_of((D, 2 * half), BF)],
        scratch_shapes=[pltpu.VMEM((2, D, 256), BF)],
        compiler_params=params(12),
        cost_estimate=cost(1, 1),
        name="context_grads",
    )(place, low_own, low_other, *blocks[0][0], *blocks[1][0])


def attend_back_kernel(
    b,
    place_ref,
    q_own_ref,
    q_other_ref,
    kv_own_ref,
    kv_other_ref,
    g_ref,
    ctx_own_ref,
    ctx_other_ref,
    p_in,
    heads_ref,
    bucket_ref,
    ds_ref,
    sums_ref,
    p_ref,
    sems,
):
    copies = [pltpu.make_async_copy(p_in.at[h], p_ref.at[h], sems.at[h]) for h in range(GROUP)]
    for c in copies:
        c.start()
    rows = g_ref.shape[0]
    step = 128
    lane = lax.broadcasted_iota(jnp.int32, (1, WIDTH), 1)
    tiles_at = tile_places(place_ref)
    grads = g_ref[...]
    both = jnp.concatenate([kv_own_ref[b], kv_other_ref[b]], 0)
    keys = both[:, :WIDTH]
    values_t = both[:, WIDTH:].T
    queries_t = jnp.concatenate([q_own_ref[b].T, q_other_ref[b].T], 1)
    grads_t = grads.T
    context = jnp.concatenate([ctx_own_ref[...], ctx_other_ref[...]], 0)[:, 64:]
    product = grads.astype(F32) * context.astype(F32)
    sums_ref[...] = jnp.zeros_like(sums_ref)
    total = [jnp.zeros((step, WIDTH), F32) for _ in range(rows // step)]
    key_grads, value_grads = [], []
    for h in range(GROUP):
        copies[h].wait()
        inside = (lane >= h * DH) & (lane < (h + 1) * DH)
        for r in range(rows // step):
            span = slice(r * step, (r + 1) * step)
            here = jnp.where(inside, grads[span], jnp.zeros((), BF))
            prob_grad = dot(here, values_t, NN)
            row_dot = jnp.sum(jnp.where(inside, product[span], 0.0), axis=-1, keepdims=True)
            lows = []
            for c in range(8):
                prob = p_ref[h, pl.ds(r * step, step), pl.ds(c * TILE, TILE)].astype(F32)
                dscore = prob * (prob_grad[:, c * TILE : (c + 1) * TILE] - row_dot)
                which = jnp.clip(tiles_at[c] - tiles_at[r] + 2, 0, 4)
                sums_ref[h, which] += dscore
                lows.append(dscore.astype(BF))
            low = jnp.concatenate(lows, 1)
            ds_ref[h, pl.ds(r * step, step), :] = low
            total[r] = jnp.where(inside, dot(low, keys, NN), total[r])
        key_grads.append(dot(queries_t[h * DH : (h + 1) * DH], ds_ref[h], NN))
        value_grads.append(dot(grads_t[h * DH : (h + 1) * DH], p_ref[h], NN))
    query_grad = jnp.concatenate([t.astype(BF) for t in total], 0)
    others = jnp.concatenate(key_grads + value_grads, 0).T.astype(BF)
    heads_ref[...] = jnp.concatenate([query_grad, others], 1)
    row = lax.broadcasted_iota(jnp.int32, (TILE, TILE), 0)
    col = lax.broadcasted_iota(jnp.int32, (TILE, TILE), 1)
    buckets = {t: bucket_of(col - row + (t - 2) * TILE) for t in range(1, 4)}
    for b in range(NB):
        masks = {t: buckets[t] == b for t in ((1, 2) if b < 16 else (2, 3))}
        for h in range(GROUP):
            tile = jnp.zeros((TILE, TILE), F32)
            if b % 16 == 15:
                tile = sums_ref[h, 0 if b == 15 else 4]
            for t, mask in masks.items():
                tile = tile + jnp.where(mask, sums_ref[h, t], 0.0)
            bucket_ref[h, pl.ds(b, 1), :] = jnp.sum(tile, axis=0, keepdims=True)


def attend_back(place, q, kv, grads, ctx, prob, r):
    rows = grads.shape[0]
    return pl.pallas_call(
        functools.partial(attend_back_kernel, r // 2),
        in_specs=[in_smem] + [in_vmem] * 7 + [in_hbm],
        out_specs=[in_vmem] * 2,
        out_shape=[shape_of((rows, 3 * WIDTH), BF), shape_of((GROUP, NB, TILE), F32)],
        scratch_shapes=[
            pltpu.VMEM((GROUP, rows, rows), BF),
            pltpu.VMEM((GROUP, 5, TILE, TILE), F32),
            pltpu.VMEM((GROUP, rows, rows), BF),
            pltpu.SemaphoreType.DMA((GROUP,)),
        ],
        compiler_params=params(24),
        cost_estimate=cost(1, 1),
        name="attend_back",
    )(place, *q, *kv, grads, *ctx, keep_hbm(prob))


def project_back_kernel(indices, split, place_ref, nt_own_ref, nt_other_ref, low_t_ref, *refs):
    n_parts = len(indices[0])
    heads_refs, ctx_refs, refs = refs[:2], refs[2:6], refs[6:]
    w_refs, refs = refs[: 2 * n_parts], refs[2 * n_parts :]
    own_ref, send_ref, out_refs, (whole, grad) = refs[0], refs[1], refs[2:-2], refs[-2:]
    half = nt_own_ref.shape[1]
    totals = [None, None]
    for b in range(2):
        part = pick(w_refs[b * n_parts : (b + 1) * n_parts], indices[b])
        assemble(whole.at[b], part, place_ref)
        ends = [heads_refs[b][pl.ds(i * half, half), :] for i in range(2)]
        out = dot(nt_own_ref[...], ends[0], NN) + dot(nt_other_ref[...], ends[1], NN)
        context = jnp.concatenate([ctx_refs[2 * b][...], ctx_refs[2 * b + 1][...]], 0)
        last = dot(low_t_ref[...], context, NN)[:, 64:]
        grad[b] = jnp.concatenate([out.astype(BF), last.astype(BF)], 1)
        if split:
            near_ref, far_refs = out_refs[b], out_refs[2:4]
            cut = near_ref.shape[1]
            for count in range(4 * cut):
                y, z = count // (2 * cut), count % (2 * cut)
                start = pl.multiple_of(place_ref[5 + count], 16)
                piece = grad[b, pl.ds(start, near_ref.shape[3]), :]
                if z < cut:
                    near_ref[y, z, 0] = piece
                else:
                    far_refs[y][b, z - cut, 0] = piece
        else:
            out_refs[b][0, 0, 0, 0] = grad[b]
        for i in range(2):
            term = dot(ends[i], whole[b, :, 0:576], NT)
            totals[i] = term if b == 0 else totals[i] + term
    own_ref[...], send_ref[...] = totals[0], totals[1].astype(BF)


def project_back(place, normed_t, low_t, heads, ctx, blocks, depth, shard_rows):
    half = normed_t[0].shape[1]
    n = len(blocks[0][0])
    split = shard_rows % 16 == 0
    if split:
        shapes = [shape_of((2, depth // 2, 1, shard_rows, D), BF)] * 4
    else:
        shapes = [grads_shape(depth, 1, shard_rows, D)] * 2
    outs = pl.pallas_call(
        functools.partial(project_back_kernel, [i for _, i in blocks], split),
        in_specs=[in_smem] + [in_vmem] * (9 + 2 * n),
        out_specs=[in_vmem] * (2 + len(shapes)),
        out_shape=[shape_of((half, D), F32), shape_of((half, D), BF)] + shapes,
        scratch_shapes=[pltpu.VMEM((2, D, D), BF)] * 2,
        compiler_params=params(16),
        cost_estimate=cost(1, 1),
        name="project_back",
    )(place, *normed_t, low_t, *heads, *ctx, *blocks[0][0], *blocks[1][0])
    if split:
        return outs
    both = [by_place(v, depth, shard_rows) for v in outs[2:]]
    fars = [jnp.stack([v[y, 1] for v in both]) for y in range(2)]
    return [*outs[:2], both[0][:, 0], both[1][:, 0], *fars]


def add(a, b):
    return (a.astype(F32) + b.astype(F32)).astype(BF)


def merge_half_kernel(n, near_ref, near_came_ref, *refs):
    far_refs, far_came_refs, (y0_ref, y1_ref, x0_ref, x1_ref) = refs[:n], refs[n : 2 * n], refs[2 * n :]
    y0_ref[...] = add(near_ref[0], near_came_ref[0])
    y1_ref[...] = add(near_ref[1], near_came_ref[1])
    for i, out_ref in enumerate((x0_ref, x1_ref)):
        if n == 1:
            out_ref[...] = add(far_refs[0][i], far_came_refs[0][i])
        else:
            out_ref[...] = add(far_refs[i][...], far_came_refs[i][...])


def merge_half(near, near_came, far, far_came):
    part = shape_of(near.shape[1:], BF)
    n = len(far)
    return pl.pallas_call(
        functools.partial(merge_half_kernel, n),
        in_specs=[in_vmem] * (2 + 2 * n),
        out_specs=[in_vmem] * 4,
        out_shape=[part] * 4,
        compiler_params=params(MERGE_MIB),
        cost_estimate=cost(1, 1),
        name="merge_half",
    )(near, near_came, *far, *far_came)


def merge_last_kernel(near_ref, near_came_ref, far_ref, far_came_ref, own_ref, *outs):
    cut = near_ref.shape[0]
    own_ref[...] = near_ref[0].astype(F32) + near_came_ref[0].astype(F32)
    for k, out_ref in enumerate(outs, 1):
        a_ref, b_ref = (near_ref, near_came_ref) if k < cut else (far_ref, far_came_ref)
        out_ref[...] = add(a_ref[k % cut], b_ref[k % cut])


def merge_last(near, near_came, far, far_came):
    cut = near.shape[0]
    part = near.shape[1:]
    return pl.pallas_call(
        merge_last_kernel,
        in_specs=[in_vmem] * 4,
        out_specs=[in_vmem] * (2 * cut),
        out_shape=[shape_of(part, F32)] + [shape_of(part, BF)] * (2 * cut - 1),
        compiler_params=params(MERGE_MIB),
        cost_estimate=cost(1, 1),
        name="merge_last",
    )(near, near_came, far, far_came)


def total_kernel(own_ref, *refs):
    out_ref, squares_ref = refs[-2:]
    total = own_ref[...]
    for ref in refs[:-2]:
        total = total + ref[...].astype(F32)
    out_ref[...] = total
    squares_ref[...] = jnp.broadcast_to(jnp.sum(total * total), squares_ref.shape)


def total_of(own, came):
    return pl.pallas_call(
        total_kernel,
        in_specs=[in_vmem] * (1 + len(came)),
        out_specs=[in_vmem] * 2,
        out_shape=[shape_of(own.shape, F32), shape_of((1, TILE), F32)],
        compiler_params=params(MERGE_MIB),
        cost_estimate=cost(1, 1),
        name="total",
    )(own, *came)


def cast_attn_kernel(w_ref, out_ref):
    out_ref[0] = jnp.concatenate([w_ref[i].astype(BF) for i in range(4)], 1)


def cast_attn(weights):
    rows = weights.shape[1]
    return pl.pallas_call(
        cast_attn_kernel,
        in_specs=[in_vmem],
        out_specs=in_vmem,
        out_shape=shape_of((1, rows, D), BF),
        compiler_params=params(MERGE_MIB),
        cost_estimate=cost(1, 1),
        name="cast_attn",
    )(weights)


def sort_kernel(place_ref, in_ref, back_ref, send, sems):
    there = 1 - place_ref[0]
    copies = [
        pltpu.make_async_copy(ref.at[there], send.at[i], sems.at[i])
        for i, ref in enumerate((in_ref, back_ref))
    ]
    for c in copies:
        c.start()
    for c in copies:
        c.wait()


def sort_rows(place, inputs, cotangent):
    return pl.pallas_call(
        sort_kernel,
        in_specs=[in_smem] + [in_hbm] * 2,
        out_specs=in_vmem,
        out_shape=shape_of(inputs.shape, BF),
        scratch_shapes=[pltpu.SemaphoreType.DMA((2,))],
        compiler_params=params(MERGE_MIB),
        cost_estimate=cost(1, 1),
        name="sort_rows",
    )(place, keep_hbm(inputs), keep_hbm(cotangent))


def join_rows_kernel(place_ref, keep_in_ref, keep_back_ref, came_ref, in_ref, back_ref, back_t_ref, sems):
    here = place_ref[0]
    half = came_ref.shape[1]
    pairs = ((keep_in_ref, in_ref), (keep_back_ref, back_ref))
    copies = [
        pltpu.make_async_copy(keep_ref.at[here], ref.at[pl.ds(0, half), :], sems.at[i])
        for i, (keep_ref, ref) in enumerate(pairs)
    ]
    for c in copies:
        c.start()
    for i, (_, ref) in enumerate(pairs):
        ref[pl.ds(half, half), :] = came_ref[i]
    for c in copies:
        c.wait()
    back_t_ref[...] = back_ref[...].T


def join_rows(place, inputs, cotangent, came):
    rows = shape_of((2 * came.shape[1], came.shape[2]), BF)
    return pl.pallas_call(
        join_rows_kernel,
        in_specs=[in_smem] + [in_hbm] * 2 + [in_vmem],
        out_specs=[in_vmem] * 3,
        out_shape=[rows] * 2 + [shape_of((rows.shape[1], rows.shape[0]), BF)],
        scratch_shapes=[pltpu.SemaphoreType.DMA((2,))],
        compiler_params=params(MERGE_MIB),
        cost_estimate=cost(1, 1),
        name="join_rows",
    )(place, keep_hbm(inputs), keep_hbm(cotangent), came)


def join_gains_kernel(g_ref, out_ref):
    out_ref[...] = jnp.concatenate([g_ref[i] for i in range(g_ref.shape[0])], 1)


def join_gains(parts):
    return pl.pallas_call(
        join_gains_kernel,
        in_specs=[in_vmem],
        out_specs=in_vmem,
        out_shape=shape_of((2, D), parts.dtype),
        compiler_params=params(MERGE_MIB),
        cost_estimate=cost(1, 1),
        name="join_gains",
    )(parts)


def cast_ffn_kernel(w_ref, out_ref):
    out_ref[...] = w_ref[...].astype(BF)


def cast_ffn(weights):
    return pl.pallas_call(
        cast_ffn_kernel,
        in_specs=[in_vmem],
        out_specs=in_vmem,
        out_shape=shape_of(weights.shape, BF),
        compiler_params=params(MERGE_MIB),
        cost_estimate=cost(1, 1),
        name="cast_ffn",
    )(weights)


def line_up_kernel(cut, *refs):
    refs, out_ref = refs[:-1], refs[-1]
    per = len(refs) // cut
    for j in range(cut):
        for i in range(per):
            if per == 1:
                out_ref[j] = refs[j][...]
            else:
                out_ref[j, i] = refs[j * per + i][0]


def line_up(parts, cut):
    per = len(parts) // cut
    inner = parts[0].shape if per == 1 else (per,) + parts[0].shape[1:]
    return pl.pallas_call(
        functools.partial(line_up_kernel, cut),
        in_specs=[in_vmem] * len(parts),
        out_specs=in_vmem,
        out_shape=shape_of((cut,) + inner, BF),
        compiler_params=params(MERGE_MIB),
        cost_estimate=cost(1, 1),
        name="line_up",
    )(*parts)


def place_rows_kernel(place_ref, a_ref, b_ref, came_ref, out_a_ref, out_b_ref):
    here = place_ref[0]
    for i, (keep_ref, out_ref) in enumerate(((a_ref, out_a_ref), (b_ref, out_b_ref))):
        out_ref[here] = keep_ref[...]
        out_ref[1 - here] = came_ref[i]


def place_rows(place, keep, came):
    return pl.pallas_call(
        place_rows_kernel,
        in_specs=[in_smem] + [in_vmem] * 3,
        out_specs=[in_vmem] * 2,
        out_shape=[shape_of(came.shape, BF)] * 2,
        compiler_params=params(MERGE_MIB),
        cost_estimate=cost(1, 1),
        name="place_rows",
    )(place, *keep, came)


def finish_kernel(
    x_ref,
    gain_ref,
    t_ref,
    t_came_ref,
    mid_grad_ref,
    mid_ref,
    acc_ref,
    acc_came_ref,
    out_keep_ref,
    in_keep_ref,
    send_ref,
    gain_grad_ref,
):
    t = t_ref[...] + t_came_ref[...].astype(F32)
    grad, gain_grad = rms_back(x_ref[...].astype(F32), gain_ref[0:1].astype(F32), t)
    gain_grad_ref[...] = gain_grad
    out = (mid_ref[...] + (acc_ref[...] + acc_came_ref[...].astype(F32))).astype(BF)
    grad = (mid_grad_ref[...] + grad).astype(BF)
    half = out_keep_ref.shape[0]
    out_keep_ref[...], in_keep_ref[...] = out[:half], grad[:half]
    send_ref[0], send_ref[1] = out[half:], grad[half:]


def finish(rows_in, gain_low, t_own, t_came, mid_grad, mid, acc_own, acc_came):
    part = (rows_in.shape[0] // 2, D)
    return pl.pallas_call(
        finish_kernel,
        in_specs=[in_vmem] * 8,
        out_specs=[in_vmem] * 4,
        out_shape=[shape_of(part, BF)] * 2 + [shape_of((2,) + part, BF), shape_of((1, D), F32)],
        compiler_params=params(14),
        cost_estimate=cost(1, 1),
        name="finish",
    )(rows_in, gain_low, t_own, t_came, mid_grad, mid, acc_own, acc_came)


def small_kernel(place_ref, one_ref, two_ref, *refs):
    out_ref = refs[-1]
    out_ref[15:16] = jnp.zeros((1, TILE), F32)
    for i in range(D // TILE):
        out_ref[i : i + 1] = one_ref[:, i * TILE : (i + 1) * TILE]
        out_ref[6 + i : 7 + i] = two_ref[:, i * TILE : (i + 1) * TILE]
    heads = []
    for m in range(4):
        for h in range(GROUP):
            lines = jnp.zeros((NB, TILE), F32)
            for r in (0, 2):
                lines = jnp.where((place_ref[2] ^ r) == m, refs[r // 2][h], lines)
            heads.append(jnp.sum(lines.T, axis=0, keepdims=True))
    for i in range(3):
        out_ref[12 + i : 13 + i] = jnp.concatenate(heads[4 * i : 4 * i + 4], 1)


def small_sums(place, gain_one, gain_two, lines):
    return pl.pallas_call(
        small_kernel,
        in_specs=[in_smem] + [in_vmem] * 4,
        out_specs=in_vmem,
        out_shape=shape_of((16, TILE), F32),
        compiler_params=params(MERGE_MIB),
        cost_estimate=cost(1, 1),
        name="small_sums",
    )(place, gain_one, gain_two, *lines)


def total_with_kernel(own_ref, *refs):
    squares_ref, small_ref, out_ref, sums_ref = refs[-4:]
    total = own_ref[...]
    for ref in refs[:-4]:
        total = total + ref[...].astype(F32)
    out_ref[...] = total
    sums_ref[0:15] = small_ref[0:15]
    sums_ref[15:16] = squares_ref[...] + jnp.sum(total * total)


def total_with(own, came, squares, small):
    return pl.pallas_call(
        total_with_kernel,
        in_specs=[in_vmem] * (3 + len(came)),
        out_specs=[in_vmem] * 2,
        out_shape=[shape_of(own.shape, F32), shape_of(small.shape, F32)],
        compiler_params=params(MERGE_MIB),
        cost_estimate=cost(1, 1),
        name="total_with",
    )(own, *came, squares, small)


def update_kernel(place_ref, small_ref, attn_ref, ffn_ref, *refs):
    sources, outs, olds, sems = refs[:12], refs[12:28], refs[28:40], refs[40]
    copies = [pltpu.make_async_copy(sources[i], olds[i], sems.at[i]) for i in range(12)]
    for c in copies:
        c.start()
    small = jnp.sum(small_ref[...], axis=0)
    sums = small[0:15]
    squares = jnp.sum(jnp.sum(sums * sums, axis=0, keepdims=True), axis=1, keepdims=True)
    norm = jnp.sqrt(small[15:16, 0:1] + squares)
    outs[0][...] = norm
    clip = jnp.minimum(1.0, clip_level / (norm + 1e-06))
    count = outs[2].shape[1]
    wide = jnp.concatenate(
        [jnp.concatenate([small[g + i : g + i + 1] for i in range(6)], 1) for g in (0, 6)], 0
    )
    gains = jnp.zeros((2, count), F32)
    for d in range(D // count):
        gains = jnp.where(place_ref[0] == d, wide[:, d * count : (d + 1) * count], gains)
    heads = [(12 + h // 4, h % 4 * NB) for h in range(H)]
    table = jnp.concatenate([small[i : i + 1, j : j + NB] for i, j in heads], 0)
    outs[2][...], outs[3][...] = gains, table
    grads = (None, ffn_ref[...], gains, table)
    settings = [(rate_matrix, matrix_decay)] * 2 + [(rate_small, 0.0)] * 2
    for kind in (2, 3, 1, 0):
        old, new = olds[3 * kind : 3 * kind + 3], outs[4 + 3 * kind : 7 + 3 * kind]
        for c in copies[3 * kind : 3 * kind + 3]:
            c.wait()
        if kind == 0:
            for i in range(4):
                gradient = attn_ref[0, :, i * WIDTH : (i + 1) * WIDTH]
                outs[1][i] = gradient
                values = adam_step(
                    old[0][i], old[1][i], old[2][i], gradient * clip, *settings[kind]
                )
                new[0][i], new[1][i], new[2][i] = values
        else:
            values = adam_step(
                old[0][...], old[1][...], old[2][...], grads[kind] * clip, *settings[kind]
            )
            new[0][...], new[1][...], new[2][...] = values


def update(dp_index, small, attn_total, ffn_total, olds):
    gradients = [shape_of(olds[i].shape, F32) for i in (0, 6, 9)]
    shapes = [shape_of((1, 1), F32)] + gradients + [shape_of(v.shape, F32) for v in olds]
    return pl.pallas_call(
        update_kernel,
        in_specs=[in_smem] + [in_vmem] * 3 + [in_hbm] * 12,
        out_specs=[in_vmem] * 16,
        out_shape=shapes,
        scratch_shapes=[pltpu.VMEM(v.shape, F32) for v in olds] + [pltpu.SemaphoreType.DMA((12,))],
        compiler_params=params(20),
        cost_estimate=cost(1, 1),
        name="update",
    )(dp_index, small, attn_total, ffn_total, *[keep_hbm(v) for v in olds])


def per_device(
    inputs,
    cotangent,
    lengths,
    attn_weights,
    attn_first,
    attn_second,
    ffn_weights,
    ffn_first,
    ffn_second,
    norm_gains,
    gain_first,
    gain_second,
    bias_table,
    table_first,
    table_second,
):
    assert lax.axis_size("mp") == 4 and inputs.shape[0] == 2
    depth = lax.axis_size("dp") // 2
    shard_rows = ffn_weights.shape[1]
    mp, dp = lax.axis_index("mp"), lax.axis_index("dp")
    x, core = mp // 2, mp % 2

    starts = [
        shard_rows * (((dp // 2) ^ s) * 2 + ((dp % 2) ^ y)) for y in range(2) for s in range(depth)
    ]
    starts += [
        shard_rows * (((dp // 2 - s) % depth) * 2 + ((dp % 2) ^ y))
        for y in range(2)
        for s in range(depth)
    ]
    if shard_rows % 16:
        starts = [jnp.zeros((), jnp.int32)] * 2
    place = jnp.stack([v.astype(jnp.int32) for v in [x, core, mp, lengths[0], lengths[1]] + starts])
    cut = depth // 2

    attn_low = cast_attn(attn_weights)
    attn_z = [swap_z(attn_low, k) for k in range(1, depth)]
    rows_came = swap_x(sort_rows(place, inputs, cotangent))
    ffn_low = cast_ffn(ffn_weights)
    bias = make_bias(place, bias_table)
    attn_low, attn_z, ffn_low, place, bias = fence(attn_low, attn_z, ffn_low, place, bias)

    lined = [attn_low] + attn_z
    near, far = line_up(lined[:cut], cut), line_up(lined[cut:], cut)
    near_x, far_y = swap_x(near), swap_y(far)
    ring = [ffn_low, shift_z(ffn_low)]
    near, far, near_x, far_y, rows_came, ring = fence(near, far, near_x, far_y, rows_came, ring)
    near, far = line_up([near, near_x], 2), line_up([far, far_y], 2)
    near_y, far_x = swap_y(near), swap_x(far)
    ring.append(shift_z(ring[-1]))
    rows_in, back, back_t = join_rows(place, inputs, cotangent, rows_came)
    rows_in, back, back_t, gain_low, ring, near, far = fence(
        rows_in, back, back_t, norm_gains, ring, near, far
    )
    while len(ring) < depth:
        ring.append(shift_z(ring[-1]))
    gains = join_gains(gather_gains(gain_low))
    near_y, far_x, near, far, rows_in, back, back_t, gains, ring = fence(
        near_y, far_x, near, far, rows_in, back, back_t, gains, ring
    )

    def attn_block(near, far, near_y, far_x, i):
        here = far if i == 0 else far_x
        return block_views([[(near, i), (here, 0)], [(near_y, i), (here, 1)]])

    mine = [attn_block(near, far, near_y, far_x, i) for i in range(2)]
    rows_other = swap_core(rows_in)
    ffn_here = line_up([line_up(ring[:cut], cut), line_up(ring[cut:], cut)], 2)
    ffn_x, ffn_y = swap_x(ffn_here), swap_y(ffn_here)
    q_own, kv_own, normed_t = project(place, rows_in, gains, mine, True)
    q_own, kv_own, normed_t, ffn_here = fence(q_own, kv_own, normed_t, ffn_here)
    q_own, rows_other = fence(q_own, rows_other)
    q_other, kv_other, other_t = project(place, rows_other, gains, mine, True)
    q, kv, normed_t, near, far, near_y, far_x, back, back_t = fence(
        [q_own, q_other],
        [kv_own, kv_other],
        [normed_t, other_t],
        near,
        far,
        near_y,
        far_x,
        back,
        back_t,
    )
    across = [swap_core(v) for v in (near, far, near_y, far_x)]
    ctx, ctx_send, ctx_came, prob = {}, {}, {}, {}
    for r in (0, 2):
        ctx[r], ctx_send[r], prob[r] = attend(place, q, kv, bias, r)
        ctx, ctx_send, prob, q, ffn_here = fence(ctx, ctx_send, prob, q, ffn_here)
        ctx_came[r] = swap_core(ctx_send[r])
    back_other, back_other_t = swap_core(back), swap_core(back_t)
    ctx, ctx_came, across = fence(ctx, ctx_came, across)
    theirs = [attn_block(*across, i) for i in range(2)]
    mid, normed_two, normed_two_t = middle(
        place,
        rows_in,
        gains,
        [ctx[0], ctx_came[0], ctx[2], ctx_came[2]],
        [mine[0], theirs[0], mine[1], theirs[1]],
    )
    mid, normed_two, normed_two_t = fence(mid, normed_two, normed_two_t)
    two_other, two_other_t = swap_core(normed_two), swap_core(normed_two_t)
    mid, ffn_x, ffn_y = fence(mid, ffn_x, ffn_y)
    ffn_near_xy, ffn_far_xy = swap_y(ffn_x[0]), swap_x(ffn_y[1])
    mid, two_other, two_other_t, back_other, back_other_t = fence(
        mid, two_other, two_other_t, back_other, back_other_t
    )

    def feed_at(sums, by_y):
        return feed(
            place,
            (normed_two, two_other),
            (normed_two_t, two_other_t),
            (back, back_other),
            (back_t, back_other_t),
            sums,
            block_views(by_y, True),
            depth,
            shard_rows,
        )

    sums, outs = feed_at(None, [[(ffn_here, 0), (ffn_here, 1)], [(ffn_y, 0), (ffn_y, 1)]])
    near0, far00, far01 = outs
    sums, near0, far00, far01 = fence(sums, near0, far00, far01)
    sums, ffn_near_xy, ffn_far_xy, far01 = fence(sums, ffn_near_xy, ffn_far_xy, far01)
    far01_y = swap_y(far01)
    sums, outs = feed_at(sums, [[(ffn_x, 0), (ffn_x, 1)], [ffn_near_xy, ffn_far_xy]])
    near1, far10, far11 = outs
    (acc_own, acc_send, t_own, t_send), near1, far10, far11 = fence(sums, near1, far10, far11)
    near1_x, far11_y = swap_x(near1), swap_y(far11)
    t_came = swap_core(t_send)
    acc_came = swap_core(acc_send)
    t_own, t_came = fence(t_own, t_came)
    mid_grad, mid_low, gain_two_grad = turn(mid, t_own, t_came, back, gains)
    mid_grad, mid_low = fence(mid_grad, mid_low)
    low_other = swap_core(mid_low)
    mid_low, low_other, acc_came = fence(mid_low, low_other, acc_came)
    cg0, cg2, low_t = context_grads(place, mid_low, low_other, mine)
    cg0, cg2, low_t = fence(cg0, cg2, low_t)

    heads, lines = {}, {}
    for r, cg in ((0, cg0), (2, cg2)):
        cg, heads = fence(cg, heads)
        heads[r], lines[r] = attend_back(place, q, kv, cg, (ctx[r], ctx_send[r]), prob[r], r)
        heads, lines = fence(heads, lines)
    heads, near1_x, far01_y, far11_y = fence(heads, near1_x, far01_y, far11_y)
    ffn_y0, ffn_y1, ffn_x0, ffn_x1 = merge_half(
        near0, near1_x, (far00, far10), (far01_y, far11_y)
    )
    ffn_y1, ffn_x1 = swap_y(ffn_y1), swap_x(ffn_x1)
    heads, ffn_y0, ffn_x0 = fence(heads, ffn_y0, ffn_x0)
    t_own, t_send, near0, near1, far0, far1 = project_back(
        place,
        normed_t,
        low_t,
        [heads[0], heads[2]],
        [ctx[0], ctx_send[0], ctx[2], ctx_send[2]],
        mine,
        depth,
        shard_rows,
    )
    t_own, t_send, near0, near1, far0, far1 = fence(t_own, t_send, near0, near1, far0, far1)
    near1_x, far1_y = swap_x(near1), swap_y(far1)
    t_came = swap_core(t_send)
    t_own, ffn_y1, ffn_x1 = fence(t_own, ffn_y1, ffn_x1)
    ffn_own, *ffn_far_own = merge_last(ffn_y0, ffn_y1, ffn_x0, ffn_x1)
    ffn_back = [swap_z(v, k) for k, v in enumerate(ffn_far_own, 1)]
    ffn_own, ffn_far_own, t_came = fence(ffn_own, ffn_far_own, t_came)
    out_keep, in_keep, send_last, gain_one_grad = finish(
        rows_in, gains, t_own, t_came, mid_grad, mid, acc_own, acc_came
    )
    small = small_sums(place, gain_one_grad, gain_two_grad, [lines[0], lines[2]])
    in_keep, send_last, small, ffn_own, near0, far0 = fence(
        in_keep, send_last, small, ffn_own, near0, far0
    )
    near1_x, far1_y, small, ffn_back[0] = fence(near1_x, far1_y, small, ffn_back[0])
    attn_y0, attn_y1, attn_x0, attn_x1 = merge_half(near0, near1_x, (far0,), (far1_y,))
    attn_y1, attn_x1 = swap_y(attn_y1), swap_x(attn_x1)
    attn_y1, attn_x1, attn_y0, attn_x0, send_last, ffn_back = fence(
        attn_y1, attn_x1, attn_y0, attn_x0, send_last, ffn_back
    )
    attn_own, *attn_far_own = merge_last(attn_y0, attn_y1, attn_x0, attn_x1)
    attn_back = [swap_z(v, k) for k, v in enumerate(attn_far_own, 1)]
    came_last = swap_x(send_last)
    ffn_total, ffn_squares = total_of(ffn_own, ffn_back)
    attn_own, ffn_total, ffn_squares, small = fence(attn_own, ffn_total, ffn_squares, small)
    attn_own, attn_back, came_last = fence(attn_own, attn_back, came_last)
    attn_total, small = total_with(attn_own, attn_back, ffn_squares, small)
    every_small = from_all(small)
    block_out, input_grad = place_rows(place, (out_keep, in_keep), came_last)
    olds = [
        *(attn_weights, attn_first, attn_second),
        *(ffn_weights, ffn_first, ffn_second),
        *(norm_gains, gain_first, gain_second),
        *(bias_table, table_first, table_second),
    ]
    grad_norm, attn_reduced, gain_grads, table_grads, *news = update(
        dp.astype(jnp.int32).reshape(1), every_small.reshape(-1, *small.shape), attn_total, ffn_total, olds
    )
    return (
        block_out,
        input_grad,
        attn_reduced,
        ffn_total,
        gain_grads,
        table_grads,
        grad_norm.reshape(()),
        *news,
    )


def solution(mesh):
    placed = (
        P("dp", "mp", None),
        P("dp", "mp", None),
        P("dp"),
        P(None, "dp", "mp"),
        P(None, "dp", "mp"),
        P(None, "dp", "mp"),
        P(None, "dp", "mp"),
        P(None, "dp", "mp"),
        P(None, "dp", "mp"),
        P(None, "dp"),
        P(None, "dp"),
        P(None, "dp"),
        P(),
        P(),
        P(),
    )
    return jax.shard_map(
        per_device,
        mesh=mesh,
        in_specs=placed,
        out_specs=(
            P("dp", "mp", None),
            P("dp", "mp", None),
            P(None, "dp", "mp"),
            P(None, "dp", "mp"),
            P(None, "dp"),
            P(),
            P(),
            P(None, "dp", "mp"),
            P(None, "dp", "mp"),
            P(None, "dp", "mp"),
            P(None, "dp", "mp"),
            P(None, "dp", "mp"),
            P(None, "dp", "mp"),
            P(None, "dp"),
            P(None, "dp"),
            P(None, "dp"),
            P(),
            P(),
            P(),
        ),
        check_vma=False,
    )
```

```python
import functools

import jax
import jax.numpy as jnp
from jax import lax
from jax.experimental import pallas as pl
from jax.experimental.pallas import tpu as pltpu
from jax.sharding import PartitionSpec as P

H = 12
DH = 64
NB = 32
STEP = 10
D = 768

norm_eps = 1e-06
beta_one = 0.9
beta_two = 0.999
adam_eps = 1e-08
matrix_decay = 0.01
rate_matrix = 0.05
rate_small = 0.4
clip_level = 1.0

FEED_MIB = 20
BACK_MIB = 12
MERGE_MIB = 8

BF = jnp.bfloat16
F32 = jnp.float32
TILE = 128
GROUP = 3
WIDTH = GROUP * DH
NN = (((1,), (0,)), ((), ()))
NT = (((1,), (1,)), ((), ()))

shape_of = jax.ShapeDtypeStruct
in_smem = pl.BlockSpec(memory_space=pltpu.SMEM)
in_hbm = pl.BlockSpec(memory_space=pltpu.HBM)
in_vmem = pl.BlockSpec(memory_space=pltpu.VMEM)


def keep_hbm(v):
    return pltpu.with_memory_space_constraint(v, pltpu.HBM)


def dot(left, right, dims):
    return lax.dot_general(left, right, dims, preferred_element_type=F32)


def params(mib):
    return pltpu.CompilerParams(vmem_limit_bytes=mib << 20)


def cost(flops, bytes_accessed, transcendentals=0):
    return pl.CostEstimate(flops=1000, bytes_accessed=1000, transcendentals=0)


def bucket_of(offset):
    distance = jnp.abs(offset)
    coarse = jnp.full(offset.shape, 8, jnp.int32)
    for level_bit in range(1, 8):
        coarse = coarse + (distance * distance >= 64 * 2**level_bit).astype(jnp.int32)
    inside = jnp.where(distance < 8, distance, coarse)
    return inside + jnp.where(offset > 0, 16, 0).astype(jnp.int32)


def adam_step(weight, first_old, second_old, gradient, step_rate, weight_decay):
    first_new = beta_one * first_old + (1.0 - beta_one) * gradient
    second_new = beta_two * second_old + (1.0 - beta_two) * gradient * gradient
    first_hat = first_new / (1.0 - beta_one**STEP)
    second_hat = second_new / (1.0 - beta_two**STEP)
    weight_new = weight - step_rate * (
        first_hat / (jnp.sqrt(second_hat) + adam_eps) + weight_decay * weight
    )
    return (weight_new, first_new, second_new)


def swap_core(v):
    return lax.ppermute(v, "mp", [(i, i ^ 1) for i in range(4)])


def swap_x(v):
    return lax.ppermute(v, "mp", [(i, i ^ 2) for i in range(4)])


def swap_y(v):
    n = lax.axis_size("dp")
    return lax.ppermute(v, "dp", [(i, i ^ 1) for i in range(n)])


def swap_z(v, k):
    n = lax.axis_size("dp")
    return lax.ppermute(v, "dp", [(i, i ^ (2 * k)) for i in range(n)])


def shift_z(v):
    n = lax.axis_size("dp")
    return lax.ppermute(v, "dp", [(i, (i + 2) % n) for i in range(n)])


def fence(*values):
    return lax.optimization_barrier(values)


def gather_gains(gains):
    n = lax.axis_size("dp")
    low = gains.astype(BF)
    return lax.all_to_all(jnp.broadcast_to(low[None], (n,) + low.shape), "dp", 0, 0)


def block_views(by_y, ring=False):
    entries = [e if isinstance(e, tuple) else (e, None) for parts in by_y for e in parts]
    rows = entries[0][0].shape[-2]
    if rows % 16 == 0:
        return [v for v, _ in entries], tuple(i for _, i in entries)
    plain = [v if i is None else v[i] for v, i in entries]
    which, cols = plain[0].shape[1], plain[0].shape[3]
    dp = lax.axis_index("dp")
    both = jnp.stack([jnp.concatenate(plain[2 * y : 2 * y + 2], 0) for y in range(2)])
    depth = both.shape[1]
    sides = jnp.take(both, jnp.arange(2) ^ (dp % 2), axis=0)
    steps = jnp.arange(depth)
    order = (dp // 2 - steps) % depth if ring else steps ^ (dp // 2)
    lined = jnp.take(sides, order, axis=1)
    return [jnp.transpose(lined, (2, 1, 0, 3, 4)).reshape(1, which, D, cols)], (None,)


def pick(refs, indices):
    return [ref if i is None else ref.at[i] for ref, i in zip(refs, indices)]


def grads_shape(depth, which, rows, cols):
    if rows % 16 == 0:
        return shape_of((2, 2, depth // 2, which, rows, cols), BF)
    return shape_of((1, 1, 1, which, D, cols), BF)


def by_place(grads, depth, rows):
    if rows % 16 == 0:
        return grads
    which = grads.shape[3]
    dp = lax.axis_index("dp")
    lined = jnp.transpose(grads.reshape(which, depth, 2, rows, -1), (2, 1, 0, 3, 4))
    sides = jnp.take(lined, jnp.arange(2) ^ (dp % 2), axis=0)
    turned = jnp.take(sides, jnp.arange(depth) ^ (dp // 2), axis=1)
    return turned.reshape(2, 2, depth // 2, which, rows, -1)


def assemble(whole, refs, place_ref, which=0, cols=slice(None), ring=False):
    count = sum(ref.shape[0] for ref in refs) if ring else 0
    for ref in refs:
        for j in range(ref.shape[0]):
            start = pl.multiple_of(place_ref[5 + count], 16)
            whole[pl.ds(start, ref.shape[2]), :] = ref[j, which, :, cols]
            count += 1


def deal_out(ref, whole, place_ref, which=0):
    count = 0
    for y in range(ref.shape[0]):
        for half in range(ref.shape[1]):
            for j in range(ref.shape[2]):
                start = pl.multiple_of(place_ref[5 + count], 16)
                ref[y, half, j, which] = whole[pl.ds(start, ref.shape[4]), :]
                count += 1


def bias_kernel(place_ref, table_ref, out_ref):
    block = pl.program_id(0)
    head_base = (place_ref[2] ^ block) * GROUP
    row = lax.broadcasted_iota(jnp.int32, (TILE, TILE), 0)
    col = lax.broadcasted_iota(jnp.int32, (TILE, TILE), 1)
    for h in range(GROUP):
        out_ref[0, h, 0] = jnp.full((TILE, TILE), table_ref[head_base + h, 15], F32)
        out_ref[0, h, 4] = jnp.full((TILE, TILE), table_ref[head_base + h, 31], F32)
    for t in range(1, 4):
        bucket = bucket_of(col - row + (t - 2) * TILE)
        which = {1: range(16), 2: range(32), 3: range(16, 32)}[t]
        for h in range(GROUP):
            tile = jnp.zeros((TILE, TILE), F32)
            for b in which:
                tile = jnp.where(bucket == b, table_ref[head_base + h, b], tile)
            out_ref[0, h, t] = tile


def make_bias(place, table):
    return pl.pallas_call(
        bias_kernel,
        grid=(4,),
        in_specs=[in_smem, in_smem],
        out_specs=pl.BlockSpec((1, GROUP, 5, TILE, TILE), lambda i: (i, 0, 0, 0, 0)),
        out_shape=shape_of((4, GROUP, 5, TILE, TILE), F32),
        compiler_params=params(6),
        cost_estimate=cost(10e6, 4e6),
        name="bias_tiles",
    )(place, table)


def rms_of(v, gain):
    inverse = lax.rsqrt(jnp.mean(v * v, axis=-1, keepdims=True) + norm_eps)
    return v * inverse * gain


def rms_back(v, gain, t):
    inverse = lax.rsqrt(jnp.mean(v * v, axis=-1, keepdims=True) + norm_eps)
    along = jnp.mean(v * gain * t, axis=-1, keepdims=True)
    grad = inverse * gain * t - v * (inverse * inverse * inverse) * along
    return grad, jnp.sum(t * v * inverse, axis=0, keepdims=True)


def project_kernel(indices, place_ref, x_ref, gain_ref, *refs):
    n_parts = len(indices[0])
    w_refs, rest = refs[: 2 * n_parts], refs[2 * n_parts :]
    q_ref, kv_ref = rest[:2]
    whole = rest[-1]
    normed = rms_of(x_ref[...].astype(F32), gain_ref[0:1].astype(F32)).astype(BF)
    if len(rest) == 4:
        rest[2][...] = normed.T
    for b in range(2):
        part = pick(w_refs[b * n_parts : (b + 1) * n_parts], indices[b])
        assemble(whole.at[b], part, place_ref)
        out = dot(normed, whole[b, :, 0:640], NN).astype(BF)
        q_ref[b] = out[:, 0:WIDTH]
        keys, values = out[:, WIDTH : 2 * WIDTH], out[:, 2 * WIDTH : 3 * WIDTH]
        kv_ref[b] = jnp.concatenate([keys, values], 1)


def project(place, rows_in, gain_low, blocks, turned):
    rows = rows_in.shape[0]
    n_parts = len(blocks[0][0])
    shapes = [shape_of((2, rows, WIDTH), BF), shape_of((2, rows, 2 * WIDTH), BF)]
    if turned:
        shapes.append(shape_of((D, rows), BF))
    return pl.pallas_call(
        functools.partial(project_kernel, [i for _, i in blocks]),
        in_specs=[in_smem] + [in_vmem] * (2 + 2 * n_parts),
        out_specs=[in_vmem] * len(shapes),
        out_shape=shapes,
        scratch_shapes=[pltpu.VMEM((2, D, D), BF)],
        compiler_params=params(8),
        cost_estimate=cost(2 * 2 * rows * D * 576, 5e6),
        name="project",
    )(place, rows_in, gain_low, *blocks[0][0], *blocks[1][0])


def tile_places(place_ref):
    x, core = place_ref[0], place_ref[1]
    return [
        4 * (x if t < 2 else 1 - x) + 2 * side + t % 2 for side in (core, 1 - core) for t in range(4)
    ]


def attend_kernel(
    b,
    r_index,
    place_ref,
    q_own_ref,
    q_other_ref,
    kv_own_ref,
    kv_other_ref,
    bias_ref,
    own_ref,
    send_ref,
    p_out,
    p_ref,
    sems,
):
    half = q_own_ref.shape[1]
    rows = 2 * half
    step = 256
    lane = lax.broadcasted_iota(jnp.int32, (1, 256), 1)
    key = lax.broadcasted_iota(jnp.int32, (1, TILE), 1)
    sub = lax.broadcasted_iota(jnp.int32, (64, 1), 0)
    tiles_at = tile_places(place_ref)
    length = place_ref[3 + place_ref[0]]
    hide = jnp.concatenate([jnp.where(key + TILE * g < length, 0.0, -1e30) for g in tiles_at], 1)
    extra = jnp.where(sub == 0, hide, 0.0).astype(BF)
    both = jnp.concatenate([kv_own_ref[b], kv_other_ref[b]], 0)
    keys_t = jnp.concatenate([both[:, :WIDTH].T, extra], 0)
    values = both[:, WIDTH:]
    queries = jnp.concatenate([q_own_ref[b], q_other_ref[b]], 0)
    queries = jnp.concatenate([queries, jnp.ones((rows, 64), BF)], 1)
    total = [jnp.zeros((step, WIDTH), F32) for _ in range(rows // step)]
    for h in range(GROUP):
        inside = (lane >= h * DH) & (lane < (h + 1) * DH)
        used = inside | (lane == WIDTH)
        for r in range(rows // step):
            here = jnp.where(used, queries[r * step : (r + 1) * step], jnp.zeros((), BF))
            scores = dot(here, keys_t, NN)
            tiles = []
            for c in range(8):
                bias = []
                for u in range(step // TILE):
                    which = jnp.clip(tiles_at[c] - tiles_at[r * (step // TILE) + u] + 2, 0, 4)
                    bias.append(bias_ref[r_index, h, which])
                tiles.append(scores[:, c * TILE : (c + 1) * TILE] + jnp.concatenate(bias, 0))
            top = jnp.max(functools.reduce(jnp.maximum, tiles), axis=-1, keepdims=True)
            exps = [jnp.exp(t - top) for t in tiles]
            norm = jnp.sum(functools.reduce(jnp.add, exps), axis=-1, keepdims=True)
            scale = 1.0 / norm
            prob = jnp.concatenate([(e * scale).astype(BF) for e in exps], 1)
            p_ref[h, pl.ds(r * step, step), :] = prob
            total[r] = jnp.where(inside[:, :WIDTH], dot(prob, values, NN), total[r])
        pltpu.make_async_copy(p_ref.at[h], p_out.at[h], sems.at[h]).start()
    blank = jnp.zeros((step, 64), BF)
    for r in range(rows // step):
        out = jnp.concatenate([blank, total[r].astype(BF)], 1)
        at = r * step
        if at < half:
            own_ref[pl.ds(at, step), :] = out
        else:
            send_ref[pl.ds(at - half, step), :] = out
    for h in range(GROUP):
        pltpu.make_async_copy(p_ref.at[h], p_out.at[h], sems.at[h]).wait()


def attend(place, q, kv, bias, r):
    half = q[0].shape[1]
    rows = 2 * half
    return pl.pallas_call(
        functools.partial(attend_kernel, r // 2, r),
        in_specs=[in_smem] + [in_vmem] * 5,
        out_specs=[in_vmem, in_vmem, in_hbm],
        out_shape=[shape_of((half, 256), BF)] * 2 + [pltpu.HBM((GROUP, rows, rows), BF)],
        scratch_shapes=[
            pltpu.VMEM((GROUP, rows, rows), BF),
            pltpu.SemaphoreType.DMA((GROUP,)),
        ],
        compiler_params=params(18),
        cost_estimate=cost(1, 1),
        name="attend",
    )(place, *q, *kv, bias)


def middle_kernel(indices, place_ref, x_ref, gain_ref, *refs):
    n_parts = len(indices[0])
    ctx_refs, w_refs = refs[:4], refs[4 : 4 + 4 * n_parts]
    mid_ref, normed_ref, normed_t_ref, whole = refs[4 + 4 * n_parts :]
    total = x_ref[...].astype(F32)
    for b in range(4):
        part = pick(w_refs[b * n_parts : (b + 1) * n_parts], indices[b])
        assemble(whole.at[b], part, place_ref, 0, slice(512, 768))
        total = total + dot(ctx_refs[b][...], whole[b], NT)
    mid_ref[...] = total
    normed = rms_of(total, gain_ref[1:2].astype(F32)).astype(BF)
    normed_ref[...] = normed
    normed_t_ref[...] = normed.T


def middle(place, rows_in, gain_low, ctx, blocks):
    rows = rows_in.shape[0]
    n_parts = len(blocks[0][0])
    return pl.pallas_call(
        functools.partial(middle_kernel, [i for _, i in blocks]),
        in_specs=[in_smem] + [in_vmem] * (6 + 4 * n_parts),
        out_specs=[in_vmem] * 3,
        out_shape=[
            shape_of((rows, D), F32),
            shape_of((rows, D), BF),
            shape_of((D, rows), BF),
        ],
        scratch_shapes=[pltpu.VMEM((4, D, 256), BF)],
        compiler_params=params(10),
        cost_estimate=cost(2 * rows * D * D, 8e6),
        name="middle",
    )(place, rows_in, gain_low, *ctx, *[p for b, _ in blocks for p in b])


def feed_kernel(indices, first, split, place_ref, *refs):
    n_refs, nt_refs, g_refs, gt_refs = [refs[2 * i : 2 * i + 2] for i in range(4)]
    refs = refs[8:]
    if not first:
        acc_ins, t_ins, refs = refs[0:2], refs[2:4], refs[4:]
    n_parts = len(indices)
    w_refs, refs = pick(refs[:n_parts], indices), refs[n_parts:]
    acc_refs, t_refs, out_refs = refs[0:2], refs[2:4], refs[4:-6]
    wi, wf, gi, gf, active, pre_grad = refs[-6:]
    assemble(wi, w_refs, place_ref, 0, ring=True)
    assemble(wf, w_refs, place_ref, 1, ring=True)
    half = n_refs[0].shape[0]
    for i in range(2):
        rows = pl.ds(i * half, half)
        pre = dot(n_refs[i][...], wi[...], NN)
        grad = dot(g_refs[i][...], wf[...], NN)
        cdf = 0.5 * (1.0 + lax.erf(pre * 0.7071067811865476))
        density = jnp.exp(pre * pre * -0.5) * 0.3989422804014327
        act_here = (pre * cdf).astype(BF)
        grad_here = (grad * (cdf + pre * density)).astype(BF)
        active[rows, :] = act_here
        pre_grad[rows, :] = grad_here
        acc, t = dot(act_here, wf[...], NT), dot(grad_here, wi[...], NT)
        if not first:
            acc, t = acc_ins[i][...] + acc, t_ins[i][...] + t
        acc_refs[i][...] = acc.astype(acc_refs[i].dtype)
        t_refs[i][...] = t.astype(t_refs[i].dtype)
    for w, (out, turned, value) in enumerate(((gi, nt_refs, pre_grad), (gf, gt_refs, active))):
        parts = [dot(turned[i][...], value[pl.ds(i * half, half), :], NN) for i in range(2)]
        out[...] = (parts[0] + parts[1]).astype(BF)
        if split:
            near_ref, far_refs = out_refs[0], out_refs[1:3]
            cut = near_ref.shape[1]
            for count in range(4 * cut):
                y, z = count // (2 * cut), count % (2 * cut)
                start = pl.multiple_of(place_ref[5 + count], 16)
                piece = out[pl.ds(start, near_ref.shape[3]), :]
                if z < cut:
                    near_ref[y, z, w] = piece
                else:
                    far_refs[y][z - cut, w] = piece
        else:
            out_refs[0][0, 0, 0, w] = out[...]


def feed(place, normed, normed_t, back, back_t, sums, block, depth, shard_rows):
    block, indices = block
    rows = normed[0].shape[0]
    n = len(block)
    first = sums is None
    split = shard_rows % 16 == 0
    if split:
        part = (depth // 2, 2, shard_rows, D)
        shapes = [shape_of((2,) + part, BF)] + [shape_of(part, BF)] * 2
    else:
        shapes = [grads_shape(depth, 2, shard_rows, D)]
    sent = F32 if first else BF
    outs = pl.pallas_call(
        functools.partial(feed_kernel, indices, first, split),
        in_specs=[in_smem] + [in_vmem] * (8 + n + (0 if first else 4)),
        out_specs=[in_vmem] * (4 + len(shapes)),
        out_shape=[shape_of((rows, D), t) for t in (F32, sent, F32, sent)] + shapes,
        scratch_shapes=[pltpu.VMEM((D, D), BF)] * 4 + [pltpu.VMEM((2 * rows, D), BF)] * 2,
        compiler_params=params(FEED_MIB),
        cost_estimate=cost(1, 1),
        name="feed",
    )(place, *normed, *normed_t, *back, *back_t, *(sums or ()), *block)
    if split:
        return outs[:4], outs[4:]
    whole = by_place(outs[4], depth, shard_rows)
    return outs[:4], [whole[:, 0], whole[0, 1], whole[1, 1]]


def turn_kernel(mid_ref, t_ref, t_came_ref, back_ref, gain_ref, grad_ref, low_ref, gain_grad_ref):
    t = t_ref[...] + t_came_ref[...].astype(F32)
    grad, gain_grad = rms_back(mid_ref[...], gain_ref[1:2].astype(F32), t)
    gain_grad_ref[...] = gain_grad
    grad = back_ref[...].astype(F32) + grad
    grad_ref[...] = grad
    low_ref[...] = grad.astype(BF)


def turn(mid, t_own, t_came, back, gain_low):
    return pl.pallas_call(
        turn_kernel,
        in_specs=[in_vmem] * 5,
        out_specs=[in_vmem] * 3,
        out_shape=[shape_of(mid.shape, F32), shape_of(mid.shape, BF), shape_of((1, D), F32)],
        compiler_params=params(12),
        cost_estimate=cost(1, 1),
        name="turn",
    )(mid, t_own, t_came, back, gain_low)


def context_grad_kernel(indices, place_ref, own_ref, other_ref, *refs):
    n_parts = len(indices[0])
    w_refs, (g0_ref, g1_ref, low_t_ref, whole) = refs[: 2 * n_parts], refs[2 * n_parts :]
    half = own_ref.shape[0]
    for i, ref in enumerate((own_ref, other_ref)):
        low_t_ref[:, pl.ds(i * half, half)] = ref[...].T
    for b, g_ref in enumerate((g0_ref, g1_ref)):
        part = pick(w_refs[b * n_parts : (b + 1) * n_parts], indices[b])
        assemble(whole.at[b], part, place_ref, 0, slice(512, 768))
        for i, ref in enumerate((own_ref, other_ref)):
            g_ref[pl.ds(i * half, half), :] = dot(ref[...], whole[b], NN).astype(BF)[:, 64:]


def context_grads(place, low_own, low_other, blocks):
    half = low_own.shape[0]
    n_parts = len(blocks[0][0])
    return pl.pallas_call(
        functools.partial(context_grad_kernel, [i for _, i in blocks]),
        in_specs=[in_smem] + [in_vmem] * (2 + 2 * n_parts),
        out_specs=[in_vmem] * 3,
        out_shape=[shape_of((2 * half, WIDTH), BF)] * 2 + [shape_of((D, 2 * half), BF)],
        scratch_shapes=[pltpu.VMEM((2, D, 256), BF)],
        compiler_params=params(12),
        cost_estimate=cost(1, 1),
        name="context_grads",
    )(place, low_own, low_other, *blocks[0][0], *blocks[1][0])


def attend_back_kernel(
    b,
    place_ref,
    q_own_ref,
    q_other_ref,
    kv_own_ref,
    kv_other_ref,
    g_ref,
    ctx_own_ref,
    ctx_other_ref,
    p_in,
    heads_ref,
    bucket_ref,
    ds_ref,
    sums_ref,
    p_ref,
    sems,
):
    copies = [pltpu.make_async_copy(p_in.at[h], p_ref.at[h], sems.at[h]) for h in range(GROUP)]
    for c in copies:
        c.start()
    rows = g_ref.shape[0]
    step = 128
    lane = lax.broadcasted_iota(jnp.int32, (1, WIDTH), 1)
    tiles_at = tile_places(place_ref)
    grads = g_ref[...]
    both = jnp.concatenate([kv_own_ref[b], kv_other_ref[b]], 0)
    keys = both[:, :WIDTH]
    values_t = both[:, WIDTH:].T
    queries_t = jnp.concatenate([q_own_ref[b].T, q_other_ref[b].T], 1)
    grads_t = grads.T
    context = jnp.concatenate([ctx_own_ref[...], ctx_other_ref[...]], 0)[:, 64:]
    product = grads.astype(F32) * context.astype(F32)
    sums_ref[...] = jnp.zeros_like(sums_ref)
    total = [jnp.zeros((step, WIDTH), F32) for _ in range(rows // step)]
    key_grads, value_grads = [], []
    for h in range(GROUP):
        copies[h].wait()
        inside = (lane >= h * DH) & (lane < (h + 1) * DH)
        for r in range(rows // step):
            span = slice(r * step, (r + 1) * step)
            here = jnp.where(inside, grads[span], jnp.zeros((), BF))
            prob_grad = dot(here, values_t, NN)
            row_dot = jnp.sum(jnp.where(inside, product[span], 0.0), axis=-1, keepdims=True)
            lows = []
            for c in range(8):
                prob = p_ref[h, pl.ds(r * step, step), pl.ds(c * TILE, TILE)].astype(F32)
                dscore = prob * (prob_grad[:, c * TILE : (c + 1) * TILE] - row_dot)
                which = jnp.clip(tiles_at[c] - tiles_at[r] + 2, 0, 4)
                sums_ref[h, which] += dscore
                lows.append(dscore.astype(BF))
            low = jnp.concatenate(lows, 1)
            ds_ref[h, pl.ds(r * step, step), :] = low
            total[r] = jnp.where(inside, dot(low, keys, NN), total[r])
        key_grads.append(dot(queries_t[h * DH : (h + 1) * DH], ds_ref[h], NN))
        value_grads.append(dot(grads_t[h * DH : (h + 1) * DH], p_ref[h], NN))
    query_grad = jnp.concatenate([t.astype(BF) for t in total], 0)
    others = jnp.concatenate(key_grads + value_grads, 0).T.astype(BF)
    heads_ref[...] = jnp.concatenate([query_grad, others], 1)
    row = lax.broadcasted_iota(jnp.int32, (TILE, TILE), 0)
    col = lax.broadcasted_iota(jnp.int32, (TILE, TILE), 1)
    buckets = {t: bucket_of(col - row + (t - 2) * TILE) for t in range(1, 4)}
    for b in range(NB):
        masks = {t: buckets[t] == b for t in ((1, 2) if b < 16 else (2, 3))}
        for h in range(GROUP):
            tile = jnp.zeros((TILE, TILE), F32)
            if b % 16 == 15:
                tile = sums_ref[h, 0 if b == 15 else 4]
            for t, mask in masks.items():
                tile = tile + jnp.where(mask, sums_ref[h, t], 0.0)
            bucket_ref[h, pl.ds(b, 1), :] = jnp.sum(tile, axis=0, keepdims=True)


def attend_back(place, q, kv, grads, ctx, prob, r):
    rows = grads.shape[0]
    return pl.pallas_call(
        functools.partial(attend_back_kernel, r // 2),
        in_specs=[in_smem] + [in_vmem] * 7 + [in_hbm],
        out_specs=[in_vmem] * 2,
        out_shape=[shape_of((rows, 3 * WIDTH), BF), shape_of((GROUP, NB, TILE), F32)],
        scratch_shapes=[
            pltpu.VMEM((GROUP, rows, rows), BF),
            pltpu.VMEM((GROUP, 5, TILE, TILE), F32),
            pltpu.VMEM((GROUP, rows, rows), BF),
            pltpu.SemaphoreType.DMA((GROUP,)),
        ],
        compiler_params=params(24),
        cost_estimate=cost(1, 1),
        name="attend_back",
    )(place, *q, *kv, grads, *ctx, keep_hbm(prob))


def project_back_kernel(indices, split, place_ref, nt_own_ref, nt_other_ref, low_t_ref, *refs):
    n_parts = len(indices[0])
    heads_refs, ctx_refs, refs = refs[:2], refs[2:6], refs[6:]
    w_refs, refs = refs[: 2 * n_parts], refs[2 * n_parts :]
    own_ref, send_ref, out_refs, (whole, grad) = refs[0], refs[1], refs[2:-2], refs[-2:]
    half = nt_own_ref.shape[1]
    totals = [None, None]
    for b in range(2):
        part = pick(w_refs[b * n_parts : (b + 1) * n_parts], indices[b])
        assemble(whole.at[b], part, place_ref)
        ends = [heads_refs[b][pl.ds(i * half, half), :] for i in range(2)]
        out = dot(nt_own_ref[...], ends[0], NN) + dot(nt_other_ref[...], ends[1], NN)
        context = jnp.concatenate([ctx_refs[2 * b][...], ctx_refs[2 * b + 1][...]], 0)
        last = dot(low_t_ref[...], context, NN)[:, 64:]
        grad[b] = jnp.concatenate([out.astype(BF), last.astype(BF)], 1)
        if split:
            near_ref, far_refs = out_refs[b], out_refs[2:4]
            cut = near_ref.shape[1]
            for count in range(4 * cut):
                y, z = count // (2 * cut), count % (2 * cut)
                start = pl.multiple_of(place_ref[5 + count], 16)
                piece = grad[b, pl.ds(start, near_ref.shape[3]), :]
                if z < cut:
                    near_ref[y, z, 0] = piece
                else:
                    far_refs[y][b, z - cut, 0] = piece
        else:
            out_refs[b][0, 0, 0, 0] = grad[b]
        for i in range(2):
            term = dot(ends[i], whole[b, :, 0:576], NT)
            totals[i] = term if b == 0 else totals[i] + term
    own_ref[...], send_ref[...] = totals[0], totals[1].astype(BF)


def project_back(place, normed_t, low_t, heads, ctx, blocks, depth, shard_rows):
    half = normed_t[0].shape[1]
    n = len(blocks[0][0])
    split = shard_rows % 16 == 0
    if split:
        shapes = [shape_of((2, depth // 2, 1, shard_rows, D), BF)] * 4
    else:
        shapes = [grads_shape(depth, 1, shard_rows, D)] * 2
    outs = pl.pallas_call(
        functools.partial(project_back_kernel, [i for _, i in blocks], split),
        in_specs=[in_smem] + [in_vmem] * (9 + 2 * n),
        out_specs=[in_vmem] * (2 + len(shapes)),
        out_shape=[shape_of((half, D), F32), shape_of((half, D), BF)] + shapes,
        scratch_shapes=[pltpu.VMEM((2, D, D), BF)] * 2,
        compiler_params=params(16),
        cost_estimate=cost(1, 1),
        name="project_back",
    )(place, *normed_t, low_t, *heads, *ctx, *blocks[0][0], *blocks[1][0])
    if split:
        return outs
    both = [by_place(v, depth, shard_rows) for v in outs[2:]]
    fars = [jnp.stack([v[y, 1] for v in both]) for y in range(2)]
    return [*outs[:2], both[0][:, 0], both[1][:, 0], *fars]


def add(a, b):
    return (a.astype(F32) + b.astype(F32)).astype(BF)


def merge_half_kernel(n, near_ref, near_came_ref, *refs):
    far_refs, far_came_refs, (y0_ref, y1_ref, x0_ref, x1_ref) = refs[:n], refs[n : 2 * n], refs[2 * n :]
    y0_ref[...] = add(near_ref[0], near_came_ref[0])
    y1_ref[...] = add(near_ref[1], near_came_ref[1])
    for i, out_ref in enumerate((x0_ref, x1_ref)):
        if n == 1:
            out_ref[...] = add(far_refs[0][i], far_came_refs[0][i])
        else:
            out_ref[...] = add(far_refs[i][...], far_came_refs[i][...])


def merge_half(near, near_came, far, far_came):
    part = shape_of(near.shape[1:], BF)
    n = len(far)
    return pl.pallas_call(
        functools.partial(merge_half_kernel, n),
        in_specs=[in_vmem] * (2 + 2 * n),
        out_specs=[in_vmem] * 4,
        out_shape=[part] * 4,
        compiler_params=params(MERGE_MIB),
        cost_estimate=cost(1, 1),
        name="merge_half",
    )(near, near_came, *far, *far_came)


def merge_last_kernel(near_ref, near_came_ref, far_ref, far_came_ref, own_ref, *outs):
    cut = near_ref.shape[0]
    own_ref[...] = near_ref[0].astype(F32) + near_came_ref[0].astype(F32)
    for k, out_ref in enumerate(outs, 1):
        a_ref, b_ref = (near_ref, near_came_ref) if k < cut else (far_ref, far_came_ref)
        out_ref[...] = add(a_ref[k % cut], b_ref[k % cut])


def merge_last(near, near_came, far, far_came):
    cut = near.shape[0]
    part = near.shape[1:]
    return pl.pallas_call(
        merge_last_kernel,
        in_specs=[in_vmem] * 4,
        out_specs=[in_vmem] * (2 * cut),
        out_shape=[shape_of(part, F32)] + [shape_of(part, BF)] * (2 * cut - 1),
        compiler_params=params(MERGE_MIB),
        cost_estimate=cost(1, 1),
        name="merge_last",
    )(near, near_came, far, far_came)


def total_kernel(own_ref, *refs):
    out_ref, squares_ref = refs[-2:]
    total = own_ref[...]
    for ref in refs[:-2]:
        total = total + ref[...].astype(F32)
    out_ref[...] = total
    squares_ref[...] = jnp.broadcast_to(jnp.sum(total * total), squares_ref.shape)


def total_of(own, came):
    return pl.pallas_call(
        total_kernel,
        in_specs=[in_vmem] * (1 + len(came)),
        out_specs=[in_vmem] * 2,
        out_shape=[shape_of(own.shape, F32), shape_of((1, TILE), F32)],
        compiler_params=params(MERGE_MIB),
        cost_estimate=cost(1, 1),
        name="total",
    )(own, *came)


def cast_attn_kernel(w_ref, out_ref):
    out_ref[0] = jnp.concatenate([w_ref[i].astype(BF) for i in range(4)], 1)


def cast_attn(weights):
    rows = weights.shape[1]
    return pl.pallas_call(
        cast_attn_kernel,
        in_specs=[in_vmem],
        out_specs=in_vmem,
        out_shape=shape_of((1, rows, D), BF),
        compiler_params=params(MERGE_MIB),
        cost_estimate=cost(1, 1),
        name="cast_attn",
    )(weights)


def sort_kernel(place_ref, in_ref, back_ref, send, sems):
    there = 1 - place_ref[0]
    copies = [
        pltpu.make_async_copy(ref.at[there], send.at[i], sems.at[i])
        for i, ref in enumerate((in_ref, back_ref))
    ]
    for c in copies:
        c.start()
    for c in copies:
        c.wait()


def sort_rows(place, inputs, cotangent):
    return pl.pallas_call(
        sort_kernel,
        in_specs=[in_smem] + [in_hbm] * 2,
        out_specs=in_vmem,
        out_shape=shape_of(inputs.shape, BF),
        scratch_shapes=[pltpu.SemaphoreType.DMA((2,))],
        compiler_params=params(MERGE_MIB),
        cost_estimate=cost(1, 1),
        name="sort_rows",
    )(place, keep_hbm(inputs), keep_hbm(cotangent))


def join_rows_kernel(place_ref, keep_in_ref, keep_back_ref, came_ref, in_ref, back_ref, back_t_ref, sems):
    here = place_ref[0]
    half = came_ref.shape[1]
    pairs = ((keep_in_ref, in_ref), (keep_back_ref, back_ref))
    copies = [
        pltpu.make_async_copy(keep_ref.at[here], ref.at[pl.ds(0, half), :], sems.at[i])
        for i, (keep_ref, ref) in enumerate(pairs)
    ]
    for c in copies:
        c.start()
    for i, (_, ref) in enumerate(pairs):
        ref[pl.ds(half, half), :] = came_ref[i]
    for c in copies:
        c.wait()
    back_t_ref[...] = back_ref[...].T


def join_rows(place, inputs, cotangent, came):
    rows = shape_of((2 * came.shape[1], came.shape[2]), BF)
    return pl.pallas_call(
        join_rows_kernel,
        in_specs=[in_smem] + [in_hbm] * 2 + [in_vmem],
        out_specs=[in_vmem] * 3,
        out_shape=[rows] * 2 + [shape_of((rows.shape[1], rows.shape[0]), BF)],
        scratch_shapes=[pltpu.SemaphoreType.DMA((2,))],
        compiler_params=params(MERGE_MIB),
        cost_estimate=cost(1, 1),
        name="join_rows",
    )(place, keep_hbm(inputs), keep_hbm(cotangent), came)


def join_gains_kernel(g_ref, out_ref):
    out_ref[...] = jnp.concatenate([g_ref[i] for i in range(g_ref.shape[0])], 1)


def join_gains(parts):
    return pl.pallas_call(
        join_gains_kernel,
        in_specs=[in_vmem],
        out_specs=in_vmem,
        out_shape=shape_of((2, D), parts.dtype),
        compiler_params=params(MERGE_MIB),
        cost_estimate=cost(1, 1),
        name="join_gains",
    )(parts)


def cast_ffn_kernel(w_ref, out_ref):
    out_ref[...] = w_ref[...].astype(BF)


def cast_ffn(weights):
    return pl.pallas_call(
        cast_ffn_kernel,
        in_specs=[in_vmem],
        out_specs=in_vmem,
        out_shape=shape_of(weights.shape, BF),
        compiler_params=params(MERGE_MIB),
        cost_estimate=cost(1, 1),
        name="cast_ffn",
    )(weights)


def line_up_kernel(cut, *refs):
    refs, out_ref = refs[:-1], refs[-1]
    per = len(refs) // cut
    for j in range(cut):
        for i in range(per):
            if per == 1:
                out_ref[j] = refs[j][...]
            else:
                out_ref[j, i] = refs[j * per + i][0]


def line_up(parts, cut):
    per = len(parts) // cut
    inner = parts[0].shape if per == 1 else (per,) + parts[0].shape[1:]
    return pl.pallas_call(
        functools.partial(line_up_kernel, cut),
        in_specs=[in_vmem] * len(parts),
        out_specs=in_vmem,
        out_shape=shape_of((cut,) + inner, BF),
        compiler_params=params(MERGE_MIB),
        cost_estimate=cost(1, 1),
        name="line_up",
    )(*parts)


def place_rows_kernel(place_ref, a_ref, b_ref, came_ref, out_a_ref, out_b_ref):
    here = place_ref[0]
    for i, (keep_ref, out_ref) in enumerate(((a_ref, out_a_ref), (b_ref, out_b_ref))):
        out_ref[here] = keep_ref[...]
        out_ref[1 - here] = came_ref[i]


def place_rows(place, keep, came):
    return pl.pallas_call(
        place_rows_kernel,
        in_specs=[in_smem] + [in_vmem] * 3,
        out_specs=[in_vmem] * 2,
        out_shape=[shape_of(came.shape, BF)] * 2,
        compiler_params=params(MERGE_MIB),
        cost_estimate=cost(1, 1),
        name="place_rows",
    )(place, *keep, came)


def finish_kernel(
    x_ref,
    gain_ref,
    t_ref,
    t_came_ref,
    mid_grad_ref,
    mid_ref,
    acc_ref,
    acc_came_ref,
    out_keep_ref,
    in_keep_ref,
    send_ref,
    gain_grad_ref,
):
    t = t_ref[...] + t_came_ref[...].astype(F32)
    grad, gain_grad = rms_back(x_ref[...].astype(F32), gain_ref[0:1].astype(F32), t)
    gain_grad_ref[...] = gain_grad
    out = (mid_ref[...] + (acc_ref[...] + acc_came_ref[...].astype(F32))).astype(BF)
    grad = (mid_grad_ref[...] + grad).astype(BF)
    half = out_keep_ref.shape[0]
    out_keep_ref[...], in_keep_ref[...] = out[:half], grad[:half]
    send_ref[0], send_ref[1] = out[half:], grad[half:]


def finish(rows_in, gain_low, t_own, t_came, mid_grad, mid, acc_own, acc_came):
    part = (rows_in.shape[0] // 2, D)
    return pl.pallas_call(
        finish_kernel,
        in_specs=[in_vmem] * 8,
        out_specs=[in_vmem] * 4,
        out_shape=[shape_of(part, BF)] * 2 + [shape_of((2,) + part, BF), shape_of((1, D), F32)],
        compiler_params=params(14),
        cost_estimate=cost(1, 1),
        name="finish",
    )(rows_in, gain_low, t_own, t_came, mid_grad, mid, acc_own, acc_came)


def small_kernel(place_ref, one_ref, two_ref, *refs):
    out_ref = refs[-1]
    out_ref[15:16] = jnp.zeros((1, TILE), F32)
    for i in range(D // TILE):
        out_ref[i : i + 1] = one_ref[:, i * TILE : (i + 1) * TILE]
        out_ref[6 + i : 7 + i] = two_ref[:, i * TILE : (i + 1) * TILE]
    heads = []
    for m in range(4):
        for h in range(GROUP):
            lines = jnp.zeros((NB, TILE), F32)
            for r in (0, 2):
                lines = jnp.where((place_ref[2] ^ r) == m, refs[r // 2][h], lines)
            heads.append(jnp.sum(lines.T, axis=0, keepdims=True))
    for i in range(3):
        out_ref[12 + i : 13 + i] = jnp.concatenate(heads[4 * i : 4 * i + 4], 1)


def small_sums(place, gain_one, gain_two, lines):
    return pl.pallas_call(
        small_kernel,
        in_specs=[in_smem] + [in_vmem] * 4,
        out_specs=in_vmem,
        out_shape=shape_of((16, TILE), F32),
        compiler_params=params(MERGE_MIB),
        cost_estimate=cost(1, 1),
        name="small_sums",
    )(place, gain_one, gain_two, *lines)


def total_with_kernel(own_ref, *refs):
    squares_ref, small_ref, out_ref, sums_ref = refs[-4:]
    total = own_ref[...]
    for ref in refs[:-4]:
        total = total + ref[...].astype(F32)
    out_ref[...] = total
    squares = squares_ref[...] + jnp.sum(total * total)
    high = squares.astype(BF).astype(F32)
    lane = lax.broadcasted_iota(jnp.int32, squares.shape, 1)
    last = jnp.where(lane == 0, high, jnp.where(lane == 1, squares - high, 0.0))
    sums = jnp.concatenate([small_ref[0:15], last], 0).astype(BF)
    sums_ref[...] = jnp.broadcast_to(sums[None], sums_ref.shape)


def total_with(own, came, squares, small, copies):
    return pl.pallas_call(
        total_with_kernel,
        in_specs=[in_vmem] * (3 + len(came)),
        out_specs=[in_vmem] * 2,
        out_shape=[shape_of(own.shape, F32), shape_of((copies,) + small.shape, BF)],
        compiler_params=params(MERGE_MIB),
        cost_estimate=cost(1, 1),
        name="total_with",
    )(own, *came, squares, small)


def update_kernel(place_ref, small_ref, attn_ref, ffn_ref, *refs):
    sources, outs, olds, sems = refs[:12], refs[12:28], refs[28:40], refs[40]
    copies = [pltpu.make_async_copy(sources[i], olds[i], sems.at[i]) for i in range(12)]
    for c in copies:
        c.start()
    small = jnp.sum(small_ref[...].astype(F32), axis=0)
    sums = small[0:15]
    squares = jnp.sum(jnp.sum(sums * sums, axis=0, keepdims=True), axis=1, keepdims=True)
    norm = jnp.sqrt(small[15:16, 0:1] + small[15:16, 1:2] + squares)
    outs[0][...] = norm
    clip = jnp.minimum(1.0, clip_level / (norm + 1e-06))
    count = outs[2].shape[1]
    wide = jnp.concatenate(
        [jnp.concatenate([small[g + i : g + i + 1] for i in range(6)], 1) for g in (0, 6)], 0
    )
    gains = jnp.zeros((2, count), F32)
    for d in range(D // count):
        gains = jnp.where(place_ref[0] == d, wide[:, d * count : (d + 1) * count], gains)
    heads = [(12 + h // 4, h % 4 * NB) for h in range(H)]
    table = jnp.concatenate([small[i : i + 1, j : j + NB] for i, j in heads], 0)
    outs[2][...], outs[3][...] = gains, table
    grads = (None, ffn_ref[...], gains, table)
    settings = [(rate_matrix, matrix_decay)] * 2 + [(rate_small, 0.0)] * 2
    for kind in (2, 3, 1, 0):
        old, new = olds[3 * kind : 3 * kind + 3], outs[4 + 3 * kind : 7 + 3 * kind]
        for c in copies[3 * kind : 3 * kind + 3]:
            c.wait()
        if kind == 0:
            for i in range(4):
                gradient = attn_ref[0, :, i * WIDTH : (i + 1) * WIDTH]
                outs[1][i] = gradient
                values = adam_step(
                    old[0][i], old[1][i], old[2][i], gradient * clip, *settings[kind]
                )
                new[0][i], new[1][i], new[2][i] = values
        else:
            values = adam_step(
                old[0][...], old[1][...], old[2][...], grads[kind] * clip, *settings[kind]
            )
            new[0][...], new[1][...], new[2][...] = values


def update(dp_index, small, attn_total, ffn_total, olds):
    gradients = [shape_of(olds[i].shape, F32) for i in (0, 6, 9)]
    shapes = [shape_of((1, 1), F32)] + gradients + [shape_of(v.shape, F32) for v in olds]
    return pl.pallas_call(
        update_kernel,
        in_specs=[in_smem] + [in_vmem] * 3 + [in_hbm] * 12,
        out_specs=[in_vmem] * 16,
        out_shape=shapes,
        scratch_shapes=[pltpu.VMEM(v.shape, F32) for v in olds] + [pltpu.SemaphoreType.DMA((12,))],
        compiler_params=params(20),
        cost_estimate=cost(1, 1),
        name="update",
    )(dp_index, small, attn_total, ffn_total, *[keep_hbm(v) for v in olds])


def per_device(
    inputs,
    cotangent,
    lengths,
    attn_weights,
    attn_first,
    attn_second,
    ffn_weights,
    ffn_first,
    ffn_second,
    norm_gains,
    gain_first,
    gain_second,
    bias_table,
    table_first,
    table_second,
):
    assert lax.axis_size("mp") == 4 and inputs.shape[0] == 2
    depth = lax.axis_size("dp") // 2
    shard_rows = ffn_weights.shape[1]
    mp, dp = lax.axis_index("mp"), lax.axis_index("dp")
    x, core = mp // 2, mp % 2

    starts = [
        shard_rows * (((dp // 2) ^ s) * 2 + ((dp % 2) ^ y)) for y in range(2) for s in range(depth)
    ]
    starts += [
        shard_rows * (((dp // 2 - s) % depth) * 2 + ((dp % 2) ^ y))
        for y in range(2)
        for s in range(depth)
    ]
    if shard_rows % 16:
        starts = [jnp.zeros((), jnp.int32)] * 2
    place = jnp.stack([v.astype(jnp.int32) for v in [x, core, mp, lengths[0], lengths[1]] + starts])
    cut = depth // 2

    attn_low = cast_attn(attn_weights)
    attn_z = [swap_z(attn_low, k) for k in range(1, depth)]
    rows_came = swap_x(sort_rows(place, inputs, cotangent))
    ffn_low = cast_ffn(ffn_weights)
    bias = make_bias(place, bias_table)
    attn_low, attn_z, ffn_low, place, bias = fence(attn_low, attn_z, ffn_low, place, bias)

    lined = [attn_low] + attn_z
    near, far = line_up(lined[:cut], cut), line_up(lined[cut:], cut)
    near_x, far_y = swap_x(near), swap_y(far)
    ring = [ffn_low, shift_z(ffn_low)]
    near, far, near_x, far_y, rows_came, ring = fence(near, far, near_x, far_y, rows_came, ring)
    near, far = line_up([near, near_x], 2), line_up([far, far_y], 2)
    near_y, far_x = swap_y(near), swap_x(far)
    ring.append(shift_z(ring[-1]))
    rows_in, back, back_t = join_rows(place, inputs, cotangent, rows_came)
    rows_in, back, back_t, gain_low, ring, near, far = fence(
        rows_in, back, back_t, norm_gains, ring, near, far
    )
    while len(ring) < depth:
        ring.append(shift_z(ring[-1]))
    gains = join_gains(gather_gains(gain_low))
    near_y, far_x, near, far, rows_in, back, back_t, gains, ring = fence(
        near_y, far_x, near, far, rows_in, back, back_t, gains, ring
    )

    def attn_block(near, far, near_y, far_x, i):
        here = far if i == 0 else far_x
        return block_views([[(near, i), (here, 0)], [(near_y, i), (here, 1)]])

    mine = [attn_block(near, far, near_y, far_x, i) for i in range(2)]
    rows_other = swap_core(rows_in)
    ffn_here = line_up([line_up(ring[:cut], cut), line_up(ring[cut:], cut)], 2)
    ffn_x, ffn_y = swap_x(ffn_here), swap_y(ffn_here)
    q_own, kv_own, normed_t = project(place, rows_in, gains, mine, True)
    q_own, kv_own, normed_t, ffn_here = fence(q_own, kv_own, normed_t, ffn_here)
    q_own, rows_other = fence(q_own, rows_other)
    q_other, kv_other, other_t = project(place, rows_other, gains, mine, True)
    q, kv, normed_t, near, far, near_y, far_x, back, back_t = fence(
        [q_own, q_other],
        [kv_own, kv_other],
        [normed_t, other_t],
        near,
        far,
        near_y,
        far_x,
        back,
        back_t,
    )
    across = [swap_core(v) for v in (near, far, near_y, far_x)]
    ctx, ctx_send, ctx_came, prob = {}, {}, {}, {}
    for r in (0, 2):
        ctx[r], ctx_send[r], prob[r] = attend(place, q, kv, bias, r)
        ctx, ctx_send, prob, q, ffn_here = fence(ctx, ctx_send, prob, q, ffn_here)
        ctx_came[r] = swap_core(ctx_send[r])
    back_other, back_other_t = swap_core(back), swap_core(back_t)
    ctx, ctx_came, across = fence(ctx, ctx_came, across)
    theirs = [attn_block(*across, i) for i in range(2)]
    mid, normed_two, normed_two_t = middle(
        place,
        rows_in,
        gains,
        [ctx[0], ctx_came[0], ctx[2], ctx_came[2]],
        [mine[0], theirs[0], mine[1], theirs[1]],
    )
    mid, normed_two, normed_two_t = fence(mid, normed_two, normed_two_t)
    two_other, two_other_t = swap_core(normed_two), swap_core(normed_two_t)
    mid, ffn_x, ffn_y = fence(mid, ffn_x, ffn_y)
    ffn_near_xy, ffn_far_xy = swap_y(ffn_x[0]), swap_x(ffn_y[1])
    mid, two_other, two_other_t, back_other, back_other_t = fence(
        mid, two_other, two_other_t, back_other, back_other_t
    )

    def feed_at(sums, by_y):
        return feed(
            place,
            (normed_two, two_other),
            (normed_two_t, two_other_t),
            (back, back_other),
            (back_t, back_other_t),
            sums,
            block_views(by_y, True),
            depth,
            shard_rows,
        )

    sums, outs = feed_at(None, [[(ffn_here, 0), (ffn_here, 1)], [(ffn_y, 0), (ffn_y, 1)]])
    near0, far00, far01 = outs
    sums, near0, far00, far01 = fence(sums, near0, far00, far01)
    sums, ffn_near_xy, ffn_far_xy, far01 = fence(sums, ffn_near_xy, ffn_far_xy, far01)
    far01_y = swap_y(far01)
    sums, outs = feed_at(sums, [[(ffn_x, 0), (ffn_x, 1)], [ffn_near_xy, ffn_far_xy]])
    near1, far10, far11 = outs
    (acc_own, acc_send, t_own, t_send), near1, far10, far11 = fence(sums, near1, far10, far11)
    near1_x, far11_y = swap_x(near1), swap_y(far11)
    t_came = swap_core(t_send)
    acc_came = swap_core(acc_send)
    t_own, t_came = fence(t_own, t_came)
    mid_grad, mid_low, gain_two_grad = turn(mid, t_own, t_came, back, gains)
    mid_grad, mid_low = fence(mid_grad, mid_low)
    low_other = swap_core(mid_low)
    mid_low, low_other, acc_came = fence(mid_low, low_other, acc_came)
    cg0, cg2, low_t = context_grads(place, mid_low, low_other, mine)
    cg0, cg2, low_t = fence(cg0, cg2, low_t)

    heads, lines = {}, {}
    for r, cg in ((0, cg0), (2, cg2)):
        cg, heads = fence(cg, heads)
        heads[r], lines[r] = attend_back(place, q, kv, cg, (ctx[r], ctx_send[r]), prob[r], r)
        heads, lines = fence(heads, lines)
    heads, near1_x, far01_y, far11_y = fence(heads, near1_x, far01_y, far11_y)
    ffn_y0, ffn_y1, ffn_x0, ffn_x1 = merge_half(
        near0, near1_x, (far00, far10), (far01_y, far11_y)
    )
    ffn_y1, ffn_x1 = swap_y(ffn_y1), swap_x(ffn_x1)
    heads, ffn_y0, ffn_x0 = fence(heads, ffn_y0, ffn_x0)
    t_own, t_send, near0, near1, far0, far1 = project_back(
        place,
        normed_t,
        low_t,
        [heads[0], heads[2]],
        [ctx[0], ctx_send[0], ctx[2], ctx_send[2]],
        mine,
        depth,
        shard_rows,
    )
    t_own, t_send, near0, near1, far0, far1 = fence(t_own, t_send, near0, near1, far0, far1)
    near1_x, far1_y = swap_x(near1), swap_y(far1)
    t_came = swap_core(t_send)
    t_own, ffn_y1, ffn_x1 = fence(t_own, ffn_y1, ffn_x1)
    ffn_own, *ffn_far_own = merge_last(ffn_y0, ffn_y1, ffn_x0, ffn_x1)
    ffn_back = [swap_z(v, k) for k, v in enumerate(ffn_far_own, 1)]
    ffn_own, ffn_far_own, t_came = fence(ffn_own, ffn_far_own, t_came)
    out_keep, in_keep, send_last, gain_one_grad = finish(
        rows_in, gains, t_own, t_came, mid_grad, mid, acc_own, acc_came
    )
    small = small_sums(place, gain_one_grad, gain_two_grad, [lines[0], lines[2]])
    in_keep, send_last, small, ffn_own, near0, far0 = fence(
        in_keep, send_last, small, ffn_own, near0, far0
    )
    near1_x, far1_y, small, ffn_back[0] = fence(near1_x, far1_y, small, ffn_back[0])
    attn_y0, attn_y1, attn_x0, attn_x1 = merge_half(near0, near1_x, (far0,), (far1_y,))
    attn_y1, attn_x1 = swap_y(attn_y1), swap_x(attn_x1)
    attn_y1, attn_x1, attn_y0, attn_x0, send_last, ffn_back = fence(
        attn_y1, attn_x1, attn_y0, attn_x0, send_last, ffn_back
    )
    attn_own, *attn_far_own = merge_last(attn_y0, attn_y1, attn_x0, attn_x1)
    attn_back = [swap_z(v, k) for k, v in enumerate(attn_far_own, 1)]
    came_last = swap_x(send_last)
    ffn_total, ffn_squares = total_of(ffn_own, ffn_back)
    attn_own, ffn_total, ffn_squares, small = fence(attn_own, ffn_total, ffn_squares, small)
    attn_own, attn_back, came_last = fence(attn_own, attn_back, came_last)
    devices = 2 * depth * lax.axis_size("mp")
    attn_total, small = total_with(attn_own, attn_back, ffn_squares, small, devices)
    every_small = lax.all_to_all(small, ("dp", "mp"), 0, 0).reshape(small.shape)
    block_out, input_grad = place_rows(place, (out_keep, in_keep), came_last)
    olds = [
        *(attn_weights, attn_first, attn_second),
        *(ffn_weights, ffn_first, ffn_second),
        *(norm_gains, gain_first, gain_second),
        *(bias_table, table_first, table_second),
    ]
    grad_norm, attn_reduced, gain_grads, table_grads, *news = update(
        dp.astype(jnp.int32).reshape(1), every_small, attn_total, ffn_total, olds
    )
    return (
        block_out,
        input_grad,
        attn_reduced,
        ffn_total,
        gain_grads,
        table_grads,
        grad_norm.reshape(()),
        *news,
    )


def solution(mesh):
    placed = (
        P("dp", "mp", None),
        P("dp", "mp", None),
        P("dp"),
        P(None, "dp", "mp"),
        P(None, "dp", "mp"),
        P(None, "dp", "mp"),
        P(None, "dp", "mp"),
        P(None, "dp", "mp"),
        P(None, "dp", "mp"),
        P(None, "dp"),
        P(None, "dp"),
        P(None, "dp"),
        P(),
        P(),
        P(),
    )
    return jax.shard_map(
        per_device,
        mesh=mesh,
        in_specs=placed,
        out_specs=(
            P("dp", "mp", None),
            P("dp", "mp", None),
            P(None, "dp", "mp"),
            P(None, "dp", "mp"),
            P(None, "dp"),
            P(),
            P(),
            P(None, "dp", "mp"),
            P(None, "dp", "mp"),
            P(None, "dp", "mp"),
            P(None, "dp", "mp"),
            P(None, "dp", "mp"),
            P(None, "dp", "mp"),
            P(None, "dp"),
            P(None, "dp"),
            P(None, "dp"),
            P(),
            P(),
            P(),
        ),
        check_vma=False,
    )
```
